32 devices in a mesh: groups: 2 (over x), row: 16 (over z, y, core).
Axes of the slice: x: 2, y: 2, z: 4, core: 2. Of those that a mesh axis runs over, the one named last changes fastest.
Arguments:
- alignment_embedding: bfloat16 [256, 256, 256], P(('groups', 'row')), parts along dimension 0, may hold values from -6 to 6
- rescaling_factor: float32 [256], replicated, may hold values from 0.1 to 1.9
- recentering_offset: float32 [256], replicated, may hold values from -3 to 3
- first_side_coefficients: bfloat16 [256, 32], replicated, may hold values from -0.375 to 0.375
- first_side_offset: float32 [32], replicated, may hold values from -2 to 2
- second_side_coefficients: bfloat16 [256, 32], replicated, may hold values from -0.375 to 0.375
- second_side_offset: float32 [32], replicated, may hold values from -2 to 2
- final_projector_coefficients: bfloat16 [1024, 128], replicated, may hold values from -2 to 2
- final_projector_offset: float32 [128], replicated, may hold values from -2 to 2
Outputs:
- pair_update: bfloat16 [512, 256, 128], P(('groups', 'row')), parts along dimension 0
The draws below stay inside these ranges and needn't reach their ends.
There are 2 independent parts, one for each index of `groups`. The reference program is written for one: setup_inputs(seed, part) draws one part's arguments, and reference() takes and returns one part's arrays. A program takes and returns all parts, laid end to end along the dimension named above; an argument that names none is the same for every part. Nothing has to cross between parts.
All inputs are finite; a program needn't handle non-finite values.
Results may differ from the reference program's by a relative error of at most 0.0053.
Values may be sent and summed in bfloat16 or wider, within the bound.
No kernel may reach another device: no remote copies, remote signals or barrier semaphores. Data moves between devices by JAX's collectives and lax.ppermute only.
A program may use at most 192 MiB of HBM per device.

```python
import jax
import jax.numpy as jnp
from jax import lax

FEATURE_BREADTH = 256
PROJECTED_WIDTH = 32
C_Z = 128
RES_DEV = 16
ALIGNED_HOMOLOGS = 128
AMINO_ACID_TALLY = 256


def levels(own_key, dims, split, smallest, top_value):
    def one(position, shards_of):
        heights = jax.random.uniform(jax.random.fold_in(jax.random.fold_in(own_key, 6), position), (shards_of,), jnp.float32, smallest / len(split), top_value / len(split))
        return jnp.repeat(jnp.exp(heights), dims[position] // shards_of).reshape((-1,) + (1,) * (len(dims) - position - 1))

    level = one(*split[0])
    for cut in split[1:]:
        level = level * one(*cut)
    return level


def bell_draw(own_key, dims, deviation, most, pieces=(), dtype=jnp.bfloat16):
    gain = levels(own_key, dims, pieces, -0.22, 0.18) if pieces else 1.0
    drawn = jax.random.normal(own_key, dims, jnp.float32) * deviation * gain
    return jnp.minimum(jnp.maximum(drawn, -most), most).astype(dtype)


def setup_inputs(seed: int = 0, part: int = 0) -> dict:
    key_list = jax.random.split(jax.random.key(seed), 10)
    part_keys = jax.random.split(jax.random.fold_in(key_list[9], part), 10)
    alignment_embedding = bell_draw(part_keys[0], (ALIGNED_HOMOLOGS, AMINO_ACID_TALLY, FEATURE_BREADTH), 1.0, 6.0, ((0, 16),))
    rescaling_factor = jnp.clip(1.0 + 0.18 * jax.random.normal(key_list[1], (FEATURE_BREADTH,), jnp.float32), 0.1, 1.9)
    recentering_offset = bell_draw(key_list[2], (FEATURE_BREADTH,), 0.5, 3.0, (), jnp.float32)
    first_side_coefficients = bell_draw(key_list[3], (FEATURE_BREADTH, PROJECTED_WIDTH), FEATURE_BREADTH ** -0.5, 0.375)
    first_side_offset = bell_draw(key_list[4], (PROJECTED_WIDTH,), 0.3, 2.0, (), jnp.float32)
    second_side_coefficients = bell_draw(key_list[5], (FEATURE_BREADTH, PROJECTED_WIDTH), FEATURE_BREADTH ** -0.5, 0.375)
    second_side_offset = bell_draw(key_list[6], (PROJECTED_WIDTH,), 0.3, 2.0, (), jnp.float32)
    final_projector_coefficients = bell_draw(key_list[7], (PROJECTED_WIDTH * PROJECTED_WIDTH, C_Z), (max(1, PROJECTED_WIDTH * PROJECTED_WIDTH // ALIGNED_HOMOLOGS)) ** -0.5, 2.0)
    final_projector_offset = bell_draw(key_list[8], (C_Z,), 0.3, 2.0, (), jnp.float32)
    return {"alignment_embedding": alignment_embedding, "rescaling_factor": rescaling_factor, "recentering_offset": recentering_offset, "first_side_coefficients": first_side_coefficients, "first_side_offset": first_side_offset, "second_side_coefficients": second_side_coefficients, "second_side_offset": second_side_offset, "final_projector_coefficients": final_projector_coefficients, "final_projector_offset": final_projector_offset}


def standardize_features(values, rescaling_factor, recentering_offset):
    values = values.astype(jnp.float32)
    center = lax.optimization_barrier(jnp.mean(values, axis=-1, keepdims=True))
    spread = lax.optimization_barrier(jnp.mean(jnp.square(values - center), axis=-1, keepdims=True))
    return (values - center) * lax.rsqrt(spread + 1e-05) * rescaling_factor + recentering_offset

def reference(alignment_embedding, rescaling_factor, recentering_offset, first_side_coefficients, first_side_offset, second_side_coefficients, second_side_offset, final_projector_coefficients, final_projector_offset):
    standardized_alignment = standardize_features(alignment_embedding, rescaling_factor, recentering_offset).astype(jnp.bfloat16)
    unrolled_lines = standardized_alignment.reshape(-1, FEATURE_BREADTH)
    left_proj = (jnp.dot(unrolled_lines, first_side_coefficients, preferred_element_type=jnp.float32) + first_side_offset).astype(jnp.bfloat16).reshape(ALIGNED_HOMOLOGS, AMINO_ACID_TALLY, PROJECTED_WIDTH)
    right_proj = (jnp.dot(unrolled_lines, second_side_coefficients, preferred_element_type=jnp.float32) + second_side_offset).astype(jnp.bfloat16).reshape(ALIGNED_HOMOLOGS, AMINO_ACID_TALLY, PROJECTED_WIDTH)
    right_wide = right_proj.astype(jnp.float32)
    left_blocks = left_proj.reshape(ALIGNED_HOMOLOGS, AMINO_ACID_TALLY // RES_DEV, RES_DEV, PROJECTED_WIDTH).transpose(1, 0, 2, 3)

    def block_rows(left_block):
        summed = jnp.einsum('sic,sje->ijce', left_block.astype(jnp.float32), right_wide)
        outer = (summed / ALIGNED_HOMOLOGS).astype(jnp.bfloat16).reshape(RES_DEV * AMINO_ACID_TALLY, PROJECTED_WIDTH * PROJECTED_WIDTH)
        result = jnp.dot(outer, final_projector_coefficients, preferred_element_type=jnp.float32) + final_projector_offset
        return result.astype(jnp.bfloat16).reshape(RES_DEV, AMINO_ACID_TALLY, C_Z)
    stacked = lax.map(block_rows, left_blocks)
    return stacked.reshape(AMINO_ACID_TALLY, AMINO_ACID_TALLY, C_Z)
```

```python
import functools

import jax
import jax.numpy as jnp
from jax import lax
from jax.experimental import pallas as pl
from jax.experimental.pallas import tpu as pltpu
from jax.sharding import PartitionSpec as P

VMEM_LIMIT = 48 * 1024 * 1024


def repeat_rows(values, times):
    rows, cols = values.shape
    return jnp.broadcast_to(values[:, None, :], (rows, times, cols)).reshape(rows * times, cols)


def project_kernel(
    rows_here,
    x_ref,
    gain_ref,
    shift_ref,
    first_ref,
    first_offset_ref,
    second_ref,
    second_offset_ref,
    *refs,
):
    messages, left_ref = refs[:-1], refs[-1]
    samples, residues, _ = x_ref.shape
    hidden = first_ref.shape[0]
    width = samples * hidden
    first = jnp.concatenate([first_ref[...].astype(jnp.float32)] * samples, axis=0)
    second = repeat_rows(second_ref[...].astype(jnp.float32), samples)
    row = lax.broadcasted_iota(jnp.int32, (width, 1), 0)
    spot = lax.broadcasted_iota(jnp.int32, (hidden, width), 1)
    channel = lax.broadcasted_iota(jnp.int32, (hidden, width), 0)

    def spread(offset_ref, owner):
        return jnp.dot(
            offset_ref[...],
            (owner == channel).astype(jnp.float32),
            precision=lax.Precision.HIGHEST,
            preferred_element_type=jnp.float32,
        )

    left = jnp.zeros((residues, width), jnp.float32)
    right = jnp.zeros((residues, width), jnp.float32)
    for s in range(samples):
        values = x_ref[s].astype(jnp.float32)
        center = jnp.mean(values, axis=-1, keepdims=True)
        values = values - center
        spread_of = jnp.mean(jnp.square(values), axis=-1, keepdims=True)
        normed = (values * lax.rsqrt(spread_of + 1e-05) * gain_ref[...] + shift_ref[...]).astype(
            jnp.bfloat16
        )
        first_here = jnp.where(row // hidden == s, first, 0.0).astype(jnp.bfloat16)
        second_here = jnp.where(row % samples == s, second, 0.0).astype(jnp.bfloat16)
        dims = (((1,), (1,)), ((), ()))
        left += lax.dot_general(normed, first_here, dims, preferred_element_type=jnp.float32)
        right += lax.dot_general(normed, second_here, dims, preferred_element_type=jnp.float32)
    left_ref[...] = (left + spread(first_offset_ref, spot % hidden)).astype(jnp.bfloat16)
    right = (right + spread(second_offset_ref, spot // samples)).astype(jnp.bfloat16)

    blocks = len(messages)
    here = lax.axis_index("row") * rows_here * blocks // residues
    for step, message in enumerate(messages):
        start = lax.rem(here + step, blocks) * (residues // blocks)
        start = pl.multiple_of(start, residues // blocks)
        message[:residues, :] = right
        message[residues:, :] = left_ref[pl.ds(start, residues // blocks), :]


def pair_kernel(count, rows_here, samples, begins, ends, *refs):
    refs = list(refs)
    messages = [refs.pop(0) for _ in range(count)]
    weight_ref = refs.pop(0)
    offset_ref = refs.pop(0)
    total_ref = None if begins else refs.pop(0)
    out_ref, mixed_ref = refs
    width, columns = weight_ref.shape
    channels = offset_ref.shape[1]
    hidden = columns // channels
    here = width // hidden
    extra, residues = None, None
    residues = out_ref.shape[1] if ends else out_ref.shape[0]
    extra = messages[0].shape[0] - residues
    slot = lax.rem(lax.axis_index("row"), extra // rows_here)
    start = pl.multiple_of(residues + slot * rows_here, rows_here)

    row = lax.broadcasted_iota(jnp.int32, (rows_here * here, width), 0)
    lane = lax.broadcasted_iota(jnp.int32, (rows_here * here, width), 1)
    keep = lane // hidden == row % here
    picked = []
    for message in messages:
        left = message[pl.ds(start, rows_here), :].astype(jnp.float32)
        picked.append(jnp.where(keep, repeat_rows(left, here), 0.0).astype(jnp.bfloat16))
    picked = jnp.concatenate(picked, axis=0)

    group = 8
    for chunk in range(hidden // group):
        mixed = jnp.dot(
            picked,
            weight_ref[:, chunk * group * channels : (chunk + 1) * group * channels],
            preferred_element_type=jnp.float32,
        )
        for n in range(count):
            for i in range(rows_here):
                top = (n * rows_here + i) * here
                piece = jnp.concatenate(
                    [mixed[top : top + here, e * channels : (e + 1) * channels] for e in range(group)],
                    axis=0,
                )
                low = n * width + chunk * group * here
                mixed_ref[low : low + group * here, i * channels : (i + 1) * channels] = piece.astype(
                    jnp.bfloat16
                )

    right = jnp.concatenate([message[:residues, :] for message in messages], axis=1)
    pair = 2
    for i in range(0, rows_here, pair):
        cols = slice(i * channels, (i + pair) * channels)
        value = jnp.dot(right, mixed_ref[:, cols], preferred_element_type=jnp.float32)
        if not begins:
            value = value + total_ref[:, cols]
        if ends:
            for k in range(pair):
                part = value[:, k * channels : (k + 1) * channels]
                out_ref[i + k] = (part * (1.0 / samples) + offset_ref[...]).astype(jnp.bfloat16)
        else:
            out_ref[:, cols] = value


def per_device(
    size,
    alignment_embedding,
    rescaling_factor,
    recentering_offset,
    first_side_coefficients,
    first_side_offset,
    second_side_coefficients,
    second_side_offset,
    final_projector_coefficients,
    final_projector_offset,
):
    here, residues, features = alignment_embedding.shape
    hidden = first_side_coefficients.shape[1]
    channels = final_projector_coefficients.shape[1]
    width = here * hidden
    samples = here * size
    rows_here = residues // size
    near = 4
    blocks = size // near
    message = jax.ShapeDtypeStruct((residues + residues // blocks, width), jnp.bfloat16)

    vmem = pl.BlockSpec(memory_space=pltpu.VMEM)
    messages = pl.pallas_call(
        functools.partial(project_kernel, rows_here),
        out_shape=[message] * blocks,
        in_specs=[vmem] * 7,
        out_specs=[vmem] * blocks,
        scratch_shapes=[pltpu.VMEM((residues, width), jnp.bfloat16)],
        compiler_params=pltpu.CompilerParams(vmem_limit_bytes=VMEM_LIMIT),
    )(
        alignment_embedding,
        rescaling_factor.reshape(1, features),
        recentering_offset.reshape(1, features),
        first_side_coefficients.T,
        first_side_offset.reshape(1, hidden),
        second_side_coefficients.T,
        second_side_offset.reshape(1, hidden),
    )

    def send(value, target):
        return lax.ppermute(value, "row", [(r, target(r)) for r in range(size)])

    weight = jnp.tile(final_projector_coefficients.reshape(hidden, hidden * channels), (here, 1))
    offset = final_projector_offset.reshape(1, channels)
    total = None
    for step in range(blocks):
        one = messages[0] if step == 0 else send(messages[step], lambda r: (r + near * step) % size)
        two = send(one, lambda r: r ^ 2)
        group = [one, two, send(one, lambda r: r ^ 1), send(two, lambda r: r ^ 1)]
        begins, ends = step == 0, step == blocks - 1
        operands = group + [weight, offset] + ([] if begins else [total])
        if ends:
            result = jax.ShapeDtypeStruct((rows_here, residues, channels), jnp.bfloat16)
        else:
            result = jax.ShapeDtypeStruct((residues, rows_here * channels), jnp.float32)
        total = pl.pallas_call(
            functools.partial(pair_kernel, len(group), rows_here, samples, begins, ends),
            out_shape=result,
            in_specs=[vmem] * len(operands),
            out_specs=vmem,
            scratch_shapes=[pltpu.VMEM((len(group) * width, rows_here * channels), jnp.bfloat16)],
            compiler_params=pltpu.CompilerParams(vmem_limit_bytes=VMEM_LIMIT),
        )(*operands)
    return total


def solution(mesh):
    return jax.shard_map(
        functools.partial(per_device, mesh.shape["row"]),
        mesh=mesh,
        in_specs=(P(("groups", "row"), None, None), P(), P(), P(), P(), P(), P(), P(), P()),
        out_specs=P(("groups", "row"), None, None),
        check_vma=False,
    )
```

```python
import functools

import jax
import jax.numpy as jnp
from jax import lax
from jax.experimental import pallas as pl
from jax.experimental.pallas import tpu as pltpu
from jax.sharding import PartitionSpec as P

MIB = 1024 * 1024


def repeat_rows(values, times):
    rows, cols = values.shape
    return jnp.broadcast_to(values[:, None, :], (rows, times, cols)).reshape(rows * times, cols)


def place_of(device, half):
    chip = device // 2
    return chip // 2 + (chip % 2) * (2 * half - 1 - 2 * (chip // 2))


def chip_at(place, half):
    return jnp.where(place < half, 2 * place, 2 * (2 * half - 1 - place) + 1)


def project_kernel(
    rows_here,
    x_hbm,
    gain_hbm,
    shift_hbm,
    first_hbm,
    first_offset_hbm,
    second_hbm,
    second_offset_hbm,
    keep_ref,
    give_ref,
    x_ref,
    gain_ref,
    shift_ref,
    first_ref,
    first_offset_ref,
    second_ref,
    second_offset_ref,
    left_ref,
    sems,
):
    samples, residues, _ = x_ref.shape
    hidden = first_ref.shape[0]
    width = samples * hidden
    small = [
        (first_hbm, first_ref),
        (second_hbm, second_ref),
        (gain_hbm, gain_ref),
        (shift_hbm, shift_ref),
        (first_offset_hbm, first_offset_ref),
        (second_offset_hbm, second_offset_ref),
    ]
    copies = [pltpu.make_async_copy(x_hbm.at[0], x_ref.at[0], sems.at[0])]
    copies += [
        pltpu.make_async_copy(src, dst, sems.at[samples + n]) for n, (src, dst) in enumerate(small)
    ]
    copies += [pltpu.make_async_copy(x_hbm.at[s], x_ref.at[s], sems.at[s]) for s in range(1, samples)]
    for copy in copies:
        copy.start()
    for copy in copies[1 : 1 + len(small)]:
        copy.wait()

    first = jnp.concatenate([first_ref[...].astype(jnp.float32)] * samples, axis=0)
    second = repeat_rows(second_ref[...].astype(jnp.float32), samples)
    row = lax.broadcasted_iota(jnp.int32, (width, 1), 0)
    spot = lax.broadcasted_iota(jnp.int32, (hidden, width), 1)
    channel = lax.broadcasted_iota(jnp.int32, (hidden, width), 0)

    def spread(offset_ref, owner):
        return jnp.dot(
            offset_ref[...],
            (owner == channel).astype(jnp.float32),
            precision=lax.Precision.HIGHEST,
            preferred_element_type=jnp.float32,
        )

    first_offset = spread(first_offset_ref, spot % hidden)
    second_offset = spread(second_offset_ref, spot // samples)
    left = jnp.zeros((residues, width), jnp.float32)
    right = jnp.zeros((residues, width), jnp.float32)
    dims = (((1,), (1,)), ((), ()))
    for s in range(samples):
        if s == 0:
            copies[0].wait()
        else:
            copies[len(small) + s].wait()
        values = x_ref[s].astype(jnp.float32)
        center = jnp.mean(values, axis=-1, keepdims=True)
        values = values - center
        variance = jnp.mean(jnp.square(values), axis=-1, keepdims=True)
        normed = (values * lax.rsqrt(variance + 1e-05) * gain_ref[...] + shift_ref[...]).astype(
            jnp.bfloat16
        )
        first_here = jnp.where(row // hidden == s, first, 0.0).astype(jnp.bfloat16)
        second_here = jnp.where(row % samples == s, second, 0.0).astype(jnp.bfloat16)
        left += lax.dot_general(normed, first_here, dims, preferred_element_type=jnp.float32)
        right += lax.dot_general(normed, second_here, dims, preferred_element_type=jnp.float32)
    left_ref[...] = (left + first_offset).astype(jnp.bfloat16)
    right = (right + second_offset).astype(jnp.bfloat16)
    keep_ref[:residues, :] = right
    give_ref[:residues, :] = right

    device = lax.axis_index("row")
    per_chip = 2 * rows_here
    half = residues // per_chip // 2
    way = 1 - 2 * (device % 2)
    place = place_of(device, half)
    for n in range(half):
        low = residues + n * per_chip
        for message, ahead in ((keep_ref, way * (half - n)), (give_ref, -way * (half - 1 - n))):
            chip = chip_at(lax.rem(place + ahead + 2 * half, 2 * half), half)
            start = pl.multiple_of(chip * per_chip, per_chip)
            message[low : low + per_chip, :] = left_ref[pl.ds(start, per_chip), :]


def pair_kernel(count, rows_here, samples, begins, ends, *refs):
    refs = list(refs)
    messages = [refs.pop(0) for _ in range(count)]
    if begins:
        final_ref, total_out, weight_ref, mixed_ref, wide_ref = refs
    elif ends:
        weight_ref, total_ref, offset_ref, out_hbm, mixed_ref, out_ref, sems = refs
    else:
        weight_ref, total_ref, total_out, mixed_ref = refs
    width, columns = weight_ref.shape
    channels = mixed_ref.shape[1] // rows_here
    hidden = columns // channels
    here = width // hidden
    residues = (total_out if begins else total_ref).shape[0]
    core = lax.rem(lax.axis_index("row"), 2)

    if begins:
        wide_ref[...] = final_ref[...].astype(jnp.float32)
        for e in range(hidden):
            rows = wide_ref[pl.ds(e, hidden, stride=hidden), :].astype(jnp.bfloat16)
            weight_ref[:, e * channels : (e + 1) * channels] = jnp.concatenate([rows] * here, axis=0)

    row = lax.broadcasted_iota(jnp.int32, (rows_here * here, width), 0)
    lane = lax.broadcasted_iota(jnp.int32, (rows_here * here, width), 1)
    mine = lane // hidden == row % here
    picked = []
    for message in messages:
        start = pl.multiple_of(message.shape[0] - (2 - core) * rows_here, rows_here)
        left = message[pl.ds(start, rows_here), :].astype(jnp.float32)
        picked.append(jnp.where(mine, repeat_rows(left, here), 0.0).astype(jnp.bfloat16))
    picked = jnp.concatenate(picked, axis=0)

    group = 8
    for chunk in range(hidden // group):
        mixed = jnp.dot(
            picked,
            weight_ref[:, chunk * group * channels : (chunk + 1) * group * channels],
            preferred_element_type=jnp.float32,
        )
        for n in range(count):
            for i in range(rows_here):
                top = (n * rows_here + i) * here
                piece = jnp.concatenate(
                    [mixed[top : top + here, e * channels : (e + 1) * channels] for e in range(group)],
                    axis=0,
                )
                low = n * width + chunk * group * here
                mixed_ref[low : low + group * here, i * channels : (i + 1) * channels] = piece.astype(
                    jnp.bfloat16
                )

    right = jnp.concatenate([message[:residues, :] for message in messages], axis=1)
    pair = 2
    copies = []
    for i in range(0, rows_here, pair):
        cols = slice(i * channels, (i + pair) * channels)
        value = jnp.dot(right, mixed_ref[:, cols], preferred_element_type=jnp.float32)
        if not begins:
            value = value + total_ref[:, cols]
        if ends:
            for k in range(pair):
                part = value[:, k * channels : (k + 1) * channels]
                out_ref[i + k] = (part * (1.0 / samples) + offset_ref[...]).astype(jnp.bfloat16)
            copies.append(
                pltpu.make_async_copy(
                    out_ref.at[pl.ds(i, pair)], out_hbm.at[pl.ds(i, pair)], sems.at[i // pair]
                )
            )
            copies[-1].start()
        else:
            total_out[:, cols] = value
    for copy in copies:
        copy.wait()


def per_device(
    size,
    alignment_embedding,
    rescaling_factor,
    recentering_offset,
    first_side_coefficients,
    first_side_offset,
    second_side_coefficients,
    second_side_offset,
    final_projector_coefficients,
    final_projector_offset,
):
    here, residues, features = alignment_embedding.shape
    hidden = first_side_coefficients.shape[1]
    channels = final_projector_coefficients.shape[1]
    width = here * hidden
    samples = here * size
    rows_here = residues // size
    per_chip = 2 * rows_here
    half = size // 4
    message = jax.ShapeDtypeStruct((residues + half * per_chip, width), jnp.bfloat16)

    vmem = pl.BlockSpec(memory_space=pltpu.VMEM)
    hbm = pl.BlockSpec(memory_space=pltpu.HBM)
    keep, give = pl.pallas_call(
        functools.partial(project_kernel, rows_here),
        out_shape=[message] * 2,
        in_specs=[hbm] * 7,
        out_specs=[vmem] * 2,
        scratch_shapes=[
            pltpu.VMEM((here, residues, features), jnp.bfloat16),
            pltpu.VMEM((1, features), jnp.float32),
            pltpu.VMEM((1, features), jnp.float32),
            pltpu.VMEM((hidden, features), jnp.bfloat16),
            pltpu.VMEM((1, hidden), jnp.float32),
            pltpu.VMEM((hidden, features), jnp.bfloat16),
            pltpu.VMEM((1, hidden), jnp.float32),
            pltpu.VMEM((residues, width), jnp.bfloat16),
            pltpu.SemaphoreType.DMA((here + 6,)),
        ],
        compiler_params=pltpu.CompilerParams(vmem_limit_bytes=32 * MIB),
        cost_estimate=pl.CostEstimate(
            flops=4 * here * residues * features * width,
            bytes_accessed=2 * here * residues * features,
            transcendentals=0,
        ),
    )(
        *[
            pltpu.with_memory_space_constraint(value, pltpu.HBM)
            for value in (
                alignment_embedding,
                rescaling_factor.reshape(1, features),
                recentering_offset.reshape(1, features),
                first_side_coefficients.T,
                first_side_offset.reshape(1, hidden),
                second_side_coefficients.T,
                second_side_offset.reshape(1, hidden),
            )
        ]
    )

    by_place = {(place_of(r, half), r % 2): r for r in range(size)}
    around = [
        (r, by_place[(place_of(r, half) + 1 - 2 * (r % 2)) % (2 * half), r % 2]) for r in range(size)
    ]
    across = [(r, r ^ 1) for r in range(size)]

    def pass_on(value):
        return lax.ppermute(value, "row", around)

    def swap(value):
        return lax.ppermute(value, "row", across)

    def accumulate(messages, total, weight, ends):
        begins = total is None
        flat = jax.ShapeDtypeStruct((residues, rows_here * channels), jnp.float32)
        spread = jax.ShapeDtypeStruct((width, hidden * channels), jnp.bfloat16)
        scratch = [pltpu.VMEM((len(messages) * width, rows_here * channels), jnp.bfloat16)]
        operands = list(messages)
        if begins:
            operands += [final_projector_coefficients]
            result, out_specs = [flat, spread], [vmem, vmem]
            scratch += [pltpu.VMEM(final_projector_coefficients.shape, jnp.float32)]
        elif ends:
            operands += [weight, total, final_projector_offset.reshape(1, channels)]
            result = jax.ShapeDtypeStruct((rows_here, residues, channels), jnp.bfloat16)
            out_specs = hbm
            scratch += [
                pltpu.VMEM((rows_here, residues, channels), jnp.bfloat16),
                pltpu.SemaphoreType.DMA((rows_here,)),
            ]
        else:
            operands += [weight, total]
            result, out_specs = flat, vmem
        work = 4 * len(messages) * residues * width * rows_here * channels
        return pl.pallas_call(
            functools.partial(pair_kernel, len(messages), rows_here, samples, begins, ends),
            out_shape=result,
            in_specs=[vmem] * len(operands),
            out_specs=out_specs,
            scratch_shapes=scratch,
            compiler_params=pltpu.CompilerParams(vmem_limit_bytes=32 * MIB),
            cost_estimate=pl.CostEstimate(flops=work, bytes_accessed=4 * MIB, transcendentals=0),
        )(*operands)

    given = swap(give)
    flying = [keep, given[: residues + (half - 1) * per_chip]]
    total, weight = accumulate([give, given], None, None, False)
    for step in range(1, half + 1):
        landed = [pass_on(value) for value in flying]
        messages = landed + [swap(value) for value in landed]
        total = accumulate(messages, total, weight, step == half)
        if step < half:
            flying = [value[: value.shape[0] - per_chip] for value in landed]
            if step == half - 1:
                flying = flying[:1]
    return total


def solution(mesh):
    return jax.shard_map(
        functools.partial(per_device, mesh.shape["row"]),
        mesh=mesh,
        in_specs=(P(("groups", "row"), None, None), P(), P(), P(), P(), P(), P(), P(), P()),
        out_specs=P(("groups", "row"), None, None),
        check_vma=False,
    )
```

```python
import functools
import math

import jax
import jax.numpy as jnp
from jax import lax
from jax.experimental import pallas as pl
from jax.experimental.pallas import tpu as pltpu
from jax.sharding import PartitionSpec as P

MIB = 1024 * 1024
LANES = 128


def repeat_rows(values, times):
    rows, cols = values.shape
    return jnp.broadcast_to(values[:, None, :], (rows, times, cols)).reshape(rows * times, cols)


def place_of(device, half):
    chip = device // 2
    return chip // 2 + (chip % 2) * (2 * half - 1 - 2 * (chip // 2))


def chip_at(place, half):
    return jnp.where(place < half, 2 * place, 2 * (2 * half - 1 - place) + 1)


def project_kernel(
    rows_here,
    x_hbm,
    gain_hbm,
    shift_hbm,
    first_hbm,
    first_offset_hbm,
    second_hbm,
    second_offset_hbm,
    keep_ref,
    give_ref,
    x_ref,
    gain_ref,
    shift_ref,
    first_ref,
    first_offset_ref,
    second_ref,
    second_offset_ref,
    packed_ref,
    left_ref,
    sems,
):
    samples, residues, features = x_ref.shape
    hidden = first_ref.shape[0]
    width = samples * hidden
    tile = keep_ref.shape[1]
    tiles = residues // tile
    fold = LANES // hidden
    groups = residues // fold
    small = [
        (first_hbm, first_ref),
        (second_hbm, second_ref),
        (gain_hbm, gain_ref),
        (shift_hbm, shift_ref),
        (first_offset_hbm, first_offset_ref),
        (second_offset_hbm, second_offset_ref),
    ]
    copies = [pltpu.make_async_copy(x_hbm.at[0], x_ref.at[0], sems.at[0])]
    copies += [
        pltpu.make_async_copy(src, dst, sems.at[samples + n]) for n, (src, dst) in enumerate(small)
    ]
    copies += [pltpu.make_async_copy(x_hbm.at[s], x_ref.at[s], sems.at[s]) for s in range(1, samples)]
    for copy in copies:
        copy.start()
    for copy in copies[1 : 1 + len(small)]:
        copy.wait()

    first = jnp.concatenate([first_ref[...]] * fold, axis=0)
    first_offset = jnp.concatenate([first_offset_ref[...]] * fold, axis=1)
    second = repeat_rows(second_ref[...].astype(jnp.float32), samples)
    row = lax.broadcasted_iota(jnp.int32, (width, 1), 0)
    spot = lax.broadcasted_iota(jnp.int32, (width, hidden), 0)
    channel = lax.broadcasted_iota(jnp.int32, (width, hidden), 1)
    second_offset = jnp.sum(
        jnp.where(spot // samples == channel, second_offset_ref[...], 0.0), axis=1, keepdims=True
    )
    residue = lax.broadcasted_iota(jnp.int32, (tile, LANES), 0)
    lane = lax.broadcasted_iota(jnp.int32, (tile, LANES), 1)
    own = residue % fold == lane // hidden
    group = lax.broadcasted_iota(jnp.int32, (tile // fold, tile), 0)
    member = lax.broadcasted_iota(jnp.int32, (tile // fold, tile), 1)
    gather = (member // fold == group).astype(jnp.bfloat16)

    dims = (((1,), (1,)), ((), ()))
    right = [jnp.zeros((width, tile), jnp.float32) for _ in range(tiles)]
    for s in range(samples):
        if s == 0:
            copies[0].wait()
        else:
            copies[len(small) + s].wait()
        values = x_ref[s].astype(jnp.float32)
        center = jnp.mean(values, axis=-1, keepdims=True)
        values = values - center
        variance = jnp.mean(jnp.square(values), axis=-1, keepdims=True)
        normed = (values * lax.rsqrt(variance + 1e-05) * gain_ref[...] + shift_ref[...]).astype(
            jnp.bfloat16
        )
        second_here = jnp.where(row % samples == s, second, 0.0).astype(jnp.bfloat16)
        for t in range(tiles):
            part = normed[t * tile : (t + 1) * tile]
            right[t] += lax.dot_general(second_here, part, dims, preferred_element_type=jnp.float32)
            left = lax.dot_general(part, first, dims, preferred_element_type=jnp.float32)
            left = jnp.where(own, left + first_offset, 0.0).astype(jnp.bfloat16)
            low = s * groups + t * (tile // fold)
            packed_ref[low : low + tile // fold, :] = jnp.dot(
                gather, left, preferred_element_type=jnp.float32
            )
    for t in range(tiles):
        value = (right[t] + second_offset).astype(jnp.bfloat16)
        keep_ref[t * width : (t + 1) * width, :] = value
        give_ref[t * width : (t + 1) * width, :] = value
    across = tile // LANES
    for low in range(0, groups, across):
        at = low // across * samples
        left_ref[at : at + samples, :] = jnp.concatenate(
            [packed_ref[pl.ds(low + n, samples, stride=groups), :] for n in range(across)], axis=1
        )

    device = lax.axis_index("row")
    per_chip = 2 * rows_here * hidden * samples // tile
    half = residues // rows_here // 4
    base = tiles * width
    way = 1 - 2 * (device % 2)
    place = place_of(device, half)
    for n in range(half):
        low = base + n * per_chip
        for message, ahead in ((keep_ref, way * (half - n)), (give_ref, -way * (half - 1 - n))):
            chip = chip_at(lax.rem(place + ahead + 2 * half, 2 * half), half)
            start = pl.multiple_of(chip * per_chip, per_chip)
            message[low : low + per_chip, :] = left_ref[pl.ds(start, per_chip), :].astype(jnp.bfloat16)


def weight_kernel(final_ref, out_ref, wide_ref):
    channels, columns = out_ref.shape
    hidden = math.isqrt(columns)
    wide_ref[...] = final_ref[...].astype(jnp.float32)
    step = LANES // hidden
    for e in range(0, hidden, step):
        rows = [wide_ref[pl.ds(e + n, hidden, stride=hidden), :] for n in range(step)]
        out_ref[:, e * hidden : (e + step) * hidden] = jnp.concatenate(rows, axis=0).T.astype(
            jnp.bfloat16
        )


def pair_kernel(count, gridded, rows_here, hidden, samples, *refs):
    refs = list(refs)
    rights = [refs.pop(0) for _ in range(count)]
    lefts = [refs.pop(0) for _ in range(count)] if gridded else rights
    weight_ref, offset_ref, out_hbm, left_ref, outer_ref, out_ref, sems = refs
    tile = rights[0].shape[1]
    here = samples // count
    span = rows_here * hidden
    deep = span * here // tile
    core = lax.rem(lax.axis_index("row"), 2)
    pieces = []
    for ref in lefts:
        start = pl.multiple_of(ref.shape[0] - (2 - core) * deep, deep)
        piece = ref[pl.ds(start, deep), :].astype(jnp.float32)
        pieces.append(
            jnp.concatenate([piece[n * here : (n + 1) * here] for n in range(span // tile)], axis=1)
        )
    left_ref[...] = jnp.concatenate(pieces, axis=0).T.astype(jnp.bfloat16)

    left = left_ref[...]
    for e in range(0, hidden, 2):
        both = [ref[e * here : (e + 2) * here, :].astype(jnp.float32) for ref in rights]
        for k in range(2):
            right = jnp.concatenate([x[k * here : (k + 1) * here] for x in both], axis=0)
            outer = jnp.dot(left, right.astype(jnp.bfloat16), preferred_element_type=jnp.float32)
            outer = outer.astype(jnp.bfloat16)
            for i in range(rows_here):
                outer_ref[i, (e + k) * hidden : (e + k + 1) * hidden, :] = outer[
                    i * hidden : (i + 1) * hidden
                ]

    first = pl.program_id(0) * tile if gridded else 0
    copies = []
    for i in range(rows_here):
        value = jnp.dot(weight_ref[...], outer_ref[i], preferred_element_type=jnp.float32)
        value = value.T * (1.0 / samples) + offset_ref[...]
        out_ref[i] = value.astype(jnp.bfloat16)
        copies.append(
            pltpu.make_async_copy(out_ref.at[i], out_hbm.at[i, pl.ds(first, tile)], sems.at[i])
        )
        copies[-1].start()
    for copy in copies:
        copy.wait()


def per_device(
    size,
    alignment_embedding,
    rescaling_factor,
    recentering_offset,
    first_side_coefficients,
    first_side_offset,
    second_side_coefficients,
    second_side_offset,
    final_projector_coefficients,
    final_projector_offset,
):
    here, residues, features = alignment_embedding.shape
    hidden = first_side_coefficients.shape[1]
    channels = final_projector_coefficients.shape[1]
    width = here * hidden
    samples = here * size
    rows_here = residues // size
    half = size // 4
    tile = 256
    tiles = residues // tile
    body = tiles * width
    per_chip = 2 * rows_here * width // tile
    message = jax.ShapeDtypeStruct((body + half * per_chip, tile), jnp.bfloat16)

    vmem = pl.BlockSpec(memory_space=pltpu.VMEM)
    hbm = pl.BlockSpec(memory_space=pltpu.HBM)
    keep, give = pl.pallas_call(
        functools.partial(project_kernel, rows_here),
        out_shape=[message] * 2,
        in_specs=[hbm] * 7,
        out_specs=[vmem] * 2,
        scratch_shapes=[
            pltpu.VMEM((here, residues, features), jnp.bfloat16),
            pltpu.VMEM((1, features), jnp.float32),
            pltpu.VMEM((1, features), jnp.float32),
            pltpu.VMEM((hidden, features), jnp.bfloat16),
            pltpu.VMEM((1, hidden), jnp.float32),
            pltpu.VMEM((hidden, features), jnp.bfloat16),
            pltpu.VMEM((1, hidden), jnp.float32),
            pltpu.VMEM((residues * width // LANES, LANES), jnp.float32),
            pltpu.VMEM((residues * width // tile, tile), jnp.float32),
            pltpu.SemaphoreType.DMA((here + 6,)),
        ],
        compiler_params=pltpu.CompilerParams(vmem_limit_bytes=32 * MIB),
        cost_estimate=pl.CostEstimate(
            flops=4 * here * residues * features * width,
            bytes_accessed=2 * here * residues * features,
            transcendentals=0,
        ),
    )(
        *[
            pltpu.with_memory_space_constraint(value, pltpu.HBM)
            for value in (
                alignment_embedding,
                rescaling_factor.reshape(1, features),
                recentering_offset.reshape(1, features),
                first_side_coefficients.T,
                first_side_offset.reshape(1, hidden),
                second_side_coefficients.T,
                second_side_offset.reshape(1, hidden),
            )
        ]
    )
    weight = pl.pallas_call(
        weight_kernel,
        out_shape=jax.ShapeDtypeStruct((channels, hidden * hidden), jnp.bfloat16),
        in_specs=[vmem],
        out_specs=vmem,
        scratch_shapes=[pltpu.VMEM((hidden * hidden, channels), jnp.float32)],
        cost_estimate=pl.CostEstimate(flops=2**28, bytes_accessed=2**20, transcendentals=0),
    )(final_projector_coefficients)

    by_place = {(place_of(r, half), r % 2): r for r in range(size)}
    around = [
        (r, by_place[(place_of(r, half) + 1 - 2 * (r % 2)) % (2 * half), r % 2]) for r in range(size)
    ]
    across = [(r, r ^ 1) for r in range(size)]

    def pass_on(value):
        return lax.ppermute(value, "row", around)

    def swap(value):
        return lax.ppermute(value, "row", across)

    given = swap(give)
    flying = [keep, given[: body + (half - 1) * per_chip]]
    messages = [give, given]
    for step in range(1, half + 1):
        landed = [pass_on(value) for value in flying]
        messages += landed + [swap(value) for value in landed]
        flying = [value[: value.shape[0] - per_chip] for value in landed]
        if step == half - 1:
            flying = flying[:1]

    count = len(messages)
    gridded = tiles > 1
    offset = final_projector_offset.reshape(1, channels)
    if gridded:
        operands = messages + messages
        specs = [pl.BlockSpec((width, tile), lambda t: (t, 0)) for _ in messages]
        specs += [
            pl.BlockSpec((per_chip, tile), lambda t, last=m.shape[0] // per_chip - 1: (last, 0))
            for m in messages
        ]
        specs += [
            pl.BlockSpec((channels, hidden * hidden), lambda t: (0, 0)),
            pl.BlockSpec((1, channels), lambda t: (0, 0)),
        ]
        grid = (tiles,)
    else:
        operands = messages
        specs = [vmem] * (count + 2)
        grid = ()
    return pl.pallas_call(
        functools.partial(pair_kernel, count, gridded, rows_here, hidden, samples),
        out_shape=jax.ShapeDtypeStruct((rows_here, residues, channels), jnp.bfloat16),
        grid=grid,
        in_specs=specs,
        out_specs=hbm,
        scratch_shapes=[
            pltpu.VMEM((rows_here * hidden, samples), jnp.bfloat16),
            pltpu.VMEM((rows_here, hidden * hidden, tile), jnp.bfloat16),
            pltpu.VMEM((rows_here, tile, channels), jnp.bfloat16),
            pltpu.SemaphoreType.DMA((rows_here,)),
        ],
        compiler_params=pltpu.CompilerParams(vmem_limit_bytes=40 * MIB),
    )(*operands, weight, offset)


def solution(mesh):
    return jax.shard_map(
        functools.partial(per_device, mesh.shape["row"]),
        mesh=mesh,
        in_specs=(P(("groups", "row"), None, None), P(), P(), P(), P(), P(), P(), P(), P()),
        out_specs=P(("groups", "row"), None, None),
        check_vma=False,
    )
```

```python
import functools
import math

import jax
import jax.numpy as jnp
from jax import lax
from jax.experimental import pallas as pl
from jax.experimental.pallas import tpu as pltpu
from jax.sharding import PartitionSpec as P

MIB = 1024 * 1024
LANES = 128
CHUNKS = 2


def repeat_rows(values, times):
    rows, cols = values.shape
    return jnp.broadcast_to(values[:, None, :], (rows, times, cols)).reshape(rows * times, cols)


def place_of(device, half):
    chip = device // 2
    return chip // 2 + (chip % 2) * (2 * half - 1 - 2 * (chip // 2))


def chip_at(place, half):
    return jnp.where(place < half, 2 * place, 2 * (2 * half - 1 - place) + 1)


def project_kernel(
    rows_here,
    x_hbm,
    gain_hbm,
    shift_hbm,
    first_hbm,
    first_offset_hbm,
    second_hbm,
    second_offset_hbm,
    keep_ref,
    give_ref,
    x_ref,
    gain_ref,
    shift_ref,
    first_ref,
    first_offset_ref,
    second_ref,
    second_offset_ref,
    packed_ref,
    left_ref,
    sems,
):
    samples, residues, features = x_ref.shape
    hidden = first_ref.shape[0]
    width = samples * hidden
    tile = keep_ref.shape[1]
    tiles = residues // tile
    fold = LANES // hidden
    groups = residues // fold
    small = [
        (first_hbm, first_ref),
        (second_hbm, second_ref),
        (gain_hbm, gain_ref),
        (shift_hbm, shift_ref),
        (first_offset_hbm, first_offset_ref),
        (second_offset_hbm, second_offset_ref),
    ]
    some = samples // CHUNKS
    large = []
    for n in range(CHUNKS):
        rows = pl.ds(n * some, some)
        large.append(pltpu.make_async_copy(x_hbm.at[rows], x_ref.at[rows], sems.at[n]))
        large[-1].start()
    copies = [
        pltpu.make_async_copy(src, dst, sems.at[CHUNKS + n]) for n, (src, dst) in enumerate(small)
    ]
    for copy in copies:
        copy.start()
    for copy in copies:
        copy.wait()

    first = jnp.concatenate([first_ref[...]] * fold, axis=0)
    first_offset = jnp.concatenate([first_offset_ref[...]] * fold, axis=1)
    second = repeat_rows(second_ref[...].astype(jnp.float32), samples)
    row = lax.broadcasted_iota(jnp.int32, (width, 1), 0)
    spot = lax.broadcasted_iota(jnp.int32, (width, hidden), 0)
    channel = lax.broadcasted_iota(jnp.int32, (width, hidden), 1)
    second_offset = jnp.sum(
        jnp.where(spot // samples == channel, second_offset_ref[...], 0.0), axis=1, keepdims=True
    )
    residue = lax.broadcasted_iota(jnp.int32, (tile, LANES), 0)
    lane = lax.broadcasted_iota(jnp.int32, (tile, LANES), 1)
    own = residue % fold == lane // hidden
    group = lax.broadcasted_iota(jnp.int32, (tile // fold, tile), 0)
    member = lax.broadcasted_iota(jnp.int32, (tile // fold, tile), 1)
    gather = (member // fold == group).astype(jnp.bfloat16)

    dims = (((1,), (1,)), ((), ()))
    right = [jnp.zeros((width, tile), jnp.float32) for _ in range(tiles)]
    for s in range(samples):
        if s % some == 0:
            large[s // some].wait()
        values = x_ref[s].astype(jnp.float32)
        center = jnp.mean(values, axis=-1, keepdims=True)
        values = values - center
        variance = jnp.mean(jnp.square(values), axis=-1, keepdims=True)
        normed = (values * lax.rsqrt(variance + 1e-05) * gain_ref[...] + shift_ref[...]).astype(
            jnp.bfloat16
        )
        second_here = jnp.where(row % samples == s, second, 0.0).astype(jnp.bfloat16)
        for t in range(tiles):
            part = normed[t * tile : (t + 1) * tile]
            right[t] += lax.dot_general(second_here, part, dims, preferred_element_type=jnp.float32)
            left = lax.dot_general(part, first, dims, preferred_element_type=jnp.float32)
            left = jnp.where(own, left + first_offset, 0.0).astype(jnp.bfloat16)
            low = s * groups + t * (tile // fold)
            packed_ref[low : low + tile // fold, :] = jnp.dot(
                gather, left, preferred_element_type=jnp.float32
            )
    for t in range(tiles):
        value = (right[t] + second_offset).astype(jnp.bfloat16)
        keep_ref[t * width : (t + 1) * width, :] = value
        give_ref[t * width : (t + 1) * width, :] = value
    across = tile // LANES
    for low in range(0, groups, across):
        at = low // across * samples
        left_ref[at : at + samples, :] = jnp.concatenate(
            [packed_ref[pl.ds(low + n, samples, stride=groups), :] for n in range(across)], axis=1
        )

    device = lax.axis_index("row")
    per_chip = 2 * rows_here * hidden * samples // tile
    half = residues // rows_here // 4
    base = tiles * width
    way = 1 - 2 * (device % 2)
    place = place_of(device, half)
    for n in range(half):
        low = base + n * per_chip
        for message, ahead in ((keep_ref, way * (half - n)), (give_ref, -way * (half - 1 - n))):
            chip = chip_at(lax.rem(place + ahead + 2 * half, 2 * half), half)
            start = pl.multiple_of(chip * per_chip, per_chip)
            message[low : low + per_chip, :] = left_ref[pl.ds(start, per_chip), :].astype(jnp.bfloat16)


def weight_kernel(final_ref, out_ref, wide_ref):
    channels, columns = out_ref.shape
    hidden = math.isqrt(columns)
    wide_ref[...] = final_ref[...].astype(jnp.float32)
    step = LANES // hidden
    for e in range(0, hidden, step):
        rows = [wide_ref[pl.ds(e + n, hidden, stride=hidden), :] for n in range(step)]
        out_ref[:, e * hidden : (e + step) * hidden] = jnp.concatenate(rows, axis=0).T.astype(
            jnp.bfloat16
        )


def pair_kernel(places, gridded, rows_here, hidden, samples, *refs):
    refs = list(refs)
    count = len(places)
    if gridded:
        shards = [(refs.pop(0), 0, refs.pop(0), 0) for _ in places]
    else:
        messages = [refs.pop(0) for _ in range(1 + max(place[0] for place in places))]
        shards = [(messages[n], right, messages[n], left) for n, right, left in places]
    weight_ref, offset_hbm, out_hbm, left_ref, outer_ref, out_ref, offset_ref, sems = refs
    offset_copy = pltpu.make_async_copy(offset_hbm, offset_ref, sems.at[rows_here])
    offset_copy.start()
    tile = shards[0][0].shape[1]
    here = samples // count
    span = rows_here * hidden
    deep = span * here // tile
    core = lax.rem(lax.axis_index("row"), 2)
    pieces = []
    for _, _, ref, base in shards:
        start = pl.multiple_of(base + core * deep, deep)
        piece = ref[pl.ds(start, deep), :].astype(jnp.float32)
        pieces.append(
            jnp.concatenate([piece[n * here : (n + 1) * here] for n in range(span // tile)], axis=1)
        )
    left_ref[...] = jnp.concatenate(pieces, axis=0).T.astype(jnp.bfloat16)

    left = left_ref[...]
    for e in range(0, hidden, 2):
        both = [
            ref[base + e * here : base + (e + 2) * here, :].astype(jnp.float32)
            for ref, base, _, _ in shards
        ]
        for k in range(2):
            right = jnp.concatenate([x[k * here : (k + 1) * here] for x in both], axis=0)
            outer = jnp.dot(left, right.astype(jnp.bfloat16), preferred_element_type=jnp.float32)
            outer = outer.astype(jnp.bfloat16)
            for i in range(rows_here):
                outer_ref[i, (e + k) * hidden : (e + k + 1) * hidden, :] = outer[
                    i * hidden : (i + 1) * hidden
                ]

    first = pl.program_id(0) * tile if gridded else 0
    offset_copy.wait()
    copies = []
    for i in range(rows_here):
        value = jnp.dot(weight_ref[...], outer_ref[i], preferred_element_type=jnp.float32)
        value = value.T * (1.0 / samples) + offset_ref[...]
        out_ref[i] = value.astype(jnp.bfloat16)
        copies.append(
            pltpu.make_async_copy(out_ref.at[i], out_hbm.at[i, pl.ds(first, tile)], sems.at[i])
        )
        copies[-1].start()
    for copy in copies:
        copy.wait()


def per_device(
    size,
    alignment_embedding,
    rescaling_factor,
    recentering_offset,
    first_side_coefficients,
    first_side_offset,
    second_side_coefficients,
    second_side_offset,
    final_projector_coefficients,
    final_projector_offset,
):
    here, residues, features = alignment_embedding.shape
    hidden = first_side_coefficients.shape[1]
    channels = final_projector_coefficients.shape[1]
    width = here * hidden
    samples = here * size
    rows_here = residues // size
    half = size // 4
    tile = 256
    tiles = residues // tile
    body = tiles * width
    per_chip = 2 * rows_here * width // tile
    message = jax.ShapeDtypeStruct((body + half * per_chip, tile), jnp.bfloat16)

    vmem = pl.BlockSpec(memory_space=pltpu.VMEM)
    hbm = pl.BlockSpec(memory_space=pltpu.HBM)
    keep, give = pl.pallas_call(
        functools.partial(project_kernel, rows_here),
        out_shape=[message] * 2,
        in_specs=[hbm] * 7,
        out_specs=[vmem] * 2,
        scratch_shapes=[
            pltpu.VMEM((here, residues, features), jnp.bfloat16),
            pltpu.VMEM((1, features), jnp.float32),
            pltpu.VMEM((1, features), jnp.float32),
            pltpu.VMEM((hidden, features), jnp.bfloat16),
            pltpu.VMEM((1, hidden), jnp.float32),
            pltpu.VMEM((hidden, features), jnp.bfloat16),
            pltpu.VMEM((1, hidden), jnp.float32),
            pltpu.VMEM((residues * width // LANES, LANES), jnp.float32),
            pltpu.VMEM((residues * width // tile, tile), jnp.float32),
            pltpu.SemaphoreType.DMA((CHUNKS + 6,)),
        ],
        compiler_params=pltpu.CompilerParams(vmem_limit_bytes=32 * MIB),
        cost_estimate=pl.CostEstimate(
            flops=4 * here * residues * features * width,
            bytes_accessed=2 * here * residues * features,
            transcendentals=0,
        ),
    )(
        *[
            pltpu.with_memory_space_constraint(value, pltpu.HBM)
            for value in (
                alignment_embedding,
                rescaling_factor.reshape(1, features),
                recentering_offset.reshape(1, features),
                first_side_coefficients.T,
                first_side_offset.reshape(1, hidden),
                second_side_coefficients.T,
                second_side_offset.reshape(1, hidden),
            )
        ]
    )
    weight = pl.pallas_call(
        weight_kernel,
        out_shape=jax.ShapeDtypeStruct((channels, hidden * hidden), jnp.bfloat16),
        in_specs=[vmem],
        out_specs=vmem,
        scratch_shapes=[pltpu.VMEM((hidden * hidden, channels), jnp.float32)],
        compiler_params=pltpu.CompilerParams(vmem_limit_bytes=16 * MIB),
        cost_estimate=pl.CostEstimate(flops=2**28, bytes_accessed=2**20, transcendentals=0),
    )(final_projector_coefficients)

    by_place = {(place_of(r, half), r % 2): r for r in range(size)}

    def neighbours(way):
        return [
            (r, by_place[(place_of(r, half) + way * (1 - 2 * (r % 2))) % (2 * half), r % 2])
            for r in range(size)
        ]

    def swap(value):
        return lax.ppermute(value, "row", [(r, r ^ 1) for r in range(size)])

    messages, places = [], []

    def take(pair):
        for value in pair:
            places.append((len(messages), 0, value.shape[0] - per_chip))
            messages.append(value)

    take([give, swap(give)])
    flying = [keep, give[: body + (half - 1) * per_chip]]
    swapped = []
    for step in range(1, half + 1):
        landed = [lax.ppermute(x, "row", neighbours(way)) for x, way in zip(flying, (1, -1))]
        if step == 1:
            landed[0], weight = lax.optimization_barrier((landed[0], weight))
        if step >= 3:
            landed[0], swapped[step - 3] = lax.optimization_barrier((landed[0], swapped[step - 3]))
        flying = [x[: x.shape[0] - per_chip] for x in landed]
        if step == half - 1:
            flying = flying[:1]
        landed = lax.optimization_barrier(landed)
        take(landed)
        swapped.append([swap(x) for x in landed])
    for pair in swapped:
        take(pair)

    gridded = tiles > 1
    offset = pltpu.with_memory_space_constraint(final_projector_offset.reshape(1, channels), pltpu.HBM)
    if gridded:
        operands, specs = [], []
        for n, right, left in places:
            operands += [messages[n]] * 2
            specs += [
                pl.BlockSpec((width, tile), lambda t, first=right // width: (first + t, 0)),
                pl.BlockSpec((per_chip, tile), lambda t, at=left // per_chip: (at, 0)),
            ]
        specs += [pl.BlockSpec((channels, hidden * hidden), lambda t: (0, 0)), hbm]
        grid = (tiles,)
    else:
        operands = messages
        specs = [vmem] * (len(messages) + 1) + [hbm]
        grid = ()
    return pl.pallas_call(
        functools.partial(pair_kernel, places, gridded, rows_here, hidden, samples),
        out_shape=jax.ShapeDtypeStruct((rows_here, residues, channels), jnp.bfloat16),
        grid=grid,
        in_specs=specs,
        out_specs=hbm,
        scratch_shapes=[
            pltpu.VMEM((rows_here * hidden, samples), jnp.bfloat16),
            pltpu.VMEM((rows_here, hidden * hidden, tile), jnp.bfloat16),
            pltpu.VMEM((rows_here, tile, channels), jnp.bfloat16),
            pltpu.VMEM((1, channels), jnp.float32),
            pltpu.SemaphoreType.DMA((rows_here + 1,)),
        ],
        compiler_params=pltpu.CompilerParams(vmem_limit_bytes=40 * MIB),
    )(*operands, weight, offset)


def solution(mesh):
    return jax.shard_map(
        functools.partial(per_device, mesh.shape["row"]),
        mesh=mesh,
        in_specs=(P(("groups", "row"), None, None), P(), P(), P(), P(), P(), P(), P(), P()),
        out_specs=P(("groups", "row"), None, None),
        check_vma=False,
    )
```

```python
import functools
import math

import jax
import jax.numpy as jnp
from jax import lax
from jax.experimental import pallas as pl
from jax.experimental.pallas import tpu as pltpu
from jax.sharding import PartitionSpec as P

MIB = 1024 * 1024
LANES = 128
CHUNKS = 2


def repeat_rows(values, times):
    rows, cols = values.shape
    return jnp.broadcast_to(values[:, None, :], (rows, times, cols)).reshape(rows * times, cols)


def place_of(device, half):
    chip = device // 2
    return chip // 2 + (chip % 2) * (2 * half - 1 - 2 * (chip // 2))


def chip_at(place, half):
    return jnp.where(place < half, 2 * place, 2 * (2 * half - 1 - place) + 1)


def project_kernel(
    rows_here,
    x_hbm,
    gain_hbm,
    shift_hbm,
    first_hbm,
    first_offset_hbm,
    second_hbm,
    second_offset_hbm,
    keep_ref,
    give_ref,
    x_ref,
    gain_ref,
    shift_ref,
    first_ref,
    first_offset_ref,
    second_ref,
    second_offset_ref,
    packed_ref,
    left_ref,
    sems,
):
    samples, residues, features = x_ref.shape
    hidden = first_ref.shape[0]
    width = samples * hidden
    tile = keep_ref.shape[1]
    tiles = residues // tile
    fold = LANES // hidden
    groups = residues // fold
    small = [
        (first_hbm, first_ref),
        (second_hbm, second_ref),
        (gain_hbm, gain_ref),
        (shift_hbm, shift_ref),
        (first_offset_hbm, first_offset_ref),
        (second_offset_hbm, second_offset_ref),
    ]
    some = samples // CHUNKS
    large = []
    for n in range(CHUNKS):
        rows = pl.ds(n * some, some)
        large.append(pltpu.make_async_copy(x_hbm.at[rows], x_ref.at[rows], sems.at[n]))
        large[-1].start()
    copies = [
        pltpu.make_async_copy(src, dst, sems.at[CHUNKS + n]) for n, (src, dst) in enumerate(small)
    ]
    for copy in copies:
        copy.start()
    for copy in copies:
        copy.wait()

    first = jnp.concatenate([first_ref[...]] * fold, axis=0)
    first_offset = jnp.concatenate([first_offset_ref[...]] * fold, axis=1)
    second = repeat_rows(second_ref[...].astype(jnp.float32), samples)
    row = lax.broadcasted_iota(jnp.int32, (width, 1), 0)
    spot = lax.broadcasted_iota(jnp.int32, (width, hidden), 0)
    channel = lax.broadcasted_iota(jnp.int32, (width, hidden), 1)
    second_offset = jnp.sum(
        jnp.where(spot // samples == channel, second_offset_ref[...], 0.0), axis=1, keepdims=True
    )
    residue = lax.broadcasted_iota(jnp.int32, (tile, LANES), 0)
    lane = lax.broadcasted_iota(jnp.int32, (tile, LANES), 1)
    own = residue % fold == lane // hidden
    group = lax.broadcasted_iota(jnp.int32, (tile // fold, tile), 0)
    member = lax.broadcasted_iota(jnp.int32, (tile // fold, tile), 1)
    gather = (member // fold == group).astype(jnp.bfloat16)

    dims = (((1,), (1,)), ((), ()))
    right = [jnp.zeros((width, tile), jnp.float32) for _ in range(tiles)]
    for s in range(samples):
        if s % some == 0:
            large[s // some].wait()
        values = x_ref[s].astype(jnp.float32)
        center = jnp.mean(values, axis=-1, keepdims=True)
        values = values - center
        variance = jnp.mean(jnp.square(values), axis=-1, keepdims=True)
        normed = (values * lax.rsqrt(variance + 1e-05) * gain_ref[...] + shift_ref[...]).astype(
            jnp.bfloat16
        )
        second_here = jnp.where(row % samples == s, second, 0.0).astype(jnp.bfloat16)
        for t in range(tiles):
            part = normed[t * tile : (t + 1) * tile]
            right[t] += lax.dot_general(second_here, part, dims, preferred_element_type=jnp.float32)
            left = lax.dot_general(part, first, dims, preferred_element_type=jnp.float32)
            left = jnp.where(own, left + first_offset, 0.0).astype(jnp.bfloat16)
            low = s * groups + t * (tile // fold)
            packed_ref[low : low + tile // fold, :] = jnp.dot(
                gather, left, preferred_element_type=jnp.float32
            )
    for t in range(tiles):
        value = (right[t] + second_offset).astype(jnp.bfloat16)
        keep_ref[t * width : (t + 1) * width, :] = value
        give_ref[t * width : (t + 1) * width, :] = value
    across = tile // LANES
    for low in range(0, groups, across):
        at = low // across * samples
        left_ref[at : at + samples, :] = jnp.concatenate(
            [packed_ref[pl.ds(low + n, samples, stride=groups), :] for n in range(across)], axis=1
        )

    device = lax.axis_index("row")
    per_chip = 2 * rows_here * hidden * samples // tile
    half = residues // rows_here // 4
    base = tiles * width
    way = 1 - 2 * (device % 2)
    place = place_of(device, half)
    for n in range(half):
        low = base + n * per_chip
        for message, ahead in ((keep_ref, way * (half - n)), (give_ref, -way * (half - 1 - n))):
            chip = chip_at(lax.rem(place + ahead + 2 * half, 2 * half), half)
            start = pl.multiple_of(chip * per_chip, per_chip)
            message[low : low + per_chip, :] = left_ref[pl.ds(start, per_chip), :].astype(jnp.bfloat16)


def weight_kernel(final_ref, offset_ref, out_ref, offset_out, wide_ref):
    offset_out[...] = offset_ref[...]
    channels, columns = out_ref.shape
    hidden = math.isqrt(columns)
    wide_ref[...] = final_ref[...].astype(jnp.float32)
    step = LANES // hidden
    for e in range(0, hidden, step):
        rows = [wide_ref[pl.ds(e + n, hidden, stride=hidden), :] for n in range(step)]
        out_ref[:, e * hidden : (e + step) * hidden] = jnp.concatenate(rows, axis=0).T.astype(
            jnp.bfloat16
        )


def pair_kernel(places, gridded, rows_here, hidden, samples, *refs):
    refs = list(refs)
    count = len(places)
    if gridded:
        shards = [(refs.pop(0), 0, refs.pop(0), 0) for _ in places]
    else:
        messages = [refs.pop(0) for _ in range(1 + max(place[0] for place in places))]
        shards = [(messages[n], right, messages[n], left) for n, right, left in places]
    weight_ref, offset_ref, out_hbm, left_ref, outer_ref, out_ref, sems = refs
    tile = shards[0][0].shape[1]
    here = samples // count
    span = rows_here * hidden
    deep = span * here // tile
    core = lax.rem(lax.axis_index("row"), 2)
    pieces = []
    for _, _, ref, base in shards:
        start = pl.multiple_of(base + core * deep, deep)
        piece = ref[pl.ds(start, deep), :].astype(jnp.float32)
        pieces.append(
            jnp.concatenate([piece[n * here : (n + 1) * here] for n in range(span // tile)], axis=1)
        )
    left_ref[...] = jnp.concatenate(pieces, axis=0).T.astype(jnp.bfloat16)

    left = left_ref[...]
    for e in range(0, hidden, 2):
        both = [
            ref[base + e * here : base + (e + 2) * here, :].astype(jnp.float32)
            for ref, base, _, _ in shards
        ]
        for k in range(2):
            right = jnp.concatenate([x[k * here : (k + 1) * here] for x in both], axis=0)
            outer = jnp.dot(left, right.astype(jnp.bfloat16), preferred_element_type=jnp.float32)
            outer = outer.astype(jnp.bfloat16)
            for i in range(rows_here):
                outer_ref[i, (e + k) * hidden : (e + k + 1) * hidden, :] = outer[
                    i * hidden : (i + 1) * hidden
                ]

    first = pl.program_id(0) * tile if gridded else 0
    copies = []
    for i in range(rows_here):
        value = jnp.dot(weight_ref[...], outer_ref[i], preferred_element_type=jnp.float32)
        value = value.T * (1.0 / samples) + offset_ref[...]
        out_ref[i] = value.astype(jnp.bfloat16)
        copies.append(
            pltpu.make_async_copy(out_ref.at[i], out_hbm.at[i, pl.ds(first, tile)], sems.at[i])
        )
        copies[-1].start()
    for copy in copies:
        copy.wait()


def per_device(
    size,
    alignment_embedding,
    rescaling_factor,
    recentering_offset,
    first_side_coefficients,
    first_side_offset,
    second_side_coefficients,
    second_side_offset,
    final_projector_coefficients,
    final_projector_offset,
):
    here, residues, features = alignment_embedding.shape
    hidden = first_side_coefficients.shape[1]
    channels = final_projector_coefficients.shape[1]
    width = here * hidden
    samples = here * size
    rows_here = residues // size
    half = size // 4
    tile = 256
    tiles = residues // tile
    body = tiles * width
    per_chip = 2 * rows_here * width // tile
    message = jax.ShapeDtypeStruct((body + half * per_chip, tile), jnp.bfloat16)

    vmem = pl.BlockSpec(memory_space=pltpu.VMEM)
    hbm = pl.BlockSpec(memory_space=pltpu.HBM)
    keep, give = pl.pallas_call(
        functools.partial(project_kernel, rows_here),
        out_shape=[message] * 2,
        in_specs=[hbm] * 7,
        out_specs=[vmem] * 2,
        scratch_shapes=[
            pltpu.VMEM((here, residues, features), jnp.bfloat16),
            pltpu.VMEM((1, features), jnp.float32),
            pltpu.VMEM((1, features), jnp.float32),
            pltpu.VMEM((hidden, features), jnp.bfloat16),
            pltpu.VMEM((1, hidden), jnp.float32),
            pltpu.VMEM((hidden, features), jnp.bfloat16),
            pltpu.VMEM((1, hidden), jnp.float32),
            pltpu.VMEM((residues * width // LANES, LANES), jnp.float32),
            pltpu.VMEM((residues * width // tile, tile), jnp.float32),
            pltpu.SemaphoreType.DMA((CHUNKS + 6,)),
        ],
        compiler_params=pltpu.CompilerParams(vmem_limit_bytes=32 * MIB),
        cost_estimate=pl.CostEstimate(
            flops=4 * here * residues * features * width,
            bytes_accessed=2 * here * residues * features,
            transcendentals=0,
        ),
    )(
        *[
            pltpu.with_memory_space_constraint(value, pltpu.HBM)
            for value in (
                alignment_embedding,
                rescaling_factor.reshape(1, features),
                recentering_offset.reshape(1, features),
                first_side_coefficients.T,
                first_side_offset.reshape(1, hidden),
                second_side_coefficients.T,
                second_side_offset.reshape(1, hidden),
            )
        ]
    )
    weight, offset = pl.pallas_call(
        weight_kernel,
        out_shape=[
            jax.ShapeDtypeStruct((channels, hidden * hidden), jnp.bfloat16),
            jax.ShapeDtypeStruct((1, channels), jnp.float32),
        ],
        in_specs=[vmem, vmem],
        out_specs=[vmem, vmem],
        scratch_shapes=[pltpu.VMEM((hidden * hidden, channels), jnp.float32)],
        compiler_params=pltpu.CompilerParams(vmem_limit_bytes=16 * MIB),
        cost_estimate=pl.CostEstimate(flops=2**28, bytes_accessed=2**20, transcendentals=0),
    )(final_projector_coefficients, final_projector_offset.reshape(1, channels))

    by_place = {(place_of(r, half), r % 2): r for r in range(size)}

    def neighbours(way):
        return [
            (r, by_place[(place_of(r, half) + way * (1 - 2 * (r % 2))) % (2 * half), r % 2])
            for r in range(size)
        ]

    def swap(value):
        return lax.ppermute(value, "row", [(r, r ^ 1) for r in range(size)])

    messages, places = [], []

    def take(pair):
        for value in pair:
            places.append((len(messages), 0, value.shape[0] - per_chip))
            messages.append(value)

    mine, theirs, weight, offset = lax.optimization_barrier((give, swap(give), weight, offset))
    take([mine, theirs])
    flying = [keep, mine[: body + (half - 1) * per_chip]]
    swapped = []
    for step in range(1, half + 1):
        landed = [lax.ppermute(x, "row", neighbours(way)) for x, way in zip(flying, (1, -1))]
        if step >= 3:
            landed[-1], swapped[step - 3] = lax.optimization_barrier((landed[-1], swapped[step - 3]))
        flying = [x[: x.shape[0] - per_chip] for x in landed]
        if step == half - 1:
            flying = flying[:1]
        landed = lax.optimization_barrier(landed)
        take(landed)
        swapped.append([swap(x) for x in landed])
    for pair in swapped:
        take(pair)

    gridded = tiles > 1
    if gridded:
        operands, specs = [], []
        for n, right, left in places:
            operands += [messages[n]] * 2
            specs += [
                pl.BlockSpec((width, tile), lambda t, first=right // width: (first + t, 0)),
                pl.BlockSpec((per_chip, tile), lambda t, at=left // per_chip: (at, 0)),
            ]
        specs += [
            pl.BlockSpec((channels, hidden * hidden), lambda t: (0, 0)),
            pl.BlockSpec((1, channels), lambda t: (0, 0)),
        ]
        grid = (tiles,)
    else:
        operands = messages
        specs = [vmem] * (len(messages) + 2)
        grid = ()
    return pl.pallas_call(
        functools.partial(pair_kernel, places, gridded, rows_here, hidden, samples),
        out_shape=jax.ShapeDtypeStruct((rows_here, residues, channels), jnp.bfloat16),
        grid=grid,
        in_specs=specs,
        out_specs=hbm,
        scratch_shapes=[
            pltpu.VMEM((rows_here * hidden, samples), jnp.bfloat16),
            pltpu.VMEM((rows_here, hidden * hidden, tile), jnp.bfloat16),
            pltpu.VMEM((rows_here, tile, channels), jnp.bfloat16),
            pltpu.SemaphoreType.DMA((rows_here,)),
        ],
        compiler_params=pltpu.CompilerParams(vmem_limit_bytes=40 * MIB),
    )(*operands, weight, offset)


def solution(mesh):
    return jax.shard_map(
        functools.partial(per_device, mesh.shape["row"]),
        mesh=mesh,
        in_specs=(P(("groups", "row"), None, None), P(), P(), P(), P(), P(), P(), P(), P()),
        out_specs=P(("groups", "row"), None, None),
        check_vma=False,
    )
```

```python
import functools
import math

import jax
import jax.numpy as jnp
from jax import lax
from jax.experimental import pallas as pl
from jax.experimental.pallas import tpu as pltpu
from jax.sharding import PartitionSpec as P

MIB = 1024 * 1024
LANES = 128
CHUNKS = 2


def repeat_rows(values, times):
    rows, cols = values.shape
    return jnp.broadcast_to(values[:, None, :], (rows, times, cols)).reshape(rows * times, cols)


def place_of(device, half):
    chip = device // 2
    return chip // 2 + (chip % 2) * (2 * half - 1 - 2 * (chip // 2))


def chip_at(place, half):
    return jnp.where(place < half, 2 * place, 2 * (2 * half - 1 - place) + 1)


def project_kernel(
    rows_here,
    x_hbm,
    gain_hbm,
    shift_hbm,
    first_hbm,
    first_offset_hbm,
    second_hbm,
    second_offset_hbm,
    keep_ref,
    give_ref,
    x_ref,
    gain_ref,
    shift_ref,
    first_ref,
    first_offset_ref,
    second_ref,
    second_offset_ref,
    packed_ref,
    left_ref,
    sems,
):
    samples, residues, features = x_ref.shape
    hidden = first_ref.shape[0]
    width = samples * hidden
    tile = keep_ref.shape[1]
    tiles = residues // tile
    fold = LANES // hidden
    groups = residues // fold
    small = [
        (first_hbm, first_ref),
        (second_hbm, second_ref),
        (gain_hbm, gain_ref),
        (shift_hbm, shift_ref),
        (first_offset_hbm, first_offset_ref),
        (second_offset_hbm, second_offset_ref),
    ]
    some = samples // CHUNKS
    large = []
    for n in range(CHUNKS):
        rows = pl.ds(n * some, some)
        large.append(pltpu.make_async_copy(x_hbm.at[rows], x_ref.at[rows], sems.at[n]))
        large[-1].start()
    copies = [
        pltpu.make_async_copy(src, dst, sems.at[CHUNKS + n]) for n, (src, dst) in enumerate(small)
    ]
    for copy in copies:
        copy.start()
    for copy in copies:
        copy.wait()

    first = jnp.concatenate([first_ref[...]] * fold, axis=0)
    first_offset = jnp.concatenate([first_offset_ref[...]] * fold, axis=1)
    second = repeat_rows(second_ref[...].astype(jnp.float32), samples)
    row = lax.broadcasted_iota(jnp.int32, (width, 1), 0)
    spot = lax.broadcasted_iota(jnp.int32, (width, hidden), 0)
    channel = lax.broadcasted_iota(jnp.int32, (width, hidden), 1)
    second_offset = jnp.sum(
        jnp.where(spot // samples == channel, second_offset_ref[...], 0.0), axis=1, keepdims=True
    )
    residue = lax.broadcasted_iota(jnp.int32, (tile, LANES), 0)
    lane = lax.broadcasted_iota(jnp.int32, (tile, LANES), 1)
    own = residue % fold == lane // hidden
    group = lax.broadcasted_iota(jnp.int32, (tile // fold, tile), 0)
    member = lax.broadcasted_iota(jnp.int32, (tile // fold, tile), 1)
    gather = (member // fold == group).astype(jnp.bfloat16)

    dims = (((1,), (1,)), ((), ()))
    right = [jnp.zeros((width, tile), jnp.float32) for _ in range(tiles)]
    for s in range(samples):
        if s % some == 0:
            large[s // some].wait()
        values = x_ref[s].astype(jnp.float32)
        center = jnp.mean(values, axis=-1, keepdims=True)
        values = values - center
        variance = jnp.mean(jnp.square(values), axis=-1, keepdims=True)
        normed = (values * lax.rsqrt(variance + 1e-05) * gain_ref[...] + shift_ref[...]).astype(
            jnp.bfloat16
        )
        second_here = jnp.where(row % samples == s, second, 0.0).astype(jnp.bfloat16)
        for t in range(tiles):
            part = normed[t * tile : (t + 1) * tile]
            right[t] += lax.dot_general(second_here, part, dims, preferred_element_type=jnp.float32)
            left = lax.dot_general(part, first, dims, preferred_element_type=jnp.float32)
            left = jnp.where(own, left + first_offset, 0.0).astype(jnp.bfloat16)
            low = s * groups + t * (tile // fold)
            packed_ref[low : low + tile // fold, :] = jnp.dot(
                gather, left, preferred_element_type=jnp.float32
            )
    for t in range(tiles):
        value = (right[t] + second_offset).astype(jnp.bfloat16)
        keep_ref[t * width : (t + 1) * width, :] = value
        give_ref[t * width : (t + 1) * width, :] = value
    across = tile // LANES
    for low in range(0, groups, across):
        at = low // across * samples
        left_ref[at : at + samples, :] = jnp.concatenate(
            [packed_ref[pl.ds(low + n, samples, stride=groups), :] for n in range(across)], axis=1
        )

    device = lax.axis_index("row")
    per_chip = 2 * rows_here * hidden * samples // tile
    half = residues // rows_here // 4
    base = tiles * width
    way = 1 - 2 * (device % 2)
    place = place_of(device, half)
    for n in range(half):
        low = base + n * per_chip
        for message, ahead in ((keep_ref, way * (half - n)), (give_ref, -way * (half - 1 - n))):
            chip = chip_at(lax.rem(place + ahead + 2 * half, 2 * half), half)
            start = pl.multiple_of(chip * per_chip, per_chip)
            message[low : low + per_chip, :] = left_ref[pl.ds(start, per_chip), :].astype(jnp.bfloat16)


def weight_kernel(final_ref, offset_ref, out_ref, offset_out, wide_ref):
    offset_out[...] = offset_ref[...]
    channels, columns = out_ref.shape
    hidden = math.isqrt(columns)
    wide_ref[...] = final_ref[...].astype(jnp.float32)
    step = LANES // hidden
    for e in range(0, hidden, step):
        rows = [wide_ref[pl.ds(e + n, hidden, stride=hidden), :] for n in range(step)]
        out_ref[:, e * hidden : (e + step) * hidden] = jnp.concatenate(rows, axis=0).T.astype(
            jnp.bfloat16
        )


def pair_kernel(places, gridded, rows_here, hidden, samples, *refs):
    refs = list(refs)
    count = len(places)
    if gridded:
        shards = [(refs.pop(0), 0, refs.pop(0), 0) for _ in places]
    else:
        messages = [refs.pop(0) for _ in range(1 + max(place[0] for place in places))]
        shards = [(messages[n], right, messages[n], left) for n, right, left in places]
    weight_ref, offset_ref, out_hbm, left_ref, outer_ref, out_ref, sems = refs
    tile = shards[0][0].shape[1]
    here = samples // count
    span = rows_here * hidden
    deep = span * here // tile
    core = lax.rem(lax.axis_index("row"), 2)
    pieces = []
    for _, _, ref, base in shards:
        start = pl.multiple_of(base + core * deep, deep)
        piece = ref[pl.ds(start, deep), :].astype(jnp.float32)
        pieces.append(
            jnp.concatenate([piece[n * here : (n + 1) * here] for n in range(span // tile)], axis=1)
        )
    left_ref[...] = jnp.concatenate(pieces, axis=0).T.astype(jnp.bfloat16)

    left = left_ref[...]
    for e in range(0, hidden, 2):
        both = [
            ref[base + e * here : base + (e + 2) * here, :].astype(jnp.float32)
            for ref, base, _, _ in shards
        ]
        for k in range(2):
            right = jnp.concatenate([x[k * here : (k + 1) * here] for x in both], axis=0)
            outer = jnp.dot(left, right.astype(jnp.bfloat16), preferred_element_type=jnp.float32)
            outer = outer.astype(jnp.bfloat16)
            for i in range(rows_here):
                outer_ref[i, (e + k) * hidden : (e + k + 1) * hidden, :] = outer[
                    i * hidden : (i + 1) * hidden
                ]

    first = pl.program_id(0) * tile if gridded else 0
    copies = []
    for i in range(rows_here):
        value = jnp.dot(weight_ref[...], outer_ref[i], preferred_element_type=jnp.float32)
        value = value.T * (1.0 / samples) + offset_ref[...]
        out_ref[i] = value.astype(jnp.bfloat16)
        copies.append(
            pltpu.make_async_copy(out_ref.at[i], out_hbm.at[i, pl.ds(first, tile)], sems.at[i])
        )
        copies[-1].start()
    for copy in copies:
        copy.wait()


def per_device(
    size,
    alignment_embedding,
    rescaling_factor,
    recentering_offset,
    first_side_coefficients,
    first_side_offset,
    second_side_coefficients,
    second_side_offset,
    final_projector_coefficients,
    final_projector_offset,
):
    here, residues, features = alignment_embedding.shape
    hidden = first_side_coefficients.shape[1]
    channels = final_projector_coefficients.shape[1]
    width = here * hidden
    samples = here * size
    rows_here = residues // size
    half = size // 4
    tile = 256
    tiles = residues // tile
    body = tiles * width
    per_chip = 2 * rows_here * width // tile
    message = jax.ShapeDtypeStruct((body + half * per_chip, tile), jnp.bfloat16)

    vmem = pl.BlockSpec(memory_space=pltpu.VMEM)
    hbm = pl.BlockSpec(memory_space=pltpu.HBM)
    keep, give = pl.pallas_call(
        functools.partial(project_kernel, rows_here),
        out_shape=[message] * 2,
        in_specs=[hbm] * 7,
        out_specs=[vmem] * 2,
        scratch_shapes=[
            pltpu.VMEM((here, residues, features), jnp.bfloat16),
            pltpu.VMEM((1, features), jnp.float32),
            pltpu.VMEM((1, features), jnp.float32),
            pltpu.VMEM((hidden, features), jnp.bfloat16),
            pltpu.VMEM((1, hidden), jnp.float32),
            pltpu.VMEM((hidden, features), jnp.bfloat16),
            pltpu.VMEM((1, hidden), jnp.float32),
            pltpu.VMEM((residues * width // LANES, LANES), jnp.float32),
            pltpu.VMEM((residues * width // tile, tile), jnp.float32),
            pltpu.SemaphoreType.DMA((CHUNKS + 6,)),
        ],
        compiler_params=pltpu.CompilerParams(vmem_limit_bytes=32 * MIB),
        cost_estimate=pl.CostEstimate(
            flops=4 * here * residues * features * width,
            bytes_accessed=2 * here * residues * features,
            transcendentals=0,
        ),
    )(
        *[
            pltpu.with_memory_space_constraint(value, pltpu.HBM)
            for value in (
                alignment_embedding,
                rescaling_factor.reshape(1, features),
                recentering_offset.reshape(1, features),
                first_side_coefficients.T,
                first_side_offset.reshape(1, hidden),
                second_side_coefficients.T,
                second_side_offset.reshape(1, hidden),
            )
        ]
    )
    weight, offset = pl.pallas_call(
        weight_kernel,
        out_shape=[
            jax.ShapeDtypeStruct((channels, hidden * hidden), jnp.bfloat16),
            jax.ShapeDtypeStruct((1, channels), jnp.float32),
        ],
        in_specs=[vmem, vmem],
        out_specs=[vmem, vmem],
        scratch_shapes=[pltpu.VMEM((hidden * hidden, channels), jnp.float32)],
        compiler_params=pltpu.CompilerParams(vmem_limit_bytes=16 * MIB),
        cost_estimate=pl.CostEstimate(flops=2**28, bytes_accessed=2**20, transcendentals=0),
    )(final_projector_coefficients, final_projector_offset.reshape(1, channels))

    by_place = {(place_of(r, half), r % 2): r for r in range(size)}
    around = [
        (r, by_place[(place_of(r, half) + 1 - 2 * (r % 2)) % (2 * half), r % 2]) for r in range(size)
    ]

    def swap(value):
        return lax.ppermute(value, "row", [(r, r ^ 1) for r in range(size)])

    messages, places = [], []

    def take(pair):
        for value in pair:
            places.append((len(messages), 0, value.shape[0] - per_chip))
            messages.append(value)

    mine, theirs, weight, offset = lax.optimization_barrier((give, swap(give), weight, offset))
    take([mine, theirs])
    flying = [keep, theirs[: body + (half - 1) * per_chip]]
    swapped = []
    for step in range(1, half + 1):
        landed = [lax.ppermute(x, "row", around) for x in flying]
        if step >= 3:
            landed[-1], swapped[step - 3] = lax.optimization_barrier((landed[-1], swapped[step - 3]))
        flying = [x[: x.shape[0] - per_chip] for x in landed]
        if step == half - 1:
            flying = flying[:1]
        landed = lax.optimization_barrier(landed)
        take(landed)
        swapped.append([swap(x) for x in landed])
    for pair in swapped:
        take(pair)

    gridded = tiles > 1
    if gridded:
        operands, specs = [], []
        for n, right, left in places:
            operands += [messages[n]] * 2
            specs += [
                pl.BlockSpec((width, tile), lambda t, first=right // width: (first + t, 0)),
                pl.BlockSpec((per_chip, tile), lambda t, at=left // per_chip: (at, 0)),
            ]
        specs += [
            pl.BlockSpec((channels, hidden * hidden), lambda t: (0, 0)),
            pl.BlockSpec((1, channels), lambda t: (0, 0)),
        ]
        grid = (tiles,)
    else:
        operands = messages
        specs = [vmem] * (len(messages) + 2)
        grid = ()
    return pl.pallas_call(
        functools.partial(pair_kernel, places, gridded, rows_here, hidden, samples),
        out_shape=jax.ShapeDtypeStruct((rows_here, residues, channels), jnp.bfloat16),
        grid=grid,
        in_specs=specs,
        out_specs=hbm,
        scratch_shapes=[
            pltpu.VMEM((rows_here * hidden, samples), jnp.bfloat16),
            pltpu.VMEM((rows_here, hidden * hidden, tile), jnp.bfloat16),
            pltpu.VMEM((rows_here, tile, channels), jnp.bfloat16),
            pltpu.SemaphoreType.DMA((rows_here,)),
        ],
        compiler_params=pltpu.CompilerParams(vmem_limit_bytes=40 * MIB),
    )(*operands, weight, offset)


def solution(mesh):
    return jax.shard_map(
        functools.partial(per_device, mesh.shape["row"]),
        mesh=mesh,
        in_specs=(P(("groups", "row"), None, None), P(), P(), P(), P(), P(), P(), P(), P()),
        out_specs=P(("groups", "row"), None, None),
        check_vma=False,
    )
```

```python
import functools
import math

import jax
import jax.numpy as jnp
from jax import lax
from jax.experimental import pallas as pl
from jax.experimental.pallas import tpu as pltpu
from jax.sharding import PartitionSpec as P

MIB = 1024 * 1024
LANES = 128
CHUNKS = 2


def repeat_rows(values, times):
    rows, cols = values.shape
    return jnp.broadcast_to(values[:, None, :], (rows, times, cols)).reshape(rows * times, cols)


def place_of(device, half):
    chip = device // 2
    return chip // 2 + (chip % 2) * (2 * half - 1 - 2 * (chip // 2))


def chip_at(place, half):
    return jnp.where(place < half, 2 * place, 2 * (2 * half - 1 - place) + 1)


def project_kernel(
    rows_here,
    x_hbm,
    gain_hbm,
    shift_hbm,
    first_hbm,
    first_offset_hbm,
    second_hbm,
    second_offset_hbm,
    keep_ref,
    give_ref,
    x_ref,
    gain_ref,
    shift_ref,
    first_ref,
    first_offset_ref,
    second_ref,
    second_offset_ref,
    packed_ref,
    left_ref,
    sems,
):
    samples, residues, features = x_ref.shape
    hidden = first_ref.shape[0]
    width = samples * hidden
    tile = keep_ref.shape[1]
    tiles = residues // tile
    fold = LANES // hidden
    groups = residues // fold
    small = [
        (first_hbm, first_ref),
        (second_hbm, second_ref),
        (gain_hbm, gain_ref),
        (shift_hbm, shift_ref),
        (first_offset_hbm, first_offset_ref),
        (second_offset_hbm, second_offset_ref),
    ]
    some = samples // CHUNKS
    large = []
    for n in range(CHUNKS):
        rows = pl.ds(n * some, some)
        large.append(pltpu.make_async_copy(x_hbm.at[rows], x_ref.at[rows], sems.at[n]))
        large[-1].start()
    copies = [
        pltpu.make_async_copy(src, dst, sems.at[CHUNKS + n]) for n, (src, dst) in enumerate(small)
    ]
    for copy in copies:
        copy.start()
    for copy in copies:
        copy.wait()

    first = jnp.concatenate([first_ref[...]] * fold, axis=0)
    first_offset = jnp.concatenate([first_offset_ref[...]] * fold, axis=1)
    second = repeat_rows(second_ref[...].astype(jnp.float32), samples)
    row = lax.broadcasted_iota(jnp.int32, (width, 1), 0)
    spot = lax.broadcasted_iota(jnp.int32, (width, hidden), 0)
    channel = lax.broadcasted_iota(jnp.int32, (width, hidden), 1)
    second_offset = jnp.sum(
        jnp.where(spot // samples == channel, second_offset_ref[...], 0.0), axis=1, keepdims=True
    )
    residue = lax.broadcasted_iota(jnp.int32, (tile, LANES), 0)
    lane = lax.broadcasted_iota(jnp.int32, (tile, LANES), 1)
    own = residue % fold == lane // hidden
    group = lax.broadcasted_iota(jnp.int32, (tile // fold, tile), 0)
    member = lax.broadcasted_iota(jnp.int32, (tile // fold, tile), 1)
    gather = (member // fold == group).astype(jnp.bfloat16)

    dims = (((1,), (1,)), ((), ()))
    right = [jnp.zeros((width, tile), jnp.float32) for _ in range(tiles)]
    for s in range(samples):
        if s % some == 0:
            large[s // some].wait()
        values = x_ref[s].astype(jnp.float32)
        center = jnp.mean(values, axis=-1, keepdims=True)
        values = values - center
        variance = jnp.mean(jnp.square(values), axis=-1, keepdims=True)
        normed = (values * lax.rsqrt(variance + 1e-05) * gain_ref[...] + shift_ref[...]).astype(
            jnp.bfloat16
        )
        second_here = jnp.where(row % samples == s, second, 0.0).astype(jnp.bfloat16)
        for t in range(tiles):
            part = normed[t * tile : (t + 1) * tile]
            right[t] += lax.dot_general(second_here, part, dims, preferred_element_type=jnp.float32)
            left = lax.dot_general(part, first, dims, preferred_element_type=jnp.float32)
            left = jnp.where(own, left + first_offset, 0.0).astype(jnp.bfloat16)
            low = s * groups + t * (tile // fold)
            packed_ref[low : low + tile // fold, :] = jnp.dot(
                gather, left, preferred_element_type=jnp.float32
            )
    for t in range(tiles):
        value = (right[t] + second_offset).astype(jnp.bfloat16)
        keep_ref[t * width : (t + 1) * width, :] = value
        give_ref[t * width : (t + 1) * width, :] = value
    across = tile // LANES
    for low in range(0, groups, across):
        at = low // across * samples
        left_ref[at : at + samples, :] = jnp.concatenate(
            [packed_ref[pl.ds(low + n, samples, stride=groups), :] for n in range(across)], axis=1
        )

    device = lax.axis_index("row")
    per_chip = 2 * rows_here * hidden * samples // tile
    half = residues // rows_here // 4
    base = tiles * width
    way = 1 - 2 * (device % 2)
    place = place_of(device, half)
    for n in range(half):
        low = base + n * per_chip
        for message, ahead in ((keep_ref, way * (half - n)), (give_ref, -way * (half - 1 - n))):
            chip = chip_at(lax.rem(place + ahead + 2 * half, 2 * half), half)
            start = pl.multiple_of(chip * per_chip, per_chip)
            message[low : low + per_chip, :] = left_ref[pl.ds(start, per_chip), :].astype(jnp.bfloat16)


def weight_kernel(final_ref, offset_ref, out_ref, offset_out, wide_ref):
    offset_out[...] = offset_ref[...]
    channels, columns = out_ref.shape
    hidden = math.isqrt(columns)
    wide_ref[...] = final_ref[...].astype(jnp.float32)
    step = LANES // hidden
    for e in range(0, hidden, step):
        rows = [wide_ref[pl.ds(e + n, hidden, stride=hidden), :] for n in range(step)]
        out_ref[:, e * hidden : (e + step) * hidden] = jnp.concatenate(rows, axis=0).T.astype(
            jnp.bfloat16
        )


def pair_kernel(places, gridded, rows_here, hidden, samples, *refs):
    refs = list(refs)
    count = len(places)
    if gridded:
        shards = [(refs.pop(0), 0, refs.pop(0), 0) for _ in places]
    else:
        messages = [refs.pop(0) for _ in range(1 + max(place[0] for place in places))]
        shards = [(messages[n], right, messages[n], left) for n, right, left in places]
    weight_ref, offset_ref, out_hbm, left_ref, outer_ref, out_ref, sems = refs
    tile = shards[0][0].shape[1]
    here = samples // count
    span = rows_here * hidden
    deep = span * here // tile
    core = lax.rem(lax.axis_index("row"), 2)
    pieces = []
    for _, _, ref, base in shards:
        start = pl.multiple_of(base + core * deep, deep)
        piece = ref[pl.ds(start, deep), :].astype(jnp.float32)
        pieces.append(
            jnp.concatenate([piece[n * here : (n + 1) * here] for n in range(span // tile)], axis=1)
        )
    left_ref[...] = jnp.concatenate(pieces, axis=0).T.astype(jnp.bfloat16)

    left = left_ref[...]
    for e in range(0, hidden, 2):
        both = [
            ref[base + e * here : base + (e + 2) * here, :].astype(jnp.float32)
            for ref, base, _, _ in shards
        ]
        for k in range(2):
            right = jnp.concatenate([x[k * here : (k + 1) * here] for x in both], axis=0)
            outer = jnp.dot(left, right.astype(jnp.bfloat16), preferred_element_type=jnp.float32)
            outer = outer.astype(jnp.bfloat16)
            for i in range(rows_here):
                outer_ref[i, (e + k) * hidden : (e + k + 1) * hidden, :] = outer[
                    i * hidden : (i + 1) * hidden
                ]

    first = pl.program_id(0) * tile if gridded else 0
    copies = []
    for i in range(rows_here):
        value = jnp.dot(weight_ref[...], outer_ref[i], preferred_element_type=jnp.float32)
        value = value.T * (1.0 / samples) + offset_ref[...]
        out_ref[i] = value.astype(jnp.bfloat16)
        copies.append(
            pltpu.make_async_copy(out_ref.at[i], out_hbm.at[i, pl.ds(first, tile)], sems.at[i])
        )
        copies[-1].start()
    for copy in copies:
        copy.wait()


def per_device(
    size,
    alignment_embedding,
    rescaling_factor,
    recentering_offset,
    first_side_coefficients,
    first_side_offset,
    second_side_coefficients,
    second_side_offset,
    final_projector_coefficients,
    final_projector_offset,
):
    here, residues, features = alignment_embedding.shape
    hidden = first_side_coefficients.shape[1]
    channels = final_projector_coefficients.shape[1]
    width = here * hidden
    samples = here * size
    rows_here = residues // size
    half = size // 4
    tile = 256
    tiles = residues // tile
    body = tiles * width
    per_chip = 2 * rows_here * width // tile
    message = jax.ShapeDtypeStruct((body + half * per_chip, tile), jnp.bfloat16)

    vmem = pl.BlockSpec(memory_space=pltpu.VMEM)
    hbm = pl.BlockSpec(memory_space=pltpu.HBM)
    keep, give = pl.pallas_call(
        functools.partial(project_kernel, rows_here),
        out_shape=[message] * 2,
        in_specs=[hbm] * 7,
        out_specs=[vmem] * 2,
        scratch_shapes=[
            pltpu.VMEM((here, residues, features), jnp.bfloat16),
            pltpu.VMEM((1, features), jnp.float32),
            pltpu.VMEM((1, features), jnp.float32),
            pltpu.VMEM((hidden, features), jnp.bfloat16),
            pltpu.VMEM((1, hidden), jnp.float32),
            pltpu.VMEM((hidden, features), jnp.bfloat16),
            pltpu.VMEM((1, hidden), jnp.float32),
            pltpu.VMEM((residues * width // LANES, LANES), jnp.float32),
            pltpu.VMEM((residues * width // tile, tile), jnp.float32),
            pltpu.SemaphoreType.DMA((CHUNKS + 6,)),
        ],
        compiler_params=pltpu.CompilerParams(vmem_limit_bytes=32 * MIB),
        cost_estimate=pl.CostEstimate(
            flops=4 * here * residues * features * width,
            bytes_accessed=2 * here * residues * features,
            transcendentals=0,
        ),
    )(
        *[
            pltpu.with_memory_space_constraint(value, pltpu.HBM)
            for value in (
                alignment_embedding,
                rescaling_factor.reshape(1, features),
                recentering_offset.reshape(1, features),
                first_side_coefficients.T,
                first_side_offset.reshape(1, hidden),
                second_side_coefficients.T,
                second_side_offset.reshape(1, hidden),
            )
        ]
    )
    weight, offset = pl.pallas_call(
        weight_kernel,
        out_shape=[
            jax.ShapeDtypeStruct((channels, hidden * hidden), jnp.bfloat16),
            jax.ShapeDtypeStruct((1, channels), jnp.float32),
        ],
        in_specs=[vmem, vmem],
        out_specs=[vmem, vmem],
        scratch_shapes=[pltpu.VMEM((hidden * hidden, channels), jnp.float32)],
        compiler_params=pltpu.CompilerParams(vmem_limit_bytes=16 * MIB),
        cost_estimate=pl.CostEstimate(flops=2**28, bytes_accessed=2**20, transcendentals=0),
    )(final_projector_coefficients, final_projector_offset.reshape(1, channels))

    by_place = {(place_of(r, half), r % 2): r for r in range(size)}
    around = [
        (r, by_place[(place_of(r, half) + 1 - 2 * (r % 2)) % (2 * half), r % 2]) for r in range(size)
    ]
    turns = [[(r, t) for r, t in around if place_of(r, half) % 2 == n] for n in range(2)]

    def swap(value):
        return lax.ppermute(value, "row", [(r, r ^ 1) for r in range(size)])

    messages, places = [], []

    def take(pair):
        for value in pair:
            places.append((len(messages), 0, value.shape[0] - per_chip))
            messages.append(value)

    mine, theirs, weight, offset = lax.optimization_barrier((give, swap(give), weight, offset))
    take([mine, theirs])
    flying = [[keep] * 2, [theirs[: body + (half - 1) * per_chip]] * 2]
    swapped = []
    for step in range(1, half + 1):
        flown = [
            [lax.ppermute(x, "row", turns[(n + step + 1) % 2]) for n, x in enumerate(pair)]
            for pair in flying
        ]
        if step >= 3:
            flown[-1], swapped[step - 3] = lax.optimization_barrier((flown[-1], swapped[step - 3]))
        flying = [[x[: x.shape[0] - per_chip] for x in pair] for pair in flown]
        if step == half - 1:
            flying = flying[:1]
        landed = lax.optimization_barrier([first + second for first, second in flown])
        take(landed)
        swapped.append([swap(x) for x in landed])
    for pair in swapped:
        take(pair)

    gridded = tiles > 1
    if gridded:
        operands, specs = [], []
        for n, right, left in places:
            operands += [messages[n]] * 2
            specs += [
                pl.BlockSpec((width, tile), lambda t, first=right // width: (first + t, 0)),
                pl.BlockSpec((per_chip, tile), lambda t, at=left // per_chip: (at, 0)),
            ]
        specs += [
            pl.BlockSpec((channels, hidden * hidden), lambda t: (0, 0)),
            pl.BlockSpec((1, channels), lambda t: (0, 0)),
        ]
        grid = (tiles,)
    else:
        operands = messages
        specs = [vmem] * (len(messages) + 2)
        grid = ()
    return pl.pallas_call(
        functools.partial(pair_kernel, places, gridded, rows_here, hidden, samples),
        out_shape=jax.ShapeDtypeStruct((rows_here, residues, channels), jnp.bfloat16),
        grid=grid,
        in_specs=specs,
        out_specs=hbm,
        scratch_shapes=[
            pltpu.VMEM((rows_here * hidden, samples), jnp.bfloat16),
            pltpu.VMEM((rows_here, hidden * hidden, tile), jnp.bfloat16),
            pltpu.VMEM((rows_here, tile, channels), jnp.bfloat16),
            pltpu.SemaphoreType.DMA((rows_here,)),
        ],
        compiler_params=pltpu.CompilerParams(vmem_limit_bytes=40 * MIB),
    )(*operands, weight, offset)


def solution(mesh):
    return jax.shard_map(
        functools.partial(per_device, mesh.shape["row"]),
        mesh=mesh,
        in_specs=(P(("groups", "row"), None, None), P(), P(), P(), P(), P(), P(), P(), P()),
        out_specs=P(("groups", "row"), None, None),
        check_vma=False,
    )
```

```python
import functools
import math

import jax
import jax.numpy as jnp
from jax import lax
from jax.experimental import pallas as pl
from jax.experimental.pallas import tpu as pltpu
from jax.sharding import PartitionSpec as P

MIB = 1024 * 1024
LANES = 128
CHUNKS = 2


def repeat_rows(values, times):
    rows, cols = values.shape
    return jnp.broadcast_to(values[:, None, :], (rows, times, cols)).reshape(rows * times, cols)


def place_of(device, half):
    chip = device // 2
    return chip // 2 + (chip % 2) * (2 * half - 1 - 2 * (chip // 2))


def chip_at(place, half):
    return jnp.where(place < half, 2 * place, 2 * (2 * half - 1 - place) + 1)


def project_kernel(
    rows_here,
    x_hbm,
    gain_hbm,
    shift_hbm,
    first_hbm,
    first_offset_hbm,
    second_hbm,
    second_offset_hbm,
    keep_ref,
    give_ref,
    x_ref,
    gain_ref,
    shift_ref,
    first_ref,
    first_offset_ref,
    second_ref,
    second_offset_ref,
    packed_ref,
    left_ref,
    sems,
):
    samples, residues, features = x_ref.shape
    hidden = first_ref.shape[0]
    width = samples * hidden
    tile = keep_ref.shape[1]
    tiles = residues // tile
    fold = LANES // hidden
    groups = residues // fold
    small = [
        (first_hbm, first_ref),
        (second_hbm, second_ref),
        (gain_hbm, gain_ref),
        (shift_hbm, shift_ref),
        (first_offset_hbm, first_offset_ref),
        (second_offset_hbm, second_offset_ref),
    ]
    some = samples // CHUNKS
    large = []
    for n in range(CHUNKS):
        rows = pl.ds(n * some, some)
        large.append(pltpu.make_async_copy(x_hbm.at[rows], x_ref.at[rows], sems.at[n]))
        large[-1].start()
    copies = [
        pltpu.make_async_copy(src, dst, sems.at[CHUNKS + n]) for n, (src, dst) in enumerate(small)
    ]
    for copy in copies:
        copy.start()
    for copy in copies:
        copy.wait()

    first = jnp.concatenate([first_ref[...]] * fold, axis=0)
    first_offset = jnp.concatenate([first_offset_ref[...]] * fold, axis=1)
    second = repeat_rows(second_ref[...].astype(jnp.float32), samples)
    row = lax.broadcasted_iota(jnp.int32, (width, 1), 0)
    spot = lax.broadcasted_iota(jnp.int32, (width, hidden), 0)
    channel = lax.broadcasted_iota(jnp.int32, (width, hidden), 1)
    second_offset = jnp.sum(
        jnp.where(spot // samples == channel, second_offset_ref[...], 0.0), axis=1, keepdims=True
    )
    residue = lax.broadcasted_iota(jnp.int32, (tile, LANES), 0)
    lane = lax.broadcasted_iota(jnp.int32, (tile, LANES), 1)
    own = residue % fold == lane // hidden
    group = lax.broadcasted_iota(jnp.int32, (tile // fold, tile), 0)
    member = lax.broadcasted_iota(jnp.int32, (tile // fold, tile), 1)
    gather = (member // fold == group).astype(jnp.bfloat16)

    dims = (((1,), (1,)), ((), ()))
    right = [jnp.zeros((width, tile), jnp.float32) for _ in range(tiles)]
    for s in range(samples):
        if s % some == 0:
            large[s // some].wait()
        values = x_ref[s].astype(jnp.float32)
        center = jnp.mean(values, axis=-1, keepdims=True)
        values = values - center
        variance = jnp.mean(jnp.square(values), axis=-1, keepdims=True)
        normed = (values * lax.rsqrt(variance + 1e-05) * gain_ref[...] + shift_ref[...]).astype(
            jnp.bfloat16
        )
        second_here = jnp.where(row % samples == s, second, 0.0).astype(jnp.bfloat16)
        for t in range(tiles):
            part = normed[t * tile : (t + 1) * tile]
            right[t] += lax.dot_general(second_here, part, dims, preferred_element_type=jnp.float32)
            left = lax.dot_general(part, first, dims, preferred_element_type=jnp.float32)
            left = jnp.where(own, left + first_offset, 0.0).astype(jnp.bfloat16)
            low = s * groups + t * (tile // fold)
            packed_ref[low : low + tile // fold, :] = jnp.dot(
                gather, left, preferred_element_type=jnp.float32
            )
    for t in range(tiles):
        value = (right[t] + second_offset).astype(jnp.bfloat16)
        keep_ref[t * width : (t + 1) * width, :] = value
        give_ref[t * width : (t + 1) * width, :] = value
    across = tile // LANES
    for low in range(0, groups, across):
        at = low // across * samples
        left_ref[at : at + samples, :] = jnp.concatenate(
            [packed_ref[pl.ds(low + n, samples, stride=groups), :] for n in range(across)], axis=1
        )

    device = lax.axis_index("row")
    per_chip = 2 * rows_here * hidden * samples // tile
    half = residues // rows_here // 4
    base = tiles * width
    way = 1 - 2 * (device % 2)
    place = place_of(device, half)
    for n in range(half):
        low = base + n * per_chip
        for message, ahead in ((keep_ref, way * (half - n)), (give_ref, -way * (half - 1 - n))):
            chip = chip_at(lax.rem(place + ahead + 2 * half, 2 * half), half)
            start = pl.multiple_of(chip * per_chip, per_chip)
            message[low : low + per_chip, :] = left_ref[pl.ds(start, per_chip), :].astype(jnp.bfloat16)


def weight_kernel(final_ref, offset_ref, out_ref, offset_out, wide_ref):
    offset_out[...] = offset_ref[...]
    channels, columns = out_ref.shape
    hidden = math.isqrt(columns)
    wide_ref[...] = final_ref[...].astype(jnp.float32)
    step = LANES // hidden
    for e in range(0, hidden, step):
        rows = [wide_ref[pl.ds(e + n, hidden, stride=hidden), :] for n in range(step)]
        out_ref[:, e * hidden : (e + step) * hidden] = jnp.concatenate(rows, axis=0).T.astype(
            jnp.bfloat16
        )


def pair_kernel(places, gridded, rows_here, hidden, samples, *refs):
    refs = list(refs)
    count = len(places)
    if gridded:
        shards = [(refs.pop(0), 0, refs.pop(0), 0) for _ in places]
    else:
        messages = [refs.pop(0) for _ in range(1 + max(place[0] for place in places))]
        shards = [(messages[n], right, messages[n], left) for n, right, left in places]
    weight_ref, offset_ref, out_hbm, left_ref, outer_ref, out_ref, sems = refs
    tile = shards[0][0].shape[1]
    here = samples // count
    span = rows_here * hidden
    deep = span * here // tile
    core = lax.rem(lax.axis_index("row"), 2)
    pieces = []
    for _, _, ref, base in shards:
        start = pl.multiple_of(base + core * deep, deep)
        piece = ref[pl.ds(start, deep), :].astype(jnp.float32)
        pieces.append(
            jnp.concatenate([piece[n * here : (n + 1) * here] for n in range(span // tile)], axis=1)
        )
    left_ref[...] = jnp.concatenate(pieces, axis=0).T.astype(jnp.bfloat16)

    left = left_ref[...]
    for e in range(0, hidden, 2):
        both = [
            ref[base + e * here : base + (e + 2) * here, :].astype(jnp.float32)
            for ref, base, _, _ in shards
        ]
        for k in range(2):
            right = jnp.concatenate([x[k * here : (k + 1) * here] for x in both], axis=0)
            outer = jnp.dot(left, right.astype(jnp.bfloat16), preferred_element_type=jnp.float32)
            outer = outer.astype(jnp.bfloat16)
            for i in range(rows_here):
                outer_ref[i, (e + k) * hidden : (e + k + 1) * hidden, :] = outer[
                    i * hidden : (i + 1) * hidden
                ]

    first = pl.program_id(0) * tile if gridded else 0
    copies = []
    for i in range(rows_here):
        value = jnp.dot(weight_ref[...], outer_ref[i], preferred_element_type=jnp.float32)
        value = value.T * (1.0 / samples) + offset_ref[...]
        out_ref[i] = value.astype(jnp.bfloat16)
        copies.append(
            pltpu.make_async_copy(out_ref.at[i], out_hbm.at[i, pl.ds(first, tile)], sems.at[i])
        )
        copies[-1].start()
    for copy in copies:
        copy.wait()


def per_device(
    size,
    alignment_embedding,
    rescaling_factor,
    recentering_offset,
    first_side_coefficients,
    first_side_offset,
    second_side_coefficients,
    second_side_offset,
    final_projector_coefficients,
    final_projector_offset,
):
    here, residues, features = alignment_embedding.shape
    hidden = first_side_coefficients.shape[1]
    channels = final_projector_coefficients.shape[1]
    width = here * hidden
    samples = here * size
    rows_here = residues // size
    half = size // 4
    tile = 256
    tiles = residues // tile
    body = tiles * width
    per_chip = 2 * rows_here * width // tile
    message = jax.ShapeDtypeStruct((body + half * per_chip, tile), jnp.bfloat16)

    vmem = pl.BlockSpec(memory_space=pltpu.VMEM)
    hbm = pl.BlockSpec(memory_space=pltpu.HBM)
    keep, give = pl.pallas_call(
        functools.partial(project_kernel, rows_here),
        out_shape=[message] * 2,
        in_specs=[hbm] * 7,
        out_specs=[vmem] * 2,
        scratch_shapes=[
            pltpu.VMEM((here, residues, features), jnp.bfloat16),
            pltpu.VMEM((1, features), jnp.float32),
            pltpu.VMEM((1, features), jnp.float32),
            pltpu.VMEM((hidden, features), jnp.bfloat16),
            pltpu.VMEM((1, hidden), jnp.float32),
            pltpu.VMEM((hidden, features), jnp.bfloat16),
            pltpu.VMEM((1, hidden), jnp.float32),
            pltpu.VMEM((residues * width // LANES, LANES), jnp.float32),
            pltpu.VMEM((residues * width // tile, tile), jnp.float32),
            pltpu.SemaphoreType.DMA((CHUNKS + 6,)),
        ],
        compiler_params=pltpu.CompilerParams(vmem_limit_bytes=32 * MIB),
        cost_estimate=pl.CostEstimate(
            flops=4 * here * residues * features * width,
            bytes_accessed=2 * here * residues * features,
            transcendentals=0,
        ),
    )(
        *[
            pltpu.with_memory_space_constraint(value, pltpu.HBM)
            for value in (
                alignment_embedding,
                rescaling_factor.reshape(1, features),
                recentering_offset.reshape(1, features),
                first_side_coefficients.T,
                first_side_offset.reshape(1, hidden),
                second_side_coefficients.T,
                second_side_offset.reshape(1, hidden),
            )
        ]
    )
    weight, offset = pl.pallas_call(
        weight_kernel,
        out_shape=[
            jax.ShapeDtypeStruct((channels, hidden * hidden), jnp.bfloat16),
            jax.ShapeDtypeStruct((1, channels), jnp.float32),
        ],
        in_specs=[vmem, vmem],
        out_specs=[vmem, vmem],
        scratch_shapes=[pltpu.VMEM((hidden * hidden, channels), jnp.float32)],
        compiler_params=pltpu.CompilerParams(vmem_limit_bytes=16 * MIB),
        cost_estimate=pl.CostEstimate(flops=2**28, bytes_accessed=2**20, transcendentals=0),
    )(final_projector_coefficients, final_projector_offset.reshape(1, channels))

    by_place = {(place_of(r, half), r % 2): r for r in range(size)}

    def hop(value, way, cross):
        pairs = []
        for r in range(size):
            place = place_of(r, half) + way * (1 - 2 * (r % 2))
            pairs.append((r, by_place[place % (2 * half), (r + cross) % 2]))
        return lax.ppermute(value, "row", pairs)

    def swap(value):
        return lax.ppermute(value, "row", [(r, r ^ 1) for r in range(size)])

    messages, places = [], []

    def take(pair):
        for value in pair:
            places.append((len(messages), 0, value.shape[0] - per_chip))
            messages.append(value)

    landed = [hop(keep, 1, 0), hop(give[: body + (half - 1) * per_chip], -1, 1)]
    take([give])
    swapped = [[swap(give)]]
    for step in range(1, half + 1):
        if step == 1:
            landed[0], weight, offset = lax.optimization_barrier((landed[0], weight, offset))
        if step >= 2:
            landed[-1], swapped[step - 2] = lax.optimization_barrier((landed[-1], swapped[step - 2]))
        flying = [x[: x.shape[0] - per_chip] for x in landed]
        landed = lax.optimization_barrier(landed)
        take(landed)
        swapped.append([swap(x) for x in landed])
        if step == half - 1:
            flying = flying[:1]
        if step < half:
            landed = [hop(x, 1, 0) for x in flying]
    for pair in swapped:
        take(pair)

    gridded = tiles > 1
    if gridded:
        operands, specs = [], []
        for n, right, left in places:
            operands += [messages[n]] * 2
            specs += [
                pl.BlockSpec((width, tile), lambda t, first=right // width: (first + t, 0)),
                pl.BlockSpec((per_chip, tile), lambda t, at=left // per_chip: (at, 0)),
            ]
        specs += [
            pl.BlockSpec((channels, hidden * hidden), lambda t: (0, 0)),
            pl.BlockSpec((1, channels), lambda t: (0, 0)),
        ]
        grid = (tiles,)
    else:
        operands = messages
        specs = [vmem] * (len(messages) + 2)
        grid = ()
    return pl.pallas_call(
        functools.partial(pair_kernel, places, gridded, rows_here, hidden, samples),
        out_shape=jax.ShapeDtypeStruct((rows_here, residues, channels), jnp.bfloat16),
        grid=grid,
        in_specs=specs,
        out_specs=hbm,
        scratch_shapes=[
            pltpu.VMEM((rows_here * hidden, samples), jnp.bfloat16),
            pltpu.VMEM((rows_here, hidden * hidden, tile), jnp.bfloat16),
            pltpu.VMEM((rows_here, tile, channels), jnp.bfloat16),
            pltpu.SemaphoreType.DMA((rows_here,)),
        ],
        compiler_params=pltpu.CompilerParams(vmem_limit_bytes=40 * MIB),
    )(*operands, weight, offset)


def solution(mesh):
    return jax.shard_map(
        functools.partial(per_device, mesh.shape["row"]),
        mesh=mesh,
        in_specs=(P(("groups", "row"), None, None), P(), P(), P(), P(), P(), P(), P(), P()),
        out_specs=P(("groups", "row"), None, None),
        check_vma=False,
    )
```

```python
import functools
import math

import jax
import jax.numpy as jnp
from jax import lax
from jax.experimental import pallas as pl
from jax.experimental.pallas import tpu as pltpu
from jax.sharding import PartitionSpec as P

MIB = 1024 * 1024
LANES = 128
CHUNKS = 2
BLOCK = 64


def repeat_rows(values, times):
    rows, cols = values.shape
    return jnp.broadcast_to(values[:, None, :], (rows, times, cols)).reshape(rows * times, cols)


def place_of(device, half):
    chip = device // 2
    return chip // 2 + (chip % 2) * (2 * half - 1 - 2 * (chip // 2))


def chip_at(place, half):
    return jnp.where(place < half, 2 * place, 2 * (2 * half - 1 - place) + 1)


def project_kernel(
    rows_here,
    x_hbm,
    gain_hbm,
    shift_hbm,
    first_hbm,
    first_offset_hbm,
    second_hbm,
    second_offset_hbm,
    keep_ref,
    give_ref,
    x_ref,
    gain_ref,
    shift_ref,
    first_ref,
    first_offset_ref,
    second_ref,
    second_offset_ref,
    packed_ref,
    left_ref,
    sems,
):
    samples, residues, features = x_ref.shape
    hidden = first_ref.shape[0]
    width = samples * hidden
    tile = keep_ref.shape[1]
    tiles = residues // tile
    fold = LANES // hidden
    groups = residues // fold
    small = [
        (first_hbm, first_ref),
        (second_hbm, second_ref),
        (gain_hbm, gain_ref),
        (shift_hbm, shift_ref),
        (first_offset_hbm, first_offset_ref),
        (second_offset_hbm, second_offset_ref),
    ]
    some = samples // CHUNKS
    large = []
    for n in range(CHUNKS):
        rows = pl.ds(n * some, some)
        large.append(pltpu.make_async_copy(x_hbm.at[rows], x_ref.at[rows], sems.at[n]))
        large[-1].start()
    copies = [
        pltpu.make_async_copy(src, dst, sems.at[CHUNKS + n]) for n, (src, dst) in enumerate(small)
    ]
    for copy in copies:
        copy.start()
    for copy in copies:
        copy.wait()

    first = jnp.concatenate([first_ref[...]] * fold, axis=0)
    first_offset = jnp.concatenate([first_offset_ref[...]] * fold, axis=1)
    second = repeat_rows(second_ref[...].astype(jnp.float32), samples)
    row = lax.broadcasted_iota(jnp.int32, (width, 1), 0)
    spot = lax.broadcasted_iota(jnp.int32, (width, hidden), 0)
    channel = lax.broadcasted_iota(jnp.int32, (width, hidden), 1)
    second_offset = jnp.sum(
        jnp.where(spot // samples == channel, second_offset_ref[...], 0.0), axis=1, keepdims=True
    )
    residue = lax.broadcasted_iota(jnp.int32, (tile, LANES), 0)
    lane = lax.broadcasted_iota(jnp.int32, (tile, LANES), 1)
    own = residue % fold == lane // hidden
    group = lax.broadcasted_iota(jnp.int32, (tile // fold, tile), 0)
    member = lax.broadcasted_iota(jnp.int32, (tile // fold, tile), 1)
    gather = (member // fold == group).astype(jnp.bfloat16)

    dims = (((1,), (1,)), ((), ()))
    right = [jnp.zeros((width, tile), jnp.float32) for _ in range(tiles)]
    for s in range(samples):
        if s % some == 0:
            large[s // some].wait()
        normed = []
        for low in range(0, residues, BLOCK):
            values = x_ref[s, low : low + BLOCK, :].astype(jnp.float32)
            center = jnp.mean(values, axis=-1, keepdims=True)
            values = values - center
            variance = jnp.mean(jnp.square(values), axis=-1, keepdims=True)
            values = values * lax.rsqrt(variance + 1e-05) * gain_ref[...] + shift_ref[...]
            normed.append(values.astype(jnp.bfloat16))
        normed = jnp.concatenate(normed, axis=0)
        second_here = jnp.where(row % samples == s, second, 0.0).astype(jnp.bfloat16)
        for t in range(tiles):
            part = normed[t * tile : (t + 1) * tile]
            right[t] += lax.dot_general(second_here, part, dims, preferred_element_type=jnp.float32)
            left = lax.dot_general(part, first, dims, preferred_element_type=jnp.float32)
            left = jnp.where(own, left + first_offset, 0.0).astype(jnp.bfloat16)
            low = s * groups + t * (tile // fold)
            packed_ref[low : low + tile // fold, :] = jnp.dot(
                gather, left, preferred_element_type=jnp.float32
            )
    for t in range(tiles):
        value = (right[t] + second_offset).astype(jnp.bfloat16)
        keep_ref[t * width : (t + 1) * width, :] = value
        give_ref[t * width : (t + 1) * width, :] = value
    across = tile // LANES
    for low in range(0, groups, across):
        at = low // across * samples
        left_ref[at : at + samples, :] = jnp.concatenate(
            [packed_ref[pl.ds(low + n, samples, stride=groups), :] for n in range(across)], axis=1
        )

    device = lax.axis_index("row")
    per_chip = 2 * rows_here * hidden * samples // tile
    half = residues // rows_here // 4
    base = tiles * width
    way = 1 - 2 * (device % 2)
    place = place_of(device, half)
    spots = [(keep_ref, base + n * per_chip, half - n) for n in range(half)]
    spots += [(give_ref, base + n * per_chip, n + 1 - half) for n in range(half)]
    for message, low, ahead in spots:
        chip = chip_at(lax.rem(place + way * ahead + 2 * half, 2 * half), half)
        start = pl.multiple_of(chip * per_chip, per_chip)
        message[low : low + per_chip, :] = left_ref[pl.ds(start, per_chip), :].astype(jnp.bfloat16)


def join_kernel(base, per_chip, mine_ref, theirs_ref, next_ref):
    next_ref[:base, :] = theirs_ref[:base, :]
    for n in range((next_ref.shape[0] - base) // (2 * per_chip)):
        low = base + n * per_chip
        at = low + n * per_chip
        next_ref[at : at + per_chip, :] = mine_ref[low + per_chip : low + 2 * per_chip, :]
        next_ref[at + per_chip : at + 2 * per_chip, :] = theirs_ref[low : low + per_chip, :]


def weight_kernel(final_ref, offset_ref, out_ref, offset_out, wide_ref):
    offset_out[...] = offset_ref[...]
    channels, columns = out_ref.shape
    hidden = math.isqrt(columns)
    wide_ref[...] = final_ref[...].astype(jnp.float32)
    step = LANES // hidden
    for e in range(0, hidden, step):
        rows = [wide_ref[pl.ds(e + n, hidden, stride=hidden), :] for n in range(step)]
        out_ref[:, e * hidden : (e + step) * hidden] = jnp.concatenate(rows, axis=0).T.astype(
            jnp.bfloat16
        )


def pair_kernel(places, gridded, rows_here, hidden, samples, *refs):
    refs = list(refs)
    count = len(places)
    if gridded:
        shards = [(refs.pop(0), 0, refs.pop(0), 0) for _ in places]
    else:
        messages = [refs.pop(0) for _ in places]
        shards = [(messages[n], right, messages[m], left) for n, right, m, left in places]
    weight_ref, offset_ref, out_hbm, left_ref, outer_ref, out_ref, sems = refs
    tile = shards[0][0].shape[1]
    here = samples // count
    span = rows_here * hidden
    deep = span * here // tile
    core = lax.rem(lax.axis_index("row"), 2)
    pieces = []
    for _, _, ref, base in shards:
        start = pl.multiple_of(base + core * deep, deep)
        piece = ref[pl.ds(start, deep), :].astype(jnp.float32)
        pieces.append(
            jnp.concatenate([piece[n * here : (n + 1) * here] for n in range(span // tile)], axis=1)
        )
    left_ref[...] = jnp.concatenate(pieces, axis=0).T.astype(jnp.bfloat16)

    left = left_ref[...]
    for e in range(0, hidden, 2):
        both = [
            ref[base + e * here : base + (e + 2) * here, :].astype(jnp.float32)
            for ref, base, _, _ in shards
        ]
        for k in range(2):
            right = jnp.concatenate([x[k * here : (k + 1) * here] for x in both], axis=0)
            outer = jnp.dot(left, right.astype(jnp.bfloat16), preferred_element_type=jnp.float32)
            outer = outer.astype(jnp.bfloat16)
            for i in range(rows_here):
                outer_ref[i, (e + k) * hidden : (e + k + 1) * hidden, :] = outer[
                    i * hidden : (i + 1) * hidden
                ]

    first = pl.program_id(0) * tile if gridded else 0
    copies = []
    for i in range(rows_here):
        value = jnp.dot(weight_ref[...], outer_ref[i], preferred_element_type=jnp.float32)
        value = value.T * (1.0 / samples) + offset_ref[...]
        out_ref[i] = value.astype(jnp.bfloat16)
        copies.append(
            pltpu.make_async_copy(out_ref.at[i], out_hbm.at[i, pl.ds(first, tile)], sems.at[i])
        )
        copies[-1].start()
    for copy in copies:
        copy.wait()


def per_device(
    size,
    alignment_embedding,
    rescaling_factor,
    recentering_offset,
    first_side_coefficients,
    first_side_offset,
    second_side_coefficients,
    second_side_offset,
    final_projector_coefficients,
    final_projector_offset,
):
    here, residues, features = alignment_embedding.shape
    hidden = first_side_coefficients.shape[1]
    channels = final_projector_coefficients.shape[1]
    width = here * hidden
    samples = here * size
    rows_here = residues // size
    half = size // 4
    tile = 256
    tiles = residues // tile
    body = tiles * width
    per_chip = 2 * rows_here * width // tile

    def rows(count):
        return jax.ShapeDtypeStruct((count, tile), jnp.bfloat16)

    vmem = pl.BlockSpec(memory_space=pltpu.VMEM)
    hbm = pl.BlockSpec(memory_space=pltpu.HBM)
    keep, give = pl.pallas_call(
        functools.partial(project_kernel, rows_here),
        out_shape=[rows(body + half * per_chip)] * 2,
        in_specs=[hbm] * 7,
        out_specs=[vmem] * 2,
        scratch_shapes=[
            pltpu.VMEM((here, residues, features), jnp.bfloat16),
            pltpu.VMEM((1, features), jnp.float32),
            pltpu.VMEM((1, features), jnp.float32),
            pltpu.VMEM((hidden, features), jnp.bfloat16),
            pltpu.VMEM((1, hidden), jnp.float32),
            pltpu.VMEM((hidden, features), jnp.bfloat16),
            pltpu.VMEM((1, hidden), jnp.float32),
            pltpu.VMEM((residues * width // LANES, LANES), jnp.float32),
            pltpu.VMEM((residues * width // tile, tile), jnp.float32),
            pltpu.SemaphoreType.DMA((CHUNKS + 6,)),
        ],
        compiler_params=pltpu.CompilerParams(vmem_limit_bytes=32 * MIB),
        cost_estimate=pl.CostEstimate(
            flops=4 * here * residues * features * width,
            bytes_accessed=2 * here * residues * features,
            transcendentals=0,
        ),
    )(
        *[
            pltpu.with_memory_space_constraint(value, pltpu.HBM)
            for value in (
                alignment_embedding,
                rescaling_factor.reshape(1, features),
                recentering_offset.reshape(1, features),
                first_side_coefficients.T,
                first_side_offset.reshape(1, hidden),
                second_side_coefficients.T,
                second_side_offset.reshape(1, hidden),
            )
        ]
    )
    by_place = {(place_of(r, half), r % 2): r for r in range(size)}
    around = [
        (r, by_place[(place_of(r, half) + 1 - 2 * (r % 2)) % (2 * half), r % 2]) for r in range(size)
    ]

    def swap(value):
        return lax.ppermute(value, "row", [(r, r ^ 1) for r in range(size)])

    weight, offset = pl.pallas_call(
        weight_kernel,
        out_shape=[
            jax.ShapeDtypeStruct((channels, hidden * hidden), jnp.bfloat16),
            jax.ShapeDtypeStruct((1, channels), jnp.float32),
        ],
        in_specs=[vmem] * 2,
        out_specs=[vmem] * 2,
        scratch_shapes=[pltpu.VMEM((hidden * hidden, channels), jnp.float32)],
        compiler_params=pltpu.CompilerParams(vmem_limit_bytes=16 * MIB),
        cost_estimate=pl.CostEstimate(flops=2**28, bytes_accessed=2**20, transcendentals=0),
    )(final_projector_coefficients, final_projector_offset.reshape(1, channels))
    theirs, weight, offset = lax.optimization_barrier((swap(give), weight, offset))
    messages = [give, theirs]
    places = [(n, 0, n, body + (half - 1) * per_chip) for n in range(2)]

    def take(*lefts):
        places.extend((len(messages) + n, 0, len(messages) + m, low) for n, (m, low) in enumerate(lefts))

    flying = [keep, theirs[: body + (half - 1) * per_chip]]
    swapped, lefts = [], []
    for step in range(1, half + 1):
        landed = [lax.ppermute(x, "row", around) for x in flying]
        if step >= 3:
            landed[-1], swapped[step - 3] = lax.optimization_barrier((landed[-1], swapped[step - 3]))
        low = [x.shape[0] - per_chip for x in landed]
        if step == 1:
            lefts.append([(0, low[0]), (1, low[1])])
        elif step < half:
            lefts.append([(1, low[1] - per_chip), (1, low[1])])
        else:
            lefts.append([(0, low[0])])
        flying = [landed[0][: body + per_chip]]
        if step == 1:
            flying += pl.pallas_call(
                functools.partial(join_kernel, body, per_chip),
                out_shape=[rows(body + 2 * (half - 2) * per_chip)],
                in_specs=[vmem] * 2,
                out_specs=[vmem],
                compiler_params=pltpu.CompilerParams(vmem_limit_bytes=16 * MIB),
                cost_estimate=pl.CostEstimate(flops=0, bytes_accessed=2**19, transcendentals=0),
            )(*landed)
        elif step < half - 1:
            flying.append(landed[1][: landed[1].shape[0] - 2 * per_chip])
        landed = lax.optimization_barrier(landed)
        take(*lefts[-1])
        messages += landed
        swapped.append([swap(x) for x in landed])
    for pair, left in zip(swapped, lefts):
        take(*left)
        messages += pair

    gridded = tiles > 1
    if gridded:
        operands, specs = [], []
        for n, right, m, left in places:
            operands += [messages[n], messages[m]]
            specs += [
                pl.BlockSpec((width, tile), lambda t, first=right // width: (first + t, 0)),
                pl.BlockSpec((per_chip, tile), lambda t, at=left // per_chip: (at, 0)),
            ]
        specs += [
            pl.BlockSpec((channels, hidden * hidden), lambda t: (0, 0)),
            pl.BlockSpec((1, channels), lambda t: (0, 0)),
        ]
        grid = (tiles,)
    else:
        operands = messages
        specs = [vmem] * (len(messages) + 2)
        grid = ()
    return pl.pallas_call(
        functools.partial(pair_kernel, places, gridded, rows_here, hidden, samples),
        out_shape=jax.ShapeDtypeStruct((rows_here, residues, channels), jnp.bfloat16),
        grid=grid,
        in_specs=specs,
        out_specs=hbm,
        scratch_shapes=[
            pltpu.VMEM((rows_here * hidden, samples), jnp.bfloat16),
            pltpu.VMEM((rows_here, hidden * hidden, tile), jnp.bfloat16),
            pltpu.VMEM((rows_here, tile, channels), jnp.bfloat16),
            pltpu.SemaphoreType.DMA((rows_here,)),
        ],
        compiler_params=pltpu.CompilerParams(vmem_limit_bytes=40 * MIB),
    )(*operands, weight, offset)


def solution(mesh):
    return jax.shard_map(
        functools.partial(per_device, mesh.shape["row"]),
        mesh=mesh,
        in_specs=(P(("groups", "row"), None, None), P(), P(), P(), P(), P(), P(), P(), P()),
        out_specs=P(("groups", "row"), None, None),
        check_vma=False,
    )
```

```python
import functools
import math

import jax
import jax.numpy as jnp
from jax import lax
from jax.experimental import pallas as pl
from jax.experimental.pallas import tpu as pltpu
from jax.sharding import PartitionSpec as P

MIB = 1024 * 1024
LANES = 128
CHUNKS = 2
BLOCK = 64


def repeat_rows(values, times):
    rows, cols = values.shape
    return jnp.broadcast_to(values[:, None, :], (rows, times, cols)).reshape(rows * times, cols)


def place_of(device, half):
    chip = device // 2
    return chip // 2 + (chip % 2) * (2 * half - 1 - 2 * (chip // 2))


def chip_at(place, half):
    return jnp.where(place < half, 2 * place, 2 * (2 * half - 1 - place) + 1)


def project_kernel(
    rows_here,
    x_hbm,
    gain_hbm,
    shift_hbm,
    first_hbm,
    first_offset_hbm,
    second_hbm,
    second_offset_hbm,
    keep_ref,
    give_ref,
    x_ref,
    gain_ref,
    shift_ref,
    first_ref,
    first_offset_ref,
    second_ref,
    second_offset_ref,
    packed_ref,
    left_ref,
    sems,
):
    samples, residues, features = x_ref.shape
    hidden = first_ref.shape[0]
    width = samples * hidden
    tile = keep_ref.shape[1]
    tiles = residues // tile
    fold = LANES // hidden
    groups = residues // fold
    small = [
        (first_hbm, first_ref),
        (second_hbm, second_ref),
        (gain_hbm, gain_ref),
        (shift_hbm, shift_ref),
        (first_offset_hbm, first_offset_ref),
        (second_offset_hbm, second_offset_ref),
    ]
    some = samples // CHUNKS
    copies = [
        pltpu.make_async_copy(src, dst, sems.at[CHUNKS + n]) for n, (src, dst) in enumerate(small)
    ]
    for copy in copies:
        copy.start()
    large = []
    for n in range(CHUNKS):
        rows = pl.ds(n * some, some)
        large.append(pltpu.make_async_copy(x_hbm.at[rows], x_ref.at[rows], sems.at[n]))
        large[-1].start()
    for copy in copies:
        copy.wait()

    first = jnp.concatenate([first_ref[...].astype(jnp.float32)] * fold, axis=0).T
    first = first.astype(jnp.bfloat16)
    first_offset = jnp.concatenate([first_offset_ref[...]] * fold, axis=1)
    second = repeat_rows(second_ref[...].astype(jnp.float32), samples).T
    column = lax.broadcasted_iota(jnp.int32, (1, width), 1)
    spot = lax.broadcasted_iota(jnp.int32, (width, hidden), 0)
    channel = lax.broadcasted_iota(jnp.int32, (width, hidden), 1)
    second_offset = jnp.sum(
        jnp.where(spot // samples == channel, second_offset_ref[...], 0.0), axis=1, keepdims=True
    )
    residue = lax.broadcasted_iota(jnp.int32, (tile, LANES), 0)
    lane = lax.broadcasted_iota(jnp.int32, (tile, LANES), 1)
    own = residue % fold == lane // hidden
    group = lax.broadcasted_iota(jnp.int32, (tile // fold, tile), 0)
    member = lax.broadcasted_iota(jnp.int32, (tile // fold, tile), 1)
    gather = (member // fold == group).astype(jnp.bfloat16)

    right = [jnp.zeros((tile, width), jnp.float32) for _ in range(tiles)]
    for s in range(samples):
        if s % some == 0:
            large[s // some].wait()
        normed = []
        for low in range(0, residues, BLOCK):
            values = x_ref[s, low : low + BLOCK, :].astype(jnp.float32)
            center = jnp.mean(values, axis=-1, keepdims=True)
            values = values - center
            variance = jnp.mean(jnp.square(values), axis=-1, keepdims=True)
            values = values * lax.rsqrt(variance + 1e-05) * gain_ref[...] + shift_ref[...]
            normed.append(values.astype(jnp.bfloat16))
        normed = jnp.concatenate(normed, axis=0)
        second_here = jnp.where(column % samples == s, second, 0.0).astype(jnp.bfloat16)
        for t in range(tiles):
            part = normed[t * tile : (t + 1) * tile]
            right[t] += jnp.dot(part, second_here, preferred_element_type=jnp.float32)
            left = jnp.dot(part, first, preferred_element_type=jnp.float32)
            left = jnp.where(own, left + first_offset, 0.0).astype(jnp.bfloat16)
            low = s * groups + t * (tile // fold)
            packed_ref[low : low + tile // fold, :] = jnp.dot(
                gather, left, preferred_element_type=jnp.float32
            )
    for t in range(tiles):
        value = (right[t].T + second_offset).astype(jnp.bfloat16)
        keep_ref[t * width : (t + 1) * width, :] = value
        give_ref[t * width : (t + 1) * width, :] = value
    across = tile // LANES
    for low in range(0, groups, across):
        at = low // across * samples
        left_ref[at : at + samples, :] = jnp.concatenate(
            [packed_ref[pl.ds(low + n, samples, stride=groups), :] for n in range(across)], axis=1
        )

    device = lax.axis_index("row")
    per_chip = 2 * rows_here * hidden * samples // tile
    half = residues // rows_here // 4
    base = tiles * width
    way = 1 - 2 * (device % 2)
    place = place_of(device, half)
    spots = [(keep_ref, base + n * per_chip, half - n) for n in range(half)]
    spots += [(give_ref, base + n * per_chip, n + 1 - half) for n in range(half)]
    for message, low, ahead in spots:
        chip = chip_at(lax.rem(place + way * ahead + 2 * half, 2 * half), half)
        start = pl.multiple_of(chip * per_chip, per_chip)
        message[low : low + per_chip, :] = left_ref[pl.ds(start, per_chip), :].astype(jnp.bfloat16)


def join_kernel(base, per_chip, mine_ref, theirs_ref, next_ref):
    next_ref[:base, :] = theirs_ref[:base, :]
    for n in range((next_ref.shape[0] - base) // (2 * per_chip)):
        low = base + n * per_chip
        at = low + n * per_chip
        next_ref[at : at + per_chip, :] = mine_ref[low + per_chip : low + 2 * per_chip, :]
        next_ref[at + per_chip : at + 2 * per_chip, :] = theirs_ref[low : low + per_chip, :]


def weight_kernel(final_ref, offset_ref, out_ref, offset_out, wide_ref):
    offset_out[...] = offset_ref[...]
    channels, columns = out_ref.shape
    hidden = math.isqrt(columns)
    wide_ref[...] = final_ref[...].astype(jnp.float32)
    step = LANES // hidden
    for e in range(0, hidden, step):
        rows = [wide_ref[pl.ds(e + n, hidden, stride=hidden), :] for n in range(step)]
        out_ref[:, e * hidden : (e + step) * hidden] = jnp.concatenate(rows, axis=0).T.astype(
            jnp.bfloat16
        )


def pair_kernel(places, gridded, rows_here, hidden, samples, *refs):
    refs = list(refs)
    count = len(places)
    if gridded:
        shards = [(refs.pop(0), 0, refs.pop(0), 0) for _ in places]
    else:
        messages = [refs.pop(0) for _ in places]
        shards = [(messages[n], right, messages[m], left) for n, right, m, left in places]
    weight_ref, offset_ref, out_hbm, left_ref, outer_ref, out_ref, sems = refs
    tile = shards[0][0].shape[1]
    here = samples // count
    span = rows_here * hidden
    deep = span * here // tile
    core = lax.rem(lax.axis_index("row"), 2)
    pieces = []
    for _, _, ref, base in shards:
        start = pl.multiple_of(base + core * deep, deep)
        piece = ref[pl.ds(start, deep), :].astype(jnp.float32)
        pieces.append(
            jnp.concatenate([piece[n * here : (n + 1) * here] for n in range(span // tile)], axis=1)
        )
    left_ref[...] = jnp.concatenate(pieces, axis=0).T.astype(jnp.bfloat16)

    left = left_ref[...]
    for e in range(0, hidden, 2):
        both = [
            ref[base + e * here : base + (e + 2) * here, :].astype(jnp.float32)
            for ref, base, _, _ in shards
        ]
        for k in range(2):
            right = jnp.concatenate([x[k * here : (k + 1) * here] for x in both], axis=0)
            outer = jnp.dot(left, right.astype(jnp.bfloat16), preferred_element_type=jnp.float32)
            outer = outer.astype(jnp.bfloat16)
            for i in range(rows_here):
                outer_ref[i, (e + k) * hidden : (e + k + 1) * hidden, :] = outer[
                    i * hidden : (i + 1) * hidden
                ]

    first = pl.program_id(0) * tile if gridded else 0
    copies = []
    for i in range(rows_here):
        value = jnp.dot(weight_ref[...], outer_ref[i], preferred_element_type=jnp.float32)
        value = value.T * (1.0 / samples) + offset_ref[...]
        out_ref[i] = value.astype(jnp.bfloat16)
        copies.append(
            pltpu.make_async_copy(out_ref.at[i], out_hbm.at[i, pl.ds(first, tile)], sems.at[i])
        )
        copies[-1].start()
    for copy in copies:
        copy.wait()


def per_device(
    size,
    alignment_embedding,
    rescaling_factor,
    recentering_offset,
    first_side_coefficients,
    first_side_offset,
    second_side_coefficients,
    second_side_offset,
    final_projector_coefficients,
    final_projector_offset,
):
    here, residues, features = alignment_embedding.shape
    hidden = first_side_coefficients.shape[1]
    channels = final_projector_coefficients.shape[1]
    width = here * hidden
    samples = here * size
    rows_here = residues // size
    half = size // 4
    tile = 256
    tiles = residues // tile
    body = tiles * width
    per_chip = 2 * rows_here * width // tile

    def rows(count):
        return jax.ShapeDtypeStruct((count, tile), jnp.bfloat16)

    vmem = pl.BlockSpec(memory_space=pltpu.VMEM)
    hbm = pl.BlockSpec(memory_space=pltpu.HBM)
    keep, give = pl.pallas_call(
        functools.partial(project_kernel, rows_here),
        out_shape=[rows(body + half * per_chip)] * 2,
        in_specs=[hbm] * 7,
        out_specs=[vmem] * 2,
        scratch_shapes=[
            pltpu.VMEM((here, residues, features), jnp.bfloat16),
            pltpu.VMEM((1, features), jnp.float32),
            pltpu.VMEM((1, features), jnp.float32),
            pltpu.VMEM((hidden, features), jnp.bfloat16),
            pltpu.VMEM((1, hidden), jnp.float32),
            pltpu.VMEM((hidden, features), jnp.bfloat16),
            pltpu.VMEM((1, hidden), jnp.float32),
            pltpu.VMEM((residues * width // LANES, LANES), jnp.float32),
            pltpu.VMEM((residues * width // tile, tile), jnp.float32),
            pltpu.SemaphoreType.DMA((CHUNKS + 6,)),
        ],
        compiler_params=pltpu.CompilerParams(vmem_limit_bytes=32 * MIB),
        cost_estimate=pl.CostEstimate(
            flops=4 * here * residues * features * width,
            bytes_accessed=2 * here * residues * features,
            transcendentals=0,
        ),
    )(
        *[
            pltpu.with_memory_space_constraint(value, pltpu.HBM)
            for value in (
                alignment_embedding,
                rescaling_factor.reshape(1, features),
                recentering_offset.reshape(1, features),
                first_side_coefficients.T,
                first_side_offset.reshape(1, hidden),
                second_side_coefficients.T,
                second_side_offset.reshape(1, hidden),
            )
        ]
    )
    by_place = {(place_of(r, half), r % 2): r for r in range(size)}
    around = [
        (r, by_place[(place_of(r, half) + 1 - 2 * (r % 2)) % (2 * half), r % 2]) for r in range(size)
    ]

    def swap(value):
        return lax.ppermute(value, "row", [(r, r ^ 1) for r in range(size)])

    weight, offset = pl.pallas_call(
        weight_kernel,
        out_shape=[
            jax.ShapeDtypeStruct((channels, hidden * hidden), jnp.bfloat16),
            jax.ShapeDtypeStruct((1, channels), jnp.float32),
        ],
        in_specs=[vmem] * 2,
        out_specs=[vmem] * 2,
        scratch_shapes=[pltpu.VMEM((hidden * hidden, channels), jnp.float32)],
        compiler_params=pltpu.CompilerParams(vmem_limit_bytes=16 * MIB),
        cost_estimate=pl.CostEstimate(flops=2**28, bytes_accessed=2**20, transcendentals=0),
    )(final_projector_coefficients, final_projector_offset.reshape(1, channels))
    theirs, weight, offset = lax.optimization_barrier((swap(give), weight, offset))
    messages = [give, theirs]
    places = [(n, 0, n, body + (half - 1) * per_chip) for n in range(2)]

    def take(*lefts):
        places.extend((len(messages) + n, 0, len(messages) + m, low) for n, (m, low) in enumerate(lefts))

    flying = [keep, theirs[: body + (half - 1) * per_chip]]
    swapped, lefts = [], []
    for step in range(1, half + 1):
        landed = [lax.ppermute(x, "row", around) for x in flying]
        if step >= 3:
            landed[-1], swapped[step - 3] = lax.optimization_barrier((landed[-1], swapped[step - 3]))
        low = [x.shape[0] - per_chip for x in landed]
        if step == 1:
            lefts.append([(0, low[0]), (1, low[1])])
        elif step < half:
            lefts.append([(1, low[1] - per_chip), (1, low[1])])
        else:
            lefts.append([(0, low[0])])
        flying = [landed[0][: body + per_chip]]
        if step == 1:
            flying += pl.pallas_call(
                functools.partial(join_kernel, body, per_chip),
                out_shape=[rows(body + 2 * (half - 2) * per_chip)],
                in_specs=[vmem] * 2,
                out_specs=[vmem],
                compiler_params=pltpu.CompilerParams(vmem_limit_bytes=16 * MIB),
                cost_estimate=pl.CostEstimate(flops=0, bytes_accessed=2**19, transcendentals=0),
            )(*landed)
        elif step < half - 1:
            flying.append(landed[1][: landed[1].shape[0] - 2 * per_chip])
        landed = lax.optimization_barrier(landed)
        take(*lefts[-1])
        messages += landed
        swapped.append([swap(x) for x in landed])
    for pair, left in zip(swapped, lefts):
        take(*left)
        messages += pair

    gridded = tiles > 1
    if gridded:
        operands, specs = [], []
        for n, right, m, left in places:
            operands += [messages[n], messages[m]]
            specs += [
                pl.BlockSpec((width, tile), lambda t, first=right // width: (first + t, 0)),
                pl.BlockSpec((per_chip, tile), lambda t, at=left // per_chip: (at, 0)),
            ]
        specs += [
            pl.BlockSpec((channels, hidden * hidden), lambda t: (0, 0)),
            pl.BlockSpec((1, channels), lambda t: (0, 0)),
        ]
        grid = (tiles,)
    else:
        operands = messages
        specs = [vmem] * (len(messages) + 2)
        grid = ()
    return pl.pallas_call(
        functools.partial(pair_kernel, places, gridded, rows_here, hidden, samples),
        out_shape=jax.ShapeDtypeStruct((rows_here, residues, channels), jnp.bfloat16),
        grid=grid,
        in_specs=specs,
        out_specs=hbm,
        scratch_shapes=[
            pltpu.VMEM((rows_here * hidden, samples), jnp.bfloat16),
            pltpu.VMEM((rows_here, hidden * hidden, tile), jnp.bfloat16),
            pltpu.VMEM((rows_here, tile, channels), jnp.bfloat16),
            pltpu.SemaphoreType.DMA((rows_here,)),
        ],
        compiler_params=pltpu.CompilerParams(vmem_limit_bytes=40 * MIB),
    )(*operands, weight, offset)


def solution(mesh):
    return jax.shard_map(
        functools.partial(per_device, mesh.shape["row"]),
        mesh=mesh,
        in_specs=(P(("groups", "row"), None, None), P(), P(), P(), P(), P(), P(), P(), P()),
        out_specs=P(("groups", "row"), None, None),
        check_vma=False,
    )
```

```python
import functools
import math

import jax
import jax.numpy as jnp
from jax import lax
from jax.experimental import pallas as pl
from jax.experimental.pallas import tpu as pltpu
from jax.sharding import PartitionSpec as P

MIB = 1024 * 1024
LANES = 128
CHUNKS = 2
BLOCK = 64


def repeat_rows(values, times):
    rows, cols = values.shape
    return jnp.broadcast_to(values[:, None, :], (rows, times, cols)).reshape(rows * times, cols)


def place_of(device, half):
    chip = device // 2
    return chip // 2 + (chip % 2) * (2 * half - 1 - 2 * (chip // 2))


def chip_at(place, half):
    return jnp.where(place < half, 2 * place, 2 * (2 * half - 1 - place) + 1)


def project_kernel(
    rows_here,
    x_hbm,
    gain_hbm,
    shift_hbm,
    first_hbm,
    first_offset_hbm,
    second_hbm,
    second_offset_hbm,
    keep_ref,
    give_ref,
    x_ref,
    gain_ref,
    shift_ref,
    first_ref,
    first_offset_ref,
    second_ref,
    second_offset_ref,
    packed_ref,
    left_ref,
    sems,
):
    samples, residues, features = x_ref.shape
    hidden = first_ref.shape[0]
    width = samples * hidden
    tile = keep_ref.shape[1]
    tiles = residues // tile
    fold = LANES // hidden
    groups = residues // fold
    small = [
        (first_hbm, first_ref),
        (second_hbm, second_ref),
        (gain_hbm, gain_ref),
        (shift_hbm, shift_ref),
        (first_offset_hbm, first_offset_ref),
        (second_offset_hbm, second_offset_ref),
    ]
    some = samples // CHUNKS
    copies = [
        pltpu.make_async_copy(src, dst, sems.at[CHUNKS + n]) for n, (src, dst) in enumerate(small)
    ]
    for copy in copies:
        copy.start()
    large = []
    for n in range(CHUNKS):
        rows = pl.ds(n * some, some)
        large.append(pltpu.make_async_copy(x_hbm.at[rows], x_ref.at[rows], sems.at[n]))
        large[-1].start()
    for copy in copies:
        copy.wait()

    first = jnp.concatenate([first_ref[...].astype(jnp.float32)] * fold, axis=0).T
    first = first.astype(jnp.bfloat16)
    first_offset = jnp.concatenate([first_offset_ref[...]] * fold, axis=1)
    second = repeat_rows(second_ref[...].astype(jnp.float32), samples).T
    column = lax.broadcasted_iota(jnp.int32, (1, width), 1)
    spot = lax.broadcasted_iota(jnp.int32, (width, hidden), 0)
    channel = lax.broadcasted_iota(jnp.int32, (width, hidden), 1)
    second_offset = jnp.sum(
        jnp.where(spot // samples == channel, second_offset_ref[...], 0.0), axis=1, keepdims=True
    )
    residue = lax.broadcasted_iota(jnp.int32, (tile, LANES), 0)
    lane = lax.broadcasted_iota(jnp.int32, (tile, LANES), 1)
    own = residue % fold == lane // hidden
    group = lax.broadcasted_iota(jnp.int32, (tile // fold, tile), 0)
    member = lax.broadcasted_iota(jnp.int32, (tile // fold, tile), 1)
    gather = (member // fold == group).astype(jnp.bfloat16)

    right = [jnp.zeros((tile, width), jnp.float32) for _ in range(tiles)]
    for chunk in range(CHUNKS):
        large[chunk].wait()
        normed, placed = [], []
        for s in range(chunk * some, (chunk + 1) * some):
            pieces = []
            for low in range(0, residues, BLOCK):
                values = x_ref[s, low : low + BLOCK, :].astype(jnp.float32)
                center = jnp.mean(values, axis=-1, keepdims=True)
                values = values - center
                variance = jnp.mean(jnp.square(values), axis=-1, keepdims=True)
                values = values * lax.rsqrt(variance + 1e-05) * gain_ref[...] + shift_ref[...]
                pieces.append(values.astype(jnp.bfloat16))
            normed.append(jnp.concatenate(pieces, axis=0))
            placed.append(jnp.where(column % samples == s, second, 0.0).astype(jnp.bfloat16))
        placed = jnp.concatenate(placed, axis=0)
        for t in range(tiles):
            parts = [x[t * tile : (t + 1) * tile] for x in normed]
            right[t] += jnp.dot(
                jnp.concatenate(parts, axis=1), placed, preferred_element_type=jnp.float32
            )
            left = jnp.dot(
                jnp.concatenate(parts, axis=0), first, preferred_element_type=jnp.float32
            )
            lefts = [
                jnp.where(own, left[n * tile : (n + 1) * tile] + first_offset, 0.0).astype(jnp.bfloat16)
                for n in range(some)
            ]
            packed = jnp.dot(
                gather, jnp.concatenate(lefts, axis=1), preferred_element_type=jnp.float32
            )
            for n in range(some):
                low = (chunk * some + n) * groups + t * (tile // fold)
                packed_ref[low : low + tile // fold, :] = packed[:, n * LANES : (n + 1) * LANES]
    for t in range(tiles):
        value = (right[t].T + second_offset).astype(jnp.bfloat16)
        keep_ref[t * width : (t + 1) * width, :] = value
        give_ref[t * width : (t + 1) * width, :] = value
    across = tile // LANES
    for low in range(0, groups, across):
        at = low // across * samples
        left_ref[at : at + samples, :] = jnp.concatenate(
            [packed_ref[pl.ds(low + n, samples, stride=groups), :] for n in range(across)], axis=1
        )

    device = lax.axis_index("row")
    per_chip = 2 * rows_here * hidden * samples // tile
    half = residues // rows_here // 4
    base = tiles * width
    way = 1 - 2 * (device % 2)
    place = place_of(device, half)
    spots = [(keep_ref, base + n * per_chip, half - n) for n in range(half)]
    spots += [(give_ref, base + n * per_chip, n + 1 - half) for n in range(half)]
    for message, low, ahead in spots:
        chip = chip_at(lax.rem(place + way * ahead + 2 * half, 2 * half), half)
        start = pl.multiple_of(chip * per_chip, per_chip)
        message[low : low + per_chip, :] = left_ref[pl.ds(start, per_chip), :].astype(jnp.bfloat16)


def join_kernel(base, per_chip, mine_ref, theirs_ref, next_ref):
    next_ref[:base, :] = theirs_ref[:base, :]
    for n in range((next_ref.shape[0] - base) // (2 * per_chip)):
        low = base + n * per_chip
        at = low + n * per_chip
        next_ref[at : at + per_chip, :] = mine_ref[low + per_chip : low + 2 * per_chip, :]
        next_ref[at + per_chip : at + 2 * per_chip, :] = theirs_ref[low : low + per_chip, :]


def weight_kernel(final_ref, offset_ref, out_ref, offset_out, wide_ref):
    offset_out[...] = offset_ref[...]
    channels, columns = out_ref.shape
    hidden = math.isqrt(columns)
    wide_ref[...] = final_ref[...].astype(jnp.float32)
    step = LANES // hidden
    for e in range(0, hidden, step):
        rows = [wide_ref[pl.ds(e + n, hidden, stride=hidden), :] for n in range(step)]
        out_ref[:, e * hidden : (e + step) * hidden] = jnp.concatenate(rows, axis=0).T.astype(
            jnp.bfloat16
        )


def pair_kernel(places, gridded, rows_here, hidden, samples, *refs):
    refs = list(refs)
    count = len(places)
    if gridded:
        shards = [(refs.pop(0), 0, refs.pop(0), 0) for _ in places]
    else:
        messages = [refs.pop(0) for _ in places]
        shards = [(messages[n], right, messages[m], left) for n, right, m, left in places]
    weight_ref, offset_ref, out_hbm, left_ref, outer_ref, out_ref, sems = refs
    tile = shards[0][0].shape[1]
    here = samples // count
    span = rows_here * hidden
    deep = span * here // tile
    core = lax.rem(lax.axis_index("row"), 2)
    pieces = []
    for _, _, ref, base in shards:
        start = pl.multiple_of(base + core * deep, deep)
        piece = ref[pl.ds(start, deep), :].astype(jnp.float32)
        pieces.append(
            jnp.concatenate([piece[n * here : (n + 1) * here] for n in range(span // tile)], axis=1)
        )
    left_ref[...] = jnp.concatenate(pieces, axis=0).T.astype(jnp.bfloat16)

    left = left_ref[...]
    for e in range(0, hidden, 2):
        both = [
            ref[base + e * here : base + (e + 2) * here, :].astype(jnp.float32)
            for ref, base, _, _ in shards
        ]
        right = [
            jnp.concatenate([x[k * here : (k + 1) * here] for x in both], axis=0).astype(jnp.bfloat16)
            for k in range(2)
        ]
        outer = jnp.dot(left, jnp.concatenate(right, axis=1), preferred_element_type=jnp.float32)
        outer = outer.astype(jnp.bfloat16)
        for k in range(2):
            low = (e + k) * hidden
            for i in range(rows_here):
                outer_ref[low : low + hidden, i * tile : (i + 1) * tile] = outer[
                    i * hidden : (i + 1) * hidden, k * tile : (k + 1) * tile
                ]

    first = pl.program_id(0) * tile if gridded else 0
    copies = []
    some = 4
    for group in range(0, rows_here, some):
        values = jnp.dot(
            weight_ref[...],
            outer_ref[:, group * tile : (group + some) * tile],
            preferred_element_type=jnp.float32,
        )
        for n in range(some):
            i = group + n
            value = values[:, n * tile : (n + 1) * tile].T * (1.0 / samples) + offset_ref[...]
            out_ref[i] = value.astype(jnp.bfloat16)
            copies.append(
                pltpu.make_async_copy(out_ref.at[i], out_hbm.at[i, pl.ds(first, tile)], sems.at[i])
            )
            copies[-1].start()
    for copy in copies:
        copy.wait()


def per_device(
    size,
    alignment_embedding,
    rescaling_factor,
    recentering_offset,
    first_side_coefficients,
    first_side_offset,
    second_side_coefficients,
    second_side_offset,
    final_projector_coefficients,
    final_projector_offset,
):
    here, residues, features = alignment_embedding.shape
    hidden = first_side_coefficients.shape[1]
    channels = final_projector_coefficients.shape[1]
    width = here * hidden
    samples = here * size
    rows_here = residues // size
    half = size // 4
    tile = 256
    tiles = residues // tile
    body = tiles * width
    per_chip = 2 * rows_here * width // tile

    def rows(count):
        return jax.ShapeDtypeStruct((count, tile), jnp.bfloat16)

    vmem = pl.BlockSpec(memory_space=pltpu.VMEM)
    hbm = pl.BlockSpec(memory_space=pltpu.HBM)
    keep, give = pl.pallas_call(
        functools.partial(project_kernel, rows_here),
        out_shape=[rows(body + half * per_chip)] * 2,
        in_specs=[hbm] * 7,
        out_specs=[vmem] * 2,
        scratch_shapes=[
            pltpu.VMEM((here, residues, features), jnp.bfloat16),
            pltpu.VMEM((1, features), jnp.float32),
            pltpu.VMEM((1, features), jnp.float32),
            pltpu.VMEM((hidden, features), jnp.bfloat16),
            pltpu.VMEM((1, hidden), jnp.float32),
            pltpu.VMEM((hidden, features), jnp.bfloat16),
            pltpu.VMEM((1, hidden), jnp.float32),
            pltpu.VMEM((residues * width // LANES, LANES), jnp.float32),
            pltpu.VMEM((residues * width // tile, tile), jnp.float32),
            pltpu.SemaphoreType.DMA((CHUNKS + 6,)),
        ],
        compiler_params=pltpu.CompilerParams(vmem_limit_bytes=32 * MIB),
        cost_estimate=pl.CostEstimate(
            flops=4 * here * residues * features * width,
            bytes_accessed=2 * here * residues * features,
            transcendentals=0,
        ),
    )(
        *[
            pltpu.with_memory_space_constraint(value, pltpu.HBM)
            for value in (
                alignment_embedding,
                rescaling_factor.reshape(1, features),
                recentering_offset.reshape(1, features),
                first_side_coefficients.T,
                first_side_offset.reshape(1, hidden),
                second_side_coefficients.T,
                second_side_offset.reshape(1, hidden),
            )
        ]
    )
    by_place = {(place_of(r, half), r % 2): r for r in range(size)}
    around = [
        (r, by_place[(place_of(r, half) + 1 - 2 * (r % 2)) % (2 * half), r % 2]) for r in range(size)
    ]

    def swap(value):
        return lax.ppermute(value, "row", [(r, r ^ 1) for r in range(size)])

    weight, offset = pl.pallas_call(
        weight_kernel,
        out_shape=[
            jax.ShapeDtypeStruct((channels, hidden * hidden), jnp.bfloat16),
            jax.ShapeDtypeStruct((1, channels), jnp.float32),
        ],
        in_specs=[vmem] * 2,
        out_specs=[vmem] * 2,
        scratch_shapes=[pltpu.VMEM((hidden * hidden, channels), jnp.float32)],
        compiler_params=pltpu.CompilerParams(vmem_limit_bytes=16 * MIB),
        cost_estimate=pl.CostEstimate(flops=2**28, bytes_accessed=2**20, transcendentals=0),
    )(final_projector_coefficients, final_projector_offset.reshape(1, channels))
    theirs, weight, offset = lax.optimization_barrier((swap(give), weight, offset))
    messages = [give, theirs]
    places = [(n, 0, n, body + (half - 1) * per_chip) for n in range(2)]

    def take(*lefts):
        places.extend((len(messages) + n, 0, len(messages) + m, low) for n, (m, low) in enumerate(lefts))

    flying = [keep, theirs[: body + (half - 1) * per_chip]]
    swapped, lefts = [], []
    for step in range(1, half + 1):
        landed = [lax.ppermute(x, "row", around) for x in flying]
        if step >= 3:
            landed[-1], swapped[step - 3] = lax.optimization_barrier((landed[-1], swapped[step - 3]))
        low = [x.shape[0] - per_chip for x in landed]
        if step == 1:
            lefts.append([(0, low[0]), (1, low[1])])
        elif step < half:
            lefts.append([(1, low[1] - per_chip), (1, low[1])])
        else:
            lefts.append([(0, low[0])])
        flying = [landed[0][: body + per_chip]]
        if step == 1:
            flying += pl.pallas_call(
                functools.partial(join_kernel, body, per_chip),
                out_shape=[rows(body + 2 * (half - 2) * per_chip)],
                in_specs=[vmem] * 2,
                out_specs=[vmem],
                compiler_params=pltpu.CompilerParams(vmem_limit_bytes=16 * MIB),
                cost_estimate=pl.CostEstimate(flops=0, bytes_accessed=2**19, transcendentals=0),
            )(*landed)
        elif step < half - 1:
            flying.append(landed[1][: landed[1].shape[0] - 2 * per_chip])
        landed = lax.optimization_barrier(landed)
        take(*lefts[-1])
        messages += landed
        swapped.append([swap(x) for x in landed])
    for pair, left in zip(swapped, lefts):
        take(*left)
        messages += pair

    gridded = tiles > 1
    if gridded:
        operands, specs = [], []
        for n, right, m, left in places:
            operands += [messages[n], messages[m]]
            specs += [
                pl.BlockSpec((width, tile), lambda t, first=right // width: (first + t, 0)),
                pl.BlockSpec((per_chip, tile), lambda t, at=left // per_chip: (at, 0)),
            ]
        specs += [
            pl.BlockSpec((channels, hidden * hidden), lambda t: (0, 0)),
            pl.BlockSpec((1, channels), lambda t: (0, 0)),
        ]
        grid = (tiles,)
    else:
        operands = messages
        specs = [vmem] * (len(messages) + 2)
        grid = ()
    return pl.pallas_call(
        functools.partial(pair_kernel, places, gridded, rows_here, hidden, samples),
        out_shape=jax.ShapeDtypeStruct((rows_here, residues, channels), jnp.bfloat16),
        grid=grid,
        in_specs=specs,
        out_specs=hbm,
        scratch_shapes=[
            pltpu.VMEM((rows_here * hidden, samples), jnp.bfloat16),
            pltpu.VMEM((hidden * hidden, rows_here * tile), jnp.bfloat16),
            pltpu.VMEM((rows_here, tile, channels), jnp.bfloat16),
            pltpu.SemaphoreType.DMA((rows_here,)),
        ],
        compiler_params=pltpu.CompilerParams(vmem_limit_bytes=40 * MIB),
    )(*operands, weight, offset)


def solution(mesh):
    return jax.shard_map(
        functools.partial(per_device, mesh.shape["row"]),
        mesh=mesh,
        in_specs=(P(("groups", "row"), None, None), P(), P(), P(), P(), P(), P(), P(), P()),
        out_specs=P(("groups", "row"), None, None),
        check_vma=False,
    )
```

```python
import functools
import math

import jax
import jax.numpy as jnp
from jax import lax
from jax.experimental import pallas as pl
from jax.experimental.pallas import tpu as pltpu
from jax.sharding import PartitionSpec as P

MIB = 1024 * 1024
LANES = 128
CHUNKS = 2
BLOCK = 64


def repeat_rows(values, times):
    rows, cols = values.shape
    return jnp.broadcast_to(values[:, None, :], (rows, times, cols)).reshape(rows * times, cols)


def place_of(device, half):
    chip = device // 2
    return chip // 2 + (chip % 2) * (2 * half - 1 - 2 * (chip // 2))


def chip_at(place, half):
    return jnp.where(place < half, 2 * place, 2 * (2 * half - 1 - place) + 1)


def project_kernel(
    rows_here,
    x_hbm,
    gain_hbm,
    shift_hbm,
    first_hbm,
    first_offset_hbm,
    second_hbm,
    second_offset_hbm,
    keep_ref,
    give_ref,
    x_ref,
    gain_ref,
    shift_ref,
    first_ref,
    first_offset_ref,
    second_ref,
    second_offset_ref,
    packed_ref,
    sems,
):
    samples, residues, features = x_ref.shape
    hidden = first_ref.shape[0]
    width = samples * hidden
    tile = keep_ref.shape[1]
    tiles = residues // tile
    fold = LANES // hidden
    small = [
        (first_hbm, first_ref),
        (second_hbm, second_ref),
        (gain_hbm, gain_ref),
        (shift_hbm, shift_ref),
        (first_offset_hbm, first_offset_ref),
        (second_offset_hbm, second_offset_ref),
    ]
    some = samples // CHUNKS
    copies = [
        pltpu.make_async_copy(src, dst, sems.at[CHUNKS + n]) for n, (src, dst) in enumerate(small)
    ]
    for copy in copies:
        copy.start()
    large = []
    for n in range(CHUNKS):
        rows = pl.ds(n * some, some)
        large.append(pltpu.make_async_copy(x_hbm.at[rows], x_ref.at[rows], sems.at[n]))
        large[-1].start()
    for copy in copies:
        copy.wait()

    first = jnp.concatenate([first_ref[...].astype(jnp.float32)] * fold, axis=0).T
    first = first.astype(jnp.bfloat16)
    first_offset = jnp.concatenate([first_offset_ref[...]] * fold, axis=1)
    second = repeat_rows(second_ref[...].astype(jnp.float32), samples).T
    column = lax.broadcasted_iota(jnp.int32, (1, width), 1)
    spot = lax.broadcasted_iota(jnp.int32, (width, hidden), 0)
    channel = lax.broadcasted_iota(jnp.int32, (width, hidden), 1)
    second_offset = jnp.sum(
        jnp.where(spot // samples == channel, second_offset_ref[...], 0.0), axis=1, keepdims=True
    )
    residue = lax.broadcasted_iota(jnp.int32, (tile, LANES), 0)
    lane = lax.broadcasted_iota(jnp.int32, (tile, LANES), 1)
    own = residue % fold == lane // hidden
    group = lax.broadcasted_iota(jnp.int32, (tile // fold, tile), 0)
    member = lax.broadcasted_iota(jnp.int32, (tile // fold, tile), 1)
    gather = (member // fold == group).astype(jnp.bfloat16)

    right = [jnp.zeros((tile, width), jnp.float32) for _ in range(tiles)]
    for s in range(samples):
        if s % some == 0:
            large[s // some].wait()
        normed = []
        for low in range(0, residues, BLOCK):
            values = x_ref[s, low : low + BLOCK, :].astype(jnp.float32)
            center = jnp.mean(values, axis=-1, keepdims=True)
            values = values - center
            variance = jnp.mean(jnp.square(values), axis=-1, keepdims=True)
            values = values * lax.rsqrt(variance + 1e-05) * gain_ref[...] + shift_ref[...]
            normed.append(values.astype(jnp.bfloat16))
        normed = jnp.concatenate(normed, axis=0)
        second_here = jnp.where(column % samples == s, second, 0.0).astype(jnp.bfloat16)
        for t in range(tiles):
            part = normed[t * tile : (t + 1) * tile]
            left = jnp.dot(part, first, preferred_element_type=jnp.float32)
            right[t] += jnp.dot(part, second_here, preferred_element_type=jnp.float32)
            left = jnp.where(own, left + first_offset, 0.0).astype(jnp.bfloat16)
            low = t * (tile // fold) * samples + s
            packed_ref[pl.ds(low, tile // fold, stride=samples), :] = jnp.dot(
                gather, left, preferred_element_type=jnp.float32
            )
    for t in range(tiles):
        value = (right[t].T + second_offset).astype(jnp.bfloat16)
        keep_ref[t * width : (t + 1) * width, :] = value
        give_ref[t * width : (t + 1) * width, :] = value
    device = lax.axis_index("row")
    per_chip = 2 * rows_here * hidden * samples // tile
    half = residues // rows_here // 4
    base = tiles * width
    way = 1 - 2 * (device % 2)
    place = place_of(device, half)
    spots = [(keep_ref, base + n * per_chip, half - n) for n in range(half)]
    spots += [(give_ref, base + n * per_chip, n + 1 - half) for n in range(half)]
    for message, low, ahead in spots:
        chip = chip_at(lax.rem(place + way * ahead + 2 * half, 2 * half), half)
        across = tile // LANES
        start = pl.multiple_of(chip * per_chip * across, per_chip * across)
        block = packed_ref[pl.ds(start, per_chip * across), :]
        block = [block[n : n + samples] for n in range(0, per_chip * across, samples)]
        block = [jnp.concatenate(block[n : n + across], axis=1) for n in range(0, len(block), across)]
        message[low : low + per_chip, :] = jnp.concatenate(block, axis=0).astype(jnp.bfloat16)


def join_kernel(base, per_chip, mine_ref, theirs_ref, next_ref):
    next_ref[:base, :] = theirs_ref[:base, :]
    for n in range((next_ref.shape[0] - base) // (2 * per_chip)):
        low = base + n * per_chip
        at = low + n * per_chip
        next_ref[at : at + per_chip, :] = mine_ref[low + per_chip : low + 2 * per_chip, :]
        next_ref[at + per_chip : at + 2 * per_chip, :] = theirs_ref[low : low + per_chip, :]


def weight_kernel(final_ref, offset_ref, out_ref, offset_out, wide_ref):
    offset_out[...] = offset_ref[...]
    channels, columns = out_ref.shape
    hidden = math.isqrt(columns)
    wide_ref[...] = final_ref[...].astype(jnp.float32)
    step = LANES // hidden
    for e in range(0, hidden, step):
        rows = [wide_ref[pl.ds(e + n, hidden, stride=hidden), :] for n in range(step)]
        out_ref[:, e * hidden : (e + step) * hidden] = jnp.concatenate(rows, axis=0).T.astype(
            jnp.bfloat16
        )


def pair_kernel(places, gridded, rows_here, hidden, samples, *refs):
    refs = list(refs)
    count = len(places)
    if gridded:
        shards = [(refs.pop(0), 0, refs.pop(0), 0) for _ in places]
    else:
        messages = [refs.pop(0) for _ in places]
        shards = [(messages[n], right, messages[m], left) for n, right, m, left in places]
    weight_ref, offset_ref, out_hbm, left_ref, outer_ref, out_ref, sems = refs
    tile = shards[0][0].shape[1]
    here = samples // count
    span = rows_here * hidden
    deep = span * here // tile
    core = lax.rem(lax.axis_index("row"), 2)
    pieces = []
    for _, _, ref, base in shards:
        start = pl.multiple_of(base + core * deep, deep)
        piece = ref[pl.ds(start, deep), :].astype(jnp.float32)
        pieces.append(
            jnp.concatenate([piece[n * here : (n + 1) * here] for n in range(span // tile)], axis=1)
        )
    left_ref[...] = jnp.concatenate(pieces, axis=0).T.astype(jnp.bfloat16)

    left = left_ref[...]
    for e in range(0, hidden, 2):
        both = [
            ref[base + e * here : base + (e + 2) * here, :].astype(jnp.float32)
            for ref, base, _, _ in shards
        ]
        for k in range(2):
            right = jnp.concatenate([x[k * here : (k + 1) * here] for x in both], axis=0)
            outer = jnp.dot(left, right.astype(jnp.bfloat16), preferred_element_type=jnp.float32)
            outer = outer.astype(jnp.bfloat16)
            for i in range(rows_here):
                outer_ref[i, (e + k) * hidden : (e + k + 1) * hidden, :] = outer[
                    i * hidden : (i + 1) * hidden
                ]

    first = pl.program_id(0) * tile if gridded else 0
    copies = []
    for i in range(rows_here):
        value = jnp.dot(weight_ref[...], outer_ref[i], preferred_element_type=jnp.float32)
        value = value.T * (1.0 / samples) + offset_ref[...]
        out_ref[i] = value.astype(jnp.bfloat16)
        copies.append(
            pltpu.make_async_copy(out_ref.at[i], out_hbm.at[i, pl.ds(first, tile)], sems.at[i])
        )
        copies[-1].start()
    for copy in copies:
        copy.wait()


def per_device(
    size,
    alignment_embedding,
    rescaling_factor,
    recentering_offset,
    first_side_coefficients,
    first_side_offset,
    second_side_coefficients,
    second_side_offset,
    final_projector_coefficients,
    final_projector_offset,
):
    here, residues, features = alignment_embedding.shape
    hidden = first_side_coefficients.shape[1]
    channels = final_projector_coefficients.shape[1]
    width = here * hidden
    samples = here * size
    rows_here = residues // size
    half = size // 4
    tile = 256
    tiles = residues // tile
    body = tiles * width
    per_chip = 2 * rows_here * width // tile

    def rows(count):
        return jax.ShapeDtypeStruct((count, tile), jnp.bfloat16)

    vmem = pl.BlockSpec(memory_space=pltpu.VMEM)
    hbm = pl.BlockSpec(memory_space=pltpu.HBM)
    keep, give = pl.pallas_call(
        functools.partial(project_kernel, rows_here),
        out_shape=[rows(body + half * per_chip)] * 2,
        in_specs=[hbm] * 7,
        out_specs=[vmem] * 2,
        scratch_shapes=[
            pltpu.VMEM((here, residues, features), jnp.bfloat16),
            pltpu.VMEM((1, features), jnp.float32),
            pltpu.VMEM((1, features), jnp.float32),
            pltpu.VMEM((hidden, features), jnp.bfloat16),
            pltpu.VMEM((1, hidden), jnp.float32),
            pltpu.VMEM((hidden, features), jnp.bfloat16),
            pltpu.VMEM((1, hidden), jnp.float32),
            pltpu.VMEM((residues * width // LANES, LANES), jnp.float32),
            pltpu.SemaphoreType.DMA((CHUNKS + 6,)),
        ],
        compiler_params=pltpu.CompilerParams(vmem_limit_bytes=32 * MIB),
        cost_estimate=pl.CostEstimate(
            flops=4 * here * residues * features * width,
            bytes_accessed=2 * here * residues * features,
            transcendentals=0,
        ),
    )(
        *[
            pltpu.with_memory_space_constraint(value, pltpu.HBM)
            for value in (
                alignment_embedding,
                rescaling_factor.reshape(1, features),
                recentering_offset.reshape(1, features),
                first_side_coefficients.T,
                first_side_offset.reshape(1, hidden),
                second_side_coefficients.T,
                second_side_offset.reshape(1, hidden),
            )
        ]
    )
    by_place = {(place_of(r, half), r % 2): r for r in range(size)}
    around = [
        (r, by_place[(place_of(r, half) + 1 - 2 * (r % 2)) % (2 * half), r % 2]) for r in range(size)
    ]

    def swap(value):
        return lax.ppermute(value, "row", [(r, r ^ 1) for r in range(size)])

    weight, offset = pl.pallas_call(
        weight_kernel,
        out_shape=[
            jax.ShapeDtypeStruct((channels, hidden * hidden), jnp.bfloat16),
            jax.ShapeDtypeStruct((1, channels), jnp.float32),
        ],
        in_specs=[vmem] * 2,
        out_specs=[vmem] * 2,
        scratch_shapes=[pltpu.VMEM((hidden * hidden, channels), jnp.float32)],
        compiler_params=pltpu.CompilerParams(vmem_limit_bytes=16 * MIB),
        cost_estimate=pl.CostEstimate(flops=2**28, bytes_accessed=2**20, transcendentals=0),
    )(final_projector_coefficients, final_projector_offset.reshape(1, channels))
    theirs, weight, offset = lax.optimization_barrier((swap(give), weight, offset))
    messages = [give, theirs]
    places = [(n, 0, n, body + (half - 1) * per_chip) for n in range(2)]

    def take(*lefts):
        places.extend((len(messages) + n, 0, len(messages) + m, low) for n, (m, low) in enumerate(lefts))

    flying = [keep, theirs[: body + (half - 1) * per_chip]]
    swapped, lefts = [], []
    for step in range(1, half + 1):
        landed = [lax.ppermute(x, "row", around) for x in flying]
        if step >= 3:
            landed[-1], swapped[step - 3] = lax.optimization_barrier((landed[-1], swapped[step - 3]))
        low = [x.shape[0] - per_chip for x in landed]
        if step == 1:
            lefts.append([(0, low[0]), (1, low[1])])
        elif step < half:
            lefts.append([(1, low[1] - per_chip), (1, low[1])])
        else:
            lefts.append([(0, low[0])])
        flying = [landed[0][: body + per_chip]]
        if step == 1:
            flying += pl.pallas_call(
                functools.partial(join_kernel, body, per_chip),
                out_shape=[rows(body + 2 * (half - 2) * per_chip)],
                in_specs=[vmem] * 2,
                out_specs=[vmem],
                compiler_params=pltpu.CompilerParams(vmem_limit_bytes=16 * MIB),
                cost_estimate=pl.CostEstimate(flops=0, bytes_accessed=2**19, transcendentals=0),
            )(*landed)
        elif step < half - 1:
            flying.append(landed[1][: landed[1].shape[0] - 2 * per_chip])
        landed = lax.optimization_barrier(landed)
        take(*lefts[-1])
        messages += landed
        swapped.append([swap(x) for x in landed])
    for pair, left in zip(swapped, lefts):
        take(*left)
        messages += pair

    gridded = tiles > 1
    if gridded:
        operands, specs = [], []
        for n, right, m, left in places:
            operands += [messages[n], messages[m]]
            specs += [
                pl.BlockSpec((width, tile), lambda t, first=right // width: (first + t, 0)),
                pl.BlockSpec((per_chip, tile), lambda t, at=left // per_chip: (at, 0)),
            ]
        specs += [
            pl.BlockSpec((channels, hidden * hidden), lambda t: (0, 0)),
            pl.BlockSpec((1, channels), lambda t: (0, 0)),
        ]
        grid = (tiles,)
    else:
        operands = messages
        specs = [vmem] * (len(messages) + 2)
        grid = ()
    return pl.pallas_call(
        functools.partial(pair_kernel, places, gridded, rows_here, hidden, samples),
        out_shape=jax.ShapeDtypeStruct((rows_here, residues, channels), jnp.bfloat16),
        grid=grid,
        in_specs=specs,
        out_specs=hbm,
        scratch_shapes=[
            pltpu.VMEM((rows_here * hidden, samples), jnp.bfloat16),
            pltpu.VMEM((rows_here, hidden * hidden, tile), jnp.bfloat16),
            pltpu.VMEM((rows_here, tile, channels), jnp.bfloat16),
            pltpu.SemaphoreType.DMA((rows_here,)),
        ],
        compiler_params=pltpu.CompilerParams(vmem_limit_bytes=40 * MIB),
    )(*operands, weight, offset)


def solution(mesh):
    return jax.shard_map(
        functools.partial(per_device, mesh.shape["row"]),
        mesh=mesh,
        in_specs=(P(("groups", "row"), None, None), P(), P(), P(), P(), P(), P(), P(), P()),
        out_specs=P(("groups", "row"), None, None),
        check_vma=False,
    )
```

```python
import functools
import math

import jax
import jax.numpy as jnp
from jax import lax
from jax.experimental import pallas as pl
from jax.experimental.pallas import tpu as pltpu
from jax.sharding import PartitionSpec as P

MIB = 1024 * 1024
LANES = 128
CHUNKS = 1
BLOCK = 64


def repeat_rows(values, times):
    rows, cols = values.shape
    return jnp.broadcast_to(values[:, None, :], (rows, times, cols)).reshape(rows * times, cols)


def place_of(device, half):
    chip = device // 2
    return chip // 2 + (chip % 2) * (2 * half - 1 - 2 * (chip // 2))


def chip_at(place, half):
    return jnp.where(place < half, 2 * place, 2 * (2 * half - 1 - place) + 1)


def project_kernel(
    rows_here,
    x_hbm,
    gain_hbm,
    shift_hbm,
    first_hbm,
    first_offset_hbm,
    second_hbm,
    second_offset_hbm,
    keep_ref,
    give_ref,
    x_ref,
    gain_ref,
    shift_ref,
    first_ref,
    first_offset_ref,
    second_ref,
    second_offset_ref,
    packed_ref,
    sems,
):
    samples, residues, features = x_ref.shape
    hidden = first_ref.shape[0]
    width = samples * hidden
    tile = keep_ref.shape[1]
    tiles = residues // tile
    fold = LANES // hidden
    small = [
        (first_hbm, first_ref),
        (second_hbm, second_ref),
        (gain_hbm, gain_ref),
        (shift_hbm, shift_ref),
        (first_offset_hbm, first_offset_ref),
        (second_offset_hbm, second_offset_ref),
    ]
    some = samples // CHUNKS
    copies = [
        pltpu.make_async_copy(src, dst, sems.at[CHUNKS + n]) for n, (src, dst) in enumerate(small)
    ]
    for copy in copies:
        copy.start()
    large = []
    for n in range(CHUNKS):
        rows = pl.ds(n * some, some)
        large.append(pltpu.make_async_copy(x_hbm.at[rows], x_ref.at[rows], sems.at[n]))
        large[-1].start()
    for copy in copies:
        copy.wait()

    first = jnp.concatenate([first_ref[...].astype(jnp.float32)] * fold, axis=0).T
    first = first.astype(jnp.bfloat16)
    first_offset = jnp.concatenate([first_offset_ref[...]] * fold, axis=1)
    second = repeat_rows(second_ref[...].astype(jnp.float32), samples).T
    column = lax.broadcasted_iota(jnp.int32, (1, width), 1)
    spot = lax.broadcasted_iota(jnp.int32, (width, hidden), 0)
    channel = lax.broadcasted_iota(jnp.int32, (width, hidden), 1)
    second_offset = jnp.sum(
        jnp.where(spot // samples == channel, second_offset_ref[...], 0.0), axis=1, keepdims=True
    )
    residue = lax.broadcasted_iota(jnp.int32, (tile, LANES), 0)
    lane = lax.broadcasted_iota(jnp.int32, (tile, LANES), 1)
    own = residue % fold == lane // hidden
    group = lax.broadcasted_iota(jnp.int32, (tile // fold, tile), 0)
    member = lax.broadcasted_iota(jnp.int32, (tile // fold, tile), 1)
    gather = (member // fold == group).astype(jnp.bfloat16)

    right = [jnp.zeros((tile, width), jnp.float32) for _ in range(tiles)]
    for s in range(samples):
        if s % some == 0:
            large[s // some].wait()
        normed = []
        for low in range(0, residues, BLOCK):
            values = x_ref[s, low : low + BLOCK, :].astype(jnp.float32)
            center = jnp.mean(values, axis=-1, keepdims=True)
            values = values - center
            variance = jnp.mean(jnp.square(values), axis=-1, keepdims=True)
            values = values * lax.rsqrt(variance + 1e-05) * gain_ref[...] + shift_ref[...]
            normed.append(values.astype(jnp.bfloat16))
        normed = jnp.concatenate(normed, axis=0)
        second_here = jnp.where(column % samples == s, second, 0.0).astype(jnp.bfloat16)
        for t in range(tiles):
            part = normed[t * tile : (t + 1) * tile]
            left = jnp.dot(part, first, preferred_element_type=jnp.float32)
            right[t] += jnp.dot(part, second_here, preferred_element_type=jnp.float32)
            left = jnp.where(own, left + first_offset, 0.0).astype(jnp.bfloat16)
            low = t * (tile // fold) * samples + s
            packed_ref[pl.ds(low, tile // fold, stride=samples), :] = jnp.dot(
                gather, left, preferred_element_type=jnp.float32
            )
    for t in range(tiles):
        value = (right[t].T + second_offset).astype(jnp.bfloat16)
        keep_ref[t * width : (t + 1) * width, :] = value
        give_ref[t * width : (t + 1) * width, :] = value
    device = lax.axis_index("row")
    per_chip = 2 * rows_here * hidden * samples // tile
    half = residues // rows_here // 4
    base = tiles * width
    way = 1 - 2 * (device % 2)
    place = place_of(device, half)
    spots = [(keep_ref, base + n * per_chip, half - n) for n in range(half)]
    spots += [(give_ref, base + n * per_chip, n + 1 - half) for n in range(half)]
    for message, low, ahead in spots:
        chip = chip_at(lax.rem(place + way * ahead + 2 * half, 2 * half), half)
        across = tile // LANES
        start = pl.multiple_of(chip * per_chip * across, per_chip * across)
        block = packed_ref[pl.ds(start, per_chip * across), :]
        block = [block[n : n + samples] for n in range(0, per_chip * across, samples)]
        block = [jnp.concatenate(block[n : n + across], axis=1) for n in range(0, len(block), across)]
        message[low : low + per_chip, :] = jnp.concatenate(block, axis=0).astype(jnp.bfloat16)


def join_kernel(base, per_chip, mine_ref, theirs_ref, next_ref):
    next_ref[:base, :] = theirs_ref[:base, :]
    for n in range((next_ref.shape[0] - base) // (2 * per_chip)):
        low = base + n * per_chip
        at = low + n * per_chip
        next_ref[at : at + per_chip, :] = mine_ref[low + per_chip : low + 2 * per_chip, :]
        next_ref[at + per_chip : at + 2 * per_chip, :] = theirs_ref[low : low + per_chip, :]


def weight_kernel(final_ref, offset_ref, out_ref, offset_out, wide_ref):
    offset_out[...] = offset_ref[...]
    channels, columns = out_ref.shape
    hidden = math.isqrt(columns)
    wide_ref[...] = final_ref[...].astype(jnp.float32)
    step = LANES // hidden
    for e in range(0, hidden, step):
        rows = [wide_ref[pl.ds(e + n, hidden, stride=hidden), :] for n in range(step)]
        out_ref[:, e * hidden : (e + step) * hidden] = jnp.concatenate(rows, axis=0).T.astype(
            jnp.bfloat16
        )


def pair_kernel(places, gridded, rows_here, hidden, samples, *refs):
    refs = list(refs)
    count = len(places)
    if gridded:
        shards = [(refs.pop(0), 0, refs.pop(0), 0) for _ in places]
    else:
        messages = [refs.pop(0) for _ in places]
        shards = [(messages[n], right, messages[m], left) for n, right, m, left in places]
    weight_ref, offset_ref, out_hbm, left_ref, outer_ref, out_ref, sems = refs
    tile = shards[0][0].shape[1]
    here = samples // count
    span = rows_here * hidden
    deep = span * here // tile
    core = lax.rem(lax.axis_index("row"), 2)
    pieces = []
    for _, _, ref, base in shards:
        start = pl.multiple_of(base + core * deep, deep)
        piece = ref[pl.ds(start, deep), :].astype(jnp.float32)
        pieces.append(
            jnp.concatenate([piece[n * here : (n + 1) * here] for n in range(span // tile)], axis=1)
        )
    left_ref[...] = jnp.concatenate(pieces, axis=0).T.astype(jnp.bfloat16)

    left = left_ref[...]
    for e in range(0, hidden, 2):
        both = [
            ref[base + e * here : base + (e + 2) * here, :].astype(jnp.float32)
            for ref, base, _, _ in shards
        ]
        for k in range(2):
            right = jnp.concatenate([x[k * here : (k + 1) * here] for x in both], axis=0)
            outer = jnp.dot(left, right.astype(jnp.bfloat16), preferred_element_type=jnp.float32)
            outer = outer.astype(jnp.bfloat16)
            for i in range(rows_here):
                outer_ref[i, (e + k) * hidden : (e + k + 1) * hidden, :] = outer[
                    i * hidden : (i + 1) * hidden
                ]

    first = pl.program_id(0) * tile if gridded else 0
    copies = []
    for i in range(rows_here):
        value = jnp.dot(weight_ref[...], outer_ref[i], preferred_element_type=jnp.float32)
        value = value.T * (1.0 / samples) + offset_ref[...]
        out_ref[i] = value.astype(jnp.bfloat16)
        copies.append(
            pltpu.make_async_copy(out_ref.at[i], out_hbm.at[i, pl.ds(first, tile)], sems.at[i])
        )
        copies[-1].start()
    for copy in copies:
        copy.wait()


def per_device(
    size,
    alignment_embedding,
    rescaling_factor,
    recentering_offset,
    first_side_coefficients,
    first_side_offset,
    second_side_coefficients,
    second_side_offset,
    final_projector_coefficients,
    final_projector_offset,
):
    here, residues, features = alignment_embedding.shape
    hidden = first_side_coefficients.shape[1]
    channels = final_projector_coefficients.shape[1]
    width = here * hidden
    samples = here * size
    rows_here = residues // size
    half = size // 4
    tile = 256
    tiles = residues // tile
    body = tiles * width
    per_chip = 2 * rows_here * width // tile

    def rows(count):
        return jax.ShapeDtypeStruct((count, tile), jnp.bfloat16)

    vmem = pl.BlockSpec(memory_space=pltpu.VMEM)
    hbm = pl.BlockSpec(memory_space=pltpu.HBM)
    keep, give = pl.pallas_call(
        functools.partial(project_kernel, rows_here),
        out_shape=[rows(body + half * per_chip)] * 2,
        in_specs=[hbm] * 7,
        out_specs=[vmem] * 2,
        scratch_shapes=[
            pltpu.VMEM((here, residues, features), jnp.bfloat16),
            pltpu.VMEM((1, features), jnp.float32),
            pltpu.VMEM((1, features), jnp.float32),
            pltpu.VMEM((hidden, features), jnp.bfloat16),
            pltpu.VMEM((1, hidden), jnp.float32),
            pltpu.VMEM((hidden, features), jnp.bfloat16),
            pltpu.VMEM((1, hidden), jnp.float32),
            pltpu.VMEM((residues * width // LANES, LANES), jnp.float32),
            pltpu.SemaphoreType.DMA((CHUNKS + 6,)),
        ],
        compiler_params=pltpu.CompilerParams(vmem_limit_bytes=32 * MIB),
        cost_estimate=pl.CostEstimate(
            flops=4 * here * residues * features * width,
            bytes_accessed=2 * here * residues * features,
            transcendentals=0,
        ),
    )(
        *[
            pltpu.with_memory_space_constraint(value, pltpu.HBM)
            for value in (
                alignment_embedding,
                rescaling_factor.reshape(1, features),
                recentering_offset.reshape(1, features),
                first_side_coefficients.T,
                first_side_offset.reshape(1, hidden),
                second_side_coefficients.T,
                second_side_offset.reshape(1, hidden),
            )
        ]
    )
    by_place = {(place_of(r, half), r % 2): r for r in range(size)}
    around = [
        (r, by_place[(place_of(r, half) + 1 - 2 * (r % 2)) % (2 * half), r % 2]) for r in range(size)
    ]

    def swap(value):
        return lax.ppermute(value, "row", [(r, r ^ 1) for r in range(size)])

    weight, offset = pl.pallas_call(
        weight_kernel,
        out_shape=[
            jax.ShapeDtypeStruct((channels, hidden * hidden), jnp.bfloat16),
            jax.ShapeDtypeStruct((1, channels), jnp.float32),
        ],
        in_specs=[vmem] * 2,
        out_specs=[vmem] * 2,
        scratch_shapes=[pltpu.VMEM((hidden * hidden, channels), jnp.float32)],
        compiler_params=pltpu.CompilerParams(vmem_limit_bytes=16 * MIB),
        cost_estimate=pl.CostEstimate(flops=2**28, bytes_accessed=2**20, transcendentals=0),
    )(final_projector_coefficients, final_projector_offset.reshape(1, channels))
    theirs, weight, offset = lax.optimization_barrier((swap(give), weight, offset))
    messages = [give, theirs]
    places = [(n, 0, n, body + (half - 1) * per_chip) for n in range(2)]

    def take(*lefts):
        places.extend((len(messages) + n, 0, len(messages) + m, low) for n, (m, low) in enumerate(lefts))

    flying = [keep, theirs[: body + (half - 1) * per_chip]]
    swapped, lefts = [], []
    for step in range(1, half + 1):
        landed = [lax.ppermute(x, "row", around) for x in flying]
        if step >= 3:
            landed[-1], swapped[step - 3] = lax.optimization_barrier((landed[-1], swapped[step - 3]))
        low = [x.shape[0] - per_chip for x in landed]
        if step == 1:
            lefts.append([(0, low[0]), (1, low[1])])
        elif step < half:
            lefts.append([(1, low[1] - per_chip), (1, low[1])])
        else:
            lefts.append([(0, low[0])])
        flying = [landed[0][: body + per_chip]]
        if step == 1:
            flying += pl.pallas_call(
                functools.partial(join_kernel, body, per_chip),
                out_shape=[rows(body + 2 * (half - 2) * per_chip)],
                in_specs=[vmem] * 2,
                out_specs=[vmem],
                compiler_params=pltpu.CompilerParams(vmem_limit_bytes=16 * MIB),
                cost_estimate=pl.CostEstimate(flops=0, bytes_accessed=2**19, transcendentals=0),
            )(*landed)
        elif step < half - 1:
            flying.append(landed[1][: landed[1].shape[0] - 2 * per_chip])
        landed = lax.optimization_barrier(landed)
        take(*lefts[-1])
        messages += landed
        swapped.append([swap(x) for x in landed])
    for pair, left in zip(swapped, lefts):
        take(*left)
        messages += pair

    gridded = tiles > 1
    if gridded:
        operands, specs = [], []
        for n, right, m, left in places:
            operands += [messages[n], messages[m]]
            specs += [
                pl.BlockSpec((width, tile), lambda t, first=right // width: (first + t, 0)),
                pl.BlockSpec((per_chip, tile), lambda t, at=left // per_chip: (at, 0)),
            ]
        specs += [
            pl.BlockSpec((channels, hidden * hidden), lambda t: (0, 0)),
            pl.BlockSpec((1, channels), lambda t: (0, 0)),
        ]
        grid = (tiles,)
    else:
        operands = messages
        specs = [vmem] * (len(messages) + 2)
        grid = ()
    return pl.pallas_call(
        functools.partial(pair_kernel, places, gridded, rows_here, hidden, samples),
        out_shape=jax.ShapeDtypeStruct((rows_here, residues, channels), jnp.bfloat16),
        grid=grid,
        in_specs=specs,
        out_specs=hbm,
        scratch_shapes=[
            pltpu.VMEM((rows_here * hidden, samples), jnp.bfloat16),
            pltpu.VMEM((rows_here, hidden * hidden, tile), jnp.bfloat16),
            pltpu.VMEM((rows_here, tile, channels), jnp.bfloat16),
            pltpu.SemaphoreType.DMA((rows_here,)),
        ],
        compiler_params=pltpu.CompilerParams(vmem_limit_bytes=40 * MIB),
    )(*operands, weight, offset)


def solution(mesh):
    return jax.shard_map(
        functools.partial(per_device, mesh.shape["row"]),
        mesh=mesh,
        in_specs=(P(("groups", "row"), None, None), P(), P(), P(), P(), P(), P(), P(), P()),
        out_specs=P(("groups", "row"), None, None),
        check_vma=False,
    )
```

```python
import functools
import math

import jax
import jax.numpy as jnp
from jax import lax
from jax.experimental import pallas as pl
from jax.experimental.pallas import tpu as pltpu
from jax.sharding import PartitionSpec as P

MIB = 1024 * 1024
LANES = 128
BLOCK = 64


def repeat_rows(values, times):
    rows, cols = values.shape
    return jnp.broadcast_to(values[:, None, :], (rows, times, cols)).reshape(rows * times, cols)


def place_of(device, half):
    chip = device // 2
    return chip // 2 + (chip % 2) * (2 * half - 1 - 2 * (chip // 2))


def chip_at(place, half):
    return jnp.where(place < half, 2 * place, 2 * (2 * half - 1 - place) + 1)


def project_kernel(
    rows_here,
    x_hbm,
    gain_hbm,
    shift_hbm,
    first_hbm,
    first_offset_hbm,
    second_hbm,
    second_offset_hbm,
    keep_ref,
    give_ref,
    x_ref,
    gain_ref,
    shift_ref,
    first_ref,
    first_offset_ref,
    second_ref,
    second_offset_ref,
    packed_ref,
    sems,
):
    samples, residues, features = x_ref.shape
    hidden = first_ref.shape[0]
    width = samples * hidden
    tile = keep_ref.shape[1]
    tiles = residues // tile
    fold = LANES // hidden
    small = [
        (first_hbm, first_ref),
        (second_hbm, second_ref),
        (gain_hbm, gain_ref),
        (shift_hbm, shift_ref),
        (first_offset_hbm, first_offset_ref),
        (second_offset_hbm, second_offset_ref),
    ]
    copies = [
        pltpu.make_async_copy(src, dst, sems.at[samples + n]) for n, (src, dst) in enumerate(small)
    ]
    for copy in copies:
        copy.start()
    large = [pltpu.make_async_copy(x_hbm.at[s], x_ref.at[s], sems.at[s]) for s in range(samples)]
    for copy in large:
        copy.start()
    for copy in copies:
        copy.wait()

    first = jnp.concatenate([first_ref[...].astype(jnp.float32)] * fold, axis=0).T
    first = first.astype(jnp.bfloat16)
    first_offset = jnp.concatenate([first_offset_ref[...]] * fold, axis=1)
    second = repeat_rows(second_ref[...].astype(jnp.float32), samples).T
    column = lax.broadcasted_iota(jnp.int32, (1, width), 1)
    spot = lax.broadcasted_iota(jnp.int32, (width, hidden), 0)
    channel = lax.broadcasted_iota(jnp.int32, (width, hidden), 1)
    second_offset = jnp.sum(
        jnp.where(spot // samples == channel, second_offset_ref[...], 0.0), axis=1, keepdims=True
    )
    residue = lax.broadcasted_iota(jnp.int32, (tile, LANES), 0)
    lane = lax.broadcasted_iota(jnp.int32, (tile, LANES), 1)
    own = residue % fold == lane // hidden
    group = lax.broadcasted_iota(jnp.int32, (tile // fold, tile), 0)
    member = lax.broadcasted_iota(jnp.int32, (tile // fold, tile), 1)
    gather = (member // fold == group).astype(jnp.bfloat16)

    right = [jnp.zeros((tile, width), jnp.float32) for _ in range(tiles)]
    for copy in large:
        copy.wait()
    for s in range(samples):
        normed = []
        for low in range(0, residues, BLOCK):
            values = x_ref[s, low : low + BLOCK, :].astype(jnp.float32)
            center = jnp.mean(values, axis=-1, keepdims=True)
            values = values - center
            variance = jnp.mean(jnp.square(values), axis=-1, keepdims=True)
            values = values * lax.rsqrt(variance + 1e-05) * gain_ref[...] + shift_ref[...]
            normed.append(values.astype(jnp.bfloat16))
        normed = jnp.concatenate(normed, axis=0)
        second_here = jnp.where(column % samples == s, second, 0.0).astype(jnp.bfloat16)
        for t in range(tiles):
            part = normed[t * tile : (t + 1) * tile]
            left = jnp.dot(part, first, preferred_element_type=jnp.float32)
            right[t] += jnp.dot(part, second_here, preferred_element_type=jnp.float32)
            left = jnp.where(own, left + first_offset, 0.0).astype(jnp.bfloat16)
            low = t * (tile // fold) * samples + s
            packed_ref[pl.ds(low, tile // fold, stride=samples), :] = jnp.dot(
                gather, left, preferred_element_type=jnp.float32
            )
    for t in range(tiles):
        value = (right[t].T + second_offset).astype(jnp.bfloat16)
        keep_ref[t * width : (t + 1) * width, :] = value
        give_ref[t * width : (t + 1) * width, :] = value
    device = lax.axis_index("row")
    per_chip = 2 * rows_here * hidden * samples // tile
    half = residues // rows_here // 4
    base = tiles * width
    way = 1 - 2 * (device % 2)
    place = place_of(device, half)
    spots = [(keep_ref, base + n * per_chip, half - n) for n in range(half)]
    spots += [(give_ref, base + n * per_chip, n + 1 - half) for n in range(half)]
    for message, low, ahead in spots:
        chip = chip_at(lax.rem(place + way * ahead + 2 * half, 2 * half), half)
        across = tile // LANES
        start = pl.multiple_of(chip * per_chip * across, per_chip * across)
        block = packed_ref[pl.ds(start, per_chip * across), :]
        block = [block[n : n + samples] for n in range(0, per_chip * across, samples)]
        block = [jnp.concatenate(block[n : n + across], axis=1) for n in range(0, len(block), across)]
        message[low : low + per_chip, :] = jnp.concatenate(block, axis=0).astype(jnp.bfloat16)


def join_kernel(base, per_chip, mine_ref, theirs_ref, next_ref):
    next_ref[:base, :] = theirs_ref[:base, :]
    for n in range((next_ref.shape[0] - base) // (2 * per_chip)):
        low = base + n * per_chip
        at = low + n * per_chip
        next_ref[at : at + per_chip, :] = mine_ref[low + per_chip : low + 2 * per_chip, :]
        next_ref[at + per_chip : at + 2 * per_chip, :] = theirs_ref[low : low + per_chip, :]


def weight_kernel(final_ref, offset_ref, out_ref, offset_out, wide_ref):
    offset_out[...] = offset_ref[...]
    channels, columns = out_ref.shape
    hidden = math.isqrt(columns)
    wide_ref[...] = final_ref[...].astype(jnp.float32)
    step = LANES // hidden
    for e in range(0, hidden, step):
        rows = [wide_ref[pl.ds(e + n, hidden, stride=hidden), :] for n in range(step)]
        out_ref[:, e * hidden : (e + step) * hidden] = jnp.concatenate(rows, axis=0).T.astype(
            jnp.bfloat16
        )


def pair_kernel(places, gridded, rows_here, hidden, samples, *refs):
    refs = list(refs)
    count = len(places)
    if gridded:
        shards = [(refs.pop(0), 0, refs.pop(0), 0) for _ in places]
    else:
        messages = [refs.pop(0) for _ in places]
        shards = [(messages[n], right, messages[m], left) for n, right, m, left in places]
    weight_ref, offset_ref, out_hbm, left_ref, outer_ref, out_ref, sems = refs
    tile = shards[0][0].shape[1]
    here = samples // count
    span = rows_here * hidden
    deep = span * here // tile
    core = lax.rem(lax.axis_index("row"), 2)
    pieces = []
    for _, _, ref, base in shards:
        start = pl.multiple_of(base + core * deep, deep)
        piece = ref[pl.ds(start, deep), :].astype(jnp.float32)
        pieces.append(
            jnp.concatenate([piece[n * here : (n + 1) * here] for n in range(span // tile)], axis=1)
        )
    left_ref[...] = jnp.concatenate(pieces, axis=0).T.astype(jnp.bfloat16)

    left = left_ref[...]
    for e in range(0, hidden, 2):
        both = [
            ref[base + e * here : base + (e + 2) * here, :].astype(jnp.float32)
            for ref, base, _, _ in shards
        ]
        for k in range(2):
            right = jnp.concatenate([x[k * here : (k + 1) * here] for x in both], axis=0)
            outer = jnp.dot(left, right.astype(jnp.bfloat16), preferred_element_type=jnp.float32)
            outer = outer.astype(jnp.bfloat16)
            for i in range(rows_here):
                outer_ref[i, (e + k) * hidden : (e + k + 1) * hidden, :] = outer[
                    i * hidden : (i + 1) * hidden
                ]

    first = pl.program_id(0) * tile if gridded else 0
    copies = []
    for i in range(rows_here):
        value = jnp.dot(weight_ref[...], outer_ref[i], preferred_element_type=jnp.float32)
        value = value.T * (1.0 / samples) + offset_ref[...]
        out_ref[i] = value.astype(jnp.bfloat16)
        copies.append(
            pltpu.make_async_copy(out_ref.at[i], out_hbm.at[i, pl.ds(first, tile)], sems.at[i])
        )
        copies[-1].start()
    for copy in copies:
        copy.wait()


def per_device(
    size,
    alignment_embedding,
    rescaling_factor,
    recentering_offset,
    first_side_coefficients,
    first_side_offset,
    second_side_coefficients,
    second_side_offset,
    final_projector_coefficients,
    final_projector_offset,
):
    here, residues, features = alignment_embedding.shape
    hidden = first_side_coefficients.shape[1]
    channels = final_projector_coefficients.shape[1]
    width = here * hidden
    samples = here * size
    rows_here = residues // size
    half = size // 4
    tile = 256
    tiles = residues // tile
    body = tiles * width
    per_chip = 2 * rows_here * width // tile

    def rows(count):
        return jax.ShapeDtypeStruct((count, tile), jnp.bfloat16)

    vmem = pl.BlockSpec(memory_space=pltpu.VMEM)
    hbm = pl.BlockSpec(memory_space=pltpu.HBM)
    keep, give = pl.pallas_call(
        functools.partial(project_kernel, rows_here),
        out_shape=[rows(body + half * per_chip)] * 2,
        in_specs=[hbm] * 7,
        out_specs=[vmem] * 2,
        scratch_shapes=[
            pltpu.VMEM((here, residues, features), jnp.bfloat16),
            pltpu.VMEM((1, features), jnp.float32),
            pltpu.VMEM((1, features), jnp.float32),
            pltpu.VMEM((hidden, features), jnp.bfloat16),
            pltpu.VMEM((1, hidden), jnp.float32),
            pltpu.VMEM((hidden, features), jnp.bfloat16),
            pltpu.VMEM((1, hidden), jnp.float32),
            pltpu.VMEM((residues * width // LANES, LANES), jnp.float32),
            pltpu.SemaphoreType.DMA((here + 6,)),
        ],
        compiler_params=pltpu.CompilerParams(vmem_limit_bytes=32 * MIB),
        cost_estimate=pl.CostEstimate(
            flops=4 * here * residues * features * width,
            bytes_accessed=2 * here * residues * features,
            transcendentals=0,
        ),
    )(
        *[
            pltpu.with_memory_space_constraint(value, pltpu.HBM)
            for value in (
                alignment_embedding,
                rescaling_factor.reshape(1, features),
                recentering_offset.reshape(1, features),
                first_side_coefficients.T,
                first_side_offset.reshape(1, hidden),
                second_side_coefficients.T,
                second_side_offset.reshape(1, hidden),
            )
        ]
    )
    by_place = {(place_of(r, half), r % 2): r for r in range(size)}
    around = [
        (r, by_place[(place_of(r, half) + 1 - 2 * (r % 2)) % (2 * half), r % 2]) for r in range(size)
    ]

    def swap(value):
        return lax.ppermute(value, "row", [(r, r ^ 1) for r in range(size)])

    weight, offset = pl.pallas_call(
        weight_kernel,
        out_shape=[
            jax.ShapeDtypeStruct((channels, hidden * hidden), jnp.bfloat16),
            jax.ShapeDtypeStruct((1, channels), jnp.float32),
        ],
        in_specs=[vmem] * 2,
        out_specs=[vmem] * 2,
        scratch_shapes=[pltpu.VMEM((hidden * hidden, channels), jnp.float32)],
        compiler_params=pltpu.CompilerParams(vmem_limit_bytes=16 * MIB),
        cost_estimate=pl.CostEstimate(flops=2**28, bytes_accessed=2**20, transcendentals=0),
    )(final_projector_coefficients, final_projector_offset.reshape(1, channels))
    theirs, weight, offset = lax.optimization_barrier((swap(give), weight, offset))
    messages = [give, theirs]
    places = [(n, 0, n, body + (half - 1) * per_chip) for n in range(2)]

    def take(*lefts):
        places.extend((len(messages) + n, 0, len(messages) + m, low) for n, (m, low) in enumerate(lefts))

    flying = [keep, theirs[: body + (half - 1) * per_chip]]
    swapped, lefts = [], []
    for step in range(1, half + 1):
        landed = [lax.ppermute(x, "row", around) for x in flying]
        if step >= 3:
            landed[-1], swapped[step - 3] = lax.optimization_barrier((landed[-1], swapped[step - 3]))
        low = [x.shape[0] - per_chip for x in landed]
        if step == 1:
            lefts.append([(0, low[0]), (1, low[1])])
        elif step < half:
            lefts.append([(1, low[1] - per_chip), (1, low[1])])
        else:
            lefts.append([(0, low[0])])
        flying = [landed[0][: body + per_chip]]
        if step == 1:
            flying += pl.pallas_call(
                functools.partial(join_kernel, body, per_chip),
                out_shape=[rows(body + 2 * (half - 2) * per_chip)],
                in_specs=[vmem] * 2,
                out_specs=[vmem],
                compiler_params=pltpu.CompilerParams(vmem_limit_bytes=16 * MIB),
                cost_estimate=pl.CostEstimate(flops=0, bytes_accessed=2**19, transcendentals=0),
            )(*landed)
        elif step < half - 1:
            flying.append(landed[1][: landed[1].shape[0] - 2 * per_chip])
        landed = lax.optimization_barrier(landed)
        take(*lefts[-1])
        messages += landed
        swapped.append([swap(x) for x in landed])
    for pair, left in zip(swapped, lefts):
        take(*left)
        messages += pair

    gridded = tiles > 1
    if gridded:
        operands, specs = [], []
        for n, right, m, left in places:
            operands += [messages[n], messages[m]]
            specs += [
                pl.BlockSpec((width, tile), lambda t, first=right // width: (first + t, 0)),
                pl.BlockSpec((per_chip, tile), lambda t, at=left // per_chip: (at, 0)),
            ]
        specs += [
            pl.BlockSpec((channels, hidden * hidden), lambda t: (0, 0)),
            pl.BlockSpec((1, channels), lambda t: (0, 0)),
        ]
        grid = (tiles,)
    else:
        operands = messages
        specs = [vmem] * (len(messages) + 2)
        grid = ()
    return pl.pallas_call(
        functools.partial(pair_kernel, places, gridded, rows_here, hidden, samples),
        out_shape=jax.ShapeDtypeStruct((rows_here, residues, channels), jnp.bfloat16),
        grid=grid,
        in_specs=specs,
        out_specs=hbm,
        scratch_shapes=[
            pltpu.VMEM((rows_here * hidden, samples), jnp.bfloat16),
            pltpu.VMEM((rows_here, hidden * hidden, tile), jnp.bfloat16),
            pltpu.VMEM((rows_here, tile, channels), jnp.bfloat16),
            pltpu.SemaphoreType.DMA((rows_here,)),
        ],
        compiler_params=pltpu.CompilerParams(vmem_limit_bytes=40 * MIB),
    )(*operands, weight, offset)


def solution(mesh):
    return jax.shard_map(
        functools.partial(per_device, mesh.shape["row"]),
        mesh=mesh,
        in_specs=(P(("groups", "row"), None, None), P(), P(), P(), P(), P(), P(), P(), P()),
        out_specs=P(("groups", "row"), None, None),
        check_vma=False,
    )
```

```python
import functools
import math

import jax
import jax.numpy as jnp
from jax import lax
from jax.experimental import pallas as pl
from jax.experimental.pallas import tpu as pltpu
from jax.sharding import PartitionSpec as P

MIB = 1024 * 1024
LANES = 128
CHUNKS = 1
BLOCK = 64


def repeat_rows(values, times):
    rows, cols = values.shape
    return jnp.broadcast_to(values[:, None, :], (rows, times, cols)).reshape(rows * times, cols)


def place_of(device, half):
    chip = device // 2
    return chip // 2 + (chip % 2) * (2 * half - 1 - 2 * (chip // 2))


def chip_at(place, half):
    return jnp.where(place < half, 2 * place, 2 * (2 * half - 1 - place) + 1)


def project_kernel(
    rows_here,
    x_hbm,
    gain_hbm,
    shift_hbm,
    first_hbm,
    first_offset_hbm,
    second_hbm,
    second_offset_hbm,
    keep_ref,
    give_ref,
    x_ref,
    gain_ref,
    shift_ref,
    first_ref,
    first_offset_ref,
    second_ref,
    second_offset_ref,
    packed_ref,
    sems,
):
    samples, residues, features = x_ref.shape
    hidden = first_ref.shape[0]
    width = samples * hidden
    tile = keep_ref.shape[1]
    tiles = residues // tile
    fold = LANES // hidden
    small = [
        (first_hbm, first_ref),
        (second_hbm, second_ref),
        (gain_hbm, gain_ref),
        (shift_hbm, shift_ref),
        (first_offset_hbm, first_offset_ref),
        (second_offset_hbm, second_offset_ref),
    ]
    some = samples // CHUNKS
    copies = [
        pltpu.make_async_copy(src, dst, sems.at[CHUNKS + n]) for n, (src, dst) in enumerate(small)
    ]
    for copy in copies:
        copy.start()
    large = []
    for n in range(CHUNKS):
        rows = pl.ds(n * some, some)
        large.append(pltpu.make_async_copy(x_hbm.at[rows], x_ref.at[rows], sems.at[n]))
        large[-1].start()
    for copy in copies:
        copy.wait()

    first = jnp.concatenate([first_ref[...].astype(jnp.float32)] * fold, axis=0).T
    first = first.astype(jnp.bfloat16)
    first_offset = jnp.concatenate([first_offset_ref[...]] * fold, axis=1)
    second = repeat_rows(second_ref[...].astype(jnp.float32), samples).T
    column = lax.broadcasted_iota(jnp.int32, (1, width), 1)
    spot = lax.broadcasted_iota(jnp.int32, (width, hidden), 0)
    channel = lax.broadcasted_iota(jnp.int32, (width, hidden), 1)
    second_offset = jnp.sum(
        jnp.where(spot // samples == channel, second_offset_ref[...], 0.0), axis=1, keepdims=True
    )
    residue = lax.broadcasted_iota(jnp.int32, (tile, LANES), 0)
    lane = lax.broadcasted_iota(jnp.int32, (tile, LANES), 1)
    own = residue % fold == lane // hidden
    group = lax.broadcasted_iota(jnp.int32, (tile // fold, tile), 0)
    member = lax.broadcasted_iota(jnp.int32, (tile // fold, tile), 1)
    gather = (member // fold == group).astype(jnp.bfloat16)

    right = [jnp.zeros((tile, width), jnp.float32) for _ in range(tiles)]
    for s in range(samples):
        if s % some == 0:
            large[s // some].wait()
        normed = []
        for low in range(0, residues, BLOCK):
            values = x_ref[s, low : low + BLOCK, :].astype(jnp.float32)
            center = jnp.mean(values, axis=-1, keepdims=True)
            values = values - center
            variance = jnp.mean(jnp.square(values), axis=-1, keepdims=True)
            values = values * lax.rsqrt(variance + 1e-05) * gain_ref[...] + shift_ref[...]
            normed.append(values.astype(jnp.bfloat16))
        normed = jnp.concatenate(normed, axis=0)
        second_here = jnp.where(column % samples == s, second, 0.0).astype(jnp.bfloat16)
        for t in range(tiles):
            part = normed[t * tile : (t + 1) * tile]
            left = jnp.dot(part, first, preferred_element_type=jnp.float32)
            right[t] += jnp.dot(part, second_here, preferred_element_type=jnp.float32)
            left = jnp.where(own, left + first_offset, 0.0).astype(jnp.bfloat16)
            low = t * (tile // fold) * samples + s
            packed_ref[pl.ds(low, tile // fold, stride=samples), :] = jnp.dot(
                gather, left, preferred_element_type=jnp.float32
            )
    for t in range(tiles):
        value = (right[t].T + second_offset).astype(jnp.bfloat16)
        keep_ref[t * width : (t + 1) * width, :] = value
        give_ref[t * width : (t + 1) * width, :] = value
    device = lax.axis_index("row")
    per_chip = 2 * rows_here * hidden * samples // tile
    half = residues // rows_here // 4
    base = tiles * width
    way = 2 * (device % 2) - 1
    place = place_of(device, half)
    spots = [(keep_ref, base + n * per_chip, half - n) for n in range(half)]
    spots += [(give_ref, base + n * per_chip, n + 1 - half) for n in range(half)]
    for message, low, ahead in spots:
        chip = chip_at(lax.rem(place + way * ahead + 2 * half, 2 * half), half)
        across = tile // LANES
        start = pl.multiple_of(chip * per_chip * across, per_chip * across)
        block = packed_ref[pl.ds(start, per_chip * across), :]
        block = [block[n : n + samples] for n in range(0, per_chip * across, samples)]
        block = [jnp.concatenate(block[n : n + across], axis=1) for n in range(0, len(block), across)]
        message[low : low + per_chip, :] = jnp.concatenate(block, axis=0).astype(jnp.bfloat16)


def join_kernel(base, per_chip, mine_ref, theirs_ref, next_ref):
    next_ref[:base, :] = theirs_ref[:base, :]
    for n in range((next_ref.shape[0] - base) // (2 * per_chip)):
        low = base + n * per_chip
        at = low + n * per_chip
        next_ref[at : at + per_chip, :] = mine_ref[low + per_chip : low + 2 * per_chip, :]
        next_ref[at + per_chip : at + 2 * per_chip, :] = theirs_ref[low : low + per_chip, :]


def weight_kernel(final_ref, offset_ref, out_ref, offset_out, wide_ref):
    offset_out[...] = offset_ref[...]
    channels, columns = out_ref.shape
    hidden = math.isqrt(columns)
    wide_ref[...] = final_ref[...].astype(jnp.float32)
    step = LANES // hidden
    for e in range(0, hidden, step):
        rows = [wide_ref[pl.ds(e + n, hidden, stride=hidden), :] for n in range(step)]
        out_ref[:, e * hidden : (e + step) * hidden] = jnp.concatenate(rows, axis=0).T.astype(
            jnp.bfloat16
        )


def pair_kernel(places, gridded, rows_here, hidden, samples, *refs):
    refs = list(refs)
    count = len(places)
    if gridded:
        shards = [(refs.pop(0), 0, refs.pop(0), 0) for _ in places]
    else:
        messages = [refs.pop(0) for _ in places]
        shards = [(messages[n], right, messages[m], left) for n, right, m, left in places]
    weight_ref, offset_ref, out_hbm, left_ref, outer_ref, out_ref, sems = refs
    tile = shards[0][0].shape[1]
    here = samples // count
    span = rows_here * hidden
    deep = span * here // tile
    core = lax.rem(lax.axis_index("row"), 2)
    pieces = []
    for _, _, ref, base in shards:
        start = pl.multiple_of(base + core * deep, deep)
        piece = ref[pl.ds(start, deep), :].astype(jnp.float32)
        pieces.append(
            jnp.concatenate([piece[n * here : (n + 1) * here] for n in range(span // tile)], axis=1)
        )
    left_ref[...] = jnp.concatenate(pieces, axis=0).T.astype(jnp.bfloat16)

    left = left_ref[...]
    for e in range(0, hidden, 2):
        both = [
            ref[base + e * here : base + (e + 2) * here, :].astype(jnp.float32)
            for ref, base, _, _ in shards
        ]
        for k in range(2):
            right = jnp.concatenate([x[k * here : (k + 1) * here] for x in both], axis=0)
            outer = jnp.dot(left, right.astype(jnp.bfloat16), preferred_element_type=jnp.float32)
            outer = outer.astype(jnp.bfloat16)
            for i in range(rows_here):
                outer_ref[i, (e + k) * hidden : (e + k + 1) * hidden, :] = outer[
                    i * hidden : (i + 1) * hidden
                ]

    first = pl.program_id(0) * tile if gridded else 0
    copies = []
    for i in range(rows_here):
        value = jnp.dot(weight_ref[...], outer_ref[i], preferred_element_type=jnp.float32)
        value = value.T * (1.0 / samples) + offset_ref[...]
        out_ref[i] = value.astype(jnp.bfloat16)
        copies.append(
            pltpu.make_async_copy(out_ref.at[i], out_hbm.at[i, pl.ds(first, tile)], sems.at[i])
        )
        copies[-1].start()
    for copy in copies:
        copy.wait()


def per_device(
    size,
    alignment_embedding,
    rescaling_factor,
    recentering_offset,
    first_side_coefficients,
    first_side_offset,
    second_side_coefficients,
    second_side_offset,
    final_projector_coefficients,
    final_projector_offset,
):
    here, residues, features = alignment_embedding.shape
    hidden = first_side_coefficients.shape[1]
    channels = final_projector_coefficients.shape[1]
    width = here * hidden
    samples = here * size
    rows_here = residues // size
    half = size // 4
    tile = 256
    tiles = residues // tile
    body = tiles * width
    per_chip = 2 * rows_here * width // tile

    def rows(count):
        return jax.ShapeDtypeStruct((count, tile), jnp.bfloat16)

    vmem = pl.BlockSpec(memory_space=pltpu.VMEM)
    hbm = pl.BlockSpec(memory_space=pltpu.HBM)
    keep, give = pl.pallas_call(
        functools.partial(project_kernel, rows_here),
        out_shape=[rows(body + half * per_chip)] * 2,
        in_specs=[hbm] * 7,
        out_specs=[vmem] * 2,
        scratch_shapes=[
            pltpu.VMEM((here, residues, features), jnp.bfloat16),
            pltpu.VMEM((1, features), jnp.float32),
            pltpu.VMEM((1, features), jnp.float32),
            pltpu.VMEM((hidden, features), jnp.bfloat16),
            pltpu.VMEM((1, hidden), jnp.float32),
            pltpu.VMEM((hidden, features), jnp.bfloat16),
            pltpu.VMEM((1, hidden), jnp.float32),
            pltpu.VMEM((residues * width // LANES, LANES), jnp.float32),
            pltpu.SemaphoreType.DMA((CHUNKS + 6,)),
        ],
        compiler_params=pltpu.CompilerParams(vmem_limit_bytes=32 * MIB),
        cost_estimate=pl.CostEstimate(
            flops=4 * here * residues * features * width,
            bytes_accessed=2 * here * residues * features,
            transcendentals=0,
        ),
    )(
        *[
            pltpu.with_memory_space_constraint(value, pltpu.HBM)
            for value in (
                alignment_embedding,
                rescaling_factor.reshape(1, features),
                recentering_offset.reshape(1, features),
                first_side_coefficients.T,
                first_side_offset.reshape(1, hidden),
                second_side_coefficients.T,
                second_side_offset.reshape(1, hidden),
            )
        ]
    )
    by_place = {(place_of(r, half), r % 2): r for r in range(size)}
    around = [
        (r, by_place[(place_of(r, half) + 2 * (r % 2) - 1) % (2 * half), r % 2]) for r in range(size)
    ]

    def swap(value):
        return lax.ppermute(value, "row", [(r, r ^ 1) for r in range(size)])

    weight, offset = pl.pallas_call(
        weight_kernel,
        out_shape=[
            jax.ShapeDtypeStruct((channels, hidden * hidden), jnp.bfloat16),
            jax.ShapeDtypeStruct((1, channels), jnp.float32),
        ],
        in_specs=[vmem] * 2,
        out_specs=[vmem] * 2,
        scratch_shapes=[pltpu.VMEM((hidden * hidden, channels), jnp.float32)],
        compiler_params=pltpu.CompilerParams(vmem_limit_bytes=16 * MIB),
        cost_estimate=pl.CostEstimate(flops=2**28, bytes_accessed=2**20, transcendentals=0),
    )(final_projector_coefficients, final_projector_offset.reshape(1, channels))
    theirs, weight, offset = lax.optimization_barrier((swap(give), weight, offset))
    messages = [give, theirs]
    places = [(n, 0, n, body + (half - 1) * per_chip) for n in range(2)]

    def take(*lefts):
        places.extend((len(messages) + n, 0, len(messages) + m, low) for n, (m, low) in enumerate(lefts))

    flying = [keep, theirs[: body + (half - 1) * per_chip]]
    swapped, lefts = [], []
    for step in range(1, half + 1):
        landed = [lax.ppermute(x, "row", around) for x in flying]
        if step >= 3:
            landed[-1], swapped[step - 3] = lax.optimization_barrier((landed[-1], swapped[step - 3]))
        low = [x.shape[0] - per_chip for x in landed]
        if step == 1:
            lefts.append([(0, low[0]), (1, low[1])])
        elif step < half:
            lefts.append([(1, low[1] - per_chip), (1, low[1])])
        else:
            lefts.append([(0, low[0])])
        flying = [landed[0][: body + per_chip]]
        if step == 1:
            flying += pl.pallas_call(
                functools.partial(join_kernel, body, per_chip),
                out_shape=[rows(body + 2 * (half - 2) * per_chip)],
                in_specs=[vmem] * 2,
                out_specs=[vmem],
                compiler_params=pltpu.CompilerParams(vmem_limit_bytes=16 * MIB),
                cost_estimate=pl.CostEstimate(flops=0, bytes_accessed=2**19, transcendentals=0),
            )(*landed)
        elif step < half - 1:
            flying.append(landed[1][: landed[1].shape[0] - 2 * per_chip])
        landed = lax.optimization_barrier(landed)
        take(*lefts[-1])
        messages += landed
        swapped.append([swap(x) for x in landed])
    for pair, left in zip(swapped, lefts):
        take(*left)
        messages += pair

    gridded = tiles > 1
    if gridded:
        operands, specs = [], []
        for n, right, m, left in places:
            operands += [messages[n], messages[m]]
            specs += [
                pl.BlockSpec((width, tile), lambda t, first=right // width: (first + t, 0)),
                pl.BlockSpec((per_chip, tile), lambda t, at=left // per_chip: (at, 0)),
            ]
        specs += [
            pl.BlockSpec((channels, hidden * hidden), lambda t: (0, 0)),
            pl.BlockSpec((1, channels), lambda t: (0, 0)),
        ]
        grid = (tiles,)
    else:
        operands = messages
        specs = [vmem] * (len(messages) + 2)
        grid = ()
    return pl.pallas_call(
        functools.partial(pair_kernel, places, gridded, rows_here, hidden, samples),
        out_shape=jax.ShapeDtypeStruct((rows_here, residues, channels), jnp.bfloat16),
        grid=grid,
        in_specs=specs,
        out_specs=hbm,
        scratch_shapes=[
            pltpu.VMEM((rows_here * hidden, samples), jnp.bfloat16),
            pltpu.VMEM((rows_here, hidden * hidden, tile), jnp.bfloat16),
            pltpu.VMEM((rows_here, tile, channels), jnp.bfloat16),
            pltpu.SemaphoreType.DMA((rows_here,)),
        ],
        compiler_params=pltpu.CompilerParams(vmem_limit_bytes=40 * MIB),
    )(*operands, weight, offset)


def solution(mesh):
    return jax.shard_map(
        functools.partial(per_device, mesh.shape["row"]),
        mesh=mesh,
        in_specs=(P(("groups", "row"), None, None), P(), P(), P(), P(), P(), P(), P(), P()),
        out_specs=P(("groups", "row"), None, None),
        check_vma=False,
    )
```

```python
import functools
import math

import jax
import jax.numpy as jnp
from jax import lax
from jax.experimental import pallas as pl
from jax.experimental.pallas import tpu as pltpu
from jax.sharding import PartitionSpec as P

MIB = 1024 * 1024
LANES = 128
CHUNKS = 1
BLOCK = 64
EARLY = 4


def repeat_rows(values, times):
    rows, cols = values.shape
    return jnp.broadcast_to(values[:, None, :], (rows, times, cols)).reshape(rows * times, cols)


def place_of(device, half):
    chip = device // 2
    return chip // 2 + (chip % 2) * (2 * half - 1 - 2 * (chip // 2))


def chip_at(place, half):
    return jnp.where(place < half, 2 * place, 2 * (2 * half - 1 - place) + 1)


def project_kernel(
    rows_here,
    x_hbm,
    gain_hbm,
    shift_hbm,
    first_hbm,
    first_offset_hbm,
    second_hbm,
    second_offset_hbm,
    keep_ref,
    give_ref,
    x_ref,
    gain_ref,
    shift_ref,
    first_ref,
    first_offset_ref,
    second_ref,
    second_offset_ref,
    packed_ref,
    sems,
):
    samples, residues, features = x_ref.shape
    hidden = first_ref.shape[0]
    width = samples * hidden
    tile = keep_ref.shape[1]
    tiles = residues // tile
    fold = LANES // hidden
    small = [
        (first_hbm, first_ref),
        (second_hbm, second_ref),
        (gain_hbm, gain_ref),
        (shift_hbm, shift_ref),
        (first_offset_hbm, first_offset_ref),
        (second_offset_hbm, second_offset_ref),
    ]
    some = samples // CHUNKS
    copies = [
        pltpu.make_async_copy(src, dst, sems.at[CHUNKS + n]) for n, (src, dst) in enumerate(small)
    ]
    for copy in copies:
        copy.start()
    large = []
    for n in range(CHUNKS):
        rows = pl.ds(n * some, some)
        large.append(pltpu.make_async_copy(x_hbm.at[rows], x_ref.at[rows], sems.at[n]))
        large[-1].start()
    for copy in copies:
        copy.wait()

    first = jnp.concatenate([first_ref[...].astype(jnp.float32)] * fold, axis=0).T
    first = first.astype(jnp.bfloat16)
    first_offset = jnp.concatenate([first_offset_ref[...]] * fold, axis=1)
    second = repeat_rows(second_ref[...].astype(jnp.float32), samples).T
    column = lax.broadcasted_iota(jnp.int32, (1, width), 1)
    spot = lax.broadcasted_iota(jnp.int32, (width, hidden), 0)
    channel = lax.broadcasted_iota(jnp.int32, (width, hidden), 1)
    second_offset = jnp.sum(
        jnp.where(spot // samples == channel, second_offset_ref[...], 0.0), axis=1, keepdims=True
    )
    residue = lax.broadcasted_iota(jnp.int32, (tile, LANES), 0)
    lane = lax.broadcasted_iota(jnp.int32, (tile, LANES), 1)
    own = residue % fold == lane // hidden
    group = lax.broadcasted_iota(jnp.int32, (tile // fold, tile), 0)
    member = lax.broadcasted_iota(jnp.int32, (tile // fold, tile), 1)
    gather = (member // fold == group).astype(jnp.bfloat16)

    right = [jnp.zeros((tile, width), jnp.float32) for _ in range(tiles)]
    for s in range(samples):
        if s % some == 0:
            large[s // some].wait()
        normed = []
        for low in range(0, residues, BLOCK):
            values = x_ref[s, low : low + BLOCK, :].astype(jnp.float32)
            center = jnp.mean(values, axis=-1, keepdims=True)
            values = values - center
            variance = jnp.mean(jnp.square(values), axis=-1, keepdims=True)
            values = values * lax.rsqrt(variance + 1e-05) * gain_ref[...] + shift_ref[...]
            normed.append(values.astype(jnp.bfloat16))
        normed = jnp.concatenate(normed, axis=0)
        second_here = jnp.where(column % samples == s, second, 0.0).astype(jnp.bfloat16)
        for t in range(tiles):
            part = normed[t * tile : (t + 1) * tile]
            left = jnp.dot(part, first, preferred_element_type=jnp.float32)
            right[t] += jnp.dot(part, second_here, preferred_element_type=jnp.float32)
            left = jnp.where(own, left + first_offset, 0.0).astype(jnp.bfloat16)
            low = t * (tile // fold) * samples + s
            packed_ref[pl.ds(low, tile // fold, stride=samples), :] = jnp.dot(
                gather, left, preferred_element_type=jnp.float32
            )
    for t in range(tiles):
        value = (right[t].T + second_offset).astype(jnp.bfloat16)
        keep_ref[t * width : (t + 1) * width, :] = value
        give_ref[t * width : (t + 1) * width, :] = value
    device = lax.axis_index("row")
    per_chip = 2 * rows_here * hidden * samples // tile
    half = residues // rows_here // 4
    base = tiles * width
    way = 2 * (device % 2) - 1
    place = place_of(device, half)
    spots = [(keep_ref, base + n * per_chip, half - n) for n in range(half)]
    spots += [(give_ref, base + n * per_chip, n + 1 - half) for n in range(half)]
    for message, low, ahead in spots:
        chip = chip_at(lax.rem(place + way * ahead + 2 * half, 2 * half), half)
        across = tile // LANES
        start = pl.multiple_of(chip * per_chip * across, per_chip * across)
        block = packed_ref[pl.ds(start, per_chip * across), :]
        block = [block[n : n + samples] for n in range(0, per_chip * across, samples)]
        block = [jnp.concatenate(block[n : n + across], axis=1) for n in range(0, len(block), across)]
        message[low : low + per_chip, :] = jnp.concatenate(block, axis=0).astype(jnp.bfloat16)


def join_kernel(base, per_chip, mine_ref, theirs_ref, next_ref):
    next_ref[:base, :] = theirs_ref[:base, :]
    for n in range((next_ref.shape[0] - base) // (2 * per_chip)):
        low = base + n * per_chip
        at = low + n * per_chip
        next_ref[at : at + per_chip, :] = mine_ref[low + per_chip : low + 2 * per_chip, :]
        next_ref[at + per_chip : at + 2 * per_chip, :] = theirs_ref[low : low + per_chip, :]


def weight_kernel(final_ref, offset_ref, out_ref, mixing_out, offset_out, wide_ref):
    offset_out[...] = offset_ref[...]
    channels, columns = out_ref.shape
    hidden = math.isqrt(columns)
    wide_ref[...] = final_ref[...].astype(jnp.float32)
    step = LANES // hidden
    for e in range(0, hidden, step):
        rows = [wide_ref[pl.ds(e + n, hidden, stride=hidden), :] for n in range(step)]
        mixing_out[:, e * channels : (e + step) * channels] = jnp.concatenate(rows, axis=1).astype(
            jnp.bfloat16
        )
        out_ref[:, e * hidden : (e + step) * hidden] = jnp.concatenate(rows, axis=0).T.astype(
            jnp.bfloat16
        )


def left_pieces(shards, rows_here, hidden, here, low, high):
    core = lax.rem(lax.axis_index("row"), 2)
    span = rows_here * hidden
    pieces = []
    for _, _, ref, base in shards:
        tile = ref.shape[1]
        deep = span * here // tile
        start = pl.multiple_of(base + core * deep, deep)
        piece = ref[pl.ds(start, deep), :].astype(jnp.float32)
        wide = jnp.concatenate([piece[n * here : (n + 1) * here] for n in range(span // tile)], axis=1)
        pieces.append(wide[:, low * hidden : high * hidden])
    return pieces


def even(pieces):
    return pieces + [jnp.zeros_like(pieces[0])] * (len(pieces) % 2)


def outer_products(shards, left_ref, outer_ref, hidden, here):
    left = left_ref[...]
    for e in range(0, hidden, 2):
        both = even(
            [
                ref[base + e * here : base + (e + 2) * here, :].astype(jnp.float32)
                for ref, base, _, _ in shards
            ]
        )
        for k in range(2):
            right = jnp.concatenate([x[k * here : (k + 1) * here] for x in both], axis=0)
            outer = jnp.dot(left, right.astype(jnp.bfloat16), preferred_element_type=jnp.float32)
            outer = outer.astype(jnp.bfloat16)
            for i in range(outer_ref.shape[0]):
                outer_ref[i, (e + k) * hidden : (e + k + 1) * hidden, :] = outer[
                    i * hidden : (i + 1) * hidden
                ]


def early_kernel(places, rows_here, hidden, here, *refs):
    refs = list(refs)
    messages = [refs.pop(0) for _ in range(1 + max(max(n, m) for n, _, m, _ in places))]
    shards = [(messages[n], right, messages[m], left) for n, right, m, left in places]
    weight_ref = refs.pop(0)
    total_ref = refs.pop(0) if len(refs) == 4 else None
    total_out, left_ref, outer_ref = refs
    count = total_out.shape[0]
    pieces = even(left_pieces(shards, rows_here, hidden, here, 0, count))
    left_ref[...] = jnp.concatenate(pieces, axis=0).T.astype(jnp.bfloat16)
    outer_products(shards, left_ref, outer_ref, hidden, here)
    for i in range(count):
        value = jnp.dot(weight_ref[...], outer_ref[i], preferred_element_type=jnp.float32).T
        total_out[i] = value if total_ref is None else value + total_ref[i]


def pair_kernel(places, gridded, early, rows_here, hidden, samples, *refs):
    refs = list(refs)
    here = samples // len(places)
    if gridded:
        shards = [(refs.pop(0), 0, refs.pop(0), 0) for _ in places]
    else:
        messages = [refs.pop(0) for _ in places]
        shards = [(messages[n], right, messages[m], left) for n, right, m, left in places]
    weight_ref, offset_ref = refs.pop(0), refs.pop(0)
    total_ref, mixing_ref = (refs.pop(0), refs.pop(0)) if early else (None, None)
    out_hbm, left_ref, outer_ref, out_ref, sems = refs
    tile = shards[0][0].shape[1]
    channels = out_ref.shape[2]
    first = pl.program_id(0) * tile if gridded else 0
    copies = []

    def finish(i, value):
        out_ref[i] = (value * (1.0 / samples) + offset_ref[...]).astype(jnp.bfloat16)
        copies.append(
            pltpu.make_async_copy(out_ref.at[i], out_hbm.at[i, pl.ds(first, tile)], sems.at[i])
        )
        copies[-1].start()

    pieces = left_pieces(shards, rows_here, hidden, here, early, rows_here)
    left_ref[...] = jnp.concatenate(pieces, axis=0).T.astype(jnp.bfloat16)
    if early:
        last = left_pieces(shards[-1:], rows_here, hidden, here, 0, early)[0]
        last = [last[:, i * hidden : (i + 1) * hidden] for i in range(early)]
        mixed = jnp.dot(
            jnp.concatenate(last, axis=0).astype(jnp.bfloat16),
            mixing_ref[...],
            preferred_element_type=jnp.float32,
        )
        ref, base, _, _ = shards[-1]
        right = ref[base : base + hidden * here, :].astype(jnp.float32).T.astype(jnp.bfloat16)
        for i in range(early):
            part = mixed[i * here : (i + 1) * here]
            part = [part[:, e * channels : (e + 1) * channels] for e in range(hidden)]
            part = jnp.concatenate(part, axis=0).astype(jnp.bfloat16)
            value = jnp.dot(right, part, preferred_element_type=jnp.float32)
            finish(i, value + total_ref[i])
    outer_products(shards, left_ref, outer_ref, hidden, here)
    for i in range(early, rows_here):
        value = jnp.dot(weight_ref[...], outer_ref[i - early], preferred_element_type=jnp.float32)
        finish(i, value.T)
    for copy in copies:
        copy.wait()


def per_device(
    size,
    alignment_embedding,
    rescaling_factor,
    recentering_offset,
    first_side_coefficients,
    first_side_offset,
    second_side_coefficients,
    second_side_offset,
    final_projector_coefficients,
    final_projector_offset,
):
    here, residues, features = alignment_embedding.shape
    hidden = first_side_coefficients.shape[1]
    channels = final_projector_coefficients.shape[1]
    width = here * hidden
    samples = here * size
    rows_here = residues // size
    half = size // 4
    tile = 256
    tiles = residues // tile
    body = tiles * width
    per_chip = 2 * rows_here * width // tile

    def rows(count):
        return jax.ShapeDtypeStruct((count, tile), jnp.bfloat16)

    vmem = pl.BlockSpec(memory_space=pltpu.VMEM)
    hbm = pl.BlockSpec(memory_space=pltpu.HBM)
    keep, give = pl.pallas_call(
        functools.partial(project_kernel, rows_here),
        out_shape=[rows(body + half * per_chip)] * 2,
        in_specs=[hbm] * 7,
        out_specs=[vmem] * 2,
        scratch_shapes=[
            pltpu.VMEM((here, residues, features), jnp.bfloat16),
            pltpu.VMEM((1, features), jnp.float32),
            pltpu.VMEM((1, features), jnp.float32),
            pltpu.VMEM((hidden, features), jnp.bfloat16),
            pltpu.VMEM((1, hidden), jnp.float32),
            pltpu.VMEM((hidden, features), jnp.bfloat16),
            pltpu.VMEM((1, hidden), jnp.float32),
            pltpu.VMEM((residues * width // LANES, LANES), jnp.float32),
            pltpu.SemaphoreType.DMA((CHUNKS + 6,)),
        ],
        compiler_params=pltpu.CompilerParams(vmem_limit_bytes=32 * MIB),
        cost_estimate=pl.CostEstimate(
            flops=4 * here * residues * features * width,
            bytes_accessed=2 * here * residues * features,
            transcendentals=0,
        ),
    )(
        *[
            pltpu.with_memory_space_constraint(value, pltpu.HBM)
            for value in (
                alignment_embedding,
                rescaling_factor.reshape(1, features),
                recentering_offset.reshape(1, features),
                first_side_coefficients.T,
                first_side_offset.reshape(1, hidden),
                second_side_coefficients.T,
                second_side_offset.reshape(1, hidden),
            )
        ]
    )
    by_place = {(place_of(r, half), r % 2): r for r in range(size)}
    around = [
        (r, by_place[(place_of(r, half) + 2 * (r % 2) - 1) % (2 * half), r % 2]) for r in range(size)
    ]

    def swap(value):
        return lax.ppermute(value, "row", [(r, r ^ 1) for r in range(size)])

    weight, mixing, offset = pl.pallas_call(
        weight_kernel,
        out_shape=[
            jax.ShapeDtypeStruct((channels, hidden * hidden), jnp.bfloat16),
            jax.ShapeDtypeStruct((hidden, hidden * channels), jnp.bfloat16),
            jax.ShapeDtypeStruct((1, channels), jnp.float32),
        ],
        in_specs=[vmem] * 2,
        out_specs=[vmem] * 3,
        scratch_shapes=[pltpu.VMEM((hidden * hidden, channels), jnp.float32)],
        compiler_params=pltpu.CompilerParams(vmem_limit_bytes=16 * MIB),
        cost_estimate=pl.CostEstimate(flops=2**28, bytes_accessed=2**20, transcendentals=0),
    )(final_projector_coefficients, final_projector_offset.reshape(1, channels))
    theirs, weight, mixing, offset = lax.optimization_barrier((swap(give), weight, mixing, offset))
    def lay_out(groups):
        messages, places = [], []
        for values, left in groups:
            first = len(messages)
            places += [(first + n, 0, first + m, low) for n, (m, low) in enumerate(left)]
            messages += values
        return messages, places

    def early_sums(groups, total):
        messages, places = lay_out(groups)
        operands = messages + [weight] + ([] if total is None else [total])
        deep = here * (len(places) + len(places) % 2)
        return pl.pallas_call(
            functools.partial(early_kernel, places, rows_here, hidden, here),
            out_shape=jax.ShapeDtypeStruct((early, residues, channels), jnp.float32),
            in_specs=[vmem] * len(operands),
            out_specs=vmem,
            scratch_shapes=[
                pltpu.VMEM((early * hidden, deep), jnp.bfloat16),
                pltpu.VMEM((early, hidden * hidden, tile), jnp.bfloat16),
            ],
            compiler_params=pltpu.CompilerParams(vmem_limit_bytes=24 * MIB),
            cost_estimate=pl.CostEstimate(flops=2**30, bytes_accessed=2**21, transcendentals=0),
        )(*operands)

    gridded = tiles > 1
    early = 0 if gridded else EARLY
    own = ([give, theirs], [(n, body + (half - 1) * per_chip) for n in range(2)])
    flying = [keep, theirs[: body + (half - 1) * per_chip]]
    arrived, swapped, lefts, total = [], [], [], None
    for step in range(1, half + 1):
        landed = [lax.ppermute(x, "row", around) for x in flying]
        if step >= 3:
            landed[-1], swapped[step - 3] = lax.optimization_barrier((landed[-1], swapped[step - 3]))
        low = [x.shape[0] - per_chip for x in landed]
        if step == 1:
            lefts.append([(0, low[0]), (1, low[1])])
        elif step < half:
            lefts.append([(1, low[1] - per_chip), (1, low[1])])
        else:
            lefts.append([(0, low[0])])
        flying = [landed[0][: body + per_chip]]
        if step == 1:
            flying += pl.pallas_call(
                functools.partial(join_kernel, body, per_chip),
                out_shape=[rows(body + 2 * (half - 2) * per_chip)],
                in_specs=[vmem] * 2,
                out_specs=[vmem],
                compiler_params=pltpu.CompilerParams(vmem_limit_bytes=16 * MIB),
                cost_estimate=pl.CostEstimate(flops=0, bytes_accessed=2**19, transcendentals=0),
            )(*landed)
        elif step < half - 1:
            flying.append(landed[1][: landed[1].shape[0] - 2 * per_chip])
        landed = lax.optimization_barrier(landed)
        arrived.append(landed)
        if step == half - 1 and early:
            groups = [own] + list(zip(arrived, lefts)) + list(zip(swapped, lefts))
            turn, total = lax.optimization_barrier((landed[0], early_sums(groups, None)))
            landed = [turn, landed[1]]
        swapped.append([swap(x) for x in landed])
    if early:
        total = early_sums([(swapped[-2], lefts[-2]), (arrived[-1], lefts[-1])], total)

    messages, places = lay_out([own] + list(zip(arrived, lefts)) + list(zip(swapped, lefts)))
    if gridded:
        operands, specs = [], []
        for n, right, m, left in places:
            operands += [messages[n], messages[m]]
            specs += [
                pl.BlockSpec((width, tile), lambda t, first=right // width: (first + t, 0)),
                pl.BlockSpec((per_chip, tile), lambda t, at=left // per_chip: (at, 0)),
            ]
        operands += [weight, offset]
        specs += [
            pl.BlockSpec((channels, hidden * hidden), lambda t: (0, 0)),
            pl.BlockSpec((1, channels), lambda t: (0, 0)),
        ]
        grid = (tiles,)
    else:
        operands = messages + [weight, offset, total, mixing]
        specs = [vmem] * len(operands)
        grid = ()
    return pl.pallas_call(
        functools.partial(pair_kernel, places, gridded, early, rows_here, hidden, samples),
        out_shape=jax.ShapeDtypeStruct((rows_here, residues, channels), jnp.bfloat16),
        grid=grid,
        in_specs=specs,
        out_specs=hbm,
        scratch_shapes=[
            pltpu.VMEM(((rows_here - early) * hidden, samples), jnp.bfloat16),
            pltpu.VMEM((rows_here - early, hidden * hidden, tile), jnp.bfloat16),
            pltpu.VMEM((rows_here, tile, channels), jnp.bfloat16),
            pltpu.SemaphoreType.DMA((rows_here,)),
        ],
        compiler_params=pltpu.CompilerParams(vmem_limit_bytes=40 * MIB),
    )(*operands)


def solution(mesh):
    return jax.shard_map(
        functools.partial(per_device, mesh.shape["row"]),
        mesh=mesh,
        in_specs=(P(("groups", "row"), None, None), P(), P(), P(), P(), P(), P(), P(), P()),
        out_specs=P(("groups", "row"), None, None),
        check_vma=False,
    )
```

```python
import functools
import math

import jax
import jax.numpy as jnp
from jax import lax
from jax.experimental import pallas as pl
from jax.experimental.pallas import tpu as pltpu
from jax.sharding import PartitionSpec as P

MIB = 1024 * 1024
LANES = 128
CHUNKS = 1
BLOCK = 64


def repeat_rows(values, times):
    rows, cols = values.shape
    return jnp.broadcast_to(values[:, None, :], (rows, times, cols)).reshape(rows * times, cols)


def place_of(device, half):
    chip = device // 2
    return chip // 2 + (chip % 2) * (2 * half - 1 - 2 * (chip // 2))


def chip_at(place, half):
    return jnp.where(place < half, 2 * place, 2 * (2 * half - 1 - place) + 1)


def project_kernel(
    rows_here,
    x_hbm,
    gain_hbm,
    shift_hbm,
    first_hbm,
    first_offset_hbm,
    second_hbm,
    second_offset_hbm,
    keep_ref,
    rest_ref,
    give_ref,
    x_ref,
    gain_ref,
    shift_ref,
    first_ref,
    first_offset_ref,
    second_ref,
    second_offset_ref,
    packed_ref,
    sems,
):
    samples, residues, features = x_ref.shape
    hidden = first_ref.shape[0]
    width = samples * hidden
    tile = keep_ref.shape[1]
    tiles = residues // tile
    fold = LANES // hidden
    small = [
        (first_hbm, first_ref),
        (second_hbm, second_ref),
        (gain_hbm, gain_ref),
        (shift_hbm, shift_ref),
        (first_offset_hbm, first_offset_ref),
        (second_offset_hbm, second_offset_ref),
    ]
    some = samples // CHUNKS
    copies = [
        pltpu.make_async_copy(src, dst, sems.at[CHUNKS + n]) for n, (src, dst) in enumerate(small)
    ]
    for copy in copies:
        copy.start()
    large = []
    for n in range(CHUNKS):
        rows = pl.ds(n * some, some)
        large.append(pltpu.make_async_copy(x_hbm.at[rows], x_ref.at[rows], sems.at[n]))
        large[-1].start()
    for copy in copies:
        copy.wait()

    first = jnp.concatenate([first_ref[...].astype(jnp.float32)] * fold, axis=0).T
    first = first.astype(jnp.bfloat16)
    first_offset = jnp.concatenate([first_offset_ref[...]] * fold, axis=1)
    second = repeat_rows(second_ref[...].astype(jnp.float32), samples).T
    column = lax.broadcasted_iota(jnp.int32, (1, width), 1)
    spot = lax.broadcasted_iota(jnp.int32, (width, hidden), 0)
    channel = lax.broadcasted_iota(jnp.int32, (width, hidden), 1)
    second_offset = jnp.sum(
        jnp.where(spot // samples == channel, second_offset_ref[...], 0.0), axis=1, keepdims=True
    )
    residue = lax.broadcasted_iota(jnp.int32, (tile, LANES), 0)
    lane = lax.broadcasted_iota(jnp.int32, (tile, LANES), 1)
    own = residue % fold == lane // hidden
    group = lax.broadcasted_iota(jnp.int32, (tile // fold, tile), 0)
    member = lax.broadcasted_iota(jnp.int32, (tile // fold, tile), 1)
    gather = (member // fold == group).astype(jnp.bfloat16)

    right = [jnp.zeros((tile, width), jnp.float32) for _ in range(tiles)]
    for s in range(samples):
        if s % some == 0:
            large[s // some].wait()
        normed = []
        for low in range(0, residues, BLOCK):
            values = x_ref[s, low : low + BLOCK, :].astype(jnp.float32)
            center = jnp.mean(values, axis=-1, keepdims=True)
            values = values - center
            variance = jnp.mean(jnp.square(values), axis=-1, keepdims=True)
            values = values * lax.rsqrt(variance + 1e-05) * gain_ref[...] + shift_ref[...]
            normed.append(values.astype(jnp.bfloat16))
        normed = jnp.concatenate(normed, axis=0)
        second_here = jnp.where(column % samples == s, second, 0.0).astype(jnp.bfloat16)
        for t in range(tiles):
            part = normed[t * tile : (t + 1) * tile]
            left = jnp.dot(part, first, preferred_element_type=jnp.float32)
            right[t] += jnp.dot(part, second_here, preferred_element_type=jnp.float32)
            left = jnp.where(own, left + first_offset, 0.0).astype(jnp.bfloat16)
            low = t * (tile // fold) * samples + s
            packed_ref[pl.ds(low, tile // fold, stride=samples), :] = jnp.dot(
                gather, left, preferred_element_type=jnp.float32
            )
    for t in range(tiles):
        value = (right[t].T + second_offset).astype(jnp.bfloat16)
        keep_ref[t * width : (t + 1) * width, :] = value
        give_ref[t * width : (t + 1) * width, :] = value
    device = lax.axis_index("row")
    per_chip = 2 * rows_here * hidden * samples // tile
    half = residues // rows_here // 4
    base = tiles * width
    way = 2 * (device % 2) - 1
    place = place_of(device, half)
    spots = [(keep_ref, base, half)]
    spots += [(rest_ref, n * per_chip, half - 1 - n) for n in range(half - 1)]
    spots += [(give_ref, base + n * per_chip, n + 1 - half) for n in range(half)]
    for message, low, ahead in spots:
        chip = chip_at(lax.rem(place + way * ahead + 2 * half, 2 * half), half)
        across = tile // LANES
        start = pl.multiple_of(chip * per_chip * across, per_chip * across)
        block = packed_ref[pl.ds(start, per_chip * across), :]
        block = [block[n : n + samples] for n in range(0, per_chip * across, samples)]
        block = [jnp.concatenate(block[n : n + across], axis=1) for n in range(0, len(block), across)]
        message[low : low + per_chip, :] = jnp.concatenate(block, axis=0).astype(jnp.bfloat16)


def couple_kernel(base, per_chip, mine_ref, theirs_ref, out_ref):
    for low in range(0, mine_ref.shape[0], per_chip):
        out_ref[2 * low : 2 * low + per_chip, :] = mine_ref[low : low + per_chip, :]
        out_ref[2 * low + per_chip : 2 * (low + per_chip), :] = theirs_ref[
            base + low : base + low + per_chip, :
        ]


def join_kernel(per_chip, right_ref, left_ref, here_ref, next_ref):
    base, count = right_ref.shape[0], left_ref.shape[0] - 2 * per_chip
    here_ref[:base, :] = right_ref[...]
    next_ref[:base, :] = right_ref[...]
    here_ref[base:, :] = left_ref[count:, :]
    next_ref[base:, :] = left_ref[:count, :]


def weight_kernel(final_ref, offset_ref, out_ref, offset_out, wide_ref):
    offset_out[...] = offset_ref[...]
    channels, columns = out_ref.shape
    hidden = math.isqrt(columns)
    wide_ref[...] = final_ref[...].astype(jnp.float32)
    step = LANES // hidden
    for e in range(0, hidden, step):
        rows = [wide_ref[pl.ds(e + n, hidden, stride=hidden), :] for n in range(step)]
        out_ref[:, e * hidden : (e + step) * hidden] = jnp.concatenate(rows, axis=0).T.astype(
            jnp.bfloat16
        )


def pair_kernel(places, gridded, rows_here, hidden, samples, *refs):
    refs = list(refs)
    count = len(places)
    if gridded:
        shards = [(refs.pop(0), 0, refs.pop(0), 0) for _ in places]
    else:
        messages = [refs.pop(0) for _ in places]
        shards = [(messages[n], right, messages[m], left) for n, right, m, left in places]
    weight_ref, offset_ref, out_hbm, left_ref, outer_ref, out_ref, sems = refs
    tile = shards[0][0].shape[1]
    here = samples // count
    span = rows_here * hidden
    deep = span * here // tile
    core = lax.rem(lax.axis_index("row"), 2)
    pieces = []
    for _, _, ref, base in shards:
        start = pl.multiple_of(base + core * deep, deep)
        piece = ref[pl.ds(start, deep), :].astype(jnp.float32)
        pieces.append(
            jnp.concatenate([piece[n * here : (n + 1) * here] for n in range(span // tile)], axis=1)
        )
    left_ref[...] = jnp.concatenate(pieces, axis=0).T.astype(jnp.bfloat16)

    left = left_ref[...]
    for e in range(0, hidden, 2):
        both = [
            ref[base + e * here : base + (e + 2) * here, :].astype(jnp.float32)
            for ref, base, _, _ in shards
        ]
        for k in range(2):
            right = jnp.concatenate([x[k * here : (k + 1) * here] for x in both], axis=0)
            outer = jnp.dot(left, right.astype(jnp.bfloat16), preferred_element_type=jnp.float32)
            outer = outer.astype(jnp.bfloat16)
            for i in range(rows_here):
                outer_ref[i, (e + k) * hidden : (e + k + 1) * hidden, :] = outer[
                    i * hidden : (i + 1) * hidden
                ]

    first = pl.program_id(0) * tile if gridded else 0
    copies = []
    for i in range(rows_here):
        value = jnp.dot(weight_ref[...], outer_ref[i], preferred_element_type=jnp.float32)
        value = value.T * (1.0 / samples) + offset_ref[...]
        out_ref[i] = value.astype(jnp.bfloat16)
        copies.append(
            pltpu.make_async_copy(out_ref.at[i], out_hbm.at[i, pl.ds(first, tile)], sems.at[i])
        )
        copies[-1].start()
    for copy in copies:
        copy.wait()


def per_device(
    size,
    alignment_embedding,
    rescaling_factor,
    recentering_offset,
    first_side_coefficients,
    first_side_offset,
    second_side_coefficients,
    second_side_offset,
    final_projector_coefficients,
    final_projector_offset,
):
    here, residues, features = alignment_embedding.shape
    hidden = first_side_coefficients.shape[1]
    channels = final_projector_coefficients.shape[1]
    width = here * hidden
    samples = here * size
    rows_here = residues // size
    half = size // 4
    tile = 256
    tiles = residues // tile
    body = tiles * width
    per_chip = 2 * rows_here * width // tile

    def rows(count):
        return jax.ShapeDtypeStruct((count, tile), jnp.bfloat16)

    vmem = pl.BlockSpec(memory_space=pltpu.VMEM)
    hbm = pl.BlockSpec(memory_space=pltpu.HBM)
    keep, rest, give = pl.pallas_call(
        functools.partial(project_kernel, rows_here),
        out_shape=[rows(body + per_chip), rows((half - 1) * per_chip), rows(body + half * per_chip)],
        in_specs=[hbm] * 7,
        out_specs=[vmem] * 3,
        scratch_shapes=[
            pltpu.VMEM((here, residues, features), jnp.bfloat16),
            pltpu.VMEM((1, features), jnp.float32),
            pltpu.VMEM((1, features), jnp.float32),
            pltpu.VMEM((hidden, features), jnp.bfloat16),
            pltpu.VMEM((1, hidden), jnp.float32),
            pltpu.VMEM((hidden, features), jnp.bfloat16),
            pltpu.VMEM((1, hidden), jnp.float32),
            pltpu.VMEM((residues * width // LANES, LANES), jnp.float32),
            pltpu.SemaphoreType.DMA((CHUNKS + 6,)),
        ],
        compiler_params=pltpu.CompilerParams(vmem_limit_bytes=32 * MIB),
        cost_estimate=pl.CostEstimate(
            flops=4 * here * residues * features * width,
            bytes_accessed=2 * here * residues * features,
            transcendentals=0,
        ),
    )(
        *[
            pltpu.with_memory_space_constraint(value, pltpu.HBM)
            for value in (
                alignment_embedding,
                rescaling_factor.reshape(1, features),
                recentering_offset.reshape(1, features),
                first_side_coefficients.T,
                first_side_offset.reshape(1, hidden),
                second_side_coefficients.T,
                second_side_offset.reshape(1, hidden),
            )
        ]
    )
    by_place = {(place_of(r, half), r % 2): r for r in range(size)}
    around = [
        (r, by_place[(place_of(r, half) + 2 * (r % 2) - 1) % (2 * half), r % 2]) for r in range(size)
    ]

    def swap(value):
        return lax.ppermute(value, "row", [(r, r ^ 1) for r in range(size)])

    weight, offset = pl.pallas_call(
        weight_kernel,
        out_shape=[
            jax.ShapeDtypeStruct((channels, hidden * hidden), jnp.bfloat16),
            jax.ShapeDtypeStruct((1, channels), jnp.float32),
        ],
        in_specs=[vmem] * 2,
        out_specs=[vmem] * 2,
        scratch_shapes=[pltpu.VMEM((hidden * hidden, channels), jnp.float32)],
        compiler_params=pltpu.CompilerParams(vmem_limit_bytes=16 * MIB),
        cost_estimate=pl.CostEstimate(flops=2**28, bytes_accessed=2**20, transcendentals=0),
    )(final_projector_coefficients, final_projector_offset.reshape(1, channels))
    theirs, weight, offset = lax.optimization_barrier((swap(give), weight, offset))
    messages = [give, theirs]
    places = [(n, 0, n, body + (half - 1) * per_chip) for n in range(2)]

    def take(landed):
        first, last = len(messages), len(landed) - 1
        low = landed[last].shape[0] - len(landed) * per_chip
        places.extend((first + n, 0, first + last, low + n * per_chip) for n in range(len(landed)))
        messages.extend(landed)

    small = dict(
        compiler_params=pltpu.CompilerParams(vmem_limit_bytes=16 * MIB),
        cost_estimate=pl.CostEstimate(flops=0, bytes_accessed=2**19, transcendentals=0),
    )
    couples = pl.pallas_call(
        functools.partial(couple_kernel, body, per_chip),
        out_shape=rows(2 * (half - 1) * per_chip),
        in_specs=[vmem] * 2,
        out_specs=vmem,
        **small,
    )(rest, theirs)
    flying = [keep, theirs[:body], couples]
    swapped = []
    for step in range(1, half + 1):
        landed = [lax.ppermute(x, "row", around) for x in flying]
        if step >= 3:
            landed[-1], swapped[step - 3] = lax.optimization_barrier((landed[-1], swapped[step - 3]))
        flying = landed[:1]
        if step == 1:
            here_rows, next_rows = pl.pallas_call(
                functools.partial(join_kernel, per_chip),
                out_shape=[rows(body + 2 * per_chip), rows(body + 2 * (half - 2) * per_chip)],
                in_specs=[vmem] * 2,
                out_specs=[vmem] * 2,
                **small,
            )(*landed[1:])
            landed = [landed[0], here_rows]
            flying.append(next_rows)
        elif step < half - 1:
            flying.append(landed[1][: landed[1].shape[0] - 2 * per_chip])
        landed = lax.optimization_barrier(landed)
        take(landed)
        swapped.append([swap(x) for x in landed])
    for pair in swapped:
        take(pair)

    gridded = tiles > 1
    if gridded:
        operands, specs = [], []
        for n, right, m, left in places:
            operands += [messages[n], messages[m]]
            specs += [
                pl.BlockSpec((width, tile), lambda t, first=right // width: (first + t, 0)),
                pl.BlockSpec((per_chip, tile), lambda t, at=left // per_chip: (at, 0)),
            ]
        specs += [
            pl.BlockSpec((channels, hidden * hidden), lambda t: (0, 0)),
            pl.BlockSpec((1, channels), lambda t: (0, 0)),
        ]
        grid = (tiles,)
    else:
        operands = messages
        specs = [vmem] * (len(messages) + 2)
        grid = ()
    return pl.pallas_call(
        functools.partial(pair_kernel, places, gridded, rows_here, hidden, samples),
        out_shape=jax.ShapeDtypeStruct((rows_here, residues, channels), jnp.bfloat16),
        grid=grid,
        in_specs=specs,
        out_specs=hbm,
        scratch_shapes=[
            pltpu.VMEM((rows_here * hidden, samples), jnp.bfloat16),
            pltpu.VMEM((rows_here, hidden * hidden, tile), jnp.bfloat16),
            pltpu.VMEM((rows_here, tile, channels), jnp.bfloat16),
            pltpu.SemaphoreType.DMA((rows_here,)),
        ],
        compiler_params=pltpu.CompilerParams(vmem_limit_bytes=40 * MIB),
    )(*operands, weight, offset)


def solution(mesh):
    return jax.shard_map(
        functools.partial(per_device, mesh.shape["row"]),
        mesh=mesh,
        in_specs=(P(("groups", "row"), None, None), P(), P(), P(), P(), P(), P(), P(), P()),
        out_specs=P(("groups", "row"), None, None),
        check_vma=False,
    )
```

```python
import functools
import math

import jax
import jax.numpy as jnp
from jax import lax
from jax.experimental import pallas as pl
from jax.experimental.pallas import tpu as pltpu
from jax.sharding import PartitionSpec as P

MIB = 1024 * 1024
LANES = 128
CHUNKS = 1
BLOCK = 64


def repeat_rows(values, times):
    rows, cols = values.shape
    return jnp.broadcast_to(values[:, None, :], (rows, times, cols)).reshape(rows * times, cols)


def place_of(device, half):
    chip = device // 2
    return chip // 2 + (chip % 2) * (2 * half - 1 - 2 * (chip // 2))


def chip_at(place, half):
    return jnp.where(place < half, 2 * place, 2 * (2 * half - 1 - place) + 1)


def project_kernel(
    rows_here,
    x_hbm,
    gain_hbm,
    shift_hbm,
    first_hbm,
    first_offset_hbm,
    second_hbm,
    second_offset_hbm,
    keep_ref,
    give_ref,
    x_ref,
    gain_ref,
    shift_ref,
    first_ref,
    first_offset_ref,
    second_ref,
    second_offset_ref,
    packed_ref,
    sems,
):
    samples, residues, features = x_ref.shape
    hidden = first_ref.shape[0]
    width = samples * hidden
    tile = keep_ref.shape[1]
    tiles = residues // tile
    fold = LANES // hidden
    small = [
        (first_hbm, first_ref),
        (second_hbm, second_ref),
        (gain_hbm, gain_ref),
        (shift_hbm, shift_ref),
        (first_offset_hbm, first_offset_ref),
        (second_offset_hbm, second_offset_ref),
    ]
    some = samples // CHUNKS
    copies = [
        pltpu.make_async_copy(src, dst, sems.at[CHUNKS + n]) for n, (src, dst) in enumerate(small)
    ]
    for copy in copies:
        copy.start()
    large = []
    for n in range(CHUNKS):
        rows = pl.ds(n * some, some)
        large.append(pltpu.make_async_copy(x_hbm.at[rows], x_ref.at[rows], sems.at[n]))
        large[-1].start()
    for copy in copies:
        copy.wait()

    first = jnp.concatenate([first_ref[...].astype(jnp.float32)] * fold, axis=0).T
    first = first.astype(jnp.bfloat16)
    first_offset = jnp.concatenate([first_offset_ref[...]] * fold, axis=1)
    second = repeat_rows(second_ref[...].astype(jnp.float32), samples).T
    column = lax.broadcasted_iota(jnp.int32, (1, width), 1)
    spot = lax.broadcasted_iota(jnp.int32, (width, hidden), 0)
    channel = lax.broadcasted_iota(jnp.int32, (width, hidden), 1)
    second_offset = jnp.sum(
        jnp.where(spot // samples == channel, second_offset_ref[...], 0.0), axis=1, keepdims=True
    )
    residue = lax.broadcasted_iota(jnp.int32, (tile, LANES), 0)
    lane = lax.broadcasted_iota(jnp.int32, (tile, LANES), 1)
    own = residue % fold == lane // hidden
    group = lax.broadcasted_iota(jnp.int32, (tile // fold, tile), 0)
    member = lax.broadcasted_iota(jnp.int32, (tile // fold, tile), 1)
    gather = (member // fold == group).astype(jnp.bfloat16)

    right = [jnp.zeros((tile, width), jnp.float32) for _ in range(tiles)]
    for s in range(samples):
        if s % some == 0:
            large[s // some].wait()
        normed = []
        for low in range(0, residues, BLOCK):
            values = x_ref[s, low : low + BLOCK, :].astype(jnp.float32)
            center = jnp.mean(values, axis=-1, keepdims=True)
            values = values - center
            variance = jnp.mean(jnp.square(values), axis=-1, keepdims=True)
            values = values * lax.rsqrt(variance + 1e-05) * gain_ref[...] + shift_ref[...]
            normed.append(values.astype(jnp.bfloat16))
        normed = jnp.concatenate(normed, axis=0)
        second_here = jnp.where(column % samples == s, second, 0.0).astype(jnp.bfloat16)
        for t in range(tiles):
            part = normed[t * tile : (t + 1) * tile]
            left = jnp.dot(part, first, preferred_element_type=jnp.float32)
            right[t] += jnp.dot(part, second_here, preferred_element_type=jnp.float32)
            left = jnp.where(own, left + first_offset, 0.0).astype(jnp.bfloat16)
            low = t * (tile // fold) * samples + s
            packed_ref[pl.ds(low, tile // fold, stride=samples), :] = jnp.dot(
                gather, left, preferred_element_type=jnp.float32
            )
    for t in range(tiles):
        value = (right[t].T + second_offset).astype(jnp.bfloat16)
        keep_ref[t * width : (t + 1) * width, :] = value
        give_ref[t * width : (t + 1) * width, :] = value
    device = lax.axis_index("row")
    per_chip = 2 * rows_here * hidden * samples // tile
    half = residues // rows_here // 4
    base = tiles * width
    way = 2 * (device % 2) - 1
    place = place_of(device, half)
    spots = [(keep_ref, base + n * per_chip, half - n) for n in range(half)]
    spots += [(give_ref, base + n * per_chip, n + 1 - half) for n in range(half)]
    for message, low, ahead in spots:
        chip = chip_at(lax.rem(place + way * ahead + 2 * half, 2 * half), half)
        across = tile // LANES
        start = pl.multiple_of(chip * per_chip * across, per_chip * across)
        block = packed_ref[pl.ds(start, per_chip * across), :]
        block = [block[n : n + samples] for n in range(0, per_chip * across, samples)]
        block = [jnp.concatenate(block[n : n + across], axis=1) for n in range(0, len(block), across)]
        message[low : low + per_chip, :] = jnp.concatenate(block, axis=0).astype(jnp.bfloat16)


def join_kernel(base, per_chip, mine_ref, theirs_ref, next_ref):
    next_ref[:base, :] = theirs_ref[:base, :]
    for n in range((next_ref.shape[0] - base) // (2 * per_chip)):
        low = base + n * per_chip
        at = low + n * per_chip
        next_ref[at : at + per_chip, :] = mine_ref[low + per_chip : low + 2 * per_chip, :]
        next_ref[at + per_chip : at + 2 * per_chip, :] = theirs_ref[low : low + per_chip, :]


def weight_kernel(final_ref, offset_ref, out_ref, mixing_out, offset_out, wide_ref):
    offset_out[...] = offset_ref[...]
    channels, columns = out_ref.shape
    hidden = math.isqrt(columns)
    wide_ref[...] = final_ref[...].astype(jnp.float32)
    step = LANES // hidden
    for e in range(0, hidden, step):
        rows = [wide_ref[pl.ds(e + n, hidden, stride=hidden), :] for n in range(step)]
        mixing_out[:, e * channels : (e + step) * channels] = jnp.concatenate(rows, axis=1).astype(
            jnp.bfloat16
        )
        out_ref[:, e * hidden : (e + step) * hidden] = jnp.concatenate(rows, axis=0).T.astype(
            jnp.bfloat16
        )


def left_piece(ref, base, rows_here, hidden, here):
    tile = ref.shape[1]
    span = rows_here * hidden
    deep = span * here // tile
    start = pl.multiple_of(base + lax.rem(lax.axis_index("row"), 2) * deep, deep)
    piece = ref[pl.ds(start, deep), :].astype(jnp.float32)
    return jnp.concatenate([piece[n * here : (n + 1) * here] for n in range(span // tile)], axis=1)


def pair_kernel(places, gridded, rows_here, hidden, here, samples, *refs):
    refs = list(refs)
    if gridded:
        shards = [(refs.pop(0), 0, refs.pop(0), 0) for _ in places]
    else:
        messages = [refs.pop(0) for _ in places]
        shards = [(messages[n], right, messages[m], left) for n, right, m, left in places]
    weight_ref, offset_ref, out_hbm, left_ref, outer_ref, out_ref, sems = refs
    tile = shards[0][0].shape[1]
    pieces = [left_piece(ref, base, rows_here, hidden, here) for _, _, ref, base in shards]
    pieces += [jnp.zeros_like(pieces[0])] * (len(pieces) % 2)
    left_ref[...] = jnp.concatenate(pieces, axis=0).T.astype(jnp.bfloat16)

    left = left_ref[...]
    for e in range(0, hidden, 2):
        both = [
            ref[base + e * here : base + (e + 2) * here, :].astype(jnp.float32)
            for ref, base, _, _ in shards
        ]
        both += [jnp.zeros_like(both[0])] * (len(both) % 2)
        for k in range(2):
            right = jnp.concatenate([x[k * here : (k + 1) * here] for x in both], axis=0)
            outer = jnp.dot(left, right.astype(jnp.bfloat16), preferred_element_type=jnp.float32)
            outer = outer.astype(jnp.bfloat16)
            for i in range(rows_here):
                outer_ref[i, (e + k) * hidden : (e + k + 1) * hidden, :] = outer[
                    i * hidden : (i + 1) * hidden
                ]

    if not gridded:
        for i in range(rows_here):
            value = jnp.dot(weight_ref[...], outer_ref[i], preferred_element_type=jnp.float32)
            out_hbm[i] = value.T
        return
    first = pl.program_id(0) * tile
    copies = []
    for i in range(rows_here):
        value = jnp.dot(weight_ref[...], outer_ref[i], preferred_element_type=jnp.float32)
        value = value.T * (1.0 / samples) + offset_ref[...]
        out_ref[i] = value.astype(jnp.bfloat16)
        copies.append(
            pltpu.make_async_copy(out_ref.at[i], out_hbm.at[i, pl.ds(first, tile)], sems.at[i])
        )
        copies[-1].start()
    for copy in copies:
        copy.wait()


def last_kernel(base, rows_here, hidden, here, samples, ref, total_ref, mixing_ref, offset_ref, out_hbm, out_ref, sems):
    channels = out_ref.shape[2]
    right = ref[: hidden * here, :].astype(jnp.float32).T.astype(jnp.bfloat16)
    left = left_piece(ref, base, rows_here, hidden, here)
    left = [left[:, i * hidden : (i + 1) * hidden] for i in range(rows_here)]
    mixed = jnp.dot(
        jnp.concatenate(left, axis=0).astype(jnp.bfloat16),
        mixing_ref[...],
        preferred_element_type=jnp.float32,
    )
    copies = []
    for i in range(0, rows_here, 2):
        parts = []
        for k in range(2):
            part = mixed[(i + k) * here : (i + k + 1) * here]
            part = [part[:, e * channels : (e + 1) * channels] for e in range(hidden)]
            parts.append(jnp.concatenate(part, axis=0).astype(jnp.bfloat16))
        value = jnp.dot(
            right, jnp.concatenate(parts, axis=1), preferred_element_type=jnp.float32
        )
        for k in range(2):
            part = value[:, k * channels : (k + 1) * channels] + total_ref[i + k]
            out_ref[i + k] = (part * (1.0 / samples) + offset_ref[...]).astype(jnp.bfloat16)
        rows = pl.ds(i, 2)
        copies.append(pltpu.make_async_copy(out_ref.at[rows], out_hbm.at[rows], sems.at[i // 2]))
        copies[-1].start()
    for copy in copies:
        copy.wait()


def per_device(
    size,
    alignment_embedding,
    rescaling_factor,
    recentering_offset,
    first_side_coefficients,
    first_side_offset,
    second_side_coefficients,
    second_side_offset,
    final_projector_coefficients,
    final_projector_offset,
):
    here, residues, features = alignment_embedding.shape
    hidden = first_side_coefficients.shape[1]
    channels = final_projector_coefficients.shape[1]
    width = here * hidden
    samples = here * size
    rows_here = residues // size
    half = size // 4
    tile = 256
    tiles = residues // tile
    body = tiles * width
    per_chip = 2 * rows_here * width // tile

    def rows(count):
        return jax.ShapeDtypeStruct((count, tile), jnp.bfloat16)

    vmem = pl.BlockSpec(memory_space=pltpu.VMEM)
    hbm = pl.BlockSpec(memory_space=pltpu.HBM)
    keep, give = pl.pallas_call(
        functools.partial(project_kernel, rows_here),
        out_shape=[rows(body + half * per_chip)] * 2,
        in_specs=[hbm] * 7,
        out_specs=[vmem] * 2,
        scratch_shapes=[
            pltpu.VMEM((here, residues, features), jnp.bfloat16),
            pltpu.VMEM((1, features), jnp.float32),
            pltpu.VMEM((1, features), jnp.float32),
            pltpu.VMEM((hidden, features), jnp.bfloat16),
            pltpu.VMEM((1, hidden), jnp.float32),
            pltpu.VMEM((hidden, features), jnp.bfloat16),
            pltpu.VMEM((1, hidden), jnp.float32),
            pltpu.VMEM((residues * width // LANES, LANES), jnp.float32),
            pltpu.SemaphoreType.DMA((CHUNKS + 6,)),
        ],
        compiler_params=pltpu.CompilerParams(vmem_limit_bytes=32 * MIB),
        cost_estimate=pl.CostEstimate(
            flops=4 * here * residues * features * width,
            bytes_accessed=2 * here * residues * features,
            transcendentals=0,
        ),
    )(
        *[
            pltpu.with_memory_space_constraint(value, pltpu.HBM)
            for value in (
                alignment_embedding,
                rescaling_factor.reshape(1, features),
                recentering_offset.reshape(1, features),
                first_side_coefficients.T,
                first_side_offset.reshape(1, hidden),
                second_side_coefficients.T,
                second_side_offset.reshape(1, hidden),
            )
        ]
    )
    by_place = {(place_of(r, half), r % 2): r for r in range(size)}
    around = [
        (r, by_place[(place_of(r, half) + 2 * (r % 2) - 1) % (2 * half), r % 2]) for r in range(size)
    ]

    def swap(value):
        return lax.ppermute(value, "row", [(r, r ^ 1) for r in range(size)])

    weight, mixing, offset = pl.pallas_call(
        weight_kernel,
        out_shape=[
            jax.ShapeDtypeStruct((channels, hidden * hidden), jnp.bfloat16),
            jax.ShapeDtypeStruct((hidden, hidden * channels), jnp.bfloat16),
            jax.ShapeDtypeStruct((1, channels), jnp.float32),
        ],
        in_specs=[vmem] * 2,
        out_specs=[vmem] * 3,
        scratch_shapes=[pltpu.VMEM((hidden * hidden, channels), jnp.float32)],
        compiler_params=pltpu.CompilerParams(vmem_limit_bytes=16 * MIB),
        cost_estimate=pl.CostEstimate(flops=2**28, bytes_accessed=2**20, transcendentals=0),
    )(final_projector_coefficients, final_projector_offset.reshape(1, channels))
    theirs, weight, mixing, offset = lax.optimization_barrier((swap(give), weight, mixing, offset))
    messages = [give, theirs]
    places = [(n, 0, n, body + (half - 1) * per_chip) for n in range(2)]

    def take(*lefts):
        places.extend((len(messages) + n, 0, len(messages) + m, low) for n, (m, low) in enumerate(lefts))

    flying = [keep, theirs[: body + (half - 1) * per_chip]]
    swapped, lefts = [], []
    for step in range(1, half + 1):
        landed = [lax.ppermute(x, "row", around) for x in flying]
        if step >= 3:
            landed[-1], swapped[step - 3] = lax.optimization_barrier((landed[-1], swapped[step - 3]))
        low = [x.shape[0] - per_chip for x in landed]
        if step == 1:
            lefts.append([(0, low[0]), (1, low[1])])
        elif step < half:
            lefts.append([(1, low[1] - per_chip), (1, low[1])])
        else:
            lefts.append([(0, low[0])])
        flying = [landed[0][: body + per_chip]]
        if step == 1:
            flying += pl.pallas_call(
                functools.partial(join_kernel, body, per_chip),
                out_shape=[rows(body + 2 * (half - 2) * per_chip)],
                in_specs=[vmem] * 2,
                out_specs=[vmem],
                compiler_params=pltpu.CompilerParams(vmem_limit_bytes=16 * MIB),
                cost_estimate=pl.CostEstimate(flops=0, bytes_accessed=2**19, transcendentals=0),
            )(*landed)
        elif step < half - 1:
            flying.append(landed[1][: landed[1].shape[0] - 2 * per_chip])
        landed = lax.optimization_barrier(landed)
        take(*lefts[-1])
        messages += landed
        swapped.append([swap(x) for x in landed])
    for pair, left in zip(swapped, lefts):
        take(*left)
        messages += pair

    gridded = tiles > 1
    final = jax.ShapeDtypeStruct((rows_here, residues, channels), jnp.bfloat16)
    if gridded:
        operands, specs = [], []
        for n, right, m, left in places:
            operands += [messages[n], messages[m]]
            specs += [
                pl.BlockSpec((width, tile), lambda t, first=right // width: (first + t, 0)),
                pl.BlockSpec((per_chip, tile), lambda t, at=left // per_chip: (at, 0)),
            ]
        specs += [
            pl.BlockSpec((channels, hidden * hidden), lambda t: (0, 0)),
            pl.BlockSpec((1, channels), lambda t: (0, 0)),
        ]
        grid, result, out_spec = (tiles,), final, hbm
    else:
        places, operands = places[:-1], messages[:-1]
        specs = [vmem] * (len(operands) + 2)
        grid, out_spec = (), vmem
        result = jax.ShapeDtypeStruct((rows_here, residues, channels), jnp.float32)
    deep = here * (len(places) + len(places) % 2)
    total = pl.pallas_call(
        functools.partial(pair_kernel, places, gridded, rows_here, hidden, here, samples),
        out_shape=result,
        grid=grid,
        in_specs=specs,
        out_specs=out_spec,
        scratch_shapes=[
            pltpu.VMEM((rows_here * hidden, deep), jnp.bfloat16),
            pltpu.VMEM((rows_here, hidden * hidden, tile), jnp.bfloat16),
            pltpu.VMEM((rows_here, tile, channels), jnp.bfloat16),
            pltpu.SemaphoreType.DMA((rows_here,)),
        ],
        compiler_params=pltpu.CompilerParams(vmem_limit_bytes=40 * MIB),
    )(*operands, weight, offset)
    if gridded:
        return total
    return pl.pallas_call(
        functools.partial(last_kernel, body, rows_here, hidden, here, samples),
        out_shape=final,
        in_specs=[vmem] * 4,
        out_specs=hbm,
        scratch_shapes=[
            pltpu.VMEM((rows_here, tile, channels), jnp.bfloat16),
            pltpu.SemaphoreType.DMA((rows_here // 2,)),
        ],
        compiler_params=pltpu.CompilerParams(vmem_limit_bytes=24 * MIB),
    )(messages[-1], total, mixing, offset)


def solution(mesh):
    return jax.shard_map(
        functools.partial(per_device, mesh.shape["row"]),
        mesh=mesh,
        in_specs=(P(("groups", "row"), None, None), P(), P(), P(), P(), P(), P(), P(), P()),
        out_specs=P(("groups", "row"), None, None),
        check_vma=False,
    )
```

```python
import functools
import math

import jax
import jax.numpy as jnp
from jax import lax
from jax.experimental import pallas as pl
from jax.experimental.pallas import tpu as pltpu
from jax.sharding import PartitionSpec as P

MIB = 1024 * 1024
LANES = 128
CHUNKS = 1
BLOCK = 64


def repeat_rows(values, times):
    rows, cols = values.shape
    return jnp.broadcast_to(values[:, None, :], (rows, times, cols)).reshape(rows * times, cols)


def place_of(device, half):
    chip = device // 2
    return chip // 2 + (chip % 2) * (2 * half - 1 - 2 * (chip // 2))


def chip_at(place, half):
    return jnp.where(place < half, 2 * place, 2 * (2 * half - 1 - place) + 1)


def project_kernel(
    rows_here,
    x_hbm,
    gain_hbm,
    shift_hbm,
    first_hbm,
    first_offset_hbm,
    second_hbm,
    second_offset_hbm,
    final_hbm,
    final_offset_hbm,
    keep_ref,
    give_ref,
    final_ref,
    final_offset_ref,
    x_ref,
    gain_ref,
    shift_ref,
    first_ref,
    first_offset_ref,
    second_ref,
    second_offset_ref,
    packed_ref,
    sems,
):
    samples, residues, features = x_ref.shape
    hidden = first_ref.shape[0]
    width = samples * hidden
    tile = keep_ref.shape[1]
    tiles = residues // tile
    fold = LANES // hidden
    small = [
        (first_hbm, first_ref),
        (second_hbm, second_ref),
        (gain_hbm, gain_ref),
        (shift_hbm, shift_ref),
        (first_offset_hbm, first_offset_ref),
        (second_offset_hbm, second_offset_ref),
    ]
    some = samples // CHUNKS
    copies = [
        pltpu.make_async_copy(src, dst, sems.at[CHUNKS + n]) for n, (src, dst) in enumerate(small)
    ]
    for copy in copies:
        copy.start()
    large = []
    for n in range(CHUNKS):
        rows = pl.ds(n * some, some)
        large.append(pltpu.make_async_copy(x_hbm.at[rows], x_ref.at[rows], sems.at[n]))
        large[-1].start()
    later = [
        pltpu.make_async_copy(final_hbm, final_ref, sems.at[CHUNKS + len(small)]),
        pltpu.make_async_copy(final_offset_hbm, final_offset_ref, sems.at[CHUNKS + len(small) + 1]),
    ]
    for copy in later:
        copy.start()
    for copy in copies:
        copy.wait()

    first = jnp.concatenate([first_ref[...].astype(jnp.float32)] * fold, axis=0).T
    first = first.astype(jnp.bfloat16)
    first_offset = jnp.concatenate([first_offset_ref[...]] * fold, axis=1)
    second = repeat_rows(second_ref[...].astype(jnp.float32), samples).T
    column = lax.broadcasted_iota(jnp.int32, (1, width), 1)
    spot = lax.broadcasted_iota(jnp.int32, (width, hidden), 0)
    channel = lax.broadcasted_iota(jnp.int32, (width, hidden), 1)
    second_offset = jnp.sum(
        jnp.where(spot // samples == channel, second_offset_ref[...], 0.0), axis=1, keepdims=True
    )
    residue = lax.broadcasted_iota(jnp.int32, (tile, LANES), 0)
    lane = lax.broadcasted_iota(jnp.int32, (tile, LANES), 1)
    own = residue % fold == lane // hidden
    group = lax.broadcasted_iota(jnp.int32, (tile // fold, tile), 0)
    member = lax.broadcasted_iota(jnp.int32, (tile // fold, tile), 1)
    gather = (member // fold == group).astype(jnp.bfloat16)

    right = [jnp.zeros((tile, width), jnp.float32) for _ in range(tiles)]
    for s in range(samples):
        if s % some == 0:
            large[s // some].wait()
        normed = []
        for low in range(0, residues, BLOCK):
            values = x_ref[s, low : low + BLOCK, :].astype(jnp.float32)
            center = jnp.mean(values, axis=-1, keepdims=True)
            values = values - center
            variance = jnp.mean(jnp.square(values), axis=-1, keepdims=True)
            values = values * lax.rsqrt(variance + 1e-05) * gain_ref[...] + shift_ref[...]
            normed.append(values.astype(jnp.bfloat16))
        normed = jnp.concatenate(normed, axis=0)
        second_here = jnp.where(column % samples == s, second, 0.0).astype(jnp.bfloat16)
        for t in range(tiles):
            part = normed[t * tile : (t + 1) * tile]
            left = jnp.dot(part, first, preferred_element_type=jnp.float32)
            right[t] += jnp.dot(part, second_here, preferred_element_type=jnp.float32)
            left = jnp.where(own, left + first_offset, 0.0).astype(jnp.bfloat16)
            low = t * (tile // fold) * samples + s
            packed_ref[pl.ds(low, tile // fold, stride=samples), :] = jnp.dot(
                gather, left, preferred_element_type=jnp.float32
            )
    for t in range(tiles):
        value = (right[t].T + second_offset).astype(jnp.bfloat16)
        keep_ref[t * width : (t + 1) * width, :] = value
        give_ref[t * width : (t + 1) * width, :] = value
    for copy in later:
        copy.wait()
    device = lax.axis_index("row")
    per_chip = 2 * rows_here * hidden * samples // tile
    half = residues // rows_here // 4
    base = tiles * width
    way = 2 * (device % 2) - 1
    place = place_of(device, half)
    spots = [(keep_ref, base + n * per_chip, half - n) for n in range(half)]
    spots += [(give_ref, base + n * per_chip, n + 1 - half) for n in range(half)]
    for message, low, ahead in spots:
        chip = chip_at(lax.rem(place + way * ahead + 2 * half, 2 * half), half)
        across = tile // LANES
        start = pl.multiple_of(chip * per_chip * across, per_chip * across)
        block = packed_ref[pl.ds(start, per_chip * across), :]
        block = [block[n : n + samples] for n in range(0, per_chip * across, samples)]
        block = [jnp.concatenate(block[n : n + across], axis=1) for n in range(0, len(block), across)]
        message[low : low + per_chip, :] = jnp.concatenate(block, axis=0).astype(jnp.bfloat16)


def join_kernel(base, per_chip, mine_ref, theirs_ref, next_ref):
    next_ref[:base, :] = theirs_ref[:base, :]
    for n in range((next_ref.shape[0] - base) // (2 * per_chip)):
        low = base + n * per_chip
        at = low + n * per_chip
        next_ref[at : at + per_chip, :] = mine_ref[low + per_chip : low + 2 * per_chip, :]
        next_ref[at + per_chip : at + 2 * per_chip, :] = theirs_ref[low : low + per_chip, :]


def weight_kernel(final_ref, out_ref, mixing_out, wide_ref):
    channels, columns = out_ref.shape
    hidden = math.isqrt(columns)
    wide_ref[...] = final_ref[...].astype(jnp.float32)
    step = LANES // hidden
    for e in range(0, hidden, step):
        rows = [wide_ref[pl.ds(e + n, hidden, stride=hidden), :] for n in range(step)]
        mixing_out[:, e * channels : (e + step) * channels] = jnp.concatenate(rows, axis=1).astype(
            jnp.bfloat16
        )
        out_ref[:, e * hidden : (e + step) * hidden] = jnp.concatenate(rows, axis=0).T.astype(
            jnp.bfloat16
        )


def left_piece(ref, base, rows_here, hidden, here):
    tile = ref.shape[1]
    span = rows_here * hidden
    deep = span * here // tile
    start = pl.multiple_of(base + lax.rem(lax.axis_index("row"), 2) * deep, deep)
    piece = ref[pl.ds(start, deep), :].astype(jnp.float32)
    return jnp.concatenate([piece[n * here : (n + 1) * here] for n in range(span // tile)], axis=1)


def pair_kernel(places, gridded, rows_here, hidden, here, samples, *refs):
    refs = list(refs)
    if gridded:
        shards = [(refs.pop(0), 0, refs.pop(0), 0) for _ in places]
    else:
        messages = [refs.pop(0) for _ in places]
        shards = [(messages[n], right, messages[m], left) for n, right, m, left in places]
    weight_ref, offset_ref, out_hbm, left_ref, outer_ref, out_ref, sems = refs
    tile = shards[0][0].shape[1]
    pieces = [left_piece(ref, base, rows_here, hidden, here) for _, _, ref, base in shards]
    pieces += [jnp.zeros_like(pieces[0])] * (len(pieces) % 2)
    left_ref[...] = jnp.concatenate(pieces, axis=0).T.astype(jnp.bfloat16)

    left = left_ref[...]
    for e in range(0, hidden, 2):
        both = [
            ref[base + e * here : base + (e + 2) * here, :].astype(jnp.float32)
            for ref, base, _, _ in shards
        ]
        both += [jnp.zeros_like(both[0])] * (len(both) % 2)
        for k in range(2):
            right = jnp.concatenate([x[k * here : (k + 1) * here] for x in both], axis=0)
            outer = jnp.dot(left, right.astype(jnp.bfloat16), preferred_element_type=jnp.float32)
            outer = outer.astype(jnp.bfloat16)
            for i in range(rows_here):
                outer_ref[i, (e + k) * hidden : (e + k + 1) * hidden, :] = outer[
                    i * hidden : (i + 1) * hidden
                ]

    if not gridded:
        for i in range(rows_here):
            value = jnp.dot(weight_ref[...], outer_ref[i], preferred_element_type=jnp.float32)
            out_hbm[i] = value.T
        return
    first = pl.program_id(0) * tile
    copies = []
    for i in range(rows_here):
        value = jnp.dot(weight_ref[...], outer_ref[i], preferred_element_type=jnp.float32)
        value = value.T * (1.0 / samples) + offset_ref[...]
        out_ref[i] = value.astype(jnp.bfloat16)
        copies.append(
            pltpu.make_async_copy(out_ref.at[i], out_hbm.at[i, pl.ds(first, tile)], sems.at[i])
        )
        copies[-1].start()
    for copy in copies:
        copy.wait()


def last_kernel(base, rows_here, hidden, here, samples, ref, total_ref, mixing_ref, offset_ref, out_hbm, out_ref, sems):
    channels = out_ref.shape[2]
    right = ref[: hidden * here, :].astype(jnp.float32).T.astype(jnp.bfloat16)
    left = left_piece(ref, base, rows_here, hidden, here)
    copies = []
    some = 4
    for low in range(0, rows_here, some):
        block = [left[:, i * hidden : (i + 1) * hidden] for i in range(low, low + some)]
        mixed = jnp.dot(
            jnp.concatenate(block, axis=0).astype(jnp.bfloat16),
            mixing_ref[...],
            preferred_element_type=jnp.float32,
        )
        parts = []
        for k in range(some):
            part = mixed[k * here : (k + 1) * here]
            part = [part[:, e * channels : (e + 1) * channels] for e in range(hidden)]
            parts.append(jnp.concatenate(part, axis=0).astype(jnp.bfloat16))
        value = jnp.dot(right, jnp.concatenate(parts, axis=1), preferred_element_type=jnp.float32)
        for k in range(some):
            part = value[:, k * channels : (k + 1) * channels] + total_ref[low + k]
            out_ref[low + k] = (part * (1.0 / samples) + offset_ref[...]).astype(jnp.bfloat16)
        rows = pl.ds(low, some)
        copies.append(pltpu.make_async_copy(out_ref.at[rows], out_hbm.at[rows], sems.at[low // some]))
        copies[-1].start()
    for copy in copies:
        copy.wait()


def per_device(
    size,
    alignment_embedding,
    rescaling_factor,
    recentering_offset,
    first_side_coefficients,
    first_side_offset,
    second_side_coefficients,
    second_side_offset,
    final_projector_coefficients,
    final_projector_offset,
):
    here, residues, features = alignment_embedding.shape
    hidden = first_side_coefficients.shape[1]
    channels = final_projector_coefficients.shape[1]
    width = here * hidden
    samples = here * size
    rows_here = residues // size
    half = size // 4
    tile = 256
    tiles = residues // tile
    body = tiles * width
    per_chip = 2 * rows_here * width // tile

    def rows(count):
        return jax.ShapeDtypeStruct((count, tile), jnp.bfloat16)

    vmem = pl.BlockSpec(memory_space=pltpu.VMEM)
    hbm = pl.BlockSpec(memory_space=pltpu.HBM)
    keep, give, final, offset = pl.pallas_call(
        functools.partial(project_kernel, rows_here),
        out_shape=[rows(body + half * per_chip)] * 2
        + [
            jax.ShapeDtypeStruct(final_projector_coefficients.shape, jnp.bfloat16),
            jax.ShapeDtypeStruct((1, channels), jnp.float32),
        ],
        in_specs=[hbm] * 9,
        out_specs=[vmem] * 4,
        scratch_shapes=[
            pltpu.VMEM((here, residues, features), jnp.bfloat16),
            pltpu.VMEM((1, features), jnp.float32),
            pltpu.VMEM((1, features), jnp.float32),
            pltpu.VMEM((hidden, features), jnp.bfloat16),
            pltpu.VMEM((1, hidden), jnp.float32),
            pltpu.VMEM((hidden, features), jnp.bfloat16),
            pltpu.VMEM((1, hidden), jnp.float32),
            pltpu.VMEM((residues * width // LANES, LANES), jnp.float32),
            pltpu.SemaphoreType.DMA((CHUNKS + 8,)),
        ],
        compiler_params=pltpu.CompilerParams(vmem_limit_bytes=32 * MIB),
        cost_estimate=pl.CostEstimate(
            flops=4 * here * residues * features * width,
            bytes_accessed=2 * here * residues * features,
            transcendentals=0,
        ),
    )(
        *[
            pltpu.with_memory_space_constraint(value, pltpu.HBM)
            for value in (
                alignment_embedding,
                rescaling_factor.reshape(1, features),
                recentering_offset.reshape(1, features),
                first_side_coefficients.T,
                first_side_offset.reshape(1, hidden),
                second_side_coefficients.T,
                second_side_offset.reshape(1, hidden),
                final_projector_coefficients,
                final_projector_offset.reshape(1, channels),
            )
        ]
    )
    by_place = {(place_of(r, half), r % 2): r for r in range(size)}
    around = [
        (r, by_place[(place_of(r, half) + 2 * (r % 2) - 1) % (2 * half), r % 2]) for r in range(size)
    ]

    def swap(value):
        return lax.ppermute(value, "row", [(r, r ^ 1) for r in range(size)])

    weight, mixing = pl.pallas_call(
        weight_kernel,
        out_shape=[
            jax.ShapeDtypeStruct((channels, hidden * hidden), jnp.bfloat16),
            jax.ShapeDtypeStruct((hidden, hidden * channels), jnp.bfloat16),
        ],
        in_specs=[vmem],
        out_specs=[vmem] * 2,
        scratch_shapes=[pltpu.VMEM((hidden * hidden, channels), jnp.float32)],
        compiler_params=pltpu.CompilerParams(vmem_limit_bytes=16 * MIB),
        cost_estimate=pl.CostEstimate(flops=2**28, bytes_accessed=2**20, transcendentals=0),
    )(final)
    theirs, weight, mixing = lax.optimization_barrier((swap(give), weight, mixing))
    messages = [give, theirs]
    places = [(n, 0, n, body + (half - 1) * per_chip) for n in range(2)]

    def take(*lefts):
        places.extend((len(messages) + n, 0, len(messages) + m, low) for n, (m, low) in enumerate(lefts))

    flying = [keep, theirs[: body + (half - 1) * per_chip]]
    swapped, lefts = [], []
    for step in range(1, half + 1):
        landed = [lax.ppermute(x, "row", around) for x in flying]
        if step >= 3:
            landed[-1], swapped[step - 3] = lax.optimization_barrier((landed[-1], swapped[step - 3]))
        low = [x.shape[0] - per_chip for x in landed]
        if step == 1:
            lefts.append([(0, low[0]), (1, low[1])])
        elif step < half:
            lefts.append([(1, low[1] - per_chip), (1, low[1])])
        else:
            lefts.append([(0, low[0])])
        flying = [landed[0][: body + per_chip]]
        if step == 1:
            flying += pl.pallas_call(
                functools.partial(join_kernel, body, per_chip),
                out_shape=[rows(body + 2 * (half - 2) * per_chip)],
                in_specs=[vmem] * 2,
                out_specs=[vmem],
                compiler_params=pltpu.CompilerParams(vmem_limit_bytes=16 * MIB),
                cost_estimate=pl.CostEstimate(flops=0, bytes_accessed=2**19, transcendentals=0),
            )(*landed)
        elif step < half - 1:
            flying.append(landed[1][: landed[1].shape[0] - 2 * per_chip])
        landed = lax.optimization_barrier(landed)
        take(*lefts[-1])
        messages += landed
        swapped.append([swap(x) for x in landed])
    for pair, left in zip(swapped, lefts):
        take(*left)
        messages += pair

    gridded = tiles > 1
    outcome = jax.ShapeDtypeStruct((rows_here, residues, channels), jnp.bfloat16)
    if gridded:
        operands, specs = [], []
        for n, right, m, left in places:
            operands += [messages[n], messages[m]]
            specs += [
                pl.BlockSpec((width, tile), lambda t, first=right // width: (first + t, 0)),
                pl.BlockSpec((per_chip, tile), lambda t, at=left // per_chip: (at, 0)),
            ]
        specs += [
            pl.BlockSpec((channels, hidden * hidden), lambda t: (0, 0)),
            pl.BlockSpec((1, channels), lambda t: (0, 0)),
        ]
        grid, result, out_spec = (tiles,), outcome, hbm
    else:
        places, operands = places[:-1], messages[:-1]
        specs = [vmem] * (len(operands) + 2)
        grid, out_spec = (), vmem
        result = jax.ShapeDtypeStruct((rows_here, residues, channels), jnp.float32)
    deep = here * (len(places) + len(places) % 2)
    total = pl.pallas_call(
        functools.partial(pair_kernel, places, gridded, rows_here, hidden, here, samples),
        out_shape=result,
        grid=grid,
        in_specs=specs,
        out_specs=out_spec,
        scratch_shapes=[
            pltpu.VMEM((rows_here * hidden, deep), jnp.bfloat16),
            pltpu.VMEM((rows_here, hidden * hidden, tile), jnp.bfloat16),
            pltpu.VMEM((rows_here, tile, channels), jnp.bfloat16),
            pltpu.SemaphoreType.DMA((rows_here,)),
        ],
        compiler_params=pltpu.CompilerParams(vmem_limit_bytes=40 * MIB),
    )(*operands, weight, offset)
    if gridded:
        return total
    return pl.pallas_call(
        functools.partial(last_kernel, body, rows_here, hidden, here, samples),
        out_shape=outcome,
        in_specs=[vmem] * 4,
        out_specs=hbm,
        scratch_shapes=[
            pltpu.VMEM((rows_here, tile, channels), jnp.bfloat16),
            pltpu.SemaphoreType.DMA((rows_here // 4,)),
        ],
        compiler_params=pltpu.CompilerParams(vmem_limit_bytes=24 * MIB),
    )(messages[-1], total, mixing, offset)


def solution(mesh):
    return jax.shard_map(
        functools.partial(per_device, mesh.shape["row"]),
        mesh=mesh,
        in_specs=(P(("groups", "row"), None, None), P(), P(), P(), P(), P(), P(), P(), P()),
        out_specs=P(("groups", "row"), None, None),
        check_vma=False,
    )
```

```python
import functools
import math

import jax
import jax.numpy as jnp
from jax import lax
from jax.experimental import pallas as pl
from jax.experimental.pallas import tpu as pltpu
from jax.sharding import PartitionSpec as P

MIB = 1024 * 1024
LANES = 128
CHUNKS = 1
BLOCK = 64


def repeat_rows(values, times):
    rows, cols = values.shape
    return jnp.broadcast_to(values[:, None, :], (rows, times, cols)).reshape(rows * times, cols)


def place_of(device, half):
    chip = device // 2
    return chip // 2 + (chip % 2) * (2 * half - 1 - 2 * (chip // 2))


def chip_at(place, half):
    return jnp.where(place < half, 2 * place, 2 * (2 * half - 1 - place) + 1)


def project_kernel(
    rows_here,
    x_hbm,
    gain_hbm,
    shift_hbm,
    first_hbm,
    first_offset_hbm,
    second_hbm,
    second_offset_hbm,
    final_hbm,
    final_offset_hbm,
    keep_ref,
    give_ref,
    final_ref,
    final_offset_ref,
    x_ref,
    gain_ref,
    shift_ref,
    first_ref,
    first_offset_ref,
    second_ref,
    second_offset_ref,
    packed_ref,
    sems,
):
    samples, residues, features = x_ref.shape
    hidden = first_ref.shape[0]
    width = samples * hidden
    tile = keep_ref.shape[1]
    tiles = residues // tile
    fold = LANES // hidden
    small = [
        (first_hbm, first_ref),
        (second_hbm, second_ref),
        (gain_hbm, gain_ref),
        (shift_hbm, shift_ref),
        (first_offset_hbm, first_offset_ref),
        (second_offset_hbm, second_offset_ref),
    ]
    some = samples // CHUNKS
    copies = [
        pltpu.make_async_copy(src, dst, sems.at[CHUNKS + n]) for n, (src, dst) in enumerate(small)
    ]
    for copy in copies:
        copy.start()
    large = []
    for n in range(CHUNKS):
        rows = pl.ds(n * some, some)
        large.append(pltpu.make_async_copy(x_hbm.at[rows], x_ref.at[rows], sems.at[n]))
        large[-1].start()
    later = [
        pltpu.make_async_copy(final_hbm, final_ref, sems.at[CHUNKS + len(small)]),
        pltpu.make_async_copy(final_offset_hbm, final_offset_ref, sems.at[CHUNKS + len(small) + 1]),
    ]
    for copy in later:
        copy.start()
    for copy in copies:
        copy.wait()

    first = jnp.concatenate([first_ref[...].astype(jnp.float32)] * fold, axis=0).T
    first = first.astype(jnp.bfloat16)
    first_offset = jnp.concatenate([first_offset_ref[...]] * fold, axis=1)
    second = repeat_rows(second_ref[...].astype(jnp.float32), samples).T
    column = lax.broadcasted_iota(jnp.int32, (1, width), 1)
    spot = lax.broadcasted_iota(jnp.int32, (width, hidden), 0)
    channel = lax.broadcasted_iota(jnp.int32, (width, hidden), 1)
    second_offset = jnp.sum(
        jnp.where(spot // samples == channel, second_offset_ref[...], 0.0), axis=1, keepdims=True
    )
    residue = lax.broadcasted_iota(jnp.int32, (tile, LANES), 0)
    lane = lax.broadcasted_iota(jnp.int32, (tile, LANES), 1)
    own = residue % fold == lane // hidden
    group = lax.broadcasted_iota(jnp.int32, (tile // fold, tile), 0)
    member = lax.broadcasted_iota(jnp.int32, (tile // fold, tile), 1)
    gather = (member // fold == group).astype(jnp.bfloat16)

    right = [jnp.zeros((tile, width), jnp.float32) for _ in range(tiles)]
    for s in range(samples):
        if s % some == 0:
            large[s // some].wait()
        normed = []
        for low in range(0, residues, BLOCK):
            values = x_ref[s, low : low + BLOCK, :].astype(jnp.float32)
            center = jnp.mean(values, axis=-1, keepdims=True)
            values = values - center
            variance = jnp.mean(jnp.square(values), axis=-1, keepdims=True)
            values = values * lax.rsqrt(variance + 1e-05) * gain_ref[...] + shift_ref[...]
            normed.append(values.astype(jnp.bfloat16))
        normed = jnp.concatenate(normed, axis=0)
        second_here = jnp.where(column % samples == s, second, 0.0).astype(jnp.bfloat16)
        for t in range(tiles):
            part = normed[t * tile : (t + 1) * tile]
            left = jnp.dot(part, first, preferred_element_type=jnp.float32)
            right[t] += jnp.dot(part, second_here, preferred_element_type=jnp.float32)
            left = jnp.where(own, left + first_offset, 0.0).astype(jnp.bfloat16)
            low = t * (tile // fold) * samples + s
            packed_ref[pl.ds(low, tile // fold, stride=samples), :] = jnp.dot(
                gather, left, preferred_element_type=jnp.float32
            )
    for t in range(tiles):
        value = (right[t].T + second_offset).astype(jnp.bfloat16)
        keep_ref[t * width : (t + 1) * width, :] = value
        give_ref[t * width : (t + 1) * width, :] = value
    for copy in later:
        copy.wait()
    device = lax.axis_index("row")
    per_chip = 2 * rows_here * hidden * samples // tile
    half = residues // rows_here // 4
    base = tiles * width
    way = 2 * (device % 2) - 1
    place = place_of(device, half)
    spots = [(keep_ref, base + n * per_chip, half - n) for n in range(half)]
    spots += [(give_ref, base + n * per_chip, n + 1 - half) for n in range(half)]
    for message, low, ahead in spots:
        chip = chip_at(lax.rem(place + way * ahead + 2 * half, 2 * half), half)
        across = tile // LANES
        start = pl.multiple_of(chip * per_chip * across, per_chip * across)
        block = packed_ref[pl.ds(start, per_chip * across), :]
        block = [block[n : n + samples] for n in range(0, per_chip * across, samples)]
        block = [jnp.concatenate(block[n : n + across], axis=1) for n in range(0, len(block), across)]
        message[low : low + per_chip, :] = jnp.concatenate(block, axis=0).astype(jnp.bfloat16)


def join_kernel(base, per_chip, mine_ref, theirs_ref, next_ref):
    next_ref[:base, :] = theirs_ref[:base, :]
    for n in range((next_ref.shape[0] - base) // (2 * per_chip)):
        low = base + n * per_chip
        at = low + n * per_chip
        next_ref[at : at + per_chip, :] = mine_ref[low + per_chip : low + 2 * per_chip, :]
        next_ref[at + per_chip : at + 2 * per_chip, :] = theirs_ref[low : low + per_chip, :]


def weight_kernel(final_ref, out_ref, wide_ref):
    channels, columns = out_ref.shape
    hidden = math.isqrt(columns)
    wide_ref[...] = final_ref[...].astype(jnp.float32)
    step = LANES // hidden
    for e in range(0, hidden, step):
        rows = [wide_ref[pl.ds(e + n, hidden, stride=hidden), :] for n in range(step)]
        out_ref[:, e * hidden : (e + step) * hidden] = jnp.concatenate(rows, axis=0).T.astype(
            jnp.bfloat16
        )


def pair_kernel(places, gridded, rows_here, hidden, samples, *refs):
    refs = list(refs)
    count = len(places)
    if gridded:
        shards = [(refs.pop(0), 0, refs.pop(0), 0) for _ in places]
    else:
        messages = [refs.pop(0) for _ in places]
        shards = [(messages[n], right, messages[m], left) for n, right, m, left in places]
    weight_ref, offset_ref, out_hbm, left_ref, outer_ref, out_ref, sems = refs
    tile = shards[0][0].shape[1]
    here = samples // count
    span = rows_here * hidden
    deep = span * here // tile
    core = lax.rem(lax.axis_index("row"), 2)
    pieces = []
    for _, _, ref, base in shards:
        start = pl.multiple_of(base + core * deep, deep)
        piece = ref[pl.ds(start, deep), :].astype(jnp.float32)
        pieces.append(
            jnp.concatenate([piece[n * here : (n + 1) * here] for n in range(span // tile)], axis=1)
        )
    left_ref[...] = jnp.concatenate(pieces, axis=0).T.astype(jnp.bfloat16)

    left = left_ref[...]
    for e in range(0, hidden, 2):
        both = [
            ref[base + e * here : base + (e + 2) * here, :].astype(jnp.float32)
            for ref, base, _, _ in shards
        ]
        for k in range(2):
            right = jnp.concatenate([x[k * here : (k + 1) * here] for x in both], axis=0)
            outer = jnp.dot(left, right.astype(jnp.bfloat16), preferred_element_type=jnp.float32)
            outer = outer.astype(jnp.bfloat16)
            for i in range(rows_here):
                outer_ref[i, (e + k) * hidden : (e + k + 1) * hidden, :] = outer[
                    i * hidden : (i + 1) * hidden
                ]

    first = pl.program_id(0) * tile if gridded else 0
    copies = []
    for i in range(rows_here):
        value = jnp.dot(weight_ref[...], outer_ref[i], preferred_element_type=jnp.float32)
        value = value.T * (1.0 / samples) + offset_ref[...]
        out_ref[i] = value.astype(jnp.bfloat16)
        copies.append(
            pltpu.make_async_copy(out_ref.at[i], out_hbm.at[i, pl.ds(first, tile)], sems.at[i])
        )
        copies[-1].start()
    for copy in copies:
        copy.wait()


def per_device(
    size,
    alignment_embedding,
    rescaling_factor,
    recentering_offset,
    first_side_coefficients,
    first_side_offset,
    second_side_coefficients,
    second_side_offset,
    final_projector_coefficients,
    final_projector_offset,
):
    here, residues, features = alignment_embedding.shape
    hidden = first_side_coefficients.shape[1]
    channels = final_projector_coefficients.shape[1]
    width = here * hidden
    samples = here * size
    rows_here = residues // size
    half = size // 4
    tile = 256
    tiles = residues // tile
    body = tiles * width
    per_chip = 2 * rows_here * width // tile

    def rows(count):
        return jax.ShapeDtypeStruct((count, tile), jnp.bfloat16)

    vmem = pl.BlockSpec(memory_space=pltpu.VMEM)
    hbm = pl.BlockSpec(memory_space=pltpu.HBM)
    keep, give, final, offset = pl.pallas_call(
        functools.partial(project_kernel, rows_here),
        out_shape=[rows(body + half * per_chip)] * 2
        + [
            jax.ShapeDtypeStruct(final_projector_coefficients.shape, jnp.bfloat16),
            jax.ShapeDtypeStruct((1, channels), jnp.float32),
        ],
        in_specs=[hbm] * 9,
        out_specs=[vmem] * 4,
        scratch_shapes=[
            pltpu.VMEM((here, residues, features), jnp.bfloat16),
            pltpu.VMEM((1, features), jnp.float32),
            pltpu.VMEM((1, features), jnp.float32),
            pltpu.VMEM((hidden, features), jnp.bfloat16),
            pltpu.VMEM((1, hidden), jnp.float32),
            pltpu.VMEM((hidden, features), jnp.bfloat16),
            pltpu.VMEM((1, hidden), jnp.float32),
            pltpu.VMEM((residues * width // LANES, LANES), jnp.float32),
            pltpu.SemaphoreType.DMA((CHUNKS + 8,)),
        ],
        compiler_params=pltpu.CompilerParams(vmem_limit_bytes=32 * MIB),
        cost_estimate=pl.CostEstimate(
            flops=4 * here * residues * features * width,
            bytes_accessed=2 * here * residues * features,
            transcendentals=0,
        ),
    )(
        *[
            pltpu.with_memory_space_constraint(value, pltpu.HBM)
            for value in (
                alignment_embedding,
                rescaling_factor.reshape(1, features),
                recentering_offset.reshape(1, features),
                first_side_coefficients.T,
                first_side_offset.reshape(1, hidden),
                second_side_coefficients.T,
                second_side_offset.reshape(1, hidden),
                final_projector_coefficients,
                final_projector_offset.reshape(1, channels),
            )
        ]
    )
    by_place = {(place_of(r, half), r % 2): r for r in range(size)}
    around = [
        (r, by_place[(place_of(r, half) + 2 * (r % 2) - 1) % (2 * half), r % 2]) for r in range(size)
    ]

    def swap(value):
        return lax.ppermute(value, "row", [(r, r ^ 1) for r in range(size)])

    weight = pl.pallas_call(
        weight_kernel,
        out_shape=jax.ShapeDtypeStruct((channels, hidden * hidden), jnp.bfloat16),
        in_specs=[vmem],
        out_specs=vmem,
        scratch_shapes=[pltpu.VMEM((hidden * hidden, channels), jnp.float32)],
        compiler_params=pltpu.CompilerParams(vmem_limit_bytes=16 * MIB),
        cost_estimate=pl.CostEstimate(flops=2**28, bytes_accessed=2**20, transcendentals=0),
    )(final)
    theirs, weight = lax.optimization_barrier((swap(give), weight))
    messages = [give, theirs]
    places = [(n, 0, n, body + (half - 1) * per_chip) for n in range(2)]

    def take(*lefts):
        places.extend((len(messages) + n, 0, len(messages) + m, low) for n, (m, low) in enumerate(lefts))

    flying = [keep, theirs[: body + (half - 1) * per_chip]]
    swapped, lefts = [], []
    for step in range(1, half + 1):
        landed = [lax.ppermute(x, "row", around) for x in flying]
        if step >= 3:
            landed[-1], swapped[step - 3] = lax.optimization_barrier((landed[-1], swapped[step - 3]))
        low = [x.shape[0] - per_chip for x in landed]
        if step == 1:
            lefts.append([(0, low[0]), (1, low[1])])
        elif step < half:
            lefts.append([(1, low[1] - per_chip), (1, low[1])])
        else:
            lefts.append([(0, low[0])])
        flying = [landed[0][: body + per_chip]]
        if step == 1:
            flying += pl.pallas_call(
                functools.partial(join_kernel, body, per_chip),
                out_shape=[rows(body + 2 * (half - 2) * per_chip)],
                in_specs=[vmem] * 2,
                out_specs=[vmem],
                compiler_params=pltpu.CompilerParams(vmem_limit_bytes=16 * MIB),
                cost_estimate=pl.CostEstimate(flops=0, bytes_accessed=2**19, transcendentals=0),
            )(*landed)
        elif step < half - 1:
            flying.append(landed[1][: landed[1].shape[0] - 2 * per_chip])
        landed = lax.optimization_barrier(landed)
        take(*lefts[-1])
        messages += landed
        swapped.append([swap(x) for x in landed])
    for pair, left in zip(swapped, lefts):
        take(*left)
        messages += pair

    gridded = tiles > 1
    if gridded:
        operands, specs = [], []
        for n, right, m, left in places:
            operands += [messages[n], messages[m]]
            specs += [
                pl.BlockSpec((width, tile), lambda t, first=right // width: (first + t, 0)),
                pl.BlockSpec((per_chip, tile), lambda t, at=left // per_chip: (at, 0)),
            ]
        specs += [
            pl.BlockSpec((channels, hidden * hidden), lambda t: (0, 0)),
            pl.BlockSpec((1, channels), lambda t: (0, 0)),
        ]
        grid = (tiles,)
    else:
        operands = messages
        specs = [vmem] * (len(messages) + 2)
        grid = ()
    return pl.pallas_call(
        functools.partial(pair_kernel, places, gridded, rows_here, hidden, samples),
        out_shape=jax.ShapeDtypeStruct((rows_here, residues, channels), jnp.bfloat16),
        grid=grid,
        in_specs=specs,
        out_specs=hbm,
        scratch_shapes=[
            pltpu.VMEM((rows_here * hidden, samples), jnp.bfloat16),
            pltpu.VMEM((rows_here, hidden * hidden, tile), jnp.bfloat16),
            pltpu.VMEM((rows_here, tile, channels), jnp.bfloat16),
            pltpu.SemaphoreType.DMA((rows_here,)),
        ],
        compiler_params=pltpu.CompilerParams(vmem_limit_bytes=40 * MIB),
    )(*operands, weight, offset)


def solution(mesh):
    return jax.shard_map(
        functools.partial(per_device, mesh.shape["row"]),
        mesh=mesh,
        in_specs=(P(("groups", "row"), None, None), P(), P(), P(), P(), P(), P(), P(), P()),
        out_specs=P(("groups", "row"), None, None),
        check_vma=False,
    )
```

```python
import functools
import math

import jax
import jax.numpy as jnp
from jax import lax
from jax.experimental import pallas as pl
from jax.experimental.pallas import tpu as pltpu
from jax.sharding import PartitionSpec as P

MIB = 1024 * 1024
LANES = 128
CHUNKS = 1
BLOCK = 64


def repeat_rows(values, times):
    rows, cols = values.shape
    return jnp.broadcast_to(values[:, None, :], (rows, times, cols)).reshape(rows * times, cols)


def place_of(device, half):
    chip = device // 2
    return chip // 2 + (chip % 2) * (2 * half - 1 - 2 * (chip // 2))


def chip_at(place, half):
    return jnp.where(place < half, 2 * place, 2 * (2 * half - 1 - place) + 1)


def project_kernel(
    rows_here,
    x_hbm,
    gain_hbm,
    shift_hbm,
    first_hbm,
    first_offset_hbm,
    second_hbm,
    second_offset_hbm,
    keep_ref,
    give_ref,
    x_ref,
    gain_ref,
    shift_ref,
    first_ref,
    first_offset_ref,
    second_ref,
    second_offset_ref,
    packed_ref,
    sems,
):
    samples, residues, features = x_ref.shape
    hidden = first_ref.shape[0]
    width = samples * hidden
    tile = keep_ref.shape[1]
    tiles = residues // tile
    fold = LANES // hidden
    small = [
        (first_hbm, first_ref),
        (second_hbm, second_ref),
        (gain_hbm, gain_ref),
        (shift_hbm, shift_ref),
        (first_offset_hbm, first_offset_ref),
        (second_offset_hbm, second_offset_ref),
    ]
    some = samples // CHUNKS
    copies = [
        pltpu.make_async_copy(src, dst, sems.at[CHUNKS + n]) for n, (src, dst) in enumerate(small)
    ]
    for copy in copies:
        copy.start()
    large = []
    for n in range(CHUNKS):
        rows = pl.ds(n * some, some)
        large.append(pltpu.make_async_copy(x_hbm.at[rows], x_ref.at[rows], sems.at[n]))
        large[-1].start()
    for copy in copies:
        copy.wait()

    first = jnp.concatenate([first_ref[...].astype(jnp.float32)] * fold, axis=0).T
    first = first.astype(jnp.bfloat16)
    first_offset = jnp.concatenate([first_offset_ref[...]] * fold, axis=1)
    second = repeat_rows(second_ref[...].astype(jnp.float32), samples).T
    column = lax.broadcasted_iota(jnp.int32, (1, width), 1)
    spot = lax.broadcasted_iota(jnp.int32, (width, hidden), 0)
    channel = lax.broadcasted_iota(jnp.int32, (width, hidden), 1)
    second_offset = jnp.sum(
        jnp.where(spot // samples == channel, second_offset_ref[...], 0.0), axis=1, keepdims=True
    )
    residue = lax.broadcasted_iota(jnp.int32, (tile, LANES), 0)
    lane = lax.broadcasted_iota(jnp.int32, (tile, LANES), 1)
    own = residue % fold == lane // hidden
    group = lax.broadcasted_iota(jnp.int32, (tile // fold, tile), 0)
    member = lax.broadcasted_iota(jnp.int32, (tile // fold, tile), 1)
    gather = (member // fold == group).astype(jnp.bfloat16)

    right = [jnp.zeros((tile, width), jnp.float32) for _ in range(tiles)]
    for s in range(samples):
        if s % some == 0:
            large[s // some].wait()
        normed = []
        for low in range(0, residues, BLOCK):
            values = x_ref[s, low : low + BLOCK, :].astype(jnp.float32)
            center = jnp.mean(values, axis=-1, keepdims=True)
            values = values - center
            variance = jnp.mean(jnp.square(values), axis=-1, keepdims=True)
            values = values * lax.rsqrt(variance + 1e-05) * gain_ref[...] + shift_ref[...]
            normed.append(values.astype(jnp.bfloat16))
        normed = jnp.concatenate(normed, axis=0)
        second_here = jnp.where(column % samples == s, second, 0.0).astype(jnp.bfloat16)
        for t in range(tiles):
            part = normed[t * tile : (t + 1) * tile]
            left = jnp.dot(part, first, preferred_element_type=jnp.float32)
            right[t] += jnp.dot(part, second_here, preferred_element_type=jnp.float32)
            left = jnp.where(own, left + first_offset, 0.0).astype(jnp.bfloat16)
            low = t * (tile // fold) * samples + s
            packed_ref[pl.ds(low, tile // fold, stride=samples), :] = jnp.dot(
                gather, left, preferred_element_type=jnp.float32
            )
    for t in range(tiles):
        value = (right[t].T + second_offset).astype(jnp.bfloat16)
        keep_ref[t * width : (t + 1) * width, :] = value
        give_ref[t * width : (t + 1) * width, :] = value
    device = lax.axis_index("row")
    per_chip = 2 * rows_here * hidden * samples // tile
    half = residues // rows_here // 4
    base = tiles * width
    way = 2 * (device % 2) - 1
    place = place_of(device, half)
    spots = [(keep_ref, base + n * per_chip, half - n) for n in range(half)]
    spots += [(give_ref, base + n * per_chip, n + 1 - half) for n in range(half)]
    for message, low, ahead in spots:
        chip = chip_at(lax.rem(place + way * ahead + 2 * half, 2 * half), half)
        across = tile // LANES
        start = pl.multiple_of(chip * per_chip * across, per_chip * across)
        block = packed_ref[pl.ds(start, per_chip * across), :]
        block = [block[n : n + samples] for n in range(0, per_chip * across, samples)]
        block = [jnp.concatenate(block[n : n + across], axis=1) for n in range(0, len(block), across)]
        message[low : low + per_chip, :] = jnp.concatenate(block, axis=0).astype(jnp.bfloat16)


def join_kernel(base, per_chip, mine_ref, theirs_ref, next_ref):
    next_ref[:base, :] = theirs_ref[:base, :]
    for n in range((next_ref.shape[0] - base) // (2 * per_chip)):
        low = base + n * per_chip
        at = low + n * per_chip
        next_ref[at : at + per_chip, :] = mine_ref[low + per_chip : low + 2 * per_chip, :]
        next_ref[at + per_chip : at + 2 * per_chip, :] = theirs_ref[low : low + per_chip, :]


def weight_kernel(final_ref, offset_ref, out_ref, offset_out, wide_ref):
    offset_out[...] = offset_ref[...]
    channels, columns = out_ref.shape
    hidden = math.isqrt(columns)
    wide_ref[: hidden * hidden, :] = final_ref[...].astype(jnp.float32)
    step = LANES // hidden
    for e in range(0, hidden, step):
        rows = [wide_ref[pl.ds(e + n, hidden, stride=hidden), :] for n in range(step)]
        out_ref[:, e * hidden : (e + step) * hidden] = jnp.concatenate(rows, axis=0).T.astype(
            jnp.bfloat16
        )


def pair_kernel(places, gridded, rows_here, hidden, samples, *refs):
    refs = list(refs)
    count = len(places)
    if gridded:
        shards = [(refs.pop(0), 0, refs.pop(0), 0) for _ in places]
    else:
        messages = [refs.pop(0) for _ in places]
        shards = [(messages[n], right, messages[m], left) for n, right, m, left in places]
    weight_ref, offset_ref, out_hbm, left_ref, outer_ref, out_ref, sems = refs
    tile = shards[0][0].shape[1]
    here = samples // count
    span = rows_here * hidden
    deep = span * here // tile
    core = lax.rem(lax.axis_index("row"), 2)
    pieces = []
    for _, _, ref, base in shards:
        start = pl.multiple_of(base + core * deep, deep)
        piece = ref[pl.ds(start, deep), :].astype(jnp.float32)
        pieces.append(
            jnp.concatenate([piece[n * here : (n + 1) * here] for n in range(span // tile)], axis=1)
        )
    left_ref[...] = jnp.concatenate(pieces, axis=0).T.astype(jnp.bfloat16)

    left = left_ref[...]
    for e in range(0, hidden, 2):
        both = [
            ref[base + e * here : base + (e + 2) * here, :].astype(jnp.float32)
            for ref, base, _, _ in shards
        ]
        for k in range(2):
            right = jnp.concatenate([x[k * here : (k + 1) * here] for x in both], axis=0)
            outer = jnp.dot(left, right.astype(jnp.bfloat16), preferred_element_type=jnp.float32)
            outer = outer.astype(jnp.bfloat16)
            for i in range(rows_here):
                outer_ref[i, (e + k) * hidden : (e + k + 1) * hidden, :] = outer[
                    i * hidden : (i + 1) * hidden
                ]

    first = pl.program_id(0) * tile if gridded else 0
    copies = []
    for i in range(rows_here):
        value = jnp.dot(weight_ref[...], outer_ref[i], preferred_element_type=jnp.float32)
        value = value.T * (1.0 / samples) + offset_ref[...]
        out_ref[i] = value.astype(jnp.bfloat16)
        copies.append(
            pltpu.make_async_copy(out_ref.at[i], out_hbm.at[i, pl.ds(first, tile)], sems.at[i])
        )
        copies[-1].start()
    for copy in copies:
        copy.wait()


def per_device(
    size,
    alignment_embedding,
    rescaling_factor,
    recentering_offset,
    first_side_coefficients,
    first_side_offset,
    second_side_coefficients,
    second_side_offset,
    final_projector_coefficients,
    final_projector_offset,
):
    here, residues, features = alignment_embedding.shape
    hidden = first_side_coefficients.shape[1]
    channels = final_projector_coefficients.shape[1]
    width = here * hidden
    samples = here * size
    rows_here = residues // size
    half = size // 4
    tile = 256
    tiles = residues // tile
    body = tiles * width
    per_chip = 2 * rows_here * width // tile

    def rows(count):
        return jax.ShapeDtypeStruct((count, tile), jnp.bfloat16)

    vmem = pl.BlockSpec(memory_space=pltpu.VMEM)
    hbm = pl.BlockSpec(memory_space=pltpu.HBM)
    keep, give = pl.pallas_call(
        functools.partial(project_kernel, rows_here),
        out_shape=[rows(body + half * per_chip)] * 2,
        in_specs=[hbm] * 7,
        out_specs=[vmem] * 2,
        scratch_shapes=[
            pltpu.VMEM((here, residues, features), jnp.bfloat16),
            pltpu.VMEM((1, features), jnp.float32),
            pltpu.VMEM((1, features), jnp.float32),
            pltpu.VMEM((hidden, features), jnp.bfloat16),
            pltpu.VMEM((1, hidden), jnp.float32),
            pltpu.VMEM((hidden, features), jnp.bfloat16),
            pltpu.VMEM((1, hidden), jnp.float32),
            pltpu.VMEM((residues * width // LANES + here, LANES), jnp.float32),
            pltpu.SemaphoreType.DMA((CHUNKS + 6,)),
        ],
        compiler_params=pltpu.CompilerParams(vmem_limit_bytes=32 * MIB),
        cost_estimate=pl.CostEstimate(
            flops=4 * here * residues * features * width,
            bytes_accessed=2 * here * residues * features,
            transcendentals=0,
        ),
    )(
        *[
            pltpu.with_memory_space_constraint(value, pltpu.HBM)
            for value in (
                alignment_embedding,
                rescaling_factor.reshape(1, features),
                recentering_offset.reshape(1, features),
                first_side_coefficients.T,
                first_side_offset.reshape(1, hidden),
                second_side_coefficients.T,
                second_side_offset.reshape(1, hidden),
            )
        ]
    )
    by_place = {(place_of(r, half), r % 2): r for r in range(size)}
    around = [
        (r, by_place[(place_of(r, half) + 2 * (r % 2) - 1) % (2 * half), r % 2]) for r in range(size)
    ]

    def swap(value):
        return lax.ppermute(value, "row", [(r, r ^ 1) for r in range(size)])

    weight, offset = pl.pallas_call(
        weight_kernel,
        out_shape=[
            jax.ShapeDtypeStruct((channels, hidden * hidden), jnp.bfloat16),
            jax.ShapeDtypeStruct((1, channels), jnp.float32),
        ],
        in_specs=[vmem] * 2,
        out_specs=[vmem] * 2,
        scratch_shapes=[pltpu.VMEM(((hidden + 1) * hidden, channels), jnp.float32)],
        compiler_params=pltpu.CompilerParams(vmem_limit_bytes=16 * MIB),
        cost_estimate=pl.CostEstimate(flops=2**28, bytes_accessed=2**20, transcendentals=0),
    )(final_projector_coefficients, final_projector_offset.reshape(1, channels))
    theirs, weight, offset = lax.optimization_barrier((swap(give), weight, offset))
    messages = [give, theirs]
    places = [(n, 0, n, body + (half - 1) * per_chip) for n in range(2)]

    def take(*lefts):
        places.extend((len(messages) + n, 0, len(messages) + m, low) for n, (m, low) in enumerate(lefts))

    flying = [keep, theirs[: body + (half - 1) * per_chip]]
    swapped, lefts = [], []
    for step in range(1, half + 1):
        landed = [lax.ppermute(x, "row", around) for x in flying]
        if step >= 3:
            landed[-1], swapped[step - 3] = lax.optimization_barrier((landed[-1], swapped[step - 3]))
        low = [x.shape[0] - per_chip for x in landed]
        if step == 1:
            lefts.append([(0, low[0]), (1, low[1])])
        elif step < half:
            lefts.append([(1, low[1] - per_chip), (1, low[1])])
        else:
            lefts.append([(0, low[0])])
        flying = [landed[0][: body + per_chip]]
        if step == 1:
            flying += pl.pallas_call(
                functools.partial(join_kernel, body, per_chip),
                out_shape=[rows(body + 2 * (half - 2) * per_chip)],
                in_specs=[vmem] * 2,
                out_specs=[vmem],
                compiler_params=pltpu.CompilerParams(vmem_limit_bytes=16 * MIB),
                cost_estimate=pl.CostEstimate(flops=0, bytes_accessed=2**19, transcendentals=0),
            )(*landed)
        elif step < half - 1:
            flying.append(landed[1][: landed[1].shape[0] - 2 * per_chip])
        landed = lax.optimization_barrier(landed)
        take(*lefts[-1])
        messages += landed
        swapped.append([swap(x) for x in landed])
    for pair, left in zip(swapped, lefts):
        take(*left)
        messages += pair

    gridded = tiles > 1
    if gridded:
        operands, specs = [], []
        for n, right, m, left in places:
            operands += [messages[n], messages[m]]
            specs += [
                pl.BlockSpec((width, tile), lambda t, first=right // width: (first + t, 0)),
                pl.BlockSpec((per_chip, tile), lambda t, at=left // per_chip: (at, 0)),
            ]
        specs += [
            pl.BlockSpec((channels, hidden * hidden), lambda t: (0, 0)),
            pl.BlockSpec((1, channels), lambda t: (0, 0)),
        ]
        grid = (tiles,)
    else:
        operands = messages
        specs = [vmem] * (len(messages) + 2)
        grid = ()
    return pl.pallas_call(
        functools.partial(pair_kernel, places, gridded, rows_here, hidden, samples),
        out_shape=jax.ShapeDtypeStruct((rows_here, residues, channels), jnp.bfloat16),
        grid=grid,
        in_specs=specs,
        out_specs=hbm,
        scratch_shapes=[
            pltpu.VMEM((rows_here * hidden, samples), jnp.bfloat16),
            pltpu.VMEM((rows_here, hidden * hidden, tile), jnp.bfloat16),
            pltpu.VMEM((rows_here, tile, channels), jnp.bfloat16),
            pltpu.SemaphoreType.DMA((rows_here,)),
        ],
        compiler_params=pltpu.CompilerParams(vmem_limit_bytes=40 * MIB),
    )(*operands, weight, offset)


def solution(mesh):
    return jax.shard_map(
        functools.partial(per_device, mesh.shape["row"]),
        mesh=mesh,
        in_specs=(P(("groups", "row"), None, None), P(), P(), P(), P(), P(), P(), P(), P()),
        out_specs=P(("groups", "row"), None, None),
        check_vma=False,
    )
```

```python
import functools
import math

import jax
import jax.numpy as jnp
from jax import lax
from jax.experimental import pallas as pl
from jax.experimental.pallas import tpu as pltpu
from jax.sharding import PartitionSpec as P

MIB = 1024 * 1024
LANES = 128
CHUNKS = 1
BLOCK = 64


def repeat_rows(values, times):
    rows, cols = values.shape
    return jnp.broadcast_to(values[:, None, :], (rows, times, cols)).reshape(rows * times, cols)


def place_of(device, half):
    chip = device // 2
    return chip // 2 + (chip % 2) * (2 * half - 1 - 2 * (chip // 2))


def chip_at(place, half):
    return jnp.where(place < half, 2 * place, 2 * (2 * half - 1 - place) + 1)


def project_kernel(
    rows_here,
    x_hbm,
    gain_hbm,
    shift_hbm,
    first_hbm,
    first_offset_hbm,
    second_hbm,
    second_offset_hbm,
    keep_ref,
    give_ref,
    x_ref,
    gain_ref,
    shift_ref,
    first_ref,
    first_offset_ref,
    second_ref,
    second_offset_ref,
    packed_ref,
    sems,
):
    samples, residues, features = x_ref.shape
    hidden = first_ref.shape[0]
    width = samples * hidden
    tile = keep_ref.shape[1]
    tiles = residues // tile
    fold = LANES // hidden
    small = [
        (first_hbm, first_ref),
        (second_hbm, second_ref),
        (gain_hbm, gain_ref),
        (shift_hbm, shift_ref),
        (first_offset_hbm, first_offset_ref),
        (second_offset_hbm, second_offset_ref),
    ]
    some = samples // CHUNKS
    copies = [
        pltpu.make_async_copy(src, dst, sems.at[CHUNKS + n]) for n, (src, dst) in enumerate(small)
    ]
    for copy in copies:
        copy.start()
    large = []
    for n in range(CHUNKS):
        rows = pl.ds(n * some, some)
        large.append(pltpu.make_async_copy(x_hbm.at[rows], x_ref.at[rows], sems.at[n]))
        large[-1].start()
    for copy in copies:
        copy.wait()

    first = jnp.concatenate([first_ref[...].astype(jnp.float32)] * fold, axis=0).T
    first = first.astype(jnp.bfloat16)
    first_offset = jnp.concatenate([first_offset_ref[...]] * fold, axis=1)
    second = repeat_rows(second_ref[...].astype(jnp.float32), samples).T
    column = lax.broadcasted_iota(jnp.int32, (1, width), 1)
    spot = lax.broadcasted_iota(jnp.int32, (width, hidden), 0)
    channel = lax.broadcasted_iota(jnp.int32, (width, hidden), 1)
    second_offset = jnp.sum(
        jnp.where(spot // samples == channel, second_offset_ref[...], 0.0), axis=1, keepdims=True
    )
    residue = lax.broadcasted_iota(jnp.int32, (tile, LANES), 0)
    lane = lax.broadcasted_iota(jnp.int32, (tile, LANES), 1)
    own = residue % fold == lane // hidden
    group = lax.broadcasted_iota(jnp.int32, (tile // fold, tile), 0)
    member = lax.broadcasted_iota(jnp.int32, (tile // fold, tile), 1)
    gather = (member // fold == group).astype(jnp.bfloat16)

    ones = jnp.ones((features, LANES), jnp.bfloat16)
    right = [jnp.zeros((tile, width), jnp.float32) for _ in range(tiles)]
    for s in range(samples):
        if s % some == 0:
            large[s // some].wait()
        center = jnp.dot(x_ref[s], ones, preferred_element_type=jnp.float32) * (1.0 / features)
        normed = []
        for low in range(0, residues, BLOCK):
            values = x_ref[s, low : low + BLOCK, :].astype(jnp.float32)
            values = values - jnp.concatenate([center[low : low + BLOCK]] * (features // LANES), axis=1)
            variance = jnp.mean(jnp.square(values), axis=-1, keepdims=True)
            values = values * lax.rsqrt(variance + 1e-05) * gain_ref[...] + shift_ref[...]
            normed.append(values.astype(jnp.bfloat16))
        normed = jnp.concatenate(normed, axis=0)
        second_here = jnp.where(column % samples == s, second, 0.0).astype(jnp.bfloat16)
        for t in range(tiles):
            part = normed[t * tile : (t + 1) * tile]
            left = jnp.dot(part, first, preferred_element_type=jnp.float32)
            right[t] += jnp.dot(part, second_here, preferred_element_type=jnp.float32)
            left = jnp.where(own, left + first_offset, 0.0).astype(jnp.bfloat16)
            low = t * (tile // fold) * samples + s
            packed_ref[pl.ds(low, tile // fold, stride=samples), :] = jnp.dot(
                gather, left, preferred_element_type=jnp.float32
            )
    for t in range(tiles):
        value = (right[t].T + second_offset).astype(jnp.bfloat16)
        keep_ref[t * width : (t + 1) * width, :] = value
        give_ref[t * width : (t + 1) * width, :] = value
    device = lax.axis_index("row")
    per_chip = 2 * rows_here * hidden * samples // tile
    half = residues // rows_here // 4
    base = tiles * width
    way = 2 * (device % 2) - 1
    place = place_of(device, half)
    spots = [(keep_ref, base + n * per_chip, half - n) for n in range(half)]
    spots += [(give_ref, base + n * per_chip, n + 1 - half) for n in range(half)]
    for message, low, ahead in spots:
        chip = chip_at(lax.rem(place + way * ahead + 2 * half, 2 * half), half)
        across = tile // LANES
        start = pl.multiple_of(chip * per_chip * across, per_chip * across)
        block = packed_ref[pl.ds(start, per_chip * across), :]
        block = [block[n : n + samples] for n in range(0, per_chip * across, samples)]
        block = [jnp.concatenate(block[n : n + across], axis=1) for n in range(0, len(block), across)]
        message[low : low + per_chip, :] = jnp.concatenate(block, axis=0).astype(jnp.bfloat16)


def join_kernel(base, per_chip, mine_ref, theirs_ref, next_ref):
    next_ref[:base, :] = theirs_ref[:base, :]
    for n in range((next_ref.shape[0] - base) // (2 * per_chip)):
        low = base + n * per_chip
        at = low + n * per_chip
        next_ref[at : at + per_chip, :] = mine_ref[low + per_chip : low + 2 * per_chip, :]
        next_ref[at + per_chip : at + 2 * per_chip, :] = theirs_ref[low : low + per_chip, :]


def weight_kernel(final_ref, offset_ref, out_ref, offset_out, wide_ref):
    offset_out[...] = offset_ref[...]
    channels, columns = out_ref.shape
    hidden = math.isqrt(columns)
    wide_ref[: hidden * hidden, :] = final_ref[...].astype(jnp.float32)
    step = LANES // hidden
    for e in range(0, hidden, step):
        rows = [wide_ref[pl.ds(e + n, hidden, stride=hidden), :] for n in range(step)]
        out_ref[:, e * hidden : (e + step) * hidden] = jnp.concatenate(rows, axis=0).T.astype(
            jnp.bfloat16
        )


def pair_kernel(places, gridded, rows_here, hidden, samples, *refs):
    refs = list(refs)
    count = len(places)
    if gridded:
        shards = [(refs.pop(0), 0, refs.pop(0), 0) for _ in places]
    else:
        messages = [refs.pop(0) for _ in places]
        shards = [(messages[n], right, messages[m], left) for n, right, m, left in places]
    weight_ref, offset_ref, out_hbm, left_ref, outer_ref, out_ref, sems = refs
    tile = shards[0][0].shape[1]
    here = samples // count
    span = rows_here * hidden
    deep = span * here // tile
    core = lax.rem(lax.axis_index("row"), 2)
    pieces = []
    for _, _, ref, base in shards:
        start = pl.multiple_of(base + core * deep, deep)
        piece = ref[pl.ds(start, deep), :].astype(jnp.float32)
        pieces.append(
            jnp.concatenate([piece[n * here : (n + 1) * here] for n in range(span // tile)], axis=1)
        )
    left_ref[...] = jnp.concatenate(pieces, axis=0).T.astype(jnp.bfloat16)

    left = left_ref[...]
    for e in range(0, hidden, 2):
        both = [
            ref[base + e * here : base + (e + 2) * here, :].astype(jnp.float32)
            for ref, base, _, _ in shards
        ]
        for k in range(2):
            right = jnp.concatenate([x[k * here : (k + 1) * here] for x in both], axis=0)
            outer = jnp.dot(left, right.astype(jnp.bfloat16), preferred_element_type=jnp.float32)
            outer = outer.astype(jnp.bfloat16)
            for i in range(rows_here):
                outer_ref[i, (e + k) * hidden : (e + k + 1) * hidden, :] = outer[
                    i * hidden : (i + 1) * hidden
                ]

    first = pl.program_id(0) * tile if gridded else 0
    copies = []
    for i in range(rows_here):
        value = jnp.dot(weight_ref[...], outer_ref[i], preferred_element_type=jnp.float32)
        value = value.T * (1.0 / samples) + offset_ref[...]
        out_ref[i] = value.astype(jnp.bfloat16)
        copies.append(
            pltpu.make_async_copy(out_ref.at[i], out_hbm.at[i, pl.ds(first, tile)], sems.at[i])
        )
        copies[-1].start()
    for copy in copies:
        copy.wait()


def per_device(
    size,
    alignment_embedding,
    rescaling_factor,
    recentering_offset,
    first_side_coefficients,
    first_side_offset,
    second_side_coefficients,
    second_side_offset,
    final_projector_coefficients,
    final_projector_offset,
):
    here, residues, features = alignment_embedding.shape
    hidden = first_side_coefficients.shape[1]
    channels = final_projector_coefficients.shape[1]
    width = here * hidden
    samples = here * size
    rows_here = residues // size
    half = size // 4
    tile = 256
    tiles = residues // tile
    body = tiles * width
    per_chip = 2 * rows_here * width // tile

    def rows(count):
        return jax.ShapeDtypeStruct((count, tile), jnp.bfloat16)

    vmem = pl.BlockSpec(memory_space=pltpu.VMEM)
    hbm = pl.BlockSpec(memory_space=pltpu.HBM)
    keep, give = pl.pallas_call(
        functools.partial(project_kernel, rows_here),
        out_shape=[rows(body + half * per_chip)] * 2,
        in_specs=[hbm] * 7,
        out_specs=[vmem] * 2,
        scratch_shapes=[
            pltpu.VMEM((here, residues, features), jnp.bfloat16),
            pltpu.VMEM((1, features), jnp.float32),
            pltpu.VMEM((1, features), jnp.float32),
            pltpu.VMEM((hidden, features), jnp.bfloat16),
            pltpu.VMEM((1, hidden), jnp.float32),
            pltpu.VMEM((hidden, features), jnp.bfloat16),
            pltpu.VMEM((1, hidden), jnp.float32),
            pltpu.VMEM((residues * width // LANES + here, LANES), jnp.float32),
            pltpu.SemaphoreType.DMA((CHUNKS + 6,)),
        ],
        compiler_params=pltpu.CompilerParams(vmem_limit_bytes=32 * MIB),
        cost_estimate=pl.CostEstimate(
            flops=4 * here * residues * features * width,
            bytes_accessed=2 * here * residues * features,
            transcendentals=0,
        ),
    )(
        *[
            pltpu.with_memory_space_constraint(value, pltpu.HBM)
            for value in (
                alignment_embedding,
                rescaling_factor.reshape(1, features),
                recentering_offset.reshape(1, features),
                first_side_coefficients.T,
                first_side_offset.reshape(1, hidden),
                second_side_coefficients.T,
                second_side_offset.reshape(1, hidden),
            )
        ]
    )
    by_place = {(place_of(r, half), r % 2): r for r in range(size)}
    around = [
        (r, by_place[(place_of(r, half) + 2 * (r % 2) - 1) % (2 * half), r % 2]) for r in range(size)
    ]

    def swap(value):
        return lax.ppermute(value, "row", [(r, r ^ 1) for r in range(size)])

    weight, offset = pl.pallas_call(
        weight_kernel,
        out_shape=[
            jax.ShapeDtypeStruct((channels, hidden * hidden), jnp.bfloat16),
            jax.ShapeDtypeStruct((1, channels), jnp.float32),
        ],
        in_specs=[vmem] * 2,
        out_specs=[vmem] * 2,
        scratch_shapes=[pltpu.VMEM(((hidden + 1) * hidden, channels), jnp.float32)],
        compiler_params=pltpu.CompilerParams(vmem_limit_bytes=16 * MIB),
        cost_estimate=pl.CostEstimate(flops=2**28, bytes_accessed=2**20, transcendentals=0),
    )(final_projector_coefficients, final_projector_offset.reshape(1, channels))
    theirs, weight, offset = lax.optimization_barrier((swap(give), weight, offset))
    messages = [give, theirs]
    places = [(n, 0, n, body + (half - 1) * per_chip) for n in range(2)]

    def take(*lefts):
        places.extend((len(messages) + n, 0, len(messages) + m, low) for n, (m, low) in enumerate(lefts))

    flying = [keep, theirs[: body + (half - 1) * per_chip]]
    swapped, lefts = [], []
    for step in range(1, half + 1):
        landed = [lax.ppermute(x, "row", around) for x in flying]
        if step >= 3:
            landed[-1], swapped[step - 3] = lax.optimization_barrier((landed[-1], swapped[step - 3]))
        low = [x.shape[0] - per_chip for x in landed]
        if step == 1:
            lefts.append([(0, low[0]), (1, low[1])])
        elif step < half:
            lefts.append([(1, low[1] - per_chip), (1, low[1])])
        else:
            lefts.append([(0, low[0])])
        flying = [landed[0][: body + per_chip]]
        if step == 1:
            flying += pl.pallas_call(
                functools.partial(join_kernel, body, per_chip),
                out_shape=[rows(body + 2 * (half - 2) * per_chip)],
                in_specs=[vmem] * 2,
                out_specs=[vmem],
                compiler_params=pltpu.CompilerParams(vmem_limit_bytes=16 * MIB),
                cost_estimate=pl.CostEstimate(flops=0, bytes_accessed=2**19, transcendentals=0),
            )(*landed)
        elif step < half - 1:
            flying.append(landed[1][: landed[1].shape[0] - 2 * per_chip])
        landed = lax.optimization_barrier(landed)
        take(*lefts[-1])
        messages += landed
        swapped.append([swap(x) for x in landed])
    for pair, left in zip(swapped, lefts):
        take(*left)
        messages += pair

    gridded = tiles > 1
    if gridded:
        operands, specs = [], []
        for n, right, m, left in places:
            operands += [messages[n], messages[m]]
            specs += [
                pl.BlockSpec((width, tile), lambda t, first=right // width: (first + t, 0)),
                pl.BlockSpec((per_chip, tile), lambda t, at=left // per_chip: (at, 0)),
            ]
        specs += [
            pl.BlockSpec((channels, hidden * hidden), lambda t: (0, 0)),
            pl.BlockSpec((1, channels), lambda t: (0, 0)),
        ]
        grid = (tiles,)
    else:
        operands = messages
        specs = [vmem] * (len(messages) + 2)
        grid = ()
    return pl.pallas_call(
        functools.partial(pair_kernel, places, gridded, rows_here, hidden, samples),
        out_shape=jax.ShapeDtypeStruct((rows_here, residues, channels), jnp.bfloat16),
        grid=grid,
        in_specs=specs,
        out_specs=hbm,
        scratch_shapes=[
            pltpu.VMEM((rows_here * hidden, samples), jnp.bfloat16),
            pltpu.VMEM((rows_here, hidden * hidden, tile), jnp.bfloat16),
            pltpu.VMEM((rows_here, tile, channels), jnp.bfloat16),
            pltpu.SemaphoreType.DMA((rows_here,)),
        ],
        compiler_params=pltpu.CompilerParams(vmem_limit_bytes=40 * MIB),
    )(*operands, weight, offset)


def solution(mesh):
    return jax.shard_map(
        functools.partial(per_device, mesh.shape["row"]),
        mesh=mesh,
        in_specs=(P(("groups", "row"), None, None), P(), P(), P(), P(), P(), P(), P(), P()),
        out_specs=P(("groups", "row"), None, None),
        check_vma=False,
    )
```

```python
import functools
import math

import jax
import jax.numpy as jnp
from jax import lax
from jax.experimental import pallas as pl
from jax.experimental.pallas import tpu as pltpu
from jax.sharding import PartitionSpec as P

MIB = 1024 * 1024
LANES = 128
CHUNKS = 1
BLOCK = 64


def repeat_rows(values, times):
    rows, cols = values.shape
    return jnp.broadcast_to(values[:, None, :], (rows, times, cols)).reshape(rows * times, cols)


def place_of(device, half):
    chip = device // 2
    return chip // 2 + (chip % 2) * (2 * half - 1 - 2 * (chip // 2))


def chip_at(place, half):
    return jnp.where(place < half, 2 * place, 2 * (2 * half - 1 - place) + 1)


def project_kernel(
    rows_here,
    x_hbm,
    gain_hbm,
    shift_hbm,
    first_hbm,
    first_offset_hbm,
    second_hbm,
    second_offset_hbm,
    keep_ref,
    give_ref,
    x_ref,
    gain_ref,
    shift_ref,
    first_ref,
    first_offset_ref,
    second_ref,
    second_offset_ref,
    packed_ref,
    sems,
):
    samples, residues, features = x_ref.shape
    hidden = first_ref.shape[0]
    width = samples * hidden
    tile = keep_ref.shape[1]
    tiles = residues // tile
    fold = LANES // hidden
    small = [
        (first_hbm, first_ref),
        (second_hbm, second_ref),
        (gain_hbm, gain_ref),
        (shift_hbm, shift_ref),
        (first_offset_hbm, first_offset_ref),
        (second_offset_hbm, second_offset_ref),
    ]
    some = samples // CHUNKS
    copies = [
        pltpu.make_async_copy(src, dst, sems.at[CHUNKS + n]) for n, (src, dst) in enumerate(small)
    ]
    for copy in copies:
        copy.start()
    large = []
    for n in range(CHUNKS):
        rows = pl.ds(n * some, some)
        large.append(pltpu.make_async_copy(x_hbm.at[rows], x_ref.at[rows], sems.at[n]))
        large[-1].start()
    for copy in copies:
        copy.wait()

    first = jnp.concatenate([first_ref[...].astype(jnp.float32)] * fold, axis=0).T
    first = first.astype(jnp.bfloat16)
    first_offset = jnp.concatenate([first_offset_ref[...]] * fold, axis=1)
    second = repeat_rows(second_ref[...].astype(jnp.float32), samples).T
    column = lax.broadcasted_iota(jnp.int32, (1, width), 1)
    spot = lax.broadcasted_iota(jnp.int32, (width, hidden), 0)
    channel = lax.broadcasted_iota(jnp.int32, (width, hidden), 1)
    second_offset = jnp.sum(
        jnp.where(spot // samples == channel, second_offset_ref[...], 0.0), axis=1, keepdims=True
    )
    residue = lax.broadcasted_iota(jnp.int32, (tile, LANES), 0)
    lane = lax.broadcasted_iota(jnp.int32, (tile, LANES), 1)
    own = residue % fold == lane // hidden
    group = lax.broadcasted_iota(jnp.int32, (tile // fold, tile), 0)
    member = lax.broadcasted_iota(jnp.int32, (tile // fold, tile), 1)
    gather = (member // fold == group).astype(jnp.bfloat16)

    right = [jnp.zeros((tile, width), jnp.float32) for _ in range(tiles)]
    for copy in large:
        copy.wait()

    def normalise(s):
        pieces = []
        for low in range(0, residues, BLOCK):
            values = x_ref[s, low : low + BLOCK, :].astype(jnp.float32)
            center = jnp.mean(values, axis=-1, keepdims=True)
            values = values - center
            variance = jnp.mean(jnp.square(values), axis=-1, keepdims=True)
            values = values * lax.rsqrt(variance + 1e-05) * gain_ref[...] + shift_ref[...]
            pieces.append(values.astype(jnp.bfloat16))
        return jnp.concatenate(pieces, axis=0)

    def pack(s, t, left):
        left = jnp.where(own, left + first_offset, 0.0).astype(jnp.bfloat16)
        low = t * (tile // fold) * samples + s
        packed_ref[pl.ds(low, tile // fold, stride=samples), :] = jnp.dot(
            gather, left, preferred_element_type=jnp.float32
        )

    normed, lefts = {}, {}
    for step in range(samples + 2):
        s = step - 1
        if 0 <= s < samples:
            second_here = jnp.where(column % samples == s, second, 0.0).astype(jnp.bfloat16)
            parts = [normed[s][t * tile : (t + 1) * tile] for t in range(tiles)]
            lefts[s] = [jnp.dot(x, first, preferred_element_type=jnp.float32) for x in parts]
            right = [
                total + jnp.dot(x, second_here, preferred_element_type=jnp.float32)
                for total, x in zip(right, parts)
            ]
        if step < samples:
            normed[step] = normalise(step)
        if step >= 2:
            for t in range(tiles):
                pack(step - 2, t, lefts[step - 2][t])
    for t in range(tiles):
        value = (right[t].T + second_offset).astype(jnp.bfloat16)
        keep_ref[t * width : (t + 1) * width, :] = value
        give_ref[t * width : (t + 1) * width, :] = value
    device = lax.axis_index("row")
    per_chip = 2 * rows_here * hidden * samples // tile
    half = residues // rows_here // 4
    base = tiles * width
    way = 2 * (device % 2) - 1
    place = place_of(device, half)
    spots = [(keep_ref, base + n * per_chip, half - n) for n in range(half)]
    spots += [(give_ref, base + n * per_chip, n + 1 - half) for n in range(half)]
    for message, low, ahead in spots:
        chip = chip_at(lax.rem(place + way * ahead + 2 * half, 2 * half), half)
        across = tile // LANES
        start = pl.multiple_of(chip * per_chip * across, per_chip * across)
        block = packed_ref[pl.ds(start, per_chip * across), :]
        block = [block[n : n + samples] for n in range(0, per_chip * across, samples)]
        block = [jnp.concatenate(block[n : n + across], axis=1) for n in range(0, len(block), across)]
        message[low : low + per_chip, :] = jnp.concatenate(block, axis=0).astype(jnp.bfloat16)


def join_kernel(base, per_chip, mine_ref, theirs_ref, next_ref):
    next_ref[:base, :] = theirs_ref[:base, :]
    for n in range((next_ref.shape[0] - base) // (2 * per_chip)):
        low = base + n * per_chip
        at = low + n * per_chip
        next_ref[at : at + per_chip, :] = mine_ref[low + per_chip : low + 2 * per_chip, :]
        next_ref[at + per_chip : at + 2 * per_chip, :] = theirs_ref[low : low + per_chip, :]


def weight_kernel(final_ref, offset_ref, out_ref, offset_out, wide_ref):
    offset_out[...] = offset_ref[...]
    channels, columns = out_ref.shape
    hidden = math.isqrt(columns)
    wide_ref[: hidden * hidden, :] = final_ref[...].astype(jnp.float32)
    step = LANES // hidden
    for e in range(0, hidden, step):
        rows = [wide_ref[pl.ds(e + n, hidden, stride=hidden), :] for n in range(step)]
        out_ref[:, e * hidden : (e + step) * hidden] = jnp.concatenate(rows, axis=0).T.astype(
            jnp.bfloat16
        )


def pair_kernel(places, gridded, rows_here, hidden, samples, *refs):
    refs = list(refs)
    count = len(places)
    if gridded:
        shards = [(refs.pop(0), 0, refs.pop(0), 0) for _ in places]
    else:
        messages = [refs.pop(0) for _ in places]
        shards = [(messages[n], right, messages[m], left) for n, right, m, left in places]
    weight_ref, offset_ref, out_hbm, left_ref, outer_ref, out_ref, sems = refs
    tile = shards[0][0].shape[1]
    here = samples // count
    span = rows_here * hidden
    deep = span * here // tile
    core = lax.rem(lax.axis_index("row"), 2)
    pieces = []
    for _, _, ref, base in shards:
        start = pl.multiple_of(base + core * deep, deep)
        piece = ref[pl.ds(start, deep), :].astype(jnp.float32)
        pieces.append(
            jnp.concatenate([piece[n * here : (n + 1) * here] for n in range(span // tile)], axis=1)
        )
    left_ref[...] = jnp.concatenate(pieces, axis=0).T.astype(jnp.bfloat16)

    left = left_ref[...]
    for e in range(0, hidden, 2):
        both = [
            ref[base + e * here : base + (e + 2) * here, :].astype(jnp.float32)
            for ref, base, _, _ in shards
        ]
        for k in range(2):
            right = jnp.concatenate([x[k * here : (k + 1) * here] for x in both], axis=0)
            outer = jnp.dot(left, right.astype(jnp.bfloat16), preferred_element_type=jnp.float32)
            outer = outer.astype(jnp.bfloat16)
            for i in range(rows_here):
                outer_ref[i, (e + k) * hidden : (e + k + 1) * hidden, :] = outer[
                    i * hidden : (i + 1) * hidden
                ]

    first = pl.program_id(0) * tile if gridded else 0
    copies = []
    for i in range(rows_here):
        value = jnp.dot(weight_ref[...], outer_ref[i], preferred_element_type=jnp.float32)
        value = value.T * (1.0 / samples) + offset_ref[...]
        out_ref[i] = value.astype(jnp.bfloat16)
        copies.append(
            pltpu.make_async_copy(out_ref.at[i], out_hbm.at[i, pl.ds(first, tile)], sems.at[i])
        )
        copies[-1].start()
    for copy in copies:
        copy.wait()


def per_device(
    size,
    alignment_embedding,
    rescaling_factor,
    recentering_offset,
    first_side_coefficients,
    first_side_offset,
    second_side_coefficients,
    second_side_offset,
    final_projector_coefficients,
    final_projector_offset,
):
    here, residues, features = alignment_embedding.shape
    hidden = first_side_coefficients.shape[1]
    channels = final_projector_coefficients.shape[1]
    width = here * hidden
    samples = here * size
    rows_here = residues // size
    half = size // 4
    tile = 256
    tiles = residues // tile
    body = tiles * width
    per_chip = 2 * rows_here * width // tile

    def rows(count):
        return jax.ShapeDtypeStruct((count, tile), jnp.bfloat16)

    vmem = pl.BlockSpec(memory_space=pltpu.VMEM)
    hbm = pl.BlockSpec(memory_space=pltpu.HBM)
    keep, give = pl.pallas_call(
        functools.partial(project_kernel, rows_here),
        out_shape=[rows(body + half * per_chip)] * 2,
        in_specs=[hbm] * 7,
        out_specs=[vmem] * 2,
        scratch_shapes=[
            pltpu.VMEM((here, residues, features), jnp.bfloat16),
            pltpu.VMEM((1, features), jnp.float32),
            pltpu.VMEM((1, features), jnp.float32),
            pltpu.VMEM((hidden, features), jnp.bfloat16),
            pltpu.VMEM((1, hidden), jnp.float32),
            pltpu.VMEM((hidden, features), jnp.bfloat16),
            pltpu.VMEM((1, hidden), jnp.float32),
            pltpu.VMEM((residues * width // LANES + here, LANES), jnp.float32),
            pltpu.SemaphoreType.DMA((CHUNKS + 6,)),
        ],
        compiler_params=pltpu.CompilerParams(vmem_limit_bytes=32 * MIB),
        cost_estimate=pl.CostEstimate(
            flops=4 * here * residues * features * width,
            bytes_accessed=2 * here * residues * features,
            transcendentals=0,
        ),
    )(
        *[
            pltpu.with_memory_space_constraint(value, pltpu.HBM)
            for value in (
                alignment_embedding,
                rescaling_factor.reshape(1, features),
                recentering_offset.reshape(1, features),
                first_side_coefficients.T,
                first_side_offset.reshape(1, hidden),
                second_side_coefficients.T,
                second_side_offset.reshape(1, hidden),
            )
        ]
    )
    by_place = {(place_of(r, half), r % 2): r for r in range(size)}
    around = [
        (r, by_place[(place_of(r, half) + 2 * (r % 2) - 1) % (2 * half), r % 2]) for r in range(size)
    ]

    def swap(value):
        return lax.ppermute(value, "row", [(r, r ^ 1) for r in range(size)])

    weight, offset = pl.pallas_call(
        weight_kernel,
        out_shape=[
            jax.ShapeDtypeStruct((channels, hidden * hidden), jnp.bfloat16),
            jax.ShapeDtypeStruct((1, channels), jnp.float32),
        ],
        in_specs=[vmem] * 2,
        out_specs=[vmem] * 2,
        scratch_shapes=[pltpu.VMEM(((hidden + 1) * hidden, channels), jnp.float32)],
        compiler_params=pltpu.CompilerParams(vmem_limit_bytes=16 * MIB),
        cost_estimate=pl.CostEstimate(flops=2**28, bytes_accessed=2**20, transcendentals=0),
    )(final_projector_coefficients, final_projector_offset.reshape(1, channels))
    theirs, weight, offset = lax.optimization_barrier((swap(give), weight, offset))
    messages = [give, theirs]
    places = [(n, 0, n, body + (half - 1) * per_chip) for n in range(2)]

    def take(*lefts):
        places.extend((len(messages) + n, 0, len(messages) + m, low) for n, (m, low) in enumerate(lefts))

    flying = [keep, theirs[: body + (half - 1) * per_chip]]
    swapped, lefts = [], []
    for step in range(1, half + 1):
        landed = [lax.ppermute(x, "row", around) for x in flying]
        if step >= 3:
            landed[-1], swapped[step - 3] = lax.optimization_barrier((landed[-1], swapped[step - 3]))
        low = [x.shape[0] - per_chip for x in landed]
        if step == 1:
            lefts.append([(0, low[0]), (1, low[1])])
        elif step < half:
            lefts.append([(1, low[1] - per_chip), (1, low[1])])
        else:
            lefts.append([(0, low[0])])
        flying = [landed[0][: body + per_chip]]
        if step == 1:
            flying += pl.pallas_call(
                functools.partial(join_kernel, body, per_chip),
                out_shape=[rows(body + 2 * (half - 2) * per_chip)],
                in_specs=[vmem] * 2,
                out_specs=[vmem],
                compiler_params=pltpu.CompilerParams(vmem_limit_bytes=16 * MIB),
                cost_estimate=pl.CostEstimate(flops=0, bytes_accessed=2**19, transcendentals=0),
            )(*landed)
        elif step < half - 1:
            flying.append(landed[1][: landed[1].shape[0] - 2 * per_chip])
        landed = lax.optimization_barrier(landed)
        take(*lefts[-1])
        messages += landed
        swapped.append([swap(x) for x in landed])
    for pair, left in zip(swapped, lefts):
        take(*left)
        messages += pair

    gridded = tiles > 1
    if gridded:
        operands, specs = [], []
        for n, right, m, left in places:
            operands += [messages[n], messages[m]]
            specs += [
                pl.BlockSpec((width, tile), lambda t, first=right // width: (first + t, 0)),
                pl.BlockSpec((per_chip, tile), lambda t, at=left // per_chip: (at, 0)),
            ]
        specs += [
            pl.BlockSpec((channels, hidden * hidden), lambda t: (0, 0)),
            pl.BlockSpec((1, channels), lambda t: (0, 0)),
        ]
        grid = (tiles,)
    else:
        operands = messages
        specs = [vmem] * (len(messages) + 2)
        grid = ()
    return pl.pallas_call(
        functools.partial(pair_kernel, places, gridded, rows_here, hidden, samples),
        out_shape=jax.ShapeDtypeStruct((rows_here, residues, channels), jnp.bfloat16),
        grid=grid,
        in_specs=specs,
        out_specs=hbm,
        scratch_shapes=[
            pltpu.VMEM((rows_here * hidden, samples), jnp.bfloat16),
            pltpu.VMEM((rows_here, hidden * hidden, tile), jnp.bfloat16),
            pltpu.VMEM((rows_here, tile, channels), jnp.bfloat16),
            pltpu.SemaphoreType.DMA((rows_here,)),
        ],
        compiler_params=pltpu.CompilerParams(vmem_limit_bytes=40 * MIB),
    )(*operands, weight, offset)


def solution(mesh):
    return jax.shard_map(
        functools.partial(per_device, mesh.shape["row"]),
        mesh=mesh,
        in_specs=(P(("groups", "row"), None, None), P(), P(), P(), P(), P(), P(), P(), P()),
        out_specs=P(("groups", "row"), None, None),
        check_vma=False,
    )
```

```python
import functools
import math

import jax
import jax.numpy as jnp
from jax import lax
from jax.experimental import pallas as pl
from jax.experimental.pallas import tpu as pltpu
from jax.sharding import PartitionSpec as P

MIB = 1024 * 1024
LANES = 128
CHUNKS = 1
BLOCK = 64


def repeat_rows(values, times):
    rows, cols = values.shape
    return jnp.broadcast_to(values[:, None, :], (rows, times, cols)).reshape(rows * times, cols)


def place_of(device, half):
    chip = device // 2
    return chip // 2 + (chip % 2) * (2 * half - 1 - 2 * (chip // 2))


def chip_at(place, half):
    return jnp.where(place < half, 2 * place, 2 * (2 * half - 1 - place) + 1)


def project_kernel(
    rows_here,
    x_hbm,
    gain_hbm,
    shift_hbm,
    first_hbm,
    first_offset_hbm,
    second_hbm,
    second_offset_hbm,
    keep_ref,
    give_ref,
    x_ref,
    gain_ref,
    shift_ref,
    first_ref,
    first_offset_ref,
    second_ref,
    second_offset_ref,
    packed_ref,
    placed_ref,
    sems,
):
    samples, residues, features = x_ref.shape
    hidden = first_ref.shape[0]
    width = samples * hidden
    tile = keep_ref.shape[1]
    tiles = residues // tile
    fold = LANES // hidden
    small = [
        (first_hbm, first_ref),
        (second_hbm, second_ref),
        (gain_hbm, gain_ref),
        (shift_hbm, shift_ref),
        (first_offset_hbm, first_offset_ref),
        (second_offset_hbm, second_offset_ref),
    ]
    some = samples // CHUNKS
    copies = [
        pltpu.make_async_copy(src, dst, sems.at[CHUNKS + n]) for n, (src, dst) in enumerate(small)
    ]
    for copy in copies:
        copy.start()
    large = []
    for n in range(CHUNKS):
        rows = pl.ds(n * some, some)
        large.append(pltpu.make_async_copy(x_hbm.at[rows], x_ref.at[rows], sems.at[n]))
        large[-1].start()
    for copy in copies:
        copy.wait()

    first = jnp.concatenate([first_ref[...].astype(jnp.float32)] * fold, axis=0).T
    first = first.astype(jnp.bfloat16)
    first_offset = jnp.concatenate([first_offset_ref[...]] * fold, axis=1)
    second = repeat_rows(second_ref[...].astype(jnp.float32), samples).T
    column = lax.broadcasted_iota(jnp.int32, (1, width), 1)
    spot = lax.broadcasted_iota(jnp.int32, (width, hidden), 0)
    channel = lax.broadcasted_iota(jnp.int32, (width, hidden), 1)
    second_offset = jnp.sum(
        jnp.where(spot // samples == channel, second_offset_ref[...], 0.0), axis=1, keepdims=True
    )
    residue = lax.broadcasted_iota(jnp.int32, (tile, LANES), 0)
    lane = lax.broadcasted_iota(jnp.int32, (tile, LANES), 1)
    own = residue % fold == lane // hidden
    group = lax.broadcasted_iota(jnp.int32, (tile // fold, tile), 0)
    member = lax.broadcasted_iota(jnp.int32, (tile // fold, tile), 1)
    gather = (member // fold == group).astype(jnp.bfloat16)

    right = [jnp.zeros((tile, width), jnp.float32) for _ in range(tiles)]
    for s in range(samples):
        placed_ref[s * features : (s + 1) * features, :] = jnp.where(
            column % samples == s, second, 0.0
        ).astype(jnp.bfloat16)
    for copy in large:
        copy.wait()

    def normalise(s):
        pieces = []
        for low in range(0, residues, BLOCK):
            values = x_ref[s, low : low + BLOCK, :].astype(jnp.float32)
            center = jnp.mean(values, axis=-1, keepdims=True)
            values = values - center
            variance = jnp.mean(jnp.square(values), axis=-1, keepdims=True)
            values = values * lax.rsqrt(variance + 1e-05) * gain_ref[...] + shift_ref[...]
            pieces.append(values.astype(jnp.bfloat16))
        return jnp.concatenate(pieces, axis=0)

    def pack(s, t, left):
        left = jnp.where(own, left + first_offset, 0.0).astype(jnp.bfloat16)
        low = t * (tile // fold) * samples + s
        packed_ref[pl.ds(low, tile // fold, stride=samples), :] = jnp.dot(
            gather, left, preferred_element_type=jnp.float32
        )

    normed, lefts = {}, {}
    for step in range(samples + 2):
        s = step - 1
        if 0 <= s < samples:
            second_here = placed_ref[s * features : (s + 1) * features, :]
            parts = [normed[s][t * tile : (t + 1) * tile] for t in range(tiles)]
            lefts[s] = [jnp.dot(x, first, preferred_element_type=jnp.float32) for x in parts]
            right = [
                total + jnp.dot(x, second_here, preferred_element_type=jnp.float32)
                for total, x in zip(right, parts)
            ]
        if step < samples:
            normed[step] = normalise(step)
        if step >= 2:
            for t in range(tiles):
                pack(step - 2, t, lefts[step - 2][t])
    for t in range(tiles):
        value = (right[t].T + second_offset).astype(jnp.bfloat16)
        keep_ref[t * width : (t + 1) * width, :] = value
        give_ref[t * width : (t + 1) * width, :] = value
    device = lax.axis_index("row")
    per_chip = 2 * rows_here * hidden * samples // tile
    half = residues // rows_here // 4
    base = tiles * width
    way = 2 * (device % 2) - 1
    place = place_of(device, half)
    spots = [(keep_ref, base + n * per_chip, half - n) for n in range(half)]
    spots += [(give_ref, base + n * per_chip, n + 1 - half) for n in range(half)]
    for message, low, ahead in spots:
        chip = chip_at(lax.rem(place + way * ahead + 2 * half, 2 * half), half)
        across = tile // LANES
        start = pl.multiple_of(chip * per_chip * across, per_chip * across)
        block = packed_ref[pl.ds(start, per_chip * across), :]
        block = [block[n : n + samples] for n in range(0, per_chip * across, samples)]
        block = [jnp.concatenate(block[n : n + across], axis=1) for n in range(0, len(block), across)]
        message[low : low + per_chip, :] = jnp.concatenate(block, axis=0).astype(jnp.bfloat16)


def join_kernel(base, per_chip, mine_ref, theirs_ref, next_ref):
    next_ref[:base, :] = theirs_ref[:base, :]
    for n in range((next_ref.shape[0] - base) // (2 * per_chip)):
        low = base + n * per_chip
        at = low + n * per_chip
        next_ref[at : at + per_chip, :] = mine_ref[low + per_chip : low + 2 * per_chip, :]
        next_ref[at + per_chip : at + 2 * per_chip, :] = theirs_ref[low : low + per_chip, :]


def weight_kernel(final_ref, offset_ref, out_ref, offset_out, wide_ref):
    offset_out[...] = offset_ref[...]
    channels, columns = out_ref.shape
    hidden = math.isqrt(columns)
    wide_ref[: hidden * hidden, :] = final_ref[...].astype(jnp.float32)
    step = LANES // hidden
    for e in range(0, hidden, step):
        rows = [wide_ref[pl.ds(e + n, hidden, stride=hidden), :] for n in range(step)]
        out_ref[:, e * hidden : (e + step) * hidden] = jnp.concatenate(rows, axis=0).T.astype(
            jnp.bfloat16
        )


def pair_kernel(places, gridded, rows_here, hidden, samples, *refs):
    refs = list(refs)
    count = len(places)
    if gridded:
        shards = [(refs.pop(0), 0, refs.pop(0), 0) for _ in places]
    else:
        messages = [refs.pop(0) for _ in places]
        shards = [(messages[n], right, messages[m], left) for n, right, m, left in places]
    weight_ref, offset_ref, out_hbm, left_ref, outer_ref, out_ref, sems = refs
    tile = shards[0][0].shape[1]
    here = samples // count
    span = rows_here * hidden
    deep = span * here // tile
    core = lax.rem(lax.axis_index("row"), 2)
    pieces = []
    for _, _, ref, base in shards:
        start = pl.multiple_of(base + core * deep, deep)
        piece = ref[pl.ds(start, deep), :].astype(jnp.float32)
        pieces.append(
            jnp.concatenate([piece[n * here : (n + 1) * here] for n in range(span // tile)], axis=1)
        )
    left_ref[...] = jnp.concatenate(pieces, axis=0).T.astype(jnp.bfloat16)

    left = left_ref[...]
    for e in range(0, hidden, 2):
        both = [
            ref[base + e * here : base + (e + 2) * here, :].astype(jnp.float32)
            for ref, base, _, _ in shards
        ]
        for k in range(2):
            right = jnp.concatenate([x[k * here : (k + 1) * here] for x in both], axis=0)
            outer = jnp.dot(left, right.astype(jnp.bfloat16), preferred_element_type=jnp.float32)
            outer = outer.astype(jnp.bfloat16)
            for i in range(rows_here):
                outer_ref[i, (e + k) * hidden : (e + k + 1) * hidden, :] = outer[
                    i * hidden : (i + 1) * hidden
                ]

    first = pl.program_id(0) * tile if gridded else 0
    copies = []
    for i in range(rows_here):
        value = jnp.dot(weight_ref[...], outer_ref[i], preferred_element_type=jnp.float32)
        value = value.T * (1.0 / samples) + offset_ref[...]
        out_ref[i] = value.astype(jnp.bfloat16)
        copies.append(
            pltpu.make_async_copy(out_ref.at[i], out_hbm.at[i, pl.ds(first, tile)], sems.at[i])
        )
        copies[-1].start()
    for copy in copies:
        copy.wait()


def per_device(
    size,
    alignment_embedding,
    rescaling_factor,
    recentering_offset,
    first_side_coefficients,
    first_side_offset,
    second_side_coefficients,
    second_side_offset,
    final_projector_coefficients,
    final_projector_offset,
):
    here, residues, features = alignment_embedding.shape
    hidden = first_side_coefficients.shape[1]
    channels = final_projector_coefficients.shape[1]
    width = here * hidden
    samples = here * size
    rows_here = residues // size
    half = size // 4
    tile = 256
    tiles = residues // tile
    body = tiles * width
    per_chip = 2 * rows_here * width // tile

    def rows(count):
        return jax.ShapeDtypeStruct((count, tile), jnp.bfloat16)

    vmem = pl.BlockSpec(memory_space=pltpu.VMEM)
    hbm = pl.BlockSpec(memory_space=pltpu.HBM)
    keep, give = pl.pallas_call(
        functools.partial(project_kernel, rows_here),
        out_shape=[rows(body + half * per_chip)] * 2,
        in_specs=[hbm] * 7,
        out_specs=[vmem] * 2,
        scratch_shapes=[
            pltpu.VMEM((here, residues, features), jnp.bfloat16),
            pltpu.VMEM((1, features), jnp.float32),
            pltpu.VMEM((1, features), jnp.float32),
            pltpu.VMEM((hidden, features), jnp.bfloat16),
            pltpu.VMEM((1, hidden), jnp.float32),
            pltpu.VMEM((hidden, features), jnp.bfloat16),
            pltpu.VMEM((1, hidden), jnp.float32),
            pltpu.VMEM((residues * width // LANES + here, LANES), jnp.float32),
            pltpu.VMEM((here * features, width), jnp.bfloat16),
            pltpu.SemaphoreType.DMA((CHUNKS + 6,)),
        ],
        compiler_params=pltpu.CompilerParams(vmem_limit_bytes=32 * MIB),
        cost_estimate=pl.CostEstimate(
            flops=4 * here * residues * features * width,
            bytes_accessed=2 * here * residues * features,
            transcendentals=0,
        ),
    )(
        *[
            pltpu.with_memory_space_constraint(value, pltpu.HBM)
            for value in (
                alignment_embedding,
                rescaling_factor.reshape(1, features),
                recentering_offset.reshape(1, features),
                first_side_coefficients.T,
                first_side_offset.reshape(1, hidden),
                second_side_coefficients.T,
                second_side_offset.reshape(1, hidden),
            )
        ]
    )
    by_place = {(place_of(r, half), r % 2): r for r in range(size)}
    around = [
        (r, by_place[(place_of(r, half) + 2 * (r % 2) - 1) % (2 * half), r % 2]) for r in range(size)
    ]

    def swap(value):
        return lax.ppermute(value, "row", [(r, r ^ 1) for r in range(size)])

    weight, offset = pl.pallas_call(
        weight_kernel,
        out_shape=[
            jax.ShapeDtypeStruct((channels, hidden * hidden), jnp.bfloat16),
            jax.ShapeDtypeStruct((1, channels), jnp.float32),
        ],
        in_specs=[vmem] * 2,
        out_specs=[vmem] * 2,
        scratch_shapes=[pltpu.VMEM(((hidden + 1) * hidden, channels), jnp.float32)],
        compiler_params=pltpu.CompilerParams(vmem_limit_bytes=16 * MIB),
        cost_estimate=pl.CostEstimate(flops=2**28, bytes_accessed=2**20, transcendentals=0),
    )(final_projector_coefficients, final_projector_offset.reshape(1, channels))
    theirs, weight, offset = lax.optimization_barrier((swap(give), weight, offset))
    messages = [give, theirs]
    places = [(n, 0, n, body + (half - 1) * per_chip) for n in range(2)]

    def take(*lefts):
        places.extend((len(messages) + n, 0, len(messages) + m, low) for n, (m, low) in enumerate(lefts))

    flying = [keep, theirs[: body + (half - 1) * per_chip]]
    swapped, lefts = [], []
    for step in range(1, half + 1):
        landed = [lax.ppermute(x, "row", around) for x in flying]
        if step >= 3:
            landed[-1], swapped[step - 3] = lax.optimization_barrier((landed[-1], swapped[step - 3]))
        low = [x.shape[0] - per_chip for x in landed]
        if step == 1:
            lefts.append([(0, low[0]), (1, low[1])])
        elif step < half:
            lefts.append([(1, low[1] - per_chip), (1, low[1])])
        else:
            lefts.append([(0, low[0])])
        flying = [landed[0][: body + per_chip]]
        if step == 1:
            flying += pl.pallas_call(
                functools.partial(join_kernel, body, per_chip),
                out_shape=[rows(body + 2 * (half - 2) * per_chip)],
                in_specs=[vmem] * 2,
                out_specs=[vmem],
                compiler_params=pltpu.CompilerParams(vmem_limit_bytes=16 * MIB),
                cost_estimate=pl.CostEstimate(flops=0, bytes_accessed=2**19, transcendentals=0),
            )(*landed)
        elif step < half - 1:
            flying.append(landed[1][: landed[1].shape[0] - 2 * per_chip])
        landed = lax.optimization_barrier(landed)
        take(*lefts[-1])
        messages += landed
        swapped.append([swap(x) for x in landed])
    for pair, left in zip(swapped, lefts):
        take(*left)
        messages += pair

    gridded = tiles > 1
    if gridded:
        operands, specs = [], []
        for n, right, m, left in places:
            operands += [messages[n], messages[m]]
            specs += [
                pl.BlockSpec((width, tile), lambda t, first=right // width: (first + t, 0)),
                pl.BlockSpec((per_chip, tile), lambda t, at=left // per_chip: (at, 0)),
            ]
        specs += [
            pl.BlockSpec((channels, hidden * hidden), lambda t: (0, 0)),
            pl.BlockSpec((1, channels), lambda t: (0, 0)),
        ]
        grid = (tiles,)
    else:
        operands = messages
        specs = [vmem] * (len(messages) + 2)
        grid = ()
    return pl.pallas_call(
        functools.partial(pair_kernel, places, gridded, rows_here, hidden, samples),
        out_shape=jax.ShapeDtypeStruct((rows_here, residues, channels), jnp.bfloat16),
        grid=grid,
        in_specs=specs,
        out_specs=hbm,
        scratch_shapes=[
            pltpu.VMEM((rows_here * hidden, samples), jnp.bfloat16),
            pltpu.VMEM((rows_here, hidden * hidden, tile), jnp.bfloat16),
            pltpu.VMEM((rows_here, tile, channels), jnp.bfloat16),
            pltpu.SemaphoreType.DMA((rows_here,)),
        ],
        compiler_params=pltpu.CompilerParams(vmem_limit_bytes=40 * MIB),
    )(*operands, weight, offset)


def solution(mesh):
    return jax.shard_map(
        functools.partial(per_device, mesh.shape["row"]),
        mesh=mesh,
        in_specs=(P(("groups", "row"), None, None), P(), P(), P(), P(), P(), P(), P(), P()),
        out_specs=P(("groups", "row"), None, None),
        check_vma=False,
    )
```

```python
import functools
import math

import jax
import jax.numpy as jnp
from jax import lax
from jax.experimental import pallas as pl
from jax.experimental.pallas import tpu as pltpu
from jax.sharding import PartitionSpec as P

MIB = 1024 * 1024
LANES = 128
CHUNKS = 1
BLOCK = 64


def repeat_rows(values, times):
    rows, cols = values.shape
    return jnp.broadcast_to(values[:, None, :], (rows, times, cols)).reshape(rows * times, cols)


def place_of(device, half):
    chip = device // 2
    return chip // 2 + (chip % 2) * (2 * half - 1 - 2 * (chip // 2))


def chip_at(place, half):
    return jnp.where(place < half, 2 * place, 2 * (2 * half - 1 - place) + 1)


def project_kernel(
    rows_here,
    x_hbm,
    gain_hbm,
    shift_hbm,
    first_hbm,
    first_offset_hbm,
    second_hbm,
    second_offset_hbm,
    keep_ref,
    give_ref,
    x_ref,
    gain_ref,
    shift_ref,
    first_ref,
    first_offset_ref,
    second_ref,
    second_offset_ref,
    packed_ref,
    placed_ref,
    sems,
):
    samples, residues, features = x_ref.shape
    hidden = first_ref.shape[0]
    width = samples * hidden
    tile = keep_ref.shape[1]
    tiles = residues // tile
    fold = LANES // hidden
    small = [
        (first_hbm, first_ref),
        (second_hbm, second_ref),
        (gain_hbm, gain_ref),
        (shift_hbm, shift_ref),
        (first_offset_hbm, first_offset_ref),
        (second_offset_hbm, second_offset_ref),
    ]
    some = samples // CHUNKS
    copies = [
        pltpu.make_async_copy(src, dst, sems.at[CHUNKS + n]) for n, (src, dst) in enumerate(small)
    ]
    for copy in copies:
        copy.start()
    large = []
    for n in range(CHUNKS):
        rows = pl.ds(n * some, some)
        large.append(pltpu.make_async_copy(x_hbm.at[rows], x_ref.at[rows], sems.at[n]))
        large[-1].start()
    for copy in copies:
        copy.wait()

    first = jnp.concatenate([first_ref[...].astype(jnp.float32)] * fold, axis=0).T
    first = first.astype(jnp.bfloat16)
    first_offset = jnp.concatenate([first_offset_ref[...]] * fold, axis=1)
    second = repeat_rows(second_ref[...].astype(jnp.float32), samples).T
    column = lax.broadcasted_iota(jnp.int32, (1, width), 1)
    spot = lax.broadcasted_iota(jnp.int32, (width, hidden), 0)
    channel = lax.broadcasted_iota(jnp.int32, (width, hidden), 1)
    second_offset = jnp.sum(
        jnp.where(spot // samples == channel, second_offset_ref[...], 0.0), axis=1, keepdims=True
    )
    residue = lax.broadcasted_iota(jnp.int32, (tile, LANES), 0)
    lane = lax.broadcasted_iota(jnp.int32, (tile, LANES), 1)
    own = residue % fold == lane // hidden
    group = lax.broadcasted_iota(jnp.int32, (tile // fold, tile), 0)
    member = lax.broadcasted_iota(jnp.int32, (tile // fold, tile), 1)
    gather = (member // fold == group).astype(jnp.bfloat16)

    right = [jnp.zeros((tile, width), jnp.float32) for _ in range(tiles)]
    for s in range(samples):
        placed_ref[s * features : (s + 1) * features, :] = jnp.where(
            column % samples == s, second, 0.0
        ).astype(jnp.bfloat16)
    for copy in large:
        copy.wait()

    def normalise(s):
        pieces = []
        for low in range(0, residues, BLOCK):
            values = x_ref[s, low : low + BLOCK, :].astype(jnp.float32)
            center = jnp.mean(values, axis=-1, keepdims=True)
            values = values - center
            variance = jnp.mean(jnp.square(values), axis=-1, keepdims=True)
            values = values * lax.rsqrt(variance + 1e-05) * gain_ref[...] + shift_ref[...]
            pieces.append(values.astype(jnp.bfloat16))
        return jnp.concatenate(pieces, axis=0)

    def pack(s, t, left):
        left = jnp.where(own, left + first_offset, 0.0).astype(jnp.bfloat16)
        low = t * (tile // fold) * samples + s
        packed_ref[pl.ds(low, tile // fold, stride=samples), :] = jnp.dot(
            gather, left, preferred_element_type=jnp.float32
        )

    normed, lefts = {}, {}
    for step in range(samples + 2):
        s = step - 1
        if 0 <= s < samples:
            second_here = placed_ref[s * features : (s + 1) * features, :]
            parts = [normed[s][t * tile : (t + 1) * tile] for t in range(tiles)]
            lefts[s] = [jnp.dot(x, first, preferred_element_type=jnp.float32) for x in parts]
            right = [
                total + jnp.dot(x, second_here, preferred_element_type=jnp.float32)
                for total, x in zip(right, parts)
            ]
        if step < samples:
            normed[step] = normalise(step)
        if step >= 2:
            for t in range(tiles):
                pack(step - 2, t, lefts[step - 2][t])
    for t in range(tiles):
        value = (right[t].T + second_offset).astype(jnp.bfloat16)
        keep_ref[t * width : (t + 1) * width, :] = value
        give_ref[t * width : (t + 1) * width, :] = value
    device = lax.axis_index("row")
    per_chip = 2 * rows_here * hidden * samples // tile
    half = residues // rows_here // 4
    base = tiles * width
    way = 2 * (device % 2) - 1
    place = place_of(device, half)
    spots = [(keep_ref, base + n * per_chip, half - n) for n in range(half)]
    spots += [(give_ref, base + n * per_chip, n + 1 - half) for n in range(half)]
    for message, low, ahead in spots:
        chip = chip_at(lax.rem(place + way * ahead + 2 * half, 2 * half), half)
        across = tile // LANES
        start = pl.multiple_of(chip * per_chip * across, per_chip * across)
        block = packed_ref[pl.ds(start, per_chip * across), :]
        block = [block[n : n + samples] for n in range(0, per_chip * across, samples)]
        block = [jnp.concatenate(block[n : n + across], axis=1) for n in range(0, len(block), across)]
        message[low : low + per_chip, :] = jnp.concatenate(block, axis=0).astype(jnp.bfloat16)


def join_kernel(base, per_chip, mine_ref, theirs_ref, next_ref):
    next_ref[:base, :] = theirs_ref[:base, :]
    for n in range((next_ref.shape[0] - base) // (2 * per_chip)):
        low = base + n * per_chip
        at = low + n * per_chip
        next_ref[at : at + per_chip, :] = mine_ref[low + per_chip : low + 2 * per_chip, :]
        next_ref[at + per_chip : at + 2 * per_chip, :] = theirs_ref[low : low + per_chip, :]


def weight_kernel(final_ref, offset_ref, out_ref, offset_out, wide_ref):
    offset_out[...] = offset_ref[...]
    channels, columns = out_ref.shape
    hidden = math.isqrt(columns)
    wide_ref[: hidden * hidden, :] = final_ref[...].astype(jnp.float32)
    step = LANES // hidden
    for e in range(0, hidden, step):
        rows = [wide_ref[pl.ds(e + n, hidden, stride=hidden), :] for n in range(step)]
        out_ref[:, e * hidden : (e + step) * hidden] = jnp.concatenate(rows, axis=0).T.astype(
            jnp.bfloat16
        )


def pair_kernel(places, gridded, rows_here, hidden, samples, *refs):
    refs = list(refs)
    count = len(places)
    if gridded:
        shards = [(refs.pop(0), 0, refs.pop(0), 0) for _ in places]
    else:
        messages = [refs.pop(0) for _ in places]
        shards = [(messages[n], right, messages[m], left) for n, right, m, left in places]
    weight_ref, offset_ref, out_hbm, outer_ref, out_ref, sems = refs
    tile = shards[0][0].shape[1]
    here = samples // count
    span = rows_here * hidden
    deep = span * here // tile
    core = lax.rem(lax.axis_index("row"), 2)
    pieces = []
    for _, _, ref, base in shards:
        start = pl.multiple_of(base + core * deep, deep)
        piece = ref[pl.ds(start, deep), :].astype(jnp.float32)
        pieces.append(
            jnp.concatenate([piece[n * here : (n + 1) * here] for n in range(span // tile)], axis=1)
        )
    left = jnp.concatenate(pieces, axis=0).T.astype(jnp.bfloat16)

    for e in range(0, hidden, 2):
        both = [
            ref[base + e * here : base + (e + 2) * here, :].astype(jnp.float32)
            for ref, base, _, _ in shards
        ]
        for k in range(2):
            right = jnp.concatenate([x[k * here : (k + 1) * here] for x in both], axis=0)
            outer = jnp.dot(left, right.astype(jnp.bfloat16), preferred_element_type=jnp.float32)
            outer = outer.astype(jnp.bfloat16)
            for i in range(rows_here):
                outer_ref[i, (e + k) * hidden : (e + k + 1) * hidden, :] = outer[
                    i * hidden : (i + 1) * hidden
                ]

    first = pl.program_id(0) * tile if gridded else 0
    copies = []
    for i in range(rows_here):
        value = jnp.dot(weight_ref[...], outer_ref[i], preferred_element_type=jnp.float32)
        value = value.T * (1.0 / samples) + offset_ref[...]
        out_ref[i] = value.astype(jnp.bfloat16)
        if i % 2:
            rows = pl.ds(i - 1, 2)
            copies.append(
                pltpu.make_async_copy(
                    out_ref.at[rows], out_hbm.at[rows, pl.ds(first, tile)], sems.at[i // 2]
                )
            )
            copies[-1].start()
    for copy in copies:
        copy.wait()


def per_device(
    size,
    alignment_embedding,
    rescaling_factor,
    recentering_offset,
    first_side_coefficients,
    first_side_offset,
    second_side_coefficients,
    second_side_offset,
    final_projector_coefficients,
    final_projector_offset,
):
    here, residues, features = alignment_embedding.shape
    hidden = first_side_coefficients.shape[1]
    channels = final_projector_coefficients.shape[1]
    width = here * hidden
    samples = here * size
    rows_here = residues // size
    half = size // 4
    tile = 256
    tiles = residues // tile
    body = tiles * width
    per_chip = 2 * rows_here * width // tile

    def rows(count):
        return jax.ShapeDtypeStruct((count, tile), jnp.bfloat16)

    vmem = pl.BlockSpec(memory_space=pltpu.VMEM)
    hbm = pl.BlockSpec(memory_space=pltpu.HBM)
    keep, give = pl.pallas_call(
        functools.partial(project_kernel, rows_here),
        out_shape=[rows(body + half * per_chip)] * 2,
        in_specs=[hbm] * 7,
        out_specs=[vmem] * 2,
        scratch_shapes=[
            pltpu.VMEM((here, residues, features), jnp.bfloat16),
            pltpu.VMEM((1, features), jnp.float32),
            pltpu.VMEM((1, features), jnp.float32),
            pltpu.VMEM((hidden, features), jnp.bfloat16),
            pltpu.VMEM((1, hidden), jnp.float32),
            pltpu.VMEM((hidden, features), jnp.bfloat16),
            pltpu.VMEM((1, hidden), jnp.float32),
            pltpu.VMEM((residues * width // LANES + here, LANES), jnp.float32),
            pltpu.VMEM((here * features, width), jnp.bfloat16),
            pltpu.SemaphoreType.DMA((CHUNKS + 6,)),
        ],
        compiler_params=pltpu.CompilerParams(vmem_limit_bytes=32 * MIB),
        cost_estimate=pl.CostEstimate(
            flops=4 * here * residues * features * width,
            bytes_accessed=2 * here * residues * features,
            transcendentals=0,
        ),
    )(
        *[
            pltpu.with_memory_space_constraint(value, pltpu.HBM)
            for value in (
                alignment_embedding,
                rescaling_factor.reshape(1, features),
                recentering_offset.reshape(1, features),
                first_side_coefficients.T,
                first_side_offset.reshape(1, hidden),
                second_side_coefficients.T,
                second_side_offset.reshape(1, hidden),
            )
        ]
    )
    by_place = {(place_of(r, half), r % 2): r for r in range(size)}
    around = [
        (r, by_place[(place_of(r, half) + 2 * (r % 2) - 1) % (2 * half), r % 2]) for r in range(size)
    ]

    def swap(value):
        return lax.ppermute(value, "row", [(r, r ^ 1) for r in range(size)])

    weight, offset = pl.pallas_call(
        weight_kernel,
        out_shape=[
            jax.ShapeDtypeStruct((channels, hidden * hidden), jnp.bfloat16),
            jax.ShapeDtypeStruct((1, channels), jnp.float32),
        ],
        in_specs=[vmem] * 2,
        out_specs=[vmem] * 2,
        scratch_shapes=[pltpu.VMEM(((hidden + 1) * hidden, channels), jnp.float32)],
        compiler_params=pltpu.CompilerParams(vmem_limit_bytes=16 * MIB),
        cost_estimate=pl.CostEstimate(flops=2**28, bytes_accessed=2**20, transcendentals=0),
    )(final_projector_coefficients, final_projector_offset.reshape(1, channels))
    theirs, weight, offset = lax.optimization_barrier((swap(give), weight, offset))
    messages = [give, theirs]
    places = [(n, 0, n, body + (half - 1) * per_chip) for n in range(2)]

    def take(*lefts):
        places.extend((len(messages) + n, 0, len(messages) + m, low) for n, (m, low) in enumerate(lefts))

    flying = [keep, theirs[: body + (half - 1) * per_chip]]
    swapped, lefts = [], []
    for step in range(1, half + 1):
        landed = [lax.ppermute(x, "row", around) for x in flying]
        if step >= 3:
            landed[-1], swapped[step - 3] = lax.optimization_barrier((landed[-1], swapped[step - 3]))
        low = [x.shape[0] - per_chip for x in landed]
        if step == 1:
            lefts.append([(0, low[0]), (1, low[1])])
        elif step < half:
            lefts.append([(1, low[1] - per_chip), (1, low[1])])
        else:
            lefts.append([(0, low[0])])
        flying = [landed[0][: body + per_chip]]
        if step == 1:
            flying += pl.pallas_call(
                functools.partial(join_kernel, body, per_chip),
                out_shape=[rows(body + 2 * (half - 2) * per_chip)],
                in_specs=[vmem] * 2,
                out_specs=[vmem],
                compiler_params=pltpu.CompilerParams(vmem_limit_bytes=16 * MIB),
                cost_estimate=pl.CostEstimate(flops=0, bytes_accessed=2**19, transcendentals=0),
            )(*landed)
        elif step < half - 1:
            flying.append(landed[1][: landed[1].shape[0] - 2 * per_chip])
        landed = lax.optimization_barrier(landed)
        take(*lefts[-1])
        messages += landed
        swapped.append([swap(x) for x in landed])
    for pair, left in zip(swapped, lefts):
        take(*left)
        messages += pair

    gridded = tiles > 1
    if gridded:
        operands, specs = [], []
        for n, right, m, left in places:
            operands += [messages[n], messages[m]]
            specs += [
                pl.BlockSpec((width, tile), lambda t, first=right // width: (first + t, 0)),
                pl.BlockSpec((per_chip, tile), lambda t, at=left // per_chip: (at, 0)),
            ]
        specs += [
            pl.BlockSpec((channels, hidden * hidden), lambda t: (0, 0)),
            pl.BlockSpec((1, channels), lambda t: (0, 0)),
        ]
        grid = (tiles,)
    else:
        operands = messages
        specs = [vmem] * (len(messages) + 2)
        grid = ()
    return pl.pallas_call(
        functools.partial(pair_kernel, places, gridded, rows_here, hidden, samples),
        out_shape=jax.ShapeDtypeStruct((rows_here, residues, channels), jnp.bfloat16),
        grid=grid,
        in_specs=specs,
        out_specs=hbm,
        scratch_shapes=[
            pltpu.VMEM((rows_here, hidden * hidden, tile), jnp.bfloat16),
            pltpu.VMEM((rows_here, tile, channels), jnp.bfloat16),
            pltpu.SemaphoreType.DMA((rows_here,)),
        ],
        compiler_params=pltpu.CompilerParams(vmem_limit_bytes=40 * MIB),
    )(*operands, weight, offset)


def solution(mesh):
    return jax.shard_map(
        functools.partial(per_device, mesh.shape["row"]),
        mesh=mesh,
        in_specs=(P(("groups", "row"), None, None), P(), P(), P(), P(), P(), P(), P(), P()),
        out_specs=P(("groups", "row"), None, None),
        check_vma=False,
    )
```

```python
import functools
import math

import jax
import jax.numpy as jnp
from jax import lax
from jax.experimental import pallas as pl
from jax.experimental.pallas import tpu as pltpu
from jax.sharding import PartitionSpec as P

MIB = 1024 * 1024
LANES = 128
CHUNKS = 2
BLOCK = 64


def repeat_rows(values, times):
    rows, cols = values.shape
    return jnp.broadcast_to(values[:, None, :], (rows, times, cols)).reshape(rows * times, cols)


def place_of(device, half):
    chip = device // 2
    return chip // 2 + (chip % 2) * (2 * half - 1 - 2 * (chip // 2))


def chip_at(place, half):
    return jnp.where(place < half, 2 * place, 2 * (2 * half - 1 - place) + 1)


def project_kernel(
    rows_here,
    x_hbm,
    gain_hbm,
    shift_hbm,
    first_hbm,
    first_offset_hbm,
    second_hbm,
    second_offset_hbm,
    keep_ref,
    give_ref,
    x_ref,
    gain_ref,
    shift_ref,
    first_ref,
    first_offset_ref,
    second_ref,
    second_offset_ref,
    packed_ref,
    sems,
):
    samples, residues, features = x_ref.shape
    hidden = first_ref.shape[0]
    width = samples * hidden
    tile = keep_ref.shape[1]
    tiles = residues // tile
    fold = LANES // hidden
    small = [
        (first_hbm, first_ref),
        (second_hbm, second_ref),
        (gain_hbm, gain_ref),
        (shift_hbm, shift_ref),
        (first_offset_hbm, first_offset_ref),
        (second_offset_hbm, second_offset_ref),
    ]
    some = samples // CHUNKS
    copies = [
        pltpu.make_async_copy(src, dst, sems.at[CHUNKS + n]) for n, (src, dst) in enumerate(small)
    ]
    for copy in copies:
        copy.start()
    large = []
    for n in range(CHUNKS):
        rows = pl.ds(n * some, some)
        large.append(pltpu.make_async_copy(x_hbm.at[rows], x_ref.at[rows], sems.at[n]))
        large[-1].start()
    for copy in copies:
        copy.wait()

    first = jnp.concatenate([first_ref[...].astype(jnp.float32)] * fold, axis=0).T
    first = first.astype(jnp.bfloat16)
    first_offset = jnp.concatenate([first_offset_ref[...]] * fold, axis=1)
    second = repeat_rows(second_ref[...].astype(jnp.float32), samples).T
    column = lax.broadcasted_iota(jnp.int32, (1, width), 1)
    spot = lax.broadcasted_iota(jnp.int32, (width, hidden), 0)
    channel = lax.broadcasted_iota(jnp.int32, (width, hidden), 1)
    second_offset = jnp.sum(
        jnp.where(spot // samples == channel, second_offset_ref[...], 0.0), axis=1, keepdims=True
    )
    residue = lax.broadcasted_iota(jnp.int32, (tile, LANES), 0)
    lane = lax.broadcasted_iota(jnp.int32, (tile, LANES), 1)
    own = residue % fold == lane // hidden
    group = lax.broadcasted_iota(jnp.int32, (tile // fold, tile), 0)
    member = lax.broadcasted_iota(jnp.int32, (tile // fold, tile), 1)
    gather = (member // fold == group).astype(jnp.bfloat16)

    right = [jnp.zeros((tile, width), jnp.float32) for _ in range(tiles)]
    def normalise(s):
        pieces = []
        for low in range(0, residues, BLOCK):
            values = x_ref[s, low : low + BLOCK, :].astype(jnp.float32)
            center = jnp.mean(values, axis=-1, keepdims=True)
            values = values - center
            variance = jnp.mean(jnp.square(values), axis=-1, keepdims=True)
            values = values * lax.rsqrt(variance + 1e-05) * gain_ref[...] + shift_ref[...]
            pieces.append(values.astype(jnp.bfloat16))
        return jnp.concatenate(pieces, axis=0)

    def pack(s, t, left):
        left = jnp.where(own, left + first_offset, 0.0).astype(jnp.bfloat16)
        low = t * (tile // fold) * samples + s
        packed_ref[pl.ds(low, tile // fold, stride=samples), :] = jnp.dot(
            gather, left, preferred_element_type=jnp.float32
        )

    normed, lefts = {}, {}
    for step in range(samples + 2):
        s = step - 1
        if 0 <= s < samples:
            second_here = jnp.where(column % samples == s, second, 0.0).astype(jnp.bfloat16)
            parts = [normed[s][t * tile : (t + 1) * tile] for t in range(tiles)]
            lefts[s] = [jnp.dot(x, first, preferred_element_type=jnp.float32) for x in parts]
            right = [
                total + jnp.dot(x, second_here, preferred_element_type=jnp.float32)
                for total, x in zip(right, parts)
            ]
        if step < samples:
            if step % some == 0:
                large[step // some].wait()
            normed[step] = normalise(step)
        if step >= 2:
            for t in range(tiles):
                pack(step - 2, t, lefts[step - 2][t])
    for t in range(tiles):
        value = (right[t].T + second_offset).astype(jnp.bfloat16)
        keep_ref[t * width : (t + 1) * width, :] = value
        give_ref[t * width : (t + 1) * width, :] = value
    device = lax.axis_index("row")
    per_chip = 2 * rows_here * hidden * samples // tile
    half = residues // rows_here // 4
    base = tiles * width
    way = 2 * (device % 2) - 1
    place = place_of(device, half)
    spots = [(keep_ref, base + n * per_chip, half - n) for n in range(half)]
    spots += [(give_ref, base + n * per_chip, n + 1 - half) for n in range(half)]
    for message, low, ahead in spots:
        chip = chip_at(lax.rem(place + way * ahead + 2 * half, 2 * half), half)
        across = tile // LANES
        start = pl.multiple_of(chip * per_chip * across, per_chip * across)
        block = packed_ref[pl.ds(start, per_chip * across), :]
        block = [block[n : n + samples] for n in range(0, per_chip * across, samples)]
        block = [jnp.concatenate(block[n : n + across], axis=1) for n in range(0, len(block), across)]
        message[low : low + per_chip, :] = jnp.concatenate(block, axis=0).astype(jnp.bfloat16)


def join_kernel(base, per_chip, mine_ref, theirs_ref, next_ref):
    next_ref[:base, :] = theirs_ref[:base, :]
    for n in range((next_ref.shape[0] - base) // (2 * per_chip)):
        low = base + n * per_chip
        at = low + n * per_chip
        next_ref[at : at + per_chip, :] = mine_ref[low + per_chip : low + 2 * per_chip, :]
        next_ref[at + per_chip : at + 2 * per_chip, :] = theirs_ref[low : low + per_chip, :]


def weight_kernel(final_ref, offset_ref, out_ref, offset_out, wide_ref):
    offset_out[...] = offset_ref[...]
    channels, columns = out_ref.shape
    hidden = math.isqrt(columns)
    wide_ref[: hidden * hidden, :] = final_ref[...].astype(jnp.float32)
    step = LANES // hidden
    for e in range(0, hidden, step):
        rows = [wide_ref[pl.ds(e + n, hidden, stride=hidden), :] for n in range(step)]
        out_ref[:, e * hidden : (e + step) * hidden] = jnp.concatenate(rows, axis=0).T.astype(
            jnp.bfloat16
        )


def pair_kernel(places, gridded, rows_here, hidden, samples, *refs):
    refs = list(refs)
    count = len(places)
    if gridded:
        shards = [(refs.pop(0), 0, refs.pop(0), 0) for _ in places]
    else:
        messages = [refs.pop(0) for _ in places]
        shards = [(messages[n], right, messages[m], left) for n, right, m, left in places]
    weight_ref, offset_ref, out_hbm, left_ref, outer_ref, out_ref, sems = refs
    tile = shards[0][0].shape[1]
    here = samples // count
    span = rows_here * hidden
    deep = span * here // tile
    core = lax.rem(lax.axis_index("row"), 2)
    pieces = []
    for _, _, ref, base in shards:
        start = pl.multiple_of(base + core * deep, deep)
        piece = ref[pl.ds(start, deep), :].astype(jnp.float32)
        pieces.append(
            jnp.concatenate([piece[n * here : (n + 1) * here] for n in range(span // tile)], axis=1)
        )
    left_ref[...] = jnp.concatenate(pieces, axis=0).T.astype(jnp.bfloat16)

    left = left_ref[...]
    for e in range(0, hidden, 2):
        both = [
            ref[base + e * here : base + (e + 2) * here, :].astype(jnp.float32)
            for ref, base, _, _ in shards
        ]
        for k in range(2):
            right = jnp.concatenate([x[k * here : (k + 1) * here] for x in both], axis=0)
            outer = jnp.dot(left, right.astype(jnp.bfloat16), preferred_element_type=jnp.float32)
            outer = outer.astype(jnp.bfloat16)
            for i in range(rows_here):
                outer_ref[i, (e + k) * hidden : (e + k + 1) * hidden, :] = outer[
                    i * hidden : (i + 1) * hidden
                ]

    first = pl.program_id(0) * tile if gridded else 0
    copies = []
    for i in range(rows_here):
        value = jnp.dot(weight_ref[...], outer_ref[i], preferred_element_type=jnp.float32)
        value = value.T * (1.0 / samples) + offset_ref[...]
        out_ref[i] = value.astype(jnp.bfloat16)
        copies.append(
            pltpu.make_async_copy(out_ref.at[i], out_hbm.at[i, pl.ds(first, tile)], sems.at[i])
        )
        copies[-1].start()
    for copy in copies:
        copy.wait()


def per_device(
    size,
    alignment_embedding,
    rescaling_factor,
    recentering_offset,
    first_side_coefficients,
    first_side_offset,
    second_side_coefficients,
    second_side_offset,
    final_projector_coefficients,
    final_projector_offset,
):
    here, residues, features = alignment_embedding.shape
    hidden = first_side_coefficients.shape[1]
    channels = final_projector_coefficients.shape[1]
    width = here * hidden
    samples = here * size
    rows_here = residues // size
    half = size // 4
    tile = 256
    tiles = residues // tile
    body = tiles * width
    per_chip = 2 * rows_here * width // tile

    def rows(count):
        return jax.ShapeDtypeStruct((count, tile), jnp.bfloat16)

    vmem = pl.BlockSpec(memory_space=pltpu.VMEM)
    hbm = pl.BlockSpec(memory_space=pltpu.HBM)
    keep, give = pl.pallas_call(
        functools.partial(project_kernel, rows_here),
        out_shape=[rows(body + half * per_chip)] * 2,
        in_specs=[hbm] * 7,
        out_specs=[vmem] * 2,
        scratch_shapes=[
            pltpu.VMEM((here, residues, features), jnp.bfloat16),
            pltpu.VMEM((1, features), jnp.float32),
            pltpu.VMEM((1, features), jnp.float32),
            pltpu.VMEM((hidden, features), jnp.bfloat16),
            pltpu.VMEM((1, hidden), jnp.float32),
            pltpu.VMEM((hidden, features), jnp.bfloat16),
            pltpu.VMEM((1, hidden), jnp.float32),
            pltpu.VMEM((residues * width // LANES + here, LANES), jnp.float32),
            pltpu.SemaphoreType.DMA((CHUNKS + 6,)),
        ],
        compiler_params=pltpu.CompilerParams(vmem_limit_bytes=32 * MIB),
        cost_estimate=pl.CostEstimate(
            flops=4 * here * residues * features * width,
            bytes_accessed=2 * here * residues * features,
            transcendentals=0,
        ),
    )(
        *[
            pltpu.with_memory_space_constraint(value, pltpu.HBM)
            for value in (
                alignment_embedding,
                rescaling_factor.reshape(1, features),
                recentering_offset.reshape(1, features),
                first_side_coefficients.T,
                first_side_offset.reshape(1, hidden),
                second_side_coefficients.T,
                second_side_offset.reshape(1, hidden),
            )
        ]
    )
    by_place = {(place_of(r, half), r % 2): r for r in range(size)}
    around = [
        (r, by_place[(place_of(r, half) + 2 * (r % 2) - 1) % (2 * half), r % 2]) for r in range(size)
    ]

    def swap(value):
        return lax.ppermute(value, "row", [(r, r ^ 1) for r in range(size)])

    weight, offset = pl.pallas_call(
        weight_kernel,
        out_shape=[
            jax.ShapeDtypeStruct((channels, hidden * hidden), jnp.bfloat16),
            jax.ShapeDtypeStruct((1, channels), jnp.float32),
        ],
        in_specs=[vmem] * 2,
        out_specs=[vmem] * 2,
        scratch_shapes=[pltpu.VMEM(((hidden + 1) * hidden, channels), jnp.float32)],
        compiler_params=pltpu.CompilerParams(vmem_limit_bytes=16 * MIB),
        cost_estimate=pl.CostEstimate(flops=2**28, bytes_accessed=2**20, transcendentals=0),
    )(final_projector_coefficients, final_projector_offset.reshape(1, channels))
    theirs, weight, offset = lax.optimization_barrier((swap(give), weight, offset))
    messages = [give, theirs]
    places = [(n, 0, n, body + (half - 1) * per_chip) for n in range(2)]

    def take(*lefts):
        places.extend((len(messages) + n, 0, len(messages) + m, low) for n, (m, low) in enumerate(lefts))

    flying = [keep, theirs[: body + (half - 1) * per_chip]]
    swapped, lefts = [], []
    for step in range(1, half + 1):
        landed = [lax.ppermute(x, "row", around) for x in flying]
        if step >= 3:
            landed[-1], swapped[step - 3] = lax.optimization_barrier((landed[-1], swapped[step - 3]))
        low = [x.shape[0] - per_chip for x in landed]
        if step == 1:
            lefts.append([(0, low[0]), (1, low[1])])
        elif step < half:
            lefts.append([(1, low[1] - per_chip), (1, low[1])])
        else:
            lefts.append([(0, low[0])])
        flying = [landed[0][: body + per_chip]]
        if step == 1:
            flying += pl.pallas_call(
                functools.partial(join_kernel, body, per_chip),
                out_shape=[rows(body + 2 * (half - 2) * per_chip)],
                in_specs=[vmem] * 2,
                out_specs=[vmem],
                compiler_params=pltpu.CompilerParams(vmem_limit_bytes=16 * MIB),
                cost_estimate=pl.CostEstimate(flops=0, bytes_accessed=2**19, transcendentals=0),
            )(*landed)
        elif step < half - 1:
            flying.append(landed[1][: landed[1].shape[0] - 2 * per_chip])
        landed = lax.optimization_barrier(landed)
        take(*lefts[-1])
        messages += landed
        swapped.append([swap(x) for x in landed])
    for pair, left in zip(swapped, lefts):
        take(*left)
        messages += pair

    gridded = tiles > 1
    if gridded:
        operands, specs = [], []
        for n, right, m, left in places:
            operands += [messages[n], messages[m]]
            specs += [
                pl.BlockSpec((width, tile), lambda t, first=right // width: (first + t, 0)),
                pl.BlockSpec((per_chip, tile), lambda t, at=left // per_chip: (at, 0)),
            ]
        specs += [
            pl.BlockSpec((channels, hidden * hidden), lambda t: (0, 0)),
            pl.BlockSpec((1, channels), lambda t: (0, 0)),
        ]
        grid = (tiles,)
    else:
        operands = messages
        specs = [vmem] * (len(messages) + 2)
        grid = ()
    return pl.pallas_call(
        functools.partial(pair_kernel, places, gridded, rows_here, hidden, samples),
        out_shape=jax.ShapeDtypeStruct((rows_here, residues, channels), jnp.bfloat16),
        grid=grid,
        in_specs=specs,
        out_specs=hbm,
        scratch_shapes=[
            pltpu.VMEM((rows_here * hidden, samples), jnp.bfloat16),
            pltpu.VMEM((rows_here, hidden * hidden, tile), jnp.bfloat16),
            pltpu.VMEM((rows_here, tile, channels), jnp.bfloat16),
            pltpu.SemaphoreType.DMA((rows_here,)),
        ],
        compiler_params=pltpu.CompilerParams(vmem_limit_bytes=40 * MIB),
    )(*operands, weight, offset)


def solution(mesh):
    return jax.shard_map(
        functools.partial(per_device, mesh.shape["row"]),
        mesh=mesh,
        in_specs=(P(("groups", "row"), None, None), P(), P(), P(), P(), P(), P(), P(), P()),
        out_specs=P(("groups", "row"), None, None),
        check_vma=False,
    )
```
